128 devices in a mesh: ep: 32 (over x, z, core), tp: 4 (over y).
Axes of the slice: x: 4, y: 4, z: 4, core: 2. Of those that a mesh axis runs over, the one named last changes fastest.
Arguments:
- inputs: bfloat16 [32768, 1024], P(('ep', 'tp')), may hold values from -6 to 6
- first_gain: bfloat16 [1024], replicated, may hold values from 0.25 to 1.75
- query_weight: bfloat16 [1024, 1024], P(None, 'tp'), may hold values from -0.1875 to 0.1875
- key_weight: bfloat16 [1024, 512], P(None, 'tp'), may hold values from -0.1875 to 0.1875
- value_weight: bfloat16 [1024, 512], P(None, 'tp'), may hold values from -0.1875 to 0.1875
- query_gain: bfloat16 [64], replicated, may hold values from 0.25 to 1.75
- key_gain: bfloat16 [64], replicated, may hold values from 0.25 to 1.75
- output_weight: bfloat16 [1024, 1024], P('tp'), may hold values from -1.5 to 1.5
- second_gain: bfloat16 [1024], replicated, may hold values from 0.25 to 1.75
- router_weight: bfloat16 [1024, 32], replicated, may hold values from -0.09375 to 0.09375
- gate_weight: bfloat16 [32, 1024, 512], P('ep', None, 'tp'), may hold values from -0.1875 to 0.1875
- up_weight: bfloat16 [32, 1024, 512], P('ep', None, 'tp'), may hold values from -0.1875 to 0.1875
- down_weight: bfloat16 [32, 512, 1024], P('ep', 'tp'), may hold values from -1 to 1
- segments: int32 [32768], P('ep'), may hold values from 0 to 2, as said below
- live_mask: int32 [32768], P('ep'), may hold values from 0 to 1, as said below
- routes: int32 [32768, 8], P(('ep', 'tp')), may hold values from 0 to 31, all different within a row; in each aligned block of 256 rows (0 to 255, 256 to 511, ...) at most 96 rows name the same one
- cotangent: bfloat16 [32768, 1024], P(('ep', 'tp')), may hold values from -6 to 6
Outputs:
- result: bfloat16 [32768, 1024], P(('ep', 'tp'))
- grad_inputs: bfloat16 [32768, 1024], P(('ep', 'tp'))
- grad_first_gain: float32 [1024], replicated
- grad_query_weight: float32 [1024, 1024], P(None, 'tp')
- grad_key_weight: float32 [1024, 512], P(None, 'tp')
- grad_value_weight: float32 [1024, 512], P(None, 'tp')
- grad_query_gain: float32 [64], replicated
- grad_key_gain: float32 [64], replicated
- grad_output_weight: float32 [1024, 1024], P('tp')
- grad_second_gain: float32 [1024], replicated
- grad_router_weight: float32 [1024, 32], replicated
- grad_gate_weight: float32 [32, 1024, 512], P('ep', None, 'tp')
- grad_up_weight: float32 [32, 1024, 512], P('ep', None, 'tp')
- grad_down_weight: float32 [32, 512, 1024], P('ep', 'tp')
The draws below stay inside these ranges and needn't reach their ends.
Inputs may be any that keep to these rules, and one draw needn't show every extreme that they name: `segments`: in each sequence of 1024 tokens the numbers never fall and mark three documents 0, 1, 2; document 1 holds 800 tokens and begins within the first eighth. `live_mask`: in each sequence the zeros form a tail inside document 2, which keeps live tokens. `routes`: A token's 8 experts are distinct; in the rows of one device (aligned blocks of 256 tokens) no expert is named by more than 96 tokens, a bound that some block reaches.
All inputs are finite; a program needn't handle non-finite values.
Results may differ from the reference program's by a relative error of at most 0.025.
Values may be sent and summed in bfloat16 or wider, within the bound.
A program may use at most 192 MiB of HBM per device.

```python
import math
import jax
import jax.numpy as jnp
import numpy as np
from jax import lax

D = 1024
HEADS = 16
KV_HEADS = 8
HEAD_DIM = 64
FF = 512
TOPK = 8
SEQ_LEN = 1024
EXPERTS = 32
TOKENS = 32768
ROWS_DEV = 256
CAP = 96


def layout(key):
    sequences = TOKENS // SEQ_LEN
    keys_all = jax.random.split(key, sequences)

    def one_sequence(seq_key):
        first_key, second_key = jax.random.split(seq_key)
        first_len = jax.random.randint(first_key, (), SEQ_LEN // 16, SEQ_LEN // 8 + 1)
        middle_len = SEQ_LEN * 25 // 32
        remaining = SEQ_LEN - first_len - middle_len
        padding = jax.random.randint(second_key, (), SEQ_LEN // 256 + 1, remaining - SEQ_LEN // 16 + 1)
        position = jnp.arange(SEQ_LEN)
        numbers = (position >= first_len).astype(jnp.int32) + (position >= first_len + middle_len).astype(jnp.int32)
        living = (position < SEQ_LEN - padding).astype(jnp.int32)
        return (numbers, living)
    numbers, living = jax.vmap(one_sequence)(keys_all)
    return (numbers.reshape(-1), living.reshape(-1))


def draw_segments(key, part):
    numbers, living = layout(key)
    return numbers


def draw_live_mask(key, part):
    numbers, living = layout(key)
    return living


def levels(stream_key, extent, shards, least, high):
    loudness = 1.0
    for dim, parts in shards:
        heights = jax.random.uniform(jax.random.fold_in(jax.random.fold_in(stream_key, 6), dim), (parts,), jnp.float32, least / len(shards), high / len(shards))
        loudness = loudness * jnp.repeat(jnp.exp(heights), extent[dim] // parts).reshape((-1,) + (1,) * (len(extent) - 1 - dim))
    return loudness


def deal_out(key, own, number, rows, number_of, top, reach, lean):
    order = jax.random.permutation(key, number_of)
    heavy_load, common = shares(number_of, rows * top, reach, lean, True), shares(number_of, rows * top, reach, lean, False)
    places = jnp.arange(number_of)

    def named(lengths, offset_by):
        used = int((lengths > 0).sum())
        fixed = max(1, used // 4)
        moved = fixed + (places - fixed + offset_by * (used - fixed)) % max(1, number_of - fixed)
        return jnp.zeros((number_of,), jnp.int32).at[order[jnp.where(places < fixed, places, moved)]].set(jnp.asarray(lengths, jnp.int32))

    lengths = jnp.where(number % 4 == 0, named(heavy_load, number // 4), named(common, number - number // 4 - 1))
    mixed = jax.random.permutation(jax.random.fold_in(own, 3), number_of)
    donor, sink = mixed[0:number_of // 2 * 2:2], mixed[1:number_of // 2 * 2:2]
    margin = jnp.minimum(lengths[donor] - 1, reach - lengths[sink]) // 2
    margin = jnp.where((donor == order[0]) | (sink == order[0]) | (lengths[sink] == 0), 0, jnp.maximum(margin, 0))
    moved = jax.random.randint(jax.random.fold_in(own, 4), (number_of // 2,), 0, 1 << 20) % (margin + 1)
    lengths = lengths.at[donor].add(-moved).at[sink].add(moved)
    labels = jnp.searchsorted(jnp.cumsum(lengths), jnp.arange(rows * top), side="right").astype(jnp.int32)
    grid = labels.reshape(top, rows).T
    grid = grid[jax.random.permutation(jax.random.fold_in(own, 1), rows)]
    offset_by = jax.random.randint(jax.random.fold_in(own, 2), (rows, 1), 0, top)
    return jnp.take_along_axis(grid, (jnp.arange(top)[None, :] + offset_by) % top, axis=1)


def shares(amount, total, reach, slope, full):
    portions = [(1 << 20) // math.isqrt(rank ** slope) + 1 for rank in range(1, amount + 1)]
    largest = reach if full else min(reach, max(-(-total // amount), total * portions[0] // sum(portions)))
    least = 1 if total - largest >= amount - 1 else 0
    holding, rest = [largest] + [least] * (amount - 1), total - largest - least * (amount - 1)
    while rest > 0:
        candidates = [i for i in range(1, amount) if holding[i] < largest] or [i for i in range(1, amount) if holding[i] < reach]
        mass, budget = sum([portions[i] for i in candidates]), rest
        for i in candidates:
            more = min(reach - holding[i], max(1, budget * portions[i] // mass), rest)
            holding[i] = holding[i] + more
            rest = rest - more
    return np.array(holding)


def gaussian(own_key, shape, scale, most, cuts=(), kind=jnp.bfloat16):
    level = levels(own_key, shape, cuts, -0.22, 0.18) if cuts else 1.0
    entries = jax.random.normal(own_key, shape, jnp.float32) * scale * level
    return jnp.minimum(jnp.maximum(entries, -most), most).astype(kind)


def setup_inputs(seed: int = 0) -> dict:
    key_list = jax.random.split(jax.random.key(seed), 18)
    inputs = gaussian(key_list[0], (TOKENS, D), 1.0, 6.0, ((0, 128),))
    first_gain = jnp.clip(1.0 + 0.15 * jax.random.normal(key_list[1], (D,), jnp.float32), 0.25, 1.75).astype(jnp.bfloat16)
    query_weight = gaussian(key_list[2], (D, HEADS * HEAD_DIM), D ** -0.5, 0.1875, ((1, 4),))
    key_weight = gaussian(key_list[3], (D, KV_HEADS * HEAD_DIM), D ** -0.5, 0.1875, ((1, 4),))
    value_weight = gaussian(key_list[4], (D, KV_HEADS * HEAD_DIM), D ** -0.5, 0.1875, ((1, 4),))
    query_gain = jnp.clip(1.0 + 0.15 * jax.random.normal(key_list[5], (HEAD_DIM,), jnp.float32), 0.25, 1.75).astype(jnp.bfloat16)
    key_gain = jnp.clip(1.0 + 0.15 * jax.random.normal(key_list[6], (HEAD_DIM,), jnp.float32), 0.25, 1.75).astype(jnp.bfloat16)
    output_weight = gaussian(key_list[7], (HEADS * HEAD_DIM, D), (HEADS * HEAD_DIM // 64) ** -0.5, 1.5, ((0, 4),))
    second_gain = jnp.clip(1.0 + 0.15 * jax.random.normal(key_list[8], (D,), jnp.float32), 0.25, 1.75).astype(jnp.bfloat16)
    router_weight = gaussian(key_list[9], (D, EXPERTS), (4 * D) ** -0.5, 0.09375)
    gate_weight = gaussian(key_list[10], (EXPERTS, D, FF), D ** -0.5, 0.1875, ((0, 32), (2, 4)))
    up_weight = gaussian(key_list[11], (EXPERTS, D, FF), D ** -0.5, 0.1875, ((0, 32), (2, 4)))
    down_weight = gaussian(key_list[12], (EXPERTS, FF, D), (FF // 16) ** -0.5, 1.0, ((0, 32), (1, 4)))
    segments = draw_segments(jax.random.fold_in(key_list[17], 71), 0)
    live_mask = draw_live_mask(jax.random.fold_in(key_list[17], 71), 0)
    routes_keys = jax.random.split(jax.random.fold_in(key_list[15], 1), TOKENS // ROWS_DEV)
    routes_turns = jax.random.permutation(jax.random.fold_in(key_list[15], 3), TOKENS // ROWS_DEV)
    routes = jax.vmap(lambda own, number: deal_out(jax.random.fold_in(key_list[15], 2), own, number, ROWS_DEV, EXPERTS, TOPK, CAP, 1))(routes_keys, routes_turns).reshape((TOKENS, TOPK))
    cotangent = gaussian(key_list[16], (TOKENS, D), 1.0, 6.0, ((0, 128),))
    return dict(inputs=inputs, first_gain=first_gain, query_weight=query_weight, key_weight=key_weight, value_weight=value_weight, query_gain=query_gain, key_gain=key_gain, output_weight=output_weight, second_gain=second_gain, router_weight=router_weight, gate_weight=gate_weight, up_weight=up_weight, down_weight=down_weight, segments=segments, live_mask=live_mask, routes=routes, cotangent=cotangent)


HIGHEST_PRECISION = lax.Precision.HIGHEST

@jax.custom_vjp
def low(v):
    return lax.optimization_barrier(v.astype(jnp.bfloat16)).astype(jnp.float32)

@jax.custom_vjp
def low_back(v):
    return v

def low_keep(v):
    return (low(v), None)

def low_pass(kept, grad):
    return (grad,)

def back_keep(v):
    return (v, None)

def back_low(kept, grad):
    return (low(grad),)
low.defvjp(low_keep, low_pass)
low_back.defvjp(back_keep, back_low)

def norm_rows(values, gain_vec, epsilon):
    return values * lax.rsqrt(lax.optimization_barrier(jnp.mean(values * values, axis=-1, keepdims=True)) + epsilon) * gain_vec

def softmax_rows(values):
    shifted = jnp.exp(values - lax.optimization_barrier(jnp.max(values, axis=-1, keepdims=True)))
    return shifted / lax.optimization_barrier(jnp.sum(shifted, axis=-1, keepdims=True))

def silu_values(values):
    return values * jax.nn.sigmoid(values)

def rotate(values, cosine_table, sine_table):
    half_dim = values.shape[-1] // 2
    first_half = values[..., :half_dim]
    second_half = values[..., half_dim:]
    return jnp.concatenate([first_half * cosine_table - second_half * sine_table, second_half * cosine_table + first_half * sine_table], axis=-1)

def rotary_tables():
    half_dim = HEAD_DIM // 2
    position = jnp.arange(SEQ_LEN).astype(jnp.float32)
    frequency = 10000.0 ** (-(jnp.arange(half_dim).astype(jnp.float32) * 2.0) / HEAD_DIM)
    angles = position[:, None] * frequency[None, :]
    return (jnp.cos(angles)[:, None, :], jnp.sin(angles)[:, None, :])

def slot_table(routes):
    sources = TOKENS // ROWS_DEV
    flat_routes = routes.reshape(sources, ROWS_DEV * TOPK)
    onehot_int = (flat_routes[:, :, None] == jnp.arange(EXPERTS, dtype=jnp.int32)[None, None, :]).astype(jnp.int32)
    slot_index = lax.optimization_barrier(jnp.sum(jnp.cumsum(onehot_int, axis=1) * onehot_int, axis=-1)) - 1
    column = jnp.arange(sources, dtype=jnp.int32)[:, None] * CAP + slot_index
    copy_ids = jnp.arange(TOKENS * TOPK, dtype=jnp.int32).reshape(sources, ROWS_DEV * TOPK)
    empty_table = jnp.full((EXPERTS, sources * CAP), TOKENS * TOPK, dtype=jnp.int32)
    return empty_table.at[flat_routes, column].set(copy_ids)

def attend(pieces):
    query, keys, values, segment_ids, live_ids = pieces
    length = query.shape[0]
    query_heads = query.reshape(length, KV_HEADS, HEADS // KV_HEADS, HEAD_DIM)
    key_heads = keys.reshape(length, KV_HEADS, HEAD_DIM)
    value_heads = values.reshape(length, KV_HEADS, HEAD_DIM)
    scores = jnp.einsum('qgrd,kgd->grqk', query_heads, key_heads, precision=HIGHEST_PRECISION) * HEAD_DIM ** (-0.5)
    scores = low_back(scores)
    positions = jnp.arange(length)
    allowed = (segment_ids[:, None] == segment_ids[None, :]) & ((live_ids[None, :] == 1) | (positions[:, None] == positions[None, :]))
    scores = jnp.where(allowed[None, None], scores, -1e+30)
    weights = low(softmax_rows(scores))
    mixed_heads = jnp.einsum('grqk,kgd->qgrd', weights, value_heads, precision=HIGHEST_PRECISION)
    return mixed_heads.reshape(length, HEADS * HEAD_DIM)

def forward(hidden, first_gain, query_weight, key_weight, value_weight, query_gain, key_gain, output_weight, second_gain, router_weight, gate_weight, up_weight, down_weight, segments, live_mask, routes, table):
    sequences = TOKENS // SEQ_LEN
    normed_one = low(norm_rows(hidden, first_gain, 1e-05))
    query_raw = low_back(jnp.dot(normed_one, query_weight, precision=HIGHEST_PRECISION))
    key_raw = low_back(jnp.dot(normed_one, key_weight, precision=HIGHEST_PRECISION))
    value_raw = low_back(jnp.dot(normed_one, value_weight, precision=HIGHEST_PRECISION))
    cosine_table, sine_table = rotary_tables()

    def heads_ready(raw_values, gain_vec, head_count):
        shaped = raw_values.reshape(sequences, SEQ_LEN, head_count, HEAD_DIM)
        turned = rotate(norm_rows(shaped, gain_vec, 1e-06), cosine_table, sine_table)
        return low(turned.reshape(sequences, SEQ_LEN, head_count * HEAD_DIM))
    query_low = heads_ready(query_raw, query_gain, HEADS)
    key_low = heads_ready(key_raw, key_gain, KV_HEADS)
    value_low = low(value_raw).reshape(sequences, SEQ_LEN, KV_HEADS * HEAD_DIM)
    mixed = lax.map(jax.checkpoint(attend), (query_low, key_low, value_low, segments.reshape(sequences, SEQ_LEN), live_mask.reshape(sequences, SEQ_LEN)))
    mixed_low = low(low_back(mixed.reshape(TOKENS, HEADS * HEAD_DIM)))
    attended = low_back(jnp.dot(mixed_low, output_weight, precision=HIGHEST_PRECISION))
    residual = hidden + attended
    normed_two = norm_rows(residual, second_gain, 1e-05)
    logits = jnp.dot(normed_two, router_weight, precision=HIGHEST_PRECISION)
    gate_probs = softmax_rows(jnp.take_along_axis(logits, routes, axis=1))
    padded_rows = jnp.concatenate([normed_two, jnp.zeros((1, D), normed_two.dtype)], axis=0)
    padded_gates = jnp.concatenate([gate_probs.reshape(-1), jnp.zeros((1,), gate_probs.dtype)], axis=0)

    def expert_step(combined, pieces):
        copy_ids, gate_mat, up_mat, down_mat = pieces
        token_ids = copy_ids // TOPK
        expert_rows = low(low_back(padded_rows[token_ids]))
        gate_pre = low_back(jnp.dot(expert_rows, gate_mat, precision=HIGHEST_PRECISION))
        up_pre = low_back(jnp.dot(expert_rows, up_mat, precision=HIGHEST_PRECISION))
        activated = low(silu_values(gate_pre) * up_pre)
        expert_out = low(low_back(jnp.dot(activated, down_mat, precision=HIGHEST_PRECISION)))
        return (combined.at[token_ids].add(padded_gates[copy_ids][:, None] * expert_out), None)
    combined, unused_out = lax.scan(jax.checkpoint(expert_step), jnp.zeros((TOKENS + 1, D), hidden.dtype), (table, gate_weight, up_weight, down_weight))
    return residual + combined[:TOKENS]

def reference(inputs, first_gain, query_weight, key_weight, value_weight, query_gain, key_gain, output_weight, second_gain, router_weight, gate_weight, up_weight, down_weight, segments, live_mask, routes, cotangent):
    table = slot_table(routes)

    def forward_floats(hidden, gain_one, query_mat, key_mat, value_mat, query_scale, key_scale, output_mat, gain_two, router_mat, gate_mat, up_mat, down_mat):
        return forward(hidden, gain_one, query_mat, key_mat, value_mat, query_scale, key_scale, output_mat, gain_two, router_mat, gate_mat, up_mat, down_mat, segments, live_mask, routes, table)
    output_value, backward = jax.vjp(forward_floats, inputs.astype(jnp.float32), first_gain.astype(jnp.float32), query_weight.astype(jnp.float32), key_weight.astype(jnp.float32), value_weight.astype(jnp.float32), query_gain.astype(jnp.float32), key_gain.astype(jnp.float32), output_weight.astype(jnp.float32), second_gain.astype(jnp.float32), router_weight.astype(jnp.float32), gate_weight.astype(jnp.float32), up_weight.astype(jnp.float32), down_weight.astype(jnp.float32))
    grads = backward(cotangent.astype(jnp.float32))
    return (output_value.astype(jnp.bfloat16), grads[0].astype(jnp.bfloat16), grads[1], grads[2], grads[3], grads[4], grads[5], grads[6], grads[7], grads[8], grads[9], grads[10], grads[11], grads[12])
```

```python
import functools

import jax
import jax.numpy as jnp
from jax import lax
from jax.experimental import pallas as pl
from jax.experimental.pallas import tpu as pltpu
from jax.sharding import PartitionSpec as P

SEQ_LEN = 1024
HIGHEST_PRECISION = lax.Precision.HIGHEST
CONTRACT_ROWS = (((0,), (0,)), ((), ()))
CONTRACT_LAST = (((1,), (1,)), ((), ()))
MESH = pl.DeviceIdType.MESH
ANY = pl.BlockSpec(memory_space=pl.ANY)
VMEM = pl.BlockSpec(memory_space=pltpu.VMEM)
F32 = jnp.float32
BF16 = jnp.bfloat16
SLOTS = 96
EXTRA = 16


def wrap(value):
    return lax.rem(value + 4, 4)


def pick(core, first, second):
    return first * (1 - core) + second * core


def plane_place():
    ep = lax.axis_index("ep")
    core = lax.rem(ep, 2)
    z = lax.rem(lax.div(ep, 2), 4)
    x = lax.div(ep, 8)
    return (pick(core, x, z), pick(core, z, x), core)


def plane_index(a, b, core):
    a, b = wrap(a), wrap(b)
    return (pick(core, a, b) * 4 + pick(core, b, a)) * 2 + core


def plane_partners():
    a, b, core = plane_place()
    tp = lax.axis_index("tp")
    return (
        (plane_index(a + 1, b, core), tp),
        (plane_index(a - 1, b, core), tp),
        (plane_index(a, b + 1, core), tp),
        (plane_index(a, b - 1, core), tp),
        (plane_index(b, a, 1 - core), tp),
    )


def line_partners():
    ep, tp = lax.axis_index("ep"), lax.axis_index("tp")
    return ((ep, wrap(tp + 1)), (ep, wrap(tp - 1)))


def greet(partners):
    barrier = pltpu.get_barrier_semaphore()
    for partner in partners:
        pl.semaphore_signal(barrier, inc=1, device_id=partner, device_id_type=MESH)
    pl.semaphore_wait(barrier, len(partners))


def halves(rows):
    top = (rows // 2 + 15) // 16 * 16
    return (pl.ds(0, top), pl.ds(top, rows - top))


class Post:
    def __init__(self, send_sems, recv_sems):
        self.send_sems, self.recv_sems, self.started = send_sems, recv_sems, []

    def go(self, src, dst, partner):
        number = len(self.started)
        copy = pltpu.make_async_remote_copy(
            src_ref=src,
            dst_ref=dst,
            send_sem=self.send_sems.at[number],
            recv_sem=self.recv_sems.at[number],
            device_id=partner,
            device_id_type=MESH,
        )
        copy.start()
        self.started.append(copy)
        return copy

    def finish(self):
        for copy in self.started:
            copy.wait_send()


def plane_gather_body(post, own_ref, all_ref):
    a, b, core = plane_place()
    me = plane_index(a, b, core)
    ahead_a, behind_a, ahead_b, behind_b, sibling = plane_partners()
    top, bottom = halves(own_ref.shape[0])
    go = post.go
    a_ahead = go(own_ref, all_ref.at[me], ahead_a)
    a_behind = go(own_ref, all_ref.at[me], behind_a)

    def along_b(src, index):
        return (go(src, all_ref.at[index], ahead_b), go(src, all_ref.at[index], behind_b))

    def across(src, index):
        return go(src, all_ref.at[index], sibling)

    b_copies = {0: along_b(own_ref, me)}
    others = [across(own_ref, me)]
    from_behind = plane_index(a - 1, b, core)
    from_ahead = plane_index(a + 1, b, core)
    from_far = plane_index(a + 2, b, core)
    a_ahead.wait_recv()
    far_top = go(all_ref.at[from_behind, top], all_ref.at[from_behind, top], ahead_a)
    a_behind.wait_recv()
    far_bottom = go(all_ref.at[from_ahead, bottom], all_ref.at[from_ahead, bottom], behind_a)
    b_copies[1] = along_b(all_ref.at[from_behind], from_behind)
    others.append(across(all_ref.at[from_behind], from_behind))
    b_copies[2] = along_b(all_ref.at[from_ahead], from_ahead)
    others.append(across(all_ref.at[from_ahead], from_ahead))
    column = (a, a - 1, a + 1, a + 2)
    fars = {}

    def onward(k):
        below = plane_index(column[k], b - 1, core)
        above = plane_index(column[k], b + 1, core)
        b_copies[k][0].wait_recv()
        first = go(all_ref.at[below, top], all_ref.at[below, top], ahead_b)
        b_copies[k][1].wait_recv()
        second = go(all_ref.at[above, bottom], all_ref.at[above, bottom], behind_b)
        fars[k] = (first, second)
        others.append(across(all_ref.at[below], below))
        others.append(across(all_ref.at[above], above))

    onward(0)
    far_top.wait_recv()
    far_bottom.wait_recv()
    b_copies[3] = along_b(all_ref.at[from_far], from_far)
    others.append(across(all_ref.at[from_far], from_far))
    onward(1)
    onward(2)
    onward(3)
    for k in range(4):
        index = plane_index(column[k], b + 2, core)
        fars[k][0].wait_recv()
        fars[k][1].wait_recv()
        others.append(across(all_ref.at[index], index))
    for copy in others:
        copy.wait_recv()


PLANE_COPIES = 36


def plane_gather_kernel(own_ref, all_ref, send_sems, recv_sems, local_sem):
    me = lax.axis_index("ep")
    greet(plane_partners())
    post = Post(send_sems, recv_sems)
    local = pltpu.make_async_copy(own_ref, all_ref.at[me], local_sem)
    local.start()
    plane_gather_body(post, own_ref, all_ref)
    post.finish()
    local.wait()


def plane_gather(own, number):
    return pl.pallas_call(
        plane_gather_kernel,
        out_shape=jax.ShapeDtypeStruct((32,) + own.shape, own.dtype),
        in_specs=[ANY],
        out_specs=ANY,
        scratch_shapes=[
            pltpu.SemaphoreType.DMA((PLANE_COPIES,)),
            pltpu.SemaphoreType.DMA((PLANE_COPIES,)),
            pltpu.SemaphoreType.DMA,
        ],
        compiler_params=pltpu.CompilerParams(collective_id=number, has_side_effects=True),
        name="plane_gather",
    )(own)


def add_rows(dst, sources, start, rows):
    step = 16

    @pl.loop(0, rows // step)
    def _(i):
        at = pl.multiple_of(i * step, step)
        total = None
        for ref, first in sources:
            part = ref[pl.ds(first + at, step), :].astype(F32)
            total = part if total is None else total + part
        dst[pl.ds(start + at, step), :] = total.astype(dst.dtype)


def plane_scatter_body(post, parts_ref, sum_ref, scratch):
    mine, other, b_far, b_near, a_far, a_near, local_sems = scratch
    a, b, core = plane_place()
    ahead_a, behind_a, ahead_b, behind_b, sibling = plane_partners()
    rows = mine.shape[2]
    top, bottom = halves(rows)
    high = top.size
    low = rows - high
    offsets = (2, 1, -1, 0)
    go = post.go
    loads, crossing = {}, {}
    order = [(k, 0) for k in range(4)] + [(k, j) for k in range(4) for j in (1, 2)]
    order += [(k, 3) for k in range(4)]
    for number, (k, j) in enumerate(order):
        there = plane_index(b + offsets[k], a + offsets[j], 1 - core)
        crossing[k, j] = go(parts_ref.at[there], other.at[k, j], sibling)
        here = plane_index(a + offsets[k], b + offsets[j], core)
        loads[k, j] = pltpu.make_async_copy(
            parts_ref.at[here], mine.at[k, j], local_sems.at[number]
        )
        loads[k, j].start()

    def ready(k, j):
        crossing[k, j].wait_recv()
        loads[k, j].wait()

    far_b, near_b = {}, {}
    for k in range(4):
        ready(k, 0)
        block, extra = mine.at[k, 0], other.at[k, 0]
        add_rows(block, [(block, 0), (extra, 0)], 0, rows)
        far_b[k] = (
            go(block.at[top], b_far.at[k, top], ahead_b),
            go(block.at[bottom], b_far.at[k, bottom], behind_b),
        )
    for k in range(4):
        far = b_far.at[k]
        ready(k, 1)
        block, extra = mine.at[k, 1], other.at[k, 1]
        far_b[k][0].wait_recv()
        add_rows(block, [(block, 0), (extra, 0), (far, 0)], 0, high)
        add_rows(block, [(block, high), (extra, high)], high, low)
        first = go(block, b_near.at[0, k], ahead_b)
        ready(k, 2)
        block, extra = mine.at[k, 2], other.at[k, 2]
        far_b[k][1].wait_recv()
        add_rows(block, [(block, 0), (extra, 0)], 0, high)
        add_rows(block, [(block, high), (extra, high), (far, high)], high, low)
        near_b[k] = (first, go(block, b_near.at[1, k], behind_b))
    far_a, near_a = [], []
    for k in range(4):
        ready(k, 3)
        block, extra = mine.at[k, 3], other.at[k, 3]
        near_b[k][0].wait_recv()
        near_b[k][1].wait_recv()
        base = [block, extra, b_near.at[0, k], b_near.at[1, k]]
        upper = [(ref, 0) for ref in base]
        lower = [(ref, high) for ref in base]
        if k == 0:
            add_rows(block, upper, 0, high)
            add_rows(block, lower, high, low)
            far_a = [
                go(block.at[top], a_far.at[top], ahead_a),
                go(block.at[bottom], a_far.at[bottom], behind_a),
            ]
        elif k == 1:
            far_a[0].wait_recv()
            add_rows(block, upper + [(a_far, 0)], 0, high)
            add_rows(block, lower, high, low)
            near_a.append(go(block, a_near.at[0], ahead_a))
        elif k == 2:
            far_a[1].wait_recv()
            add_rows(block, upper, 0, high)
            add_rows(block, lower + [(a_far, high)], high, low)
            near_a.append(go(block, a_near.at[1], behind_a))
        else:
            near_a[0].wait_recv()
            near_a[1].wait_recv()
            add_rows(sum_ref, upper + [(a_near.at[0], 0), (a_near.at[1], 0)], 0, rows)


def plane_scatter_scratch(rows, columns, kind):
    return [
        pltpu.VMEM((4, 4, rows, columns), kind),
        pltpu.VMEM((4, 4, rows, columns), kind),
        pltpu.VMEM((4, rows, columns), kind),
        pltpu.VMEM((2, 4, rows, columns), kind),
        pltpu.VMEM((rows, columns), kind),
        pltpu.VMEM((2, rows, columns), kind),
        pltpu.SemaphoreType.DMA((16,)),
    ]


def plane_scatter_kernel(parts_ref, sum_ref, *rest):
    post = Post(rest[-2], rest[-1])
    greet(plane_partners())
    plane_scatter_body(post, parts_ref, sum_ref, rest[:-2])
    post.finish()


def plane_scatter(parts, number):
    _, rows, columns = parts.shape
    return pl.pallas_call(
        plane_scatter_kernel,
        out_shape=jax.ShapeDtypeStruct((rows, columns), F32),
        in_specs=[ANY],
        out_specs=VMEM,
        scratch_shapes=plane_scatter_scratch(rows, columns, parts.dtype)
        + [
            pltpu.SemaphoreType.DMA((PLANE_COPIES,)),
            pltpu.SemaphoreType.DMA((PLANE_COPIES,)),
        ],
        compiler_params=pltpu.CompilerParams(
            collective_id=number, has_side_effects=True, vmem_limit_bytes=56 << 20
        ),
        name="plane_scatter",
    )(parts)


def everywhere_kernel(
    dense_ref, small_ref, dense_out, small_out, dense_own, small_own, small_line, small_sum, *rest
):
    post = Post(rest[-2], rest[-1])
    me = lax.axis_index("ep")
    ahead, behind = line_partners()
    tp = lax.axis_index("tp")
    ep = lax.axis_index("ep")
    across = (ep, wrap(tp + 2))
    greet(plane_partners() + (ahead, behind, across))
    plane_scatter_body(post, small_ref, small_own, rest[7:14])
    line = [
        post.go(small_own, small_line.at[0], ahead),
        post.go(small_own, small_line.at[1], behind),
        post.go(small_own, small_line.at[2], across),
    ]
    plane_scatter_body(post, dense_ref, dense_own, rest[:7])
    for copy in line:
        copy.wait_recv()
    small_sum[...] = small_own[...] + small_line[0] + small_line[1] + small_line[2]
    small_out[me] = small_sum[...]
    dense_out[me] = dense_own[...]
    plane_gather_body(post, small_sum, small_out)
    plane_gather_body(post, dense_own, dense_out)
    post.finish()


def everywhere(dense, small, number):
    _, rows, columns = dense.shape
    _, small_rows, small_columns = small.shape
    copies = 4 * PLANE_COPIES + 3
    return pl.pallas_call(
        everywhere_kernel,
        out_shape=[
            jax.ShapeDtypeStruct(dense.shape, dense.dtype),
            jax.ShapeDtypeStruct(small.shape, small.dtype),
        ],
        in_specs=[VMEM, VMEM],
        out_specs=[VMEM, VMEM],
        scratch_shapes=[
            pltpu.VMEM((rows, columns), dense.dtype),
            pltpu.VMEM((small_rows, small_columns), F32),
            pltpu.VMEM((3, small_rows, small_columns), F32),
            pltpu.VMEM((small_rows, small_columns), F32),
        ]
        + plane_scatter_scratch(rows, columns, dense.dtype)
        + plane_scatter_scratch(small_rows, small_columns, F32)
        + [pltpu.SemaphoreType.DMA((copies,)), pltpu.SemaphoreType.DMA((copies,))],
        compiler_params=pltpu.CompilerParams(
            collective_id=number, has_side_effects=True, vmem_limit_bytes=48 << 20
        ),
        name="everywhere",
    )(dense, small)


def line_gather_kernel(own_ref, all_ref, send_sems, recv_sems, local_sem):
    tp = lax.axis_index("tp")
    ahead, behind = line_partners()
    top, bottom = halves(own_ref.shape[0])
    greet((ahead, behind))
    post = Post(send_sems, recv_sems)
    local = pltpu.make_async_copy(own_ref, all_ref.at[tp], local_sem)
    local.start()
    first = post.go(own_ref, all_ref.at[tp], ahead)
    second = post.go(own_ref, all_ref.at[tp], behind)
    before, after = wrap(tp - 1), wrap(tp + 1)
    first.wait_recv()
    third = post.go(all_ref.at[before, top], all_ref.at[before, top], ahead)
    second.wait_recv()
    fourth = post.go(all_ref.at[after, bottom], all_ref.at[after, bottom], behind)
    third.wait_recv()
    fourth.wait_recv()
    post.finish()
    local.wait()


def line_gather(own, number):
    return pl.pallas_call(
        line_gather_kernel,
        out_shape=jax.ShapeDtypeStruct((4,) + own.shape, own.dtype),
        in_specs=[ANY],
        out_specs=ANY,
        scratch_shapes=[
            pltpu.SemaphoreType.DMA((4,)),
            pltpu.SemaphoreType.DMA((4,)),
            pltpu.SemaphoreType.DMA,
        ],
        compiler_params=pltpu.CompilerParams(collective_id=number, has_side_effects=True),
        name="line_gather",
    )(own)


def line_scatter_kernel(parts_ref, sum_ref, mine, far, near, send_sems, recv_sems, local_sems):
    tp = lax.axis_index("tp")
    ahead, behind = line_partners()
    rows = mine.shape[1]
    top, bottom = halves(rows)
    high = top.size
    low = rows - high
    loads = []
    for number, offset in enumerate((2, 1, -1, 0)):
        load = pltpu.make_async_copy(
            parts_ref.at[wrap(tp + offset)], mine.at[number], local_sems.at[number]
        )
        load.start()
        loads.append(load)
    greet((ahead, behind))
    post = Post(send_sems, recv_sems)
    there = wrap(tp + 2)
    first = post.go(parts_ref.at[there, top], far.at[top], ahead)
    second = post.go(parts_ref.at[there, bottom], far.at[bottom], behind)
    loads[0].wait()
    loads[1].wait()
    block = mine.at[1]
    first.wait_recv()
    add_rows(block, [(block, 0), (far, 0)], 0, high)
    third = post.go(block, near.at[0], ahead)
    loads[2].wait()
    block = mine.at[2]
    second.wait_recv()
    add_rows(block, [(block, high), (far, high)], high, low)
    fourth = post.go(block, near.at[1], behind)
    loads[3].wait()
    third.wait_recv()
    fourth.wait_recv()
    add_rows(sum_ref, [(mine.at[3], 0), (near.at[0], 0), (near.at[1], 0)], 0, rows)
    post.finish()


def line_scatter(parts, number):
    _, rows, columns = parts.shape
    kind = parts.dtype
    return pl.pallas_call(
        line_scatter_kernel,
        out_shape=jax.ShapeDtypeStruct((rows, columns), F32),
        in_specs=[ANY],
        out_specs=VMEM,
        scratch_shapes=[
            pltpu.VMEM((4, rows, columns), kind),
            pltpu.VMEM((rows, columns), kind),
            pltpu.VMEM((2, rows, columns), kind),
            pltpu.SemaphoreType.DMA((4,)),
            pltpu.SemaphoreType.DMA((4,)),
            pltpu.SemaphoreType.DMA((4,)),
        ],
        compiler_params=pltpu.CompilerParams(
            collective_id=number, has_side_effects=True, vmem_limit_bytes=32 << 20
        ),
        name="line_scatter",
    )(parts)


def exchange(values):
    return jnp.concatenate([values[:, 64:], values[:, :64]], axis=1)


def head_pairs(block):
    rows = block.shape[0]
    low = lax.broadcasted_iota(jnp.int32, (rows, 128), 1) < 64
    left, right = block[:, :128], block[:, 128:]
    zero = jnp.zeros_like(left)
    straight = jnp.concatenate([jnp.where(low, left, zero), jnp.where(low, zero, right)], axis=0)
    crossed = jnp.concatenate([jnp.where(low, zero, left), jnp.where(low, right, zero)], axis=0)
    return (straight, crossed)


def heads_back(straight, crossed):
    rows = straight.shape[0] // 2
    low = lax.broadcasted_iota(jnp.int32, (rows, 128), 1) < 64
    left = jnp.where(low, straight[:rows], crossed[:rows])
    right = jnp.where(low, crossed[rows:], straight[rows:])
    return jnp.concatenate([left, right], axis=1)


def attend_kernel(query, keys, values, seg_column, seg_row, live_row, mixed):
    rows = query.shape[0]
    start = pl.program_id(0) * rows
    total = keys.shape[0]
    position = start + lax.broadcasted_iota(jnp.int32, (rows, total), 0)
    key_position = lax.broadcasted_iota(jnp.int32, (rows, total), 1)
    allowed = (seg_column[...] == seg_row[...]) & (
        (live_row[...] == 1) | (position == key_position)
    )
    bias = jnp.where(allowed, 0.0, -1e30).astype(F32)
    outs = []
    for pair, key_part, value_part in zip(
        head_pairs(query[...]),
        (keys[...], exchange(keys[...])),
        (values[...], exchange(values[...])),
        strict=True,
    ):
        halves_out = []
        for number in range(2):
            part = pair[number * rows : (number + 1) * rows]
            scores = lax.dot_general(part, key_part, CONTRACT_LAST, preferred_element_type=F32)
            weights = jnp.exp(scores * 0.125 + bias)
            total_weight = jnp.sum(weights, axis=1, keepdims=True)
            out = jnp.dot(weights.astype(BF16), value_part, preferred_element_type=F32)
            halves_out.append(out / total_weight)
        outs.append(jnp.concatenate(halves_out, axis=0))
    mixed[...] = heads_back(*outs).astype(BF16)


def attend(query, keys, values, seg_column, seg_row, live_row):
    total, width = query.shape
    rows = 256
    return pl.pallas_call(
        attend_kernel,
        out_shape=jax.ShapeDtypeStruct((total, width), BF16),
        grid=(total // rows,),
        in_specs=[
            pl.BlockSpec((rows, width), lambda i: (i, 0)),
            pl.BlockSpec((total, 128), lambda i: (0, 0)),
            pl.BlockSpec((total, 128), lambda i: (0, 0)),
            pl.BlockSpec((rows, 1), lambda i: (i, 0)),
            pl.BlockSpec((1, total), lambda i: (0, 0)),
            pl.BlockSpec((1, total), lambda i: (0, 0)),
        ],
        out_specs=pl.BlockSpec((rows, width), lambda i: (i, 0)),
        compiler_params=pltpu.CompilerParams(vmem_limit_bytes=48 << 20),
        name="attend",
    )(query, keys, values, seg_column, seg_row, live_row)


def attend_back_kernel(
    query, grad, keys, values, seg_column, seg_row, live_column,
    grad_query, grad_keys, grad_values, keys_sum, values_sum,
):
    rows = query.shape[0]
    step = pl.program_id(0)
    total = keys.shape[0]
    key_position = lax.broadcasted_iota(jnp.int32, (total, rows), 0)
    position = step * rows + lax.broadcasted_iota(jnp.int32, (total, rows), 1)
    allowed = (seg_column[...] == seg_row[...]) & (
        (live_column[...] == 1) | (position == key_position)
    )
    bias = jnp.where(allowed, 0.0, -1e30).astype(F32)

    @pl.when(step == 0)
    def _():
        keys_sum[...] = jnp.zeros_like(keys_sum)
        values_sum[...] = jnp.zeros_like(values_sum)

    query_pairs = head_pairs(query[...])
    grad_pairs = head_pairs(grad[...])
    key_parts = (keys[...], exchange(keys[...]))
    value_parts = (values[...], exchange(values[...]))
    outs = []
    for side in range(2):
        halves_out = []
        for number in range(2):
            part = query_pairs[side][number * rows : (number + 1) * rows]
            grad_part = grad_pairs[side][number * rows : (number + 1) * rows]
            scores = lax.dot_general(
                key_parts[side], part, CONTRACT_LAST, preferred_element_type=F32
            )
            raw = jnp.exp(scores * 0.125 + bias)
            weights = raw * (1.0 / jnp.sum(raw, axis=0, keepdims=True))
            grad_weights = lax.dot_general(
                value_parts[side], grad_part, CONTRACT_LAST, preferred_element_type=F32
            )
            inner = jnp.sum(weights * grad_weights, axis=0, keepdims=True)
            grad_scores = (weights * (grad_weights - inner)).astype(BF16)
            halves_out.append(
                lax.dot_general(
                    grad_scores, key_parts[side], CONTRACT_ROWS, preferred_element_type=F32
                )
            )
            keys_sum[side] += jnp.dot(grad_scores, part, preferred_element_type=F32)
            values_sum[side] += jnp.dot(
                weights.astype(BF16), grad_part, preferred_element_type=F32
            )
        outs.append(jnp.concatenate(halves_out, axis=0))
    grad_query[...] = heads_back(*outs) * 0.125

    @pl.when(step == pl.num_programs(0) - 1)
    def _():
        grad_keys[...] = (keys_sum[0] + exchange(keys_sum[1])) * 0.125
        grad_values[...] = (values_sum[0] + exchange(values_sum[1])).astype(BF16)


def attend_back(query, grad, keys, values, seg_column, seg_row, live_column):
    total, width = query.shape
    rows = 256
    return pl.pallas_call(
        attend_back_kernel,
        out_shape=[
            jax.ShapeDtypeStruct((total, width), F32),
            jax.ShapeDtypeStruct((total, 128), F32),
            jax.ShapeDtypeStruct((total, 128), BF16),
        ],
        grid=(total // rows,),
        in_specs=[
            pl.BlockSpec((rows, width), lambda i: (i, 0)),
            pl.BlockSpec((rows, width), lambda i: (i, 0)),
            pl.BlockSpec((total, 128), lambda i: (0, 0)),
            pl.BlockSpec((total, 128), lambda i: (0, 0)),
            pl.BlockSpec((total, 1), lambda i: (0, 0)),
            pl.BlockSpec((1, rows), lambda i: (0, i)),
            pl.BlockSpec((total, 1), lambda i: (0, 0)),
        ],
        out_specs=[
            pl.BlockSpec((rows, width), lambda i: (i, 0)),
            pl.BlockSpec((total, 128), lambda i: (0, 0)),
            pl.BlockSpec((total, 128), lambda i: (0, 0)),
        ],
        scratch_shapes=[pltpu.VMEM((2, total, 128), F32), pltpu.VMEM((2, total, 128), F32)],
        compiler_params=pltpu.CompilerParams(vmem_limit_bytes=48 << 20),
        name="attend_back",
    )(query, grad, keys, values, seg_column, seg_row, live_column)


GROUP = 4


def split_float(values):
    high = values.astype(BF16)
    return (high, (values - high.astype(F32)).astype(BF16))


def experts_kernel(
    number_ref, rows_ref, grads_ref, pair_ref, down_ref,
    out_ref, back_ref, weight_grads_ref,
    gate_full, up_full, gate_sum, up_sum, down_sum, rows_own, grads_own, gates_own, select,
):
    step = pl.program_id(0)
    expert = number_ref[0]
    lane_row = lax.rem(expert, 16)
    upper = expert >= 16

    @pl.when(step == 0)
    def _():
        for part in range(4):
            columns = slice(part * 128, (part + 1) * 128)
            gate_full[:, columns] = pair_ref[part, :1024, :]
            up_full[:, columns] = pair_ref[part, 1024:, :]
        gate_sum[...] = jnp.zeros_like(gate_sum)
        up_sum[...] = jnp.zeros_like(up_sum)
        down_sum[...] = jnp.zeros_like(down_sum)

    earlier = (
        lax.broadcasted_iota(jnp.int32, (256, 256), 0)
        <= lax.broadcasted_iota(jnp.int32, (256, 256), 1)
    ).astype(BF16)
    slot = lax.broadcasted_iota(jnp.int32, (SLOTS, 256), 0).astype(F32)
    extra_row = lax.broadcasted_iota(jnp.int32, (EXTRA, 1024), 0) == lane_row
    for part in range(GROUP):
        extras = jnp.where(extra_row, rows_ref[part, 256:, :].astype(F32), 0.0)
        extras = jnp.sum(extras, axis=0, keepdims=True)
        gates = jnp.where(
            upper, extras[:, 512:768] + extras[:, 768:], extras[:, :256] + extras[:, 256:512]
        )
        named = jnp.broadcast_to(gates, (16, 256)) > 0.0
        rank = jnp.dot(named.astype(BF16), earlier, preferred_element_type=F32)[:1] - 1.0
        chosen = (slot == rank) & (gates > 0.0)
        chosen_low = chosen.astype(BF16)
        at = slice(part * SLOTS, (part + 1) * SLOTS)
        select[at, :] = chosen_low
        rows_own[at, :] = jnp.dot(
            chosen_low, rows_ref[part, :256, :], preferred_element_type=F32
        ).astype(BF16)
        grads_own[at, :] = jnp.dot(
            chosen_low, grads_ref[part], preferred_element_type=F32
        ).astype(BF16)
        gates_own[at, :] = jnp.sum(jnp.where(chosen, gates, 0.0), axis=1, keepdims=True)

    rows_in = rows_own[...]
    gate_pre = jnp.dot(rows_in, gate_full[...], preferred_element_type=F32)
    up_pre = jnp.dot(rows_in, up_full[...], preferred_element_type=F32)
    sigmoid = 1.0 / (1.0 + jnp.exp(-gate_pre))
    silu = gate_pre * sigmoid
    act = (silu * up_pre).astype(BF16)
    out = jnp.dot(act, down_ref[...], preferred_element_type=F32).astype(BF16).astype(F32)
    gate_factor = gates_own[...]
    grads_in = grads_own[...].astype(F32)
    grad_gates = jnp.sum(grads_in * out, axis=1, keepdims=True)
    weighted = (gate_factor * out).astype(BF16)
    grad_out = (gate_factor * grads_in).astype(BF16)
    grad_act = lax.dot_general(
        grad_out, down_ref[...], CONTRACT_LAST, preferred_element_type=F32
    )
    down_sum[...] += lax.dot_general(
        grad_out, act, CONTRACT_ROWS, preferred_element_type=F32
    )
    grad_gate_pre = (grad_act * up_pre * sigmoid * (1.0 + gate_pre * (1.0 - sigmoid))).astype(BF16)
    grad_up_pre = (grad_act * silu).astype(BF16)
    gate_sum[...] += lax.dot_general(
        rows_in, grad_gate_pre, CONTRACT_ROWS, preferred_element_type=F32
    )
    up_sum[...] += lax.dot_general(
        rows_in, grad_up_pre, CONTRACT_ROWS, preferred_element_type=F32
    )
    grad_rows = lax.dot_general(
        grad_gate_pre, gate_full[...], CONTRACT_LAST, preferred_element_type=F32
    )
    grad_rows = grad_rows + lax.dot_general(
        grad_up_pre, up_full[...], CONTRACT_LAST, preferred_element_type=F32
    )
    grad_rows = grad_rows.astype(BF16)
    nothing = jnp.zeros((1, 512), F32)
    for part in range(GROUP):
        at = slice(part * SLOTS, (part + 1) * SLOTS)
        chosen_low = select[at, :]
        out_ref[part] = lax.dot_general(
            chosen_low, weighted[at], CONTRACT_ROWS, preferred_element_type=F32
        ).astype(BF16)
        back_ref[part, :256, :] = lax.dot_general(
            chosen_low, grad_rows[at], CONTRACT_ROWS, preferred_element_type=F32
        ).astype(BF16)
        spread = jnp.sum(chosen_low.astype(F32) * grad_gates[at], axis=0, keepdims=True)
        high = spread.astype(BF16).astype(F32)
        both = jnp.concatenate([high, spread - high], axis=1)
        line = jnp.concatenate(
            [jnp.where(upper, nothing, both), jnp.where(upper, both, nothing)], axis=1
        )
        back_ref[part, 256:, :] = jnp.where(extra_row, line, 0.0).astype(BF16)

    @pl.when(step == pl.num_programs(0) - 1)
    def _():
        for part in range(4):
            columns = slice(part * 128, (part + 1) * 128)
            weight_grads_ref[part, :1024, :] = gate_sum[:, columns].astype(BF16)
            weight_grads_ref[part, 1024:2048, :] = up_sum[:, columns].astype(BF16)
            weight_grads_ref[part, 2048:, :] = down_sum[:, columns].astype(BF16)


def run_experts(number, rows, grads, pair, down):
    sources = rows.shape[0]
    count = GROUP * SLOTS
    return pl.pallas_call(
        experts_kernel,
        out_shape=[
            jax.ShapeDtypeStruct((sources, 256, 1024), BF16),
            jax.ShapeDtypeStruct((sources, 256 + EXTRA, 1024), BF16),
            jax.ShapeDtypeStruct((4, 3072, 128), BF16),
        ],
        grid=(sources // GROUP,),
        in_specs=[
            pl.BlockSpec(memory_space=pltpu.SMEM),
            pl.BlockSpec((GROUP, 256 + EXTRA, 1024), lambda i: (i, 0, 0)),
            pl.BlockSpec((GROUP, 256, 1024), lambda i: (i, 0, 0)),
            pl.BlockSpec((4, 2048, 128), lambda i: (0, 0, 0)),
            pl.BlockSpec((512, 1024), lambda i: (0, 0)),
        ],
        out_specs=[
            pl.BlockSpec((GROUP, 256, 1024), lambda i: (i, 0, 0)),
            pl.BlockSpec((GROUP, 256 + EXTRA, 1024), lambda i: (i, 0, 0)),
            pl.BlockSpec((4, 3072, 128), lambda i: (0, 0, 0)),
        ],
        scratch_shapes=[
            pltpu.VMEM((1024, 512), BF16),
            pltpu.VMEM((1024, 512), BF16),
            pltpu.VMEM((1024, 512), F32),
            pltpu.VMEM((1024, 512), F32),
            pltpu.VMEM((1024, 512), F32),
            pltpu.VMEM((count, 1024), BF16),
            pltpu.VMEM((count, 1024), BF16),
            pltpu.VMEM((count, 1), F32),
            pltpu.VMEM((count, 256), BF16),
        ],
        compiler_params=pltpu.CompilerParams(vmem_limit_bytes=60 << 20),
        name="run_experts",
    )(number, rows, grads, pair, down)


def norm_rows(values, gain_vec, epsilon):
    return (
        values * lax.rsqrt(jnp.mean(values * values, axis=-1, keepdims=True) + epsilon) * gain_vec
    )


def norm_plain(values, gain_vec):
    return norm_rows(values, gain_vec, 1e-05)


def rotate(values, cosine_table, sine_table):
    half_dim = values.shape[-1] // 2
    first_half = values[..., :half_dim]
    second_half = values[..., half_dim:]
    return jnp.concatenate(
        [
            first_half * cosine_table - second_half * sine_table,
            second_half * cosine_table + first_half * sine_table,
        ],
        axis=-1,
    )


def rotary_tables(row_total, head_dim, seq_len):
    half_dim = head_dim // 2
    position = (jnp.arange(row_total) % seq_len).astype(jnp.float32)
    frequency = 10000.0 ** (-(jnp.arange(half_dim).astype(jnp.float32) * 2.0) / head_dim)
    angles = position[:, None] * frequency[None, :]
    return (jnp.cos(angles)[:, None, :], jnp.sin(angles)[:, None, :])


def prepare(query_raw, key_raw, query_scale, key_scale, cosine_table, sine_table, head_dim):
    row_total = query_raw.shape[0]
    query_heads = norm_rows(query_raw.reshape(row_total, -1, head_dim), query_scale, 1e-06)
    key_heads = norm_rows(key_raw.reshape(row_total, -1, head_dim), key_scale, 1e-06)
    query_rot = rotate(query_heads, cosine_table, sine_table).reshape(row_total, -1)
    key_rot = rotate(key_heads, cosine_table, sine_table).reshape(row_total, -1)
    return (query_rot, key_rot)


def gate_lines(table):
    high, low = split_float(table.T)
    return jnp.concatenate([high[:16], low[:16], high[16:], low[16:]], axis=1)


def gate_table(lines):
    first = lines[:, :256] + lines[:, 256:512]
    second = lines[:, 512:768] + lines[:, 768:]
    return jnp.concatenate([first, second], axis=0).T


def shards(
    inputs,
    first_gain,
    query_weight,
    key_weight,
    value_weight,
    query_gain,
    key_gain,
    output_weight,
    second_gain,
    router_weight,
    gate_weight,
    up_weight,
    down_weight,
    segments,
    live_mask,
    routes,
    cotangent,
):
    row_count, model_width = inputs.shape
    head_dim = query_gain.shape[0]
    experts = router_weight.shape[1]
    gain_one = first_gain.astype(F32)
    gain_two = second_gain.astype(F32)
    query_scale = query_gain.astype(F32)
    key_scale = key_gain.astype(F32)
    router_float = router_weight.astype(F32)
    hidden = inputs.astype(F32)
    grad_all = lax.all_gather(cotangent, "ep", axis=0)
    pair = jnp.concatenate([gate_weight[0], up_weight[0]], axis=0)
    pair_all = lax.all_gather(pair, "tp", axis=0)
    down_all = lax.all_gather(down_weight[0], "tp", axis=0, tiled=True)

    normed_one = norm_plain(hidden, gain_one)
    gathered = line_gather(normed_one.astype(BF16), 1).reshape(-1, model_width)
    group_rows = gathered.shape[0]
    query_raw = jnp.dot(gathered, query_weight, preferred_element_type=F32)
    key_raw = jnp.dot(gathered, key_weight, preferred_element_type=F32)
    value_raw = jnp.dot(gathered, value_weight, preferred_element_type=F32)
    cosine_table, sine_table = rotary_tables(group_rows, head_dim, SEQ_LEN)

    def prepare_local(query_part, key_part, query_factor, key_factor):
        return prepare(
            query_part, key_part, query_factor, key_factor, cosine_table, sine_table, head_dim
        )

    (query_rot, key_rot), prepare_back = jax.vjp(
        prepare_local, query_raw, key_raw, query_scale, key_scale
    )
    query_low = query_rot.astype(BF16)
    key_low = key_rot.astype(BF16)
    value_low = value_raw.astype(BF16)
    seg_column, seg_row = segments.reshape(-1, 1), segments.reshape(1, -1)
    live_column, live_row = live_mask.reshape(-1, 1), live_mask.reshape(1, -1)
    mixed_heads = attend(query_low, key_low, value_low, seg_column, seg_row, live_row)
    attended = line_scatter(
        jnp.dot(mixed_heads, output_weight, preferred_element_type=F32)
        .astype(BF16)
        .reshape(-1, row_count, model_width),
        2,
    )
    residual = hidden + attended
    normed_two, norm_two_back = jax.vjp(norm_plain, residual, gain_two)
    logits = jnp.dot(normed_two, router_float, precision=HIGHEST_PRECISION)
    named = jnp.any(routes[:, :, None] == jnp.arange(experts)[None, None, :], axis=1)
    top_logit = jnp.max(jnp.where(named, logits, -jnp.inf), axis=1, keepdims=True)
    raised = jnp.where(named, jnp.exp(jnp.where(named, logits - top_logit, 0.0)), 0.0)
    gate_probs = raised / jnp.sum(raised, axis=1, keepdims=True)
    block = jnp.concatenate([normed_two.astype(BF16), gate_lines(gate_probs)], axis=0)
    rows_all = plane_gather(block, 3)
    number = lax.axis_index("ep").astype(jnp.int32).reshape(1)
    out_parts, back_parts, weight_parts = run_experts(
        number, rows_all, grad_all, pair_all, down_all
    )
    back_sum = plane_scatter(back_parts, 4)
    combined = lax.psum_scatter(out_parts, "ep", scatter_dimension=0).astype(F32)
    weight_sums = lax.psum_scatter(weight_parts, "tp", scatter_dimension=0).astype(F32)
    result = (residual + combined).astype(BF16)
    grad_out = cotangent.astype(F32)
    grad_gates = gate_table(back_sum[row_count:])
    grad_logits = gate_probs * (
        grad_gates - jnp.sum(gate_probs * grad_gates, axis=-1, keepdims=True)
    )
    grad_normed_two = back_sum[:row_count] + lax.dot_general(
        grad_logits, router_float, CONTRACT_LAST, precision=HIGHEST_PRECISION
    )
    grad_router = lax.dot_general(
        normed_two, grad_logits, CONTRACT_ROWS, precision=HIGHEST_PRECISION
    )
    grad_residual_norm, grad_gain_two = norm_two_back(grad_normed_two)
    grad_residual = grad_out + grad_residual_norm
    grad_attn_all = line_gather(grad_residual.astype(BF16), 5).reshape(-1, model_width)
    grad_output_mat = lax.dot_general(
        mixed_heads, grad_attn_all, CONTRACT_ROWS, preferred_element_type=F32
    )
    grad_mixed = lax.dot_general(
        grad_attn_all, output_weight, CONTRACT_LAST, preferred_element_type=F32
    ).astype(BF16)
    grad_query, grad_keys, grad_value_low = attend_back(
        query_low, grad_mixed, key_low, value_low, seg_column, seg_row, live_column
    )
    grad_query_raw, grad_key_raw, grad_query_scale, grad_key_scale = prepare_back(
        (grad_query, grad_keys)
    )
    grad_low = jnp.concatenate(
        [grad_query_raw.astype(BF16), grad_key_raw.astype(BF16), grad_value_low], axis=1
    )
    weights_in = jnp.concatenate([query_weight, key_weight, value_weight], axis=1)
    summed = lax.dot_general(grad_low, weights_in, CONTRACT_LAST, preferred_element_type=F32)
    grad_normed_one = line_scatter(
        summed.astype(BF16).reshape(-1, row_count, model_width), 6
    )
    grad_in_mats = lax.dot_general(gathered, grad_low, CONTRACT_ROWS, preferred_element_type=F32)
    unused_norm, norm_one_back = jax.vjp(norm_plain, hidden, gain_one)
    grad_hidden_norm, grad_gain_one = norm_one_back(grad_normed_one)
    grad_inputs = (grad_residual + grad_hidden_norm).astype(BF16)
    dense = jnp.concatenate(
        [grad_in_mats.astype(BF16), grad_output_mat.astype(BF16).reshape(1024, 256)], axis=1
    ).reshape(32, 32, 768)
    small = jnp.concatenate(
        [
            grad_router.reshape(-1),
            grad_gain_one,
            grad_gain_two,
            grad_query_scale,
            grad_key_scale,
        ]
    )
    length = small.shape[0]
    small = jnp.pad(small, (0, 32 * 32 * 128 - length)).reshape(32, 32, 128)
    dense, small = everywhere(dense, small, 7)
    dense = dense.reshape(1024, 768).astype(F32)
    small = small.reshape(-1)
    base = model_width * experts
    return (
        result,
        grad_inputs,
        small[base : base + 1024],
        dense[:, :256],
        dense[:, 256:384],
        dense[:, 384:512],
        small[base + 2048 : base + 2112],
        small[base + 2112 : base + 2176],
        dense[:, 512:].reshape(256, 1024),
        small[base + 1024 : base + 2048],
        small[:base].reshape(model_width, experts),
        weight_sums[None, :1024],
        weight_sums[None, 1024:2048],
        weight_sums[2048:].T[None],
    )


def solution(mesh):
    return jax.shard_map(
        shards,
        mesh=mesh,
        in_specs=(
            P(("ep", "tp"), None),
            P(),
            P(None, "tp"),
            P(None, "tp"),
            P(None, "tp"),
            P(),
            P(),
            P("tp", None),
            P(),
            P(),
            P("ep", None, "tp"),
            P("ep", None, "tp"),
            P("ep", "tp", None),
            P("ep"),
            P("ep"),
            P(("ep", "tp"), None),
            P(("ep", "tp"), None),
        ),
        out_specs=(
            P(("ep", "tp"), None),
            P(("ep", "tp"), None),
            P(),
            P(None, "tp"),
            P(None, "tp"),
            P(None, "tp"),
            P(),
            P(),
            P("tp", None),
            P(),
            P(),
            P("ep", None, "tp"),
            P("ep", None, "tp"),
            P("ep", "tp", None),
        ),
        check_vma=False,
    )
```

```python
import jax
import jax.numpy as jnp
import numpy as np
from jax import lax
from jax.experimental import pallas as pl
from jax.experimental.pallas import tpu as pltpu
from jax.sharding import PartitionSpec as P

SEQ_LEN = 1024
HIGHEST_PRECISION = lax.Precision.HIGHEST
CONTRACT_ROWS = (((0,), (0,)), ((), ()))
CONTRACT_LAST = (((1,), (1,)), ((), ()))
MESH = pl.DeviceIdType.MESH
ANY = pl.BlockSpec(memory_space=pl.ANY)
VMEM = pl.BlockSpec(memory_space=pltpu.VMEM)
F32 = jnp.float32
BF16 = jnp.bfloat16
SLOTS = 96
EXTRA = 16


def wrap(value):
    return lax.rem(value + 4, 4)


def pick(core, first, second):
    return first * (1 - core) + second * core


def plane_place():
    ep = lax.axis_index("ep")
    core = lax.rem(ep, 2)
    z = lax.rem(lax.div(ep, 2), 4)
    x = lax.div(ep, 8)
    return (pick(core, x, z), pick(core, z, x), core)


def plane_index(a, b, core):
    a, b = wrap(a), wrap(b)
    return (pick(core, a, b) * 4 + pick(core, b, a)) * 2 + core


def plane_partners():
    a, b, core = plane_place()
    tp = lax.axis_index("tp")
    return (
        (plane_index(a + 1, b, core), tp),
        (plane_index(a - 1, b, core), tp),
        (plane_index(a, b + 1, core), tp),
        (plane_index(a, b - 1, core), tp),
        (plane_index(b, a, 1 - core), tp),
    )


def line_partners():
    ep, tp = lax.axis_index("ep"), lax.axis_index("tp")
    return ((ep, wrap(tp + 1)), (ep, wrap(tp - 1)))


def greet(partners):
    barrier = pltpu.get_barrier_semaphore()
    for partner in partners:
        pl.semaphore_signal(barrier, inc=1, device_id=partner, device_id_type=MESH)
    pl.semaphore_wait(barrier, len(partners))


def halves(ref):
    unit = 16 if ref.dtype == BF16 else 8
    rows = ref.shape[-2]
    top = (rows // 2 + unit - 1) // unit * unit
    return (pl.ds(0, top), pl.ds(top, rows - top))


def together(*tasks):
    tasks = list(tasks)
    while tasks:
        for task in list(tasks):
            if next(task, "ended") == "ended":
                tasks.remove(task)


def chain(*tasks):
    for task in tasks:
        yield from task


class Post:
    def __init__(self, send_sems, recv_sems):
        self.send_sems, self.recv_sems, self.started = send_sems, recv_sems, []

    def go(self, src, dst, partner):
        number = len(self.started)
        copy = pltpu.make_async_remote_copy(
            src_ref=src,
            dst_ref=dst,
            send_sem=self.send_sems.at[number],
            recv_sem=self.recv_sems.at[number],
            device_id=partner,
            device_id_type=MESH,
        )
        copy.start()
        self.started.append(copy)
        return copy

    def finish(self):
        for copy in self.started:
            copy.wait_send()


def plane_gather_steps(post, own_ref, all_ref):
    a, b, core = plane_place()
    me = plane_index(a, b, core)
    ahead_a, behind_a, ahead_b, behind_b, sibling = plane_partners()
    top, bottom = halves(own_ref)
    go = post.go
    a_ahead = go(own_ref, all_ref.at[me], ahead_a)
    a_behind = go(own_ref, all_ref.at[me], behind_a)

    def along_b(src, index):
        return (go(src, all_ref.at[index], ahead_b), go(src, all_ref.at[index], behind_b))

    def across(src, index):
        return go(src, all_ref.at[index], sibling)

    b_copies = {0: along_b(own_ref, me)}
    others = [across(own_ref, me)]
    from_behind = plane_index(a - 1, b, core)
    from_ahead = plane_index(a + 1, b, core)
    from_far = plane_index(a + 2, b, core)
    yield
    a_ahead.wait_recv()
    far_top = go(all_ref.at[from_behind, top], all_ref.at[from_behind, top], ahead_a)
    b_copies[1] = along_b(all_ref.at[from_behind], from_behind)
    yield
    a_behind.wait_recv()
    far_bottom = go(all_ref.at[from_ahead, bottom], all_ref.at[from_ahead, bottom], behind_a)
    others.append(across(all_ref.at[from_behind], from_behind))
    b_copies[2] = along_b(all_ref.at[from_ahead], from_ahead)
    others.append(across(all_ref.at[from_ahead], from_ahead))
    column = (a, a - 1, a + 1, a + 2)
    fars = {}

    def onward(k):
        below = plane_index(column[k], b - 1, core)
        above = plane_index(column[k], b + 1, core)
        yield
        b_copies[k][0].wait_recv()
        first = go(all_ref.at[below, top], all_ref.at[below, top], ahead_b)
        b_copies[k][1].wait_recv()
        second = go(all_ref.at[above, bottom], all_ref.at[above, bottom], behind_b)
        fars[k] = (first, second)
        others.append(across(all_ref.at[below], below))
        others.append(across(all_ref.at[above], above))

    yield from onward(0)
    yield
    far_top.wait_recv()
    far_bottom.wait_recv()
    b_copies[3] = along_b(all_ref.at[from_far], from_far)
    others.append(across(all_ref.at[from_far], from_far))
    yield from onward(1)
    yield from onward(2)
    yield from onward(3)
    for k in range(4):
        index = plane_index(column[k], b + 2, core)
        yield
        fars[k][0].wait_recv()
        fars[k][1].wait_recv()
        others.append(across(all_ref.at[index], index))
    yield
    for copy in others:
        copy.wait_recv()


PLANE_COPIES = 36


def add_rows(dst, sources, start, rows):
    step = 16 if rows % 16 == 0 else 8

    @pl.loop(0, rows // step)
    def _(i):
        at = pl.multiple_of(i * step, step)
        total = None
        for ref, first in sources:
            part = ref[pl.ds(first + at, step), :].astype(F32)
            total = part if total is None else total + part
        dst[pl.ds(start + at, step), :] = total.astype(dst.dtype)


def plane_scatter_steps(post, parts_ref, sum_ref, scratch):
    mine, other, b_far, b_near, a_far, a_near, local_sems = scratch
    a, b, core = plane_place()
    ahead_a, behind_a, ahead_b, behind_b, sibling = plane_partners()
    rows = a_far.shape[0]
    top, bottom = halves(a_far)
    high = top.size
    low = rows - high
    offsets = (2, 1, -1, 0)
    go = post.go
    crossing = {}
    order = [(k, 0) for k in range(4)] + [(k, j) for k in range(4) for j in (1, 2)]
    order += [(k, 3) for k in range(4)]
    for k, j in order:
        there = plane_index(b + offsets[k], a + offsets[j], 1 - core)
        crossing[k, j] = go(parts_ref.at[there], other.at[k, j], sibling)
    slots = mine.shape[0]
    loads = []

    def load():
        number = len(loads)
        if number < len(order):
            k, j = order[number]
            here = plane_index(a + offsets[k], b + offsets[j], core)
            slot = number % slots
            copy = pltpu.make_async_copy(
                parts_ref.at[here], mine.at[slot], local_sems.at[slot]
            )
            copy.start()
            loads.append(copy)

    for _ in range(slots - 1):
        load()

    def ready(k, j):
        number = order.index((k, j))
        load()
        crossing[k, j].wait_recv()
        loads[number].wait()
        return (other.at[k, j], mine.at[number % slots])

    far_b, near_b = {}, {}
    yield
    for k in range(4):
        block, extra = ready(k, 0)
        add_rows(block, [(block, 0), (extra, 0)], 0, rows)
        far_b[k] = (
            go(block.at[top], b_far.at[k, top], ahead_b),
            go(block.at[bottom], b_far.at[k, bottom], behind_b),
        )
    for k in range(4):
        far = b_far.at[k]
        yield
        block, extra = ready(k, 1)
        far_b[k][0].wait_recv()
        add_rows(block, [(block, 0), (extra, 0), (far, 0)], 0, high)
        add_rows(block, [(block, high), (extra, high)], high, low)
        first = go(block, b_near.at[0, k], ahead_b)
        block, extra = ready(k, 2)
        far_b[k][1].wait_recv()
        add_rows(block, [(block, 0), (extra, 0)], 0, high)
        add_rows(block, [(block, high), (extra, high), (far, high)], high, low)
        near_b[k] = (first, go(block, b_near.at[1, k], behind_b))
    far_a, near_a = [], []
    for k in range(4):
        yield
        block, extra = ready(k, 3)
        near_b[k][0].wait_recv()
        near_b[k][1].wait_recv()
        base = [block, extra, b_near.at[0, k], b_near.at[1, k]]
        upper = [(ref, 0) for ref in base]
        lower = [(ref, high) for ref in base]
        if k == 0:
            add_rows(block, upper, 0, high)
            add_rows(block, lower, high, low)
            far_a = [
                go(block.at[top], a_far.at[top], ahead_a),
                go(block.at[bottom], a_far.at[bottom], behind_a),
            ]
        elif k == 1:
            far_a[0].wait_recv()
            add_rows(block, upper + [(a_far, 0)], 0, high)
            add_rows(block, lower, high, low)
            near_a.append(go(block, a_near.at[0], ahead_a))
        elif k == 2:
            far_a[1].wait_recv()
            add_rows(block, upper, 0, high)
            add_rows(block, lower + [(a_far, high)], high, low)
            near_a.append(go(block, a_near.at[1], behind_a))
        else:
            near_a[0].wait_recv()
            near_a[1].wait_recv()
            add_rows(sum_ref, upper + [(a_near.at[0], 0), (a_near.at[1], 0)], 0, rows)


def plane_scatter_scratch(rows, columns, kind):
    return [
        pltpu.VMEM((4, rows, columns), kind),
        pltpu.VMEM((4, 4, rows, columns), kind),
        pltpu.VMEM((4, rows, columns), kind),
        pltpu.VMEM((2, 4, rows, columns), kind),
        pltpu.VMEM((rows, columns), kind),
        pltpu.VMEM((2, rows, columns), kind),
        pltpu.SemaphoreType.DMA((4,)),
    ]


OFFSETS = (2, 1, -1, 0)


def ring_places(a, b, core, tp):
    along_a = [(plane_index(a + offset, b, core), tp) for offset in OFFSETS[:3]]
    along_b = [(plane_index(a, b + offset, core), tp) for offset in OFFSETS[:3]]
    return (along_a, along_b, (plane_index(b, a, 1 - core), tp))


def brief_partners():
    along_a, along_b, sibling = ring_places(*plane_place(), lax.axis_index("tp"))
    return tuple(along_a + along_b + [sibling])


BRIEF_COPIES = 16 + 12 + 3


def brief_scatter_steps(post, parts_ref, sum_ref, scratch):
    other, from_b, from_a = scratch
    a, b, core = plane_place()
    along_a, along_b, sibling = ring_places(a, b, core, lax.axis_index("tp"))
    go = post.go
    crossing, copies_b, copies_a = {}, {}, {}
    for k in range(4):
        for j in range(4):
            there = plane_index(b + OFFSETS[k], a + OFFSETS[j], 1 - core)
            crossing[k, j] = go(parts_ref.at[there], other.at[k, j], sibling)
    yield
    for k in range(4):
        for j in range(4):
            here = plane_index(a + OFFSETS[k], b + OFFSETS[j], core)
            crossing[k, j].wait_recv()
            block = other.at[k, j]
            block[...] = (block[...].astype(F32) + parts_ref[here].astype(F32)).astype(block.dtype)
            if j < 3:
                copies_b[k, j] = go(block, from_b.at[k, j], along_b[j])
    yield
    for k in range(4):
        total = other[k, 3].astype(F32)
        for j in range(3):
            copies_b[k, j].wait_recv()
            total = total + from_b[k, j].astype(F32)
        if k < 3:
            other[k, 3] = total.astype(other.dtype)
            copies_a[k] = go(other.at[k, 3], from_a.at[k], along_a[k])
    yield
    for k in range(3):
        copies_a[k].wait_recv()
        total = total + from_a[k].astype(F32)
    sum_ref[...] = total.astype(sum_ref.dtype)


def brief_scatter_scratch(rows, columns, kind):
    return [
        pltpu.VMEM((4, 4, rows, columns), kind),
        pltpu.VMEM((4, 3, rows, columns), kind),
        pltpu.VMEM((3, rows, columns), kind),
    ]


def brief_gather_steps(post, own_ref, all_ref):
    a, b, core = plane_place()
    along_a, along_b, sibling = ring_places(a, b, core, lax.axis_index("tp"))
    go = post.go
    me = plane_index(a, b, core)
    copies_a = [go(own_ref, all_ref.at[me], place) for place in along_a]
    copies_b, crossing = [], []

    def onward(src, index):
        copies_b.extend(go(src, all_ref.at[index], place) for place in along_b)
        crossing.append(go(src, all_ref.at[index], sibling))

    onward(own_ref, me)
    yield
    for k in range(3):
        index = plane_index(a - OFFSETS[k], b, core)
        copies_a[k].wait_recv()
        onward(all_ref.at[index], index)
    yield
    for k, offset in enumerate((0, 2, 1, -1)):
        for j in range(3):
            index = plane_index(a - offset, b - OFFSETS[j], core)
            copies_b[3 * k + j].wait_recv()
            crossing.append(go(all_ref.at[index], all_ref.at[index], sibling))
    yield
    for copy in crossing:
        copy.wait_recv()


LINE_COPIES = 4


def line_gather_steps(post, own_ref, all_ref, arrived=None):
    tp = lax.axis_index("tp")
    ahead, behind = line_partners()
    top, bottom = halves(own_ref)
    before, after, far = wrap(tp - 1), wrap(tp + 1), wrap(tp + 2)
    first = post.go(own_ref, all_ref.at[tp], ahead)
    second = post.go(own_ref, all_ref.at[tp], behind)
    if arrived is not None:
        arrived(tp)
    yield
    first.wait_recv()
    third = post.go(all_ref.at[before, top], all_ref.at[before, top], ahead)
    second.wait_recv()
    fourth = post.go(all_ref.at[after, bottom], all_ref.at[after, bottom], behind)
    if arrived is not None:
        yield
        arrived(before)
        yield
        arrived(after)
    yield
    third.wait_recv()
    fourth.wait_recv()
    if arrived is not None:
        arrived(far)


def line_scatter_steps(post, make, far, near, finish):
    ahead, behind = line_partners()
    top, bottom = halves(far)
    high = top.size
    rows = far.shape[0]
    block = make(2)
    first = post.go(block.at[top], far.at[top], ahead)
    second = post.go(block.at[bottom], far.at[bottom], behind)
    yield
    block = make(1)
    yield
    first.wait_recv()
    add_rows(block, [(block, 0), (far, 0)], 0, high)
    third = post.go(block, near.at[0], ahead)
    other = make(-1)
    yield
    second.wait_recv()
    add_rows(other, [(other, high), (far, high)], high, rows - high)
    fourth = post.go(other, near.at[1], behind)
    own = make(0)
    yield
    third.wait_recv()
    fourth.wait_recv()
    finish(own, near.at[0], near.at[1])


def dispatch_kernel(own_ref, pair_ref, down_ref, all_ref, pair_all, down_all, *rest):
    send_sems, recv_sems, local_sems = rest
    me = lax.axis_index("ep")
    tp = lax.axis_index("tp")
    greet(plane_partners() + line_partners())
    post = Post(send_sems, recv_sems)
    locals_ = [
        pltpu.make_async_copy(own_ref, all_ref.at[me], local_sems.at[0]),
        pltpu.make_async_copy(pair_ref, pair_all.at[tp], local_sems.at[1]),
        pltpu.make_async_copy(down_ref, down_all.at[tp], local_sems.at[2]),
    ]
    for copy in locals_:
        copy.start()
    together(
        plane_gather_steps(post, own_ref, all_ref),
        line_gather_steps(post, pair_ref, pair_all),
        line_gather_steps(post, down_ref, down_all),
    )
    post.finish()
    for copy in locals_:
        copy.wait()


def dispatch(own, pair, down, number):
    count = PLANE_COPIES + 2 * LINE_COPIES
    return pl.pallas_call(
        dispatch_kernel,
        out_shape=[
            jax.ShapeDtypeStruct((32,) + own.shape, own.dtype),
            jax.ShapeDtypeStruct((4,) + pair.shape, pair.dtype),
            jax.ShapeDtypeStruct((4,) + down.shape, down.dtype),
        ],
        in_specs=[ANY] * 3,
        out_specs=[ANY] * 3,
        scratch_shapes=[
            pltpu.SemaphoreType.DMA((count,)),
            pltpu.SemaphoreType.DMA((count,)),
            pltpu.SemaphoreType.DMA((3,)),
        ],
        compiler_params=pltpu.CompilerParams(collective_id=number, has_side_effects=True),
        name="dispatch",
    )(own, pair, down)


def collect_kernel(parts_ref, weights_ref, sum_ref, weight_sum, *rest):
    send_sems, recv_sems = rest[-2:]
    line, line_far, line_near, line_sems = rest[7:11]
    tp = lax.axis_index("tp")
    loads = {}
    for number, offset in enumerate((2, 1, -1, 0)):
        loads[offset] = pltpu.make_async_copy(
            weights_ref.at[wrap(tp + offset)], line.at[number], line_sems.at[number]
        )
        loads[offset].start()
    greet(plane_partners() + line_partners())
    post = Post(send_sems, recv_sems)

    def make(offset):
        loads[offset].wait()
        return line.at[(2, 1, -1, 0).index(offset)]

    def finish(own, first, second):
        add_rows(weight_sum, [(own, 0), (first, 0), (second, 0)], 0, own.shape[0])

    together(
        plane_scatter_steps(post, parts_ref, sum_ref, rest[:7]),
        line_scatter_steps(post, make, line_far, line_near, finish),
    )
    post.finish()


def collect(parts, weights, number):
    _, rows, columns = parts.shape
    _, weight_rows, weight_columns = weights.shape
    count = PLANE_COPIES + LINE_COPIES
    return pl.pallas_call(
        collect_kernel,
        out_shape=[
            jax.ShapeDtypeStruct((rows, columns), F32),
            jax.ShapeDtypeStruct((weight_rows, weight_columns), F32),
        ],
        in_specs=[ANY, ANY],
        out_specs=[VMEM, VMEM],
        scratch_shapes=plane_scatter_scratch(rows, columns, parts.dtype)
        + [
            pltpu.VMEM((4, weight_rows, weight_columns), BF16),
            pltpu.VMEM((weight_rows, weight_columns), BF16),
            pltpu.VMEM((2, weight_rows, weight_columns), BF16),
            pltpu.SemaphoreType.DMA((4,)),
            pltpu.SemaphoreType.DMA((count,)),
            pltpu.SemaphoreType.DMA((count,)),
        ],
        compiler_params=pltpu.CompilerParams(
            collective_id=number, has_side_effects=True, vmem_limit_bytes=56 << 20
        ),
        name="collect",
    )(parts, weights)


def split_float(values):
    high = values.astype(BF16)
    return (high, (values - high.astype(F32)).astype(BF16))


def split_three(values):
    high = values.astype(BF16)
    rest = values - high.astype(F32)
    middle = rest.astype(BF16)
    return (high, middle, (rest - middle.astype(F32)).astype(BF16))


def head_mean(values):
    same = (
        lax.broadcasted_iota(jnp.int32, (128, 128), 0) // 64
        == lax.broadcasted_iota(jnp.int32, (128, 128), 1) // 64
    ).astype(BF16)
    high, low = split_float(values)
    total = jnp.dot(high, same, preferred_element_type=F32)
    total = total + jnp.dot(low, same, preferred_element_type=F32)
    return total * (1.0 / 64.0)


def other_half(values):
    lane = lax.broadcasted_iota(jnp.int32, values.shape, 1)
    return jnp.where(
        lax.rem(lane, 64) < 32, pltpu.roll(values, 96, 1), pltpu.roll(values, 32, 1)
    )


def head_ready(raw, gain, cosine, sine):
    normed = raw * lax.rsqrt(head_mean(raw * raw) + 1e-06) * gain
    return normed * cosine + other_half(normed) * sine


def head_back(grad, raw, gain, cosine, sine):
    grad = grad * cosine + other_half(grad * sine)
    scale = lax.rsqrt(head_mean(raw * raw) + 1e-06)
    plain = raw * scale
    grad_gain = jnp.sum(grad * plain, axis=0, keepdims=True)
    grad = grad * gain
    return (scale * (grad - plain * head_mean(grad * plain)), grad_gain)


def row_scale(values):
    return lax.rsqrt(jnp.mean(values * values, axis=1, keepdims=True) + 1e-05)


def exchange(values):
    return jnp.concatenate([values[:, 64:], values[:, :64]], axis=1)


def head_pairs(block):
    rows = block.shape[0]
    low = lax.broadcasted_iota(jnp.int32, (rows, 128), 1) < 64
    left, right = block[:, :128], block[:, 128:]
    zero = jnp.zeros_like(left)
    straight = jnp.concatenate([jnp.where(low, left, zero), jnp.where(low, zero, right)], axis=0)
    crossed = jnp.concatenate([jnp.where(low, zero, left), jnp.where(low, right, zero)], axis=0)
    return (straight, crossed)


def heads_back(straight, crossed):
    rows = straight.shape[0] // 2
    low = lax.broadcasted_iota(jnp.int32, (rows, 128), 1) < 64
    left = jnp.where(low, straight[:rows], crossed[:rows])
    right = jnp.where(low, crossed[rows:], straight[rows:])
    return jnp.concatenate([left, right], axis=1)


def attend_block(query, keys, values, bias):
    rows = query.shape[0]
    outs = []
    for pair, key_part, value_part in zip(
        head_pairs(query), (keys, exchange(keys)), (values, exchange(values)), strict=True
    ):
        halves_out = []
        for number in range(2):
            part = pair[number * rows : (number + 1) * rows]
            scores = lax.dot_general(part, key_part, CONTRACT_LAST, preferred_element_type=F32)
            weights = jnp.exp(scores * 0.125 + bias)
            total_weight = jnp.sum(weights, axis=1, keepdims=True)
            out = jnp.dot(weights.astype(BF16), value_part, preferred_element_type=F32)
            halves_out.append(out / total_weight)
        outs.append(jnp.concatenate(halves_out, axis=0))
    return heads_back(*outs).astype(BF16)


def block_rows(block):
    return pl.ds(pl.multiple_of(block * 256, 256), 256)


def opening_kernel(
    inputs, gain_one, query_weight, key_weight, value_weight, query_gain, key_gain, cosine, sine,
    seg_column, seg_row, live_row, output_weight, gain_two, router, routes, cotangent,
    normed, raw, query, keys, values, mixed, residual, block, gates, grad_all,
    parts, far, near, send_sems, recv_sems, local_sem,
):
    tp = lax.axis_index("tp")
    local = pltpu.make_async_copy(cotangent, grad_all.at[lax.axis_index("ep")], local_sem)
    local.start()
    hidden = inputs[...].astype(F32)
    normed[tp] = (hidden * row_scale(hidden) * gain_one[...]).astype(BF16)
    greet(plane_partners() + line_partners())
    post = Post(send_sems, recv_sems)

    def project(place):
        rows = block_rows(place)
        part = normed[place]
        cos, sin = cosine[rows, :], sine[rows, :]
        both = jnp.dot(part, query_weight[...], preferred_element_type=F32)
        raw[rows, :256] = both
        for lanes in (slice(0, 128), slice(128, 256)):
            query[rows, lanes] = head_ready(both[:, lanes], query_gain[...], cos, sin).astype(BF16)
        one = jnp.dot(part, key_weight[...], preferred_element_type=F32)
        raw[rows, 256:] = one
        keys[rows, :] = head_ready(one, key_gain[...], cos, sin).astype(BF16)
        values[rows, :] = jnp.dot(part, value_weight[...], preferred_element_type=F32).astype(BF16)

    def make(offset):
        place = wrap(tp + offset)
        rows = block_rows(place)
        position = place * 256 + lax.broadcasted_iota(jnp.int32, (256, 1024), 0)
        key_position = lax.broadcasted_iota(jnp.int32, (256, 1024), 1)
        allowed = (seg_column[rows, :] == seg_row[...]) & (
            (live_row[...] == 1) | (position == key_position)
        )
        bias = jnp.where(allowed, 0.0, -1e30).astype(F32)
        out = attend_block(query[rows, :], keys[...], values[...], bias)
        mixed[rows, :] = out
        part = parts.at[(2, 1, -1, 0).index(offset)]
        part[...] = jnp.dot(out, output_weight[...], preferred_element_type=F32).astype(BF16)
        return part

    def finish(own, first, second):
        total = own[...].astype(F32) + first[...].astype(F32) + second[...].astype(F32)
        total = inputs[...].astype(F32) + total
        residual[...] = total
        normed_two = total * row_scale(total) * gain_two[...]
        block[:256, :] = normed_two.astype(BF16)
        logits = jnp.zeros((32, 256), F32)
        for piece in split_three(normed_two):
            logits = logits + lax.dot_general(
                router[...], piece, CONTRACT_LAST, preferred_element_type=F32
            )
        expert = lax.broadcasted_iota(jnp.int32, (32, 256), 0)
        named = expert < 0
        for choice in range(8):
            named = named | (routes[choice : choice + 1, :] == expert)
        top_logit = jnp.max(jnp.where(named, logits, -1e30), axis=0, keepdims=True)
        raised = jnp.where(named, jnp.exp(jnp.where(named, logits - top_logit, 0.0)), 0.0)
        probs = raised / jnp.sum(raised, axis=0, keepdims=True)
        gates[...] = probs
        high, low = split_float(probs)
        block[256:, :] = jnp.concatenate([high[:16], low[:16], high[16:], low[16:]], axis=1)

    together(
        chain(
            line_gather_steps(post, normed.at[tp], normed, project),
            line_scatter_steps(post, make, far, near, finish),
        ),
        plane_gather_steps(post, cotangent, grad_all),
    )
    post.finish()
    local.wait()


def opening(arguments, number):
    count = 2 * LINE_COPIES + PLANE_COPIES
    return pl.pallas_call(
        opening_kernel,
        out_shape=[
            jax.ShapeDtypeStruct((4, 256, 1024), BF16),
            jax.ShapeDtypeStruct((1024, 384), F32),
            jax.ShapeDtypeStruct((1024, 256), BF16),
            jax.ShapeDtypeStruct((1024, 128), BF16),
            jax.ShapeDtypeStruct((1024, 128), BF16),
            jax.ShapeDtypeStruct((1024, 256), BF16),
            jax.ShapeDtypeStruct((256, 1024), F32),
            jax.ShapeDtypeStruct((256 + EXTRA, 1024), BF16),
            jax.ShapeDtypeStruct((32, 256), F32),
            jax.ShapeDtypeStruct((32, 256, 1024), BF16),
        ],
        in_specs=[VMEM] * (len(arguments) - 1) + [ANY],
        out_specs=[VMEM] * 9 + [ANY],
        scratch_shapes=[
            pltpu.VMEM((4, 256, 1024), BF16),
            pltpu.VMEM((256, 1024), BF16),
            pltpu.VMEM((2, 256, 1024), BF16),
            pltpu.SemaphoreType.DMA((count,)),
            pltpu.SemaphoreType.DMA((count,)),
            pltpu.SemaphoreType.DMA,
        ],
        compiler_params=pltpu.CompilerParams(
            collective_id=number, has_side_effects=True, vmem_limit_bytes=56 << 20
        ),
        name="opening",
    )(*arguments)


def attend_back_block(query, grad, keys, values, bias, keys_sum, values_sum):
    rows = query.shape[0]
    query_pairs = head_pairs(query)
    grad_pairs = head_pairs(grad)
    key_parts = (keys, exchange(keys))
    value_parts = (values, exchange(values))
    outs = []
    for side in range(2):
        halves_out = []
        for number in range(2):
            part = query_pairs[side][number * rows : (number + 1) * rows]
            grad_part = grad_pairs[side][number * rows : (number + 1) * rows]
            scores = lax.dot_general(
                key_parts[side], part, CONTRACT_LAST, preferred_element_type=F32
            )
            raised = jnp.exp(scores * 0.125 + bias)
            weights = raised * (1.0 / jnp.sum(raised, axis=0, keepdims=True))
            grad_weights = lax.dot_general(
                value_parts[side], grad_part, CONTRACT_LAST, preferred_element_type=F32
            )
            inner = jnp.sum(weights * grad_weights, axis=0, keepdims=True)
            grad_scores = (weights * (grad_weights - inner)).astype(BF16)
            halves_out.append(
                lax.dot_general(
                    grad_scores, key_parts[side], CONTRACT_ROWS, preferred_element_type=F32
                )
            )
            keys_sum[side] += jnp.dot(grad_scores, part, preferred_element_type=F32)
            values_sum[side] += jnp.dot(
                weights.astype(BF16), grad_part, preferred_element_type=F32
            )
        outs.append(jnp.concatenate(halves_out, axis=0))
    return heads_back(*outs) * 0.125


SMALL_ROWS = 16


def closing_kernel(
    back, residual, gates, cotangent, gain_two, router, query, keys, values, mixed,
    output_weight, query_weight, key_weight, value_weight, raw, normed, inputs, gain_one,
    query_gain, key_gain, cosine, sine, seg_column, seg_row, live_column, out_parts,
    grad_inputs, dense_all, small_all, combined,
    grad_all, grad_residual, low, keys_sum, values_sum, output_sum, parts, far, near,
    dense, dense_own, small, small_own, small_line, small_sum, query_gain_sum, gain_one_sum, *rest,
):
    out_scratch, dense_scratch, small_scratch = rest[:7], rest[7:10], rest[10:13]
    post = Post(rest[13], rest[14])
    me = lax.axis_index("ep")
    tp = lax.axis_index("tp")
    ahead, behind = line_partners()
    across = (me, wrap(tp + 2))

    lines = back[256:, :]
    grad_gates = jnp.concatenate(
        [lines[:, :256] + lines[:, 256:512], lines[:, 512:768] + lines[:, 768:]], axis=0
    )
    probs = gates[...]
    grad_logits = probs * (grad_gates - jnp.sum(probs * grad_gates, axis=0, keepdims=True))
    grad_two = back[:256, :]
    logit_pieces = split_three(grad_logits)
    for piece in logit_pieces:
        grad_two = grad_two + lax.dot_general(
            piece, router[...], CONTRACT_ROWS, preferred_element_type=F32
        )
    total = residual[...]
    scale = row_scale(total)
    plain = total * scale
    grad_gain_two = jnp.sum(grad_two * plain, axis=0, keepdims=True)
    normed_pieces = split_three(plain * gain_two[...])
    grad_router = jnp.zeros((32, 1024), F32)
    for first, second in ((0, 0), (0, 1), (1, 0), (1, 1), (0, 2), (2, 0)):
        grad_router = grad_router + jnp.dot(
            logit_pieces[first], normed_pieces[second], preferred_element_type=F32
        )
    grad_two = grad_two * gain_two[...]
    grad_total = cotangent[...].astype(F32) + scale * (
        grad_two - plain * jnp.mean(grad_two * plain, axis=1, keepdims=True)
    )
    grad_residual[...] = grad_total
    grad_all[tp] = grad_total.astype(BF16)
    greet(brief_partners() + (ahead, behind, across))

    keys_sum[...] = jnp.zeros_like(keys_sum)
    values_sum[...] = jnp.zeros_like(values_sum)
    output_sum[...] = jnp.zeros_like(output_sum)
    query_gain_sum[...] = jnp.zeros_like(query_gain_sum)
    gain_one_sum[...] = jnp.zeros_like(gain_one_sum)

    def attention(place):
        rows = block_rows(place)
        grad = grad_all[place]
        output_sum[...] += lax.dot_general(
            mixed[rows, :], grad, CONTRACT_ROWS, preferred_element_type=F32
        )
        grad_mixed = lax.dot_general(
            grad, output_weight[...], CONTRACT_LAST, preferred_element_type=F32
        ).astype(BF16)
        key_position = lax.broadcasted_iota(jnp.int32, (1024, 256), 0)
        position = place * 256 + lax.broadcasted_iota(jnp.int32, (1024, 256), 1)
        allowed = (seg_column[...] == seg_row[:, rows]) & (
            (live_column[...] == 1) | (position == key_position)
        )
        bias = jnp.where(allowed, 0.0, -1e30).astype(F32)
        grad_query = attend_back_block(
            query[rows, :], grad_mixed, keys[...], values[...], bias, keys_sum, values_sum
        )
        for lanes in (slice(0, 128), slice(128, 256)):
            grad_raw, grad_gain = head_back(
                grad_query[:, lanes],
                raw[rows, lanes],
                query_gain[...],
                cosine[rows, :],
                sine[rows, :],
            )
            low[rows, lanes] = grad_raw.astype(BF16)
            query_gain_sum[...] += grad_gain

    out_steps = plane_scatter_steps(post, out_parts, combined, out_scratch)
    line_steps = line_gather_steps(post, grad_all.at[tp], grad_all, attention)
    for _ in line_steps:
        next(out_steps, None)
    grad_raw, grad_key_gain = head_back(
        (keys_sum[0] + exchange(keys_sum[1])) * 0.125,
        raw[:, 256:],
        key_gain[...],
        cosine[...],
        sine[...],
    )
    low[:, 256:384] = grad_raw.astype(BF16)
    low[:, 384:] = (values_sum[0] + exchange(values_sum[1])).astype(BF16)

    def make(offset):
        rows = block_rows(wrap(tp + offset))
        total = lax.dot_general(
            low[rows, :256], query_weight[...], CONTRACT_LAST, preferred_element_type=F32
        )
        total = total + lax.dot_general(
            low[rows, 256:384], key_weight[...], CONTRACT_LAST, preferred_element_type=F32
        )
        total = total + lax.dot_general(
            low[rows, 384:], value_weight[...], CONTRACT_LAST, preferred_element_type=F32
        )
        gain_one_sum[...] += jnp.sum(
            total * normed[rows, :].astype(F32), axis=0, keepdims=True
        )
        part = parts.at[(2, 1, -1, 0).index(offset)]
        part[...] = total.astype(BF16)
        return part

    def finish(own, first, second):
        grad_one = own[...].astype(F32) + first[...].astype(F32) + second[...].astype(F32)
        hidden = inputs[...].astype(F32)
        scale = row_scale(hidden)
        plain = hidden * scale
        grad_one = grad_one * gain_one[...]
        grad_inputs[...] = (
            grad_residual[...]
            + scale * (grad_one - plain * jnp.mean(grad_one * plain, axis=1, keepdims=True))
        ).astype(BF16)

    def fill_small():
        grad_gain_one = gain_one_sum[...] / gain_one[...]
        small[...] = jnp.zeros_like(small)
        for part in range(8):
            lanes = slice(part * 128, (part + 1) * 128)
            small[2 * part] = grad_router[:16, lanes]
            small[2 * part + 1] = grad_router[16:, lanes]
            small[16, part : part + 1, :] = grad_gain_one[:, lanes]
            small[16, 8 + part : 9 + part, :] = grad_gain_two[:, lanes]
        small[17, 0:1, :] = query_gain_sum[...]
        small[17, 1:2, :] = grad_key_gain

    def dense_steps():
        weights = lax.dot_general(
            normed[...], low[...], CONTRACT_ROWS, preferred_element_type=F32
        ).astype(BF16)
        for part in range(32):
            dense[part, :, :512] = weights[part * 32 : (part + 1) * 32]
        for part in range(4):
            block = output_sum[:, part * 256 : (part + 1) * 256].astype(BF16)
            for piece in range(8):
                dense[part * 8 + piece, :, 512:] = block[piece * 32 : (piece + 1) * 32]
        yield from brief_scatter_steps(post, dense, dense_own, dense_scratch)
        dense_all[me] = dense_own[...]
        yield from brief_gather_steps(post, dense_own, dense_all)

    def small_steps():
        fill_small()
        yield from brief_scatter_steps(post, small, small_own, small_scratch)
        line = [
            post.go(small_own, small_line.at[0], ahead),
            post.go(small_own, small_line.at[1], behind),
            post.go(small_own, small_line.at[2], across),
        ]
        yield
        for copy in line:
            copy.wait_recv()
        small_sum[...] = small_own[...] + small_line[0] + small_line[1] + small_line[2]
        small_all[me] = small_sum[...]
        yield from brief_gather_steps(post, small_sum, small_all)

    line_steps = line_scatter_steps(post, make, far, near, finish)
    for _ in range(4):
        next(line_steps)
    together(dense_steps(), small_steps(), line_steps, out_steps)
    post.finish()


def closing(arguments, number):
    count = 2 * LINE_COPIES + PLANE_COPIES + 4 * BRIEF_COPIES + 3
    return pl.pallas_call(
        closing_kernel,
        out_shape=[
            jax.ShapeDtypeStruct((256, 1024), BF16),
            jax.ShapeDtypeStruct((32, 32, 768), BF16),
            jax.ShapeDtypeStruct((32, SMALL_ROWS, 128), F32),
            jax.ShapeDtypeStruct((256, 1024), F32),
        ],
        in_specs=[VMEM] * (len(arguments) - 1) + [ANY],
        out_specs=[VMEM] * 4,
        scratch_shapes=[
            pltpu.VMEM((4, 256, 1024), BF16),
            pltpu.VMEM((256, 1024), F32),
            pltpu.VMEM((1024, 512), BF16),
            pltpu.VMEM((2, 1024, 128), F32),
            pltpu.VMEM((2, 1024, 128), F32),
            pltpu.VMEM((256, 1024), F32),
            pltpu.VMEM((4, 256, 1024), BF16),
            pltpu.VMEM((256, 1024), BF16),
            pltpu.VMEM((2, 256, 1024), BF16),
            pltpu.VMEM((32, 32, 768), BF16),
            pltpu.VMEM((32, 768), BF16),
            pltpu.VMEM((32, SMALL_ROWS, 128), F32),
            pltpu.VMEM((SMALL_ROWS, 128), F32),
            pltpu.VMEM((3, SMALL_ROWS, 128), F32),
            pltpu.VMEM((SMALL_ROWS, 128), F32),
            pltpu.VMEM((1, 128), F32),
            pltpu.VMEM((1, 1024), F32),
        ]
        + plane_scatter_scratch(256, 1024, BF16)
        + brief_scatter_scratch(32, 768, BF16)
        + brief_scatter_scratch(SMALL_ROWS, 128, F32)
        + [pltpu.SemaphoreType.DMA((count,)), pltpu.SemaphoreType.DMA((count,))],
        compiler_params=pltpu.CompilerParams(
            collective_id=number, has_side_effects=True, vmem_limit_bytes=58 << 20
        ),
        name="closing",
    )(*arguments)


def finish_kernel(
    dense, weights, residual, combined,
    result, grad_query, grad_key, grad_value, grad_output, grad_gate, grad_up, grad_down,
):
    result[...] = (residual[...] + combined[...]).astype(BF16)
    grad_query[...] = dense[:, :256].astype(F32)
    grad_key[...] = dense[:, 256:384].astype(F32)
    grad_value[...] = dense[:, 384:512].astype(F32)
    for part in range(4):
        grad_output[:, part * 256 : (part + 1) * 256] = dense[
            part * 256 : (part + 1) * 256, 512:
        ].astype(F32)
    grad_gate[0] = weights[:1024, :]
    grad_up[0] = weights[1024:2048, :]
    grad_down[0] = weights[2048:, :].T


def finish_all(dense, weights, residual, combined):
    return pl.pallas_call(
        finish_kernel,
        out_shape=[
            jax.ShapeDtypeStruct((256, 1024), BF16),
            jax.ShapeDtypeStruct((1024, 256), F32),
            jax.ShapeDtypeStruct((1024, 128), F32),
            jax.ShapeDtypeStruct((1024, 128), F32),
            jax.ShapeDtypeStruct((256, 1024), F32),
            jax.ShapeDtypeStruct((1, 1024, 128), F32),
            jax.ShapeDtypeStruct((1, 1024, 128), F32),
            jax.ShapeDtypeStruct((1, 128, 1024), F32),
        ],
        in_specs=[VMEM] * 4,
        out_specs=[VMEM] * 8,
        compiler_params=pltpu.CompilerParams(vmem_limit_bytes=40 << 20),
        name="finish_all",
    )(dense, weights, residual, combined)


GROUP = 4


def experts_kernel(
    number_ref, rows_ref, grads_ref, pair_ref, down_ref,
    out_ref, back_ref, weight_grads_ref,
    gate_full, up_full, gate_sum, up_sum, down_sum, rows_own, grads_own, gates_own, select,
):
    step = pl.program_id(0)
    expert = number_ref[0]
    lane_row = lax.rem(expert, 16)
    upper = expert >= 16

    @pl.when(step == 0)
    def _():
        for part in range(4):
            columns = slice(part * 128, (part + 1) * 128)
            gate_full[:, columns] = pair_ref[part, :1024, :]
            up_full[:, columns] = pair_ref[part, 1024:, :]
        gate_sum[...] = jnp.zeros_like(gate_sum)
        up_sum[...] = jnp.zeros_like(up_sum)
        down_sum[...] = jnp.zeros_like(down_sum)

    earlier = (
        lax.broadcasted_iota(jnp.int32, (256, 256), 0)
        <= lax.broadcasted_iota(jnp.int32, (256, 256), 1)
    ).astype(BF16)
    slot = lax.broadcasted_iota(jnp.int32, (SLOTS, 256), 0).astype(F32)
    extra_row = lax.broadcasted_iota(jnp.int32, (EXTRA, 1024), 0) == lane_row
    for part in range(GROUP):
        extras = jnp.where(extra_row, rows_ref[part, 256:, :].astype(F32), 0.0)
        extras = jnp.sum(extras, axis=0, keepdims=True)
        gates = jnp.where(
            upper, extras[:, 512:768] + extras[:, 768:], extras[:, :256] + extras[:, 256:512]
        )
        named = jnp.broadcast_to(gates, (16, 256)) > 0.0
        rank = jnp.dot(named.astype(BF16), earlier, preferred_element_type=F32)[:1] - 1.0
        chosen = (slot == rank) & (gates > 0.0)
        chosen_low = chosen.astype(BF16)
        at = slice(part * SLOTS, (part + 1) * SLOTS)
        select[at, :] = chosen_low
        rows_own[at, :] = jnp.dot(
            chosen_low, rows_ref[part, :256, :], preferred_element_type=F32
        ).astype(BF16)
        grads_own[at, :] = jnp.dot(
            chosen_low, grads_ref[part], preferred_element_type=F32
        ).astype(BF16)
        gates_own[at, :] = jnp.sum(jnp.where(chosen, gates, 0.0), axis=1, keepdims=True)

    rows_in = rows_own[...]
    gate_pre = jnp.dot(rows_in, gate_full[...], preferred_element_type=F32)
    up_pre = jnp.dot(rows_in, up_full[...], preferred_element_type=F32)
    sigmoid = 1.0 / (1.0 + jnp.exp(-gate_pre))
    silu = gate_pre * sigmoid
    act = (silu * up_pre).astype(BF16)
    out = jnp.dot(act, down_ref[...], preferred_element_type=F32).astype(BF16).astype(F32)
    gate_factor = gates_own[...]
    grads_in = grads_own[...].astype(F32)
    grad_gates = jnp.sum(grads_in * out, axis=1, keepdims=True)
    weighted = (gate_factor * out).astype(BF16)
    grad_out = (gate_factor * grads_in).astype(BF16)
    grad_act = lax.dot_general(
        grad_out, down_ref[...], CONTRACT_LAST, preferred_element_type=F32
    )
    down_sum[...] += lax.dot_general(
        grad_out, act, CONTRACT_ROWS, preferred_element_type=F32
    )
    grad_gate_pre = (grad_act * up_pre * sigmoid * (1.0 + gate_pre * (1.0 - sigmoid))).astype(BF16)
    grad_up_pre = (grad_act * silu).astype(BF16)
    gate_sum[...] += lax.dot_general(
        rows_in, grad_gate_pre, CONTRACT_ROWS, preferred_element_type=F32
    )
    up_sum[...] += lax.dot_general(
        rows_in, grad_up_pre, CONTRACT_ROWS, preferred_element_type=F32
    )
    grad_rows = lax.dot_general(
        grad_gate_pre, gate_full[...], CONTRACT_LAST, preferred_element_type=F32
    )
    grad_rows = grad_rows + lax.dot_general(
        grad_up_pre, up_full[...], CONTRACT_LAST, preferred_element_type=F32
    )
    grad_rows = grad_rows.astype(BF16)
    nothing = jnp.zeros((1, 512), F32)
    for part in range(GROUP):
        at = slice(part * SLOTS, (part + 1) * SLOTS)
        chosen_low = select[at, :]
        out_ref[part] = lax.dot_general(
            chosen_low, weighted[at], CONTRACT_ROWS, preferred_element_type=F32
        ).astype(BF16)
        back_ref[part, :256, :] = lax.dot_general(
            chosen_low, grad_rows[at], CONTRACT_ROWS, preferred_element_type=F32
        ).astype(BF16)
        spread = jnp.sum(chosen_low.astype(F32) * grad_gates[at], axis=0, keepdims=True)
        high = spread.astype(BF16).astype(F32)
        both = jnp.concatenate([high, spread - high], axis=1)
        line = jnp.concatenate(
            [jnp.where(upper, nothing, both), jnp.where(upper, both, nothing)], axis=1
        )
        back_ref[part, 256:, :] = jnp.where(extra_row, line, 0.0).astype(BF16)

    @pl.when(step == pl.num_programs(0) - 1)
    def _():
        for part in range(4):
            columns = slice(part * 128, (part + 1) * 128)
            weight_grads_ref[part, :1024, :] = gate_sum[:, columns].astype(BF16)
            weight_grads_ref[part, 1024:2048, :] = up_sum[:, columns].astype(BF16)
            weight_grads_ref[part, 2048:, :] = down_sum[:, columns].astype(BF16)


def run_experts(number, rows, grads, pair, down):
    sources = rows.shape[0]
    count = GROUP * SLOTS
    return pl.pallas_call(
        experts_kernel,
        out_shape=[
            jax.ShapeDtypeStruct((sources, 256, 1024), BF16),
            jax.ShapeDtypeStruct((sources, 256 + EXTRA, 1024), BF16),
            jax.ShapeDtypeStruct((4, 3072, 128), BF16),
        ],
        grid=(sources // GROUP,),
        in_specs=[
            pl.BlockSpec(memory_space=pltpu.SMEM),
            pl.BlockSpec((GROUP, 256 + EXTRA, 1024), lambda i: (i, 0, 0)),
            pl.BlockSpec((GROUP, 256, 1024), lambda i: (i, 0, 0)),
            pl.BlockSpec((4, 2048, 128), lambda i: (0, 0, 0)),
            pl.BlockSpec((512, 1024), lambda i: (0, 0)),
        ],
        out_specs=[
            pl.BlockSpec((GROUP, 256, 1024), lambda i: (i, 0, 0)),
            pl.BlockSpec((GROUP, 256 + EXTRA, 1024), lambda i: (i, 0, 0)),
            pl.BlockSpec((4, 3072, 128), lambda i: (0, 0, 0)),
        ],
        scratch_shapes=[
            pltpu.VMEM((1024, 512), BF16),
            pltpu.VMEM((1024, 512), BF16),
            pltpu.VMEM((1024, 512), F32),
            pltpu.VMEM((1024, 512), F32),
            pltpu.VMEM((1024, 512), F32),
            pltpu.VMEM((count, 1024), BF16),
            pltpu.VMEM((count, 1024), BF16),
            pltpu.VMEM((count, 1), F32),
            pltpu.VMEM((count, 256), BF16),
        ],
        compiler_params=pltpu.CompilerParams(vmem_limit_bytes=60 << 20),
        name="run_experts",
    )(number, rows, grads, pair, down)


def rotary_constants():
    position = np.arange(SEQ_LEN, dtype=np.float32)
    power = -(np.arange(32, dtype=np.float32) * np.float32(2.0)) / np.float32(64.0)
    frequency = np.float32(10000.0) ** power
    angles = position[:, None] * frequency[None, :]
    cosine, sine = np.cos(angles), np.sin(angles)
    return (np.tile(cosine, (1, 4)), np.concatenate([-sine, sine, -sine, sine], axis=1))


def shards(
    inputs,
    first_gain,
    query_weight,
    key_weight,
    value_weight,
    query_gain,
    key_gain,
    output_weight,
    second_gain,
    router_weight,
    gate_weight,
    up_weight,
    down_weight,
    segments,
    live_mask,
    routes,
    cotangent,
):
    gain_one = first_gain.astype(F32).reshape(1, -1)
    gain_two = second_gain.astype(F32).reshape(1, -1)
    query_scale = jnp.tile(query_gain.astype(F32), 2).reshape(1, -1)
    key_scale = jnp.tile(key_gain.astype(F32), 2).reshape(1, -1)
    cosine, sine = rotary_constants()
    seg_column, seg_row = segments.reshape(-1, 1), segments.reshape(1, -1)
    live_column, live_row = live_mask.reshape(-1, 1), live_mask.reshape(1, -1)
    router = router_weight.T
    normed, raw, query, keys, values, mixed, residual, block, gates, grad_all = opening(
        (
            inputs, gain_one, query_weight, key_weight, value_weight, query_scale, key_scale,
            cosine, sine, seg_column, seg_row, live_row, output_weight, gain_two, router, routes.T,
            cotangent,
        ),
        1,
    )
    pair = jnp.concatenate([gate_weight[0], up_weight[0]], axis=0)
    rows_all, pair_all, down_all = dispatch(block, pair, down_weight[0], 2)
    number = lax.axis_index("ep").astype(jnp.int32).reshape(1)
    out_parts, back_parts, weight_parts = run_experts(
        number, rows_all, grad_all, pair_all, down_all.reshape(512, 1024)
    )
    back, weight_sums = collect(back_parts, weight_parts, 3)
    grad_inputs, dense, small, combined = closing(
        (
            back, residual, gates, cotangent, gain_two, router, query, keys, values, mixed,
            output_weight, query_weight, key_weight, value_weight, raw, normed.reshape(1024, 1024),
            inputs, gain_one, query_scale, key_scale, cosine, sine, seg_column, seg_row,
            live_column, out_parts,
        ),
        4,
    )
    result, grad_query, grad_key, grad_value, grad_output, grad_gate, grad_up, grad_down = (
        finish_all(dense.reshape(1024, 768), weight_sums, residual, combined)
    )
    grad_router = small[:16].reshape(8, 32, 128).transpose(0, 2, 1).reshape(1024, 32)
    query_gain_sum, key_gain_sum = small[17, 0], small[17, 1]
    return (
        result,
        grad_inputs,
        small[16, :8].reshape(-1),
        grad_query,
        grad_key,
        grad_value,
        query_gain_sum[:64] + query_gain_sum[64:],
        key_gain_sum[:64] + key_gain_sum[64:],
        grad_output,
        small[16, 8:].reshape(-1),
        grad_router,
        grad_gate,
        grad_up,
        grad_down,
    )


def solution(mesh):
    return jax.shard_map(
        shards,
        mesh=mesh,
        in_specs=(
            P(("ep", "tp"), None),
            P(),
            P(None, "tp"),
            P(None, "tp"),
            P(None, "tp"),
            P(),
            P(),
            P("tp", None),
            P(),
            P(),
            P("ep", None, "tp"),
            P("ep", None, "tp"),
            P("ep", "tp", None),
            P("ep"),
            P("ep"),
            P(("ep", "tp"), None),
            P(("ep", "tp"), None),
        ),
        out_specs=(
            P(("ep", "tp"), None),
            P(("ep", "tp"), None),
            P(),
            P(None, "tp"),
            P(None, "tp"),
            P(None, "tp"),
            P(),
            P(),
            P("tp", None),
            P(),
            P(),
            P("ep", None, "tp"),
            P("ep", None, "tp"),
            P("ep", "tp", None),
        ),
        check_vma=False,
    )
```

```python
import jax
import jax.numpy as jnp
import numpy as np
from jax import lax
from jax.experimental import pallas as pl
from jax.experimental.pallas import tpu as pltpu
from jax.sharding import PartitionSpec as P

SEQ_LEN = 1024
HIGHEST_PRECISION = lax.Precision.HIGHEST
CONTRACT_ROWS = (((0,), (0,)), ((), ()))
CONTRACT_LAST = (((1,), (1,)), ((), ()))
MESH = pl.DeviceIdType.MESH
ANY = pl.BlockSpec(memory_space=pl.ANY)
VMEM = pl.BlockSpec(memory_space=pltpu.VMEM)
F32 = jnp.float32
BF16 = jnp.bfloat16
SLOTS = 96
EXTRA = 16


def wrap(value):
    return lax.rem(value + 4, 4)


def pick(core, first, second):
    return first * (1 - core) + second * core


def plane_place():
    ep = lax.axis_index("ep")
    core = lax.rem(ep, 2)
    z = lax.rem(lax.div(ep, 2), 4)
    x = lax.div(ep, 8)
    return (pick(core, x, z), pick(core, z, x), core)


def plane_index(a, b, core):
    a, b = wrap(a), wrap(b)
    return (pick(core, a, b) * 4 + pick(core, b, a)) * 2 + core


def plane_partners():
    a, b, core = plane_place()
    tp = lax.axis_index("tp")
    return (
        (plane_index(a + 1, b, core), tp),
        (plane_index(a - 1, b, core), tp),
        (plane_index(a, b + 1, core), tp),
        (plane_index(a, b - 1, core), tp),
        (plane_index(b, a, 1 - core), tp),
    )


def line_partners():
    ep, tp = lax.axis_index("ep"), lax.axis_index("tp")
    return ((ep, wrap(tp + 1)), (ep, wrap(tp - 1)))


def greet(partners):
    barrier = pltpu.get_barrier_semaphore()
    for partner in partners:
        pl.semaphore_signal(barrier, inc=1, device_id=partner, device_id_type=MESH)
    pl.semaphore_wait(barrier, len(partners))


def halves(ref):
    unit = 16 if ref.dtype == BF16 else 8
    rows = ref.shape[-2]
    top = (rows // 2 + unit - 1) // unit * unit
    return (pl.ds(0, top), pl.ds(top, rows - top))


def together(*tasks):
    waiting = [(0.0, number, task) for number, task in enumerate(tasks)]
    while waiting:
        waiting.sort(key=lambda entry: entry[:2])
        _, number, task = waiting.pop(0)
        due = next(task, None)
        if due is not None:
            waiting.append((due, number, task))


def resumed(due, task):
    yield due
    yield from task


def until_count(task, count):
    for number in range(count):
        due = next(task)
        if number < count - 1:
            yield due
    return due


def side_by_side(*tasks):
    waiting = [(due, number, task) for number, (due, task) in enumerate(tasks)]
    while waiting:
        waiting.sort(key=lambda entry: entry[:2])
        due, number, task = waiting.pop(0)
        yield due
        due = next(task, None)
        if due is not None:
            waiting.append((due, number, task))


class Clock:
    def __init__(self, now=0.0):
        self.now = now

    def spend(self, amount):
        self.now += amount
        return self.now

    def until(self, moment):
        self.now = max(self.now, moment)
        return self.now


def at(ref, *where):
    return lambda: ref.at[where]


def part_of(place):
    return place() if callable(place) else place


class Remote:
    def __init__(self, src, dst, send_sem, recv_sem, partner):
        self.all = (src, dst, send_sem, recv_sem, partner)

    def copy(self):
        src, dst, send_sem, recv_sem, partner = self.all
        return pltpu.make_async_remote_copy(
            src_ref=part_of(src),
            dst_ref=part_of(dst),
            send_sem=part_of(send_sem),
            recv_sem=part_of(recv_sem),
            device_id=partner,
            device_id_type=MESH,
        )

    def start(self):
        self.copy().start()

    def wait_send(self):
        self.copy().wait_send()

    def wait_recv(self):
        self.copy().wait_recv()


class Local:
    def __init__(self, src, dst, sem):
        self.all = (src, dst, sem)

    def start(self):
        pltpu.make_async_copy(*map(part_of, self.all)).start()

    def wait(self):
        pltpu.make_async_copy(*map(part_of, self.all)).wait()


class Post:
    def __init__(self, send_sems, recv_sems):
        self.send_sems, self.recv_sems, self.started = send_sems, recv_sems, []

    def go(self, src, dst, partner):
        copy = self.prepare(src, dst, partner)
        copy.start()
        return copy

    def prepare(self, src, dst, partner):
        number = len(self.started)
        copy = Remote(src, dst, at(self.send_sems, number), at(self.recv_sems, number), partner)
        self.started.append(copy)
        return copy

    def finish(self):
        for copy in self.started:
            copy.wait_send()


ARRIVAL = (
    (0, 0), (-1, 0), (1, 0), (0, -1), (0, 1), (2, 0), (-1, -1), (-1, 1),
    (1, -1), (1, 1), (2, -1), (2, 1), (0, 2), (-1, 2), (1, 2), (2, 2),
)


def plane_gather_events(post, own_ref, all_ref):
    a, b, core = plane_place()
    ahead_a, behind_a, ahead_b, behind_b, sibling = plane_partners()
    index = {place: plane_index(a + place[0], b + place[1], core) for place in ARRIVAL}
    top, bottom = halves(own_ref)

    def block(place):
        return own_ref if place == (0, 0) else at(all_ref, index[place])

    def copy(place, partner):
        return post.prepare(block(place), at(all_ref, index[place]), partner)

    def half_copy(place, half, partner):
        part = at(all_ref, index[place], half)
        return post.prepare(part, part, partner)

    a_copies = (copy((0, 0), ahead_a), copy((0, 0), behind_a))
    a_halves = (half_copy((-1, 0), top, ahead_a), half_copy((1, 0), bottom, behind_a))
    column = (0, -1, 1, 2)
    b_copies = [(copy((k, 0), ahead_b), copy((k, 0), behind_b)) for k in column]
    b_halves = [
        (half_copy((k, -1), top, ahead_b), half_copy((k, 1), bottom, behind_b)) for k in column
    ]
    crossing = [copy(place, sibling) for place in ARRIVAL]

    def start(*copies):
        for one in copies:
            one.start()

    def begin():
        start(*a_copies, *b_copies[0], crossing[0])

    def near_a(number):
        a_copies[number].wait_recv()
        start(a_halves[number], *b_copies[1 + number], crossing[1 + number])

    def far_a():
        a_halves[0].wait_recv()
        a_halves[1].wait_recv()
        start(*b_copies[3], crossing[5])

    def near_b(k):
        first = ARRIVAL.index((column[k], -1))
        for number in range(2):
            b_copies[k][number].wait_recv()
            start(b_halves[k][number], crossing[first + number])

    def far_b(k):
        b_halves[k][0].wait_recv()
        b_halves[k][1].wait_recv()
        start(crossing[12 + k])

    events = [
        (0.0, begin),
        (6.5, lambda: near_a(0)),
        (6.5, lambda: near_a(1)),
        (7.5, lambda: near_b(0)),
        (11.0, far_a),
        (15.0, lambda: near_b(1)),
        (21.0, lambda: near_b(2)),
        (24.0, lambda: far_b(0)),
        (28.0, lambda: near_b(3)),
        (32.0, lambda: far_b(1)),
        (40.0, lambda: far_b(2)),
        (44.0, lambda: far_b(3)),
    ]
    return (events, crossing)


def plane_gather_steps(post, own_ref, all_ref):
    events, crossing = plane_gather_events(post, own_ref, all_ref)
    for due, event in events:
        if due > 0.0:
            yield due
        event()
    yield 46.0
    for copy in crossing:
        copy.wait_recv()


PLANE_COPIES = 36


def add_rows(dst, sources, start, rows):
    step = 16 if rows % 16 == 0 else 8

    @pl.loop(0, rows // step)
    def _(i):
        at = pl.multiple_of(i * step, step)
        total = None
        for ref, first in sources:
            part = ref[pl.ds(first + at, step), :].astype(F32)
            total = part if total is None else total + part
        dst[pl.ds(start + at, step), :] = total.astype(dst.dtype)


def plane_scatter_steps(post, parts_ref, sum_ref, scratch, begin=0.0):
    mine, other, b_far, b_near, a_far, a_near, local_sems = scratch
    a, b, core = plane_place()
    ahead_a, behind_a, ahead_b, behind_b, sibling = plane_partners()
    rows = a_far.shape[0]
    top, bottom = halves(a_far)
    high = top.size
    low = rows - high
    offsets = (2, 1, -1, 0)
    go = post.go
    crossing = {}
    order = [(k, 0) for k in range(4)] + [(k, j) for k in range(4) for j in (1, 2)]
    order += [(k, 3) for k in range(4)]
    for k, j in order:
        there = plane_index(b + offsets[k], a + offsets[j], 1 - core)
        crossing[k, j] = go(parts_ref.at[there], other.at[k, j], sibling)
    slots = mine.shape[0]
    loads = []

    def load():
        number = len(loads)
        if number < len(order):
            k, j = order[number]
            here = plane_index(a + offsets[k], b + offsets[j], core)
            slot = number % slots
            copy = pltpu.make_async_copy(
                parts_ref.at[here], mine.at[slot], local_sems.at[slot]
            )
            copy.start()
            loads.append(copy)

    for _ in range(slots - 1):
        load()

    def ready(k, j):
        number = order.index((k, j))
        load()
        crossing[k, j].wait_recv()
        loads[number].wait()
        return (other.at[k, j], mine.at[number % slots])

    far_b, near_b = {}, {}
    for k in range(4):
        yield begin + 2.0 + 1.5 * k
        block, extra = ready(k, 0)
        add_rows(block, [(block, 0), (extra, 0)], 0, rows)
        far_b[k] = (
            go(block.at[top], b_far.at[k, top], ahead_b),
            go(block.at[bottom], b_far.at[k, bottom], behind_b),
        )
    for k in range(4):
        far = b_far.at[k]
        yield begin + 9.0 + 3.0 * k
        block, extra = ready(k, 1)
        far_b[k][0].wait_recv()
        add_rows(block, [(block, 0), (extra, 0), (far, 0)], 0, high)
        add_rows(block, [(block, high), (extra, high)], high, low)
        first = go(block, b_near.at[0, k], ahead_b)
        block, extra = ready(k, 2)
        far_b[k][1].wait_recv()
        add_rows(block, [(block, 0), (extra, 0)], 0, high)
        add_rows(block, [(block, high), (extra, high), (far, high)], high, low)
        near_b[k] = (first, go(block, b_near.at[1, k], behind_b))
    far_a, near_a = [], []
    for k in range(4):
        yield begin + (25.0, 31.0, 37.0, 45.0)[k]
        block, extra = ready(k, 3)
        near_b[k][0].wait_recv()
        near_b[k][1].wait_recv()
        base = [block, extra, b_near.at[0, k], b_near.at[1, k]]
        upper = [(ref, 0) for ref in base]
        lower = [(ref, high) for ref in base]
        if k == 0:
            add_rows(block, upper, 0, high)
            add_rows(block, lower, high, low)
            far_a = [
                go(block.at[top], a_far.at[top], ahead_a),
                go(block.at[bottom], a_far.at[bottom], behind_a),
            ]
        elif k == 1:
            far_a[0].wait_recv()
            add_rows(block, upper + [(a_far, 0)], 0, high)
            add_rows(block, lower, high, low)
            near_a.append(go(block, a_near.at[0], ahead_a))
        elif k == 2:
            far_a[1].wait_recv()
            add_rows(block, upper, 0, high)
            add_rows(block, lower + [(a_far, high)], high, low)
            near_a.append(go(block, a_near.at[1], behind_a))
        else:
            near_a[0].wait_recv()
            near_a[1].wait_recv()
            add_rows(sum_ref, upper + [(a_near.at[0], 0), (a_near.at[1], 0)], 0, rows)


def plane_scatter_scratch(rows, columns, kind):
    return [
        pltpu.VMEM((4, rows, columns), kind),
        pltpu.VMEM((4, 4, rows, columns), kind),
        pltpu.VMEM((4, rows, columns), kind),
        pltpu.VMEM((2, 4, rows, columns), kind),
        pltpu.VMEM((rows, columns), kind),
        pltpu.VMEM((2, rows, columns), kind),
        pltpu.SemaphoreType.DMA((4,)),
    ]


OFFSETS = (2, 1, -1, 0)


def ring_places(a, b, core, tp):
    along_a = [(plane_index(a + offset, b, core), tp) for offset in OFFSETS[:3]]
    along_b = [(plane_index(a, b + offset, core), tp) for offset in OFFSETS[:3]]
    return (along_a, along_b, (plane_index(b, a, 1 - core), tp))


def brief_partners():
    along_a, along_b, sibling = ring_places(*plane_place(), lax.axis_index("tp"))
    return tuple(along_a + along_b + [sibling])


BRIEF_COPIES = 16 + 12 + 3


def brief_scatter_steps(post, parts_ref, sum_ref, scratch, begin=0.0):
    other, from_b, from_a = scratch
    a, b, core = plane_place()
    along_a, along_b, sibling = ring_places(a, b, core, lax.axis_index("tp"))
    go = post.go
    crossing, copies_b, copies_a = {}, {}, {}
    for k in range(4):
        for j in range(4):
            there = plane_index(b + OFFSETS[k], a + OFFSETS[j], 1 - core)
            crossing[k, j] = go(parts_ref.at[there], other.at[k, j], sibling)
    yield begin + 3.0
    for k in range(4):
        for j in range(4):
            here = plane_index(a + OFFSETS[k], b + OFFSETS[j], core)
            crossing[k, j].wait_recv()
            block = other.at[k, j]
            block[...] = (block[...].astype(F32) + parts_ref[here].astype(F32)).astype(block.dtype)
            if j < 3:
                copies_b[k, j] = go(block, from_b.at[k, j], along_b[j])
    yield begin + 6.5
    for k in range(4):
        total = other[k, 3].astype(F32)
        for j in range(3):
            copies_b[k, j].wait_recv()
            total = total + from_b[k, j].astype(F32)
        if k < 3:
            other[k, 3] = total.astype(other.dtype)
            copies_a[k] = go(other.at[k, 3], from_a.at[k], along_a[k])
    yield begin + 10.0
    for k in range(3):
        copies_a[k].wait_recv()
        total = total + from_a[k].astype(F32)
    sum_ref[...] = total.astype(sum_ref.dtype)


def brief_scatter_scratch(rows, columns, kind):
    return [
        pltpu.VMEM((4, 4, rows, columns), kind),
        pltpu.VMEM((4, 3, rows, columns), kind),
        pltpu.VMEM((3, rows, columns), kind),
    ]


def brief_gather_steps(post, own_ref, all_ref, begin=0.0):
    a, b, core = plane_place()
    along_a, along_b, sibling = ring_places(a, b, core, lax.axis_index("tp"))
    go = post.go
    me = plane_index(a, b, core)
    copies_a = [go(own_ref, all_ref.at[me], place) for place in along_a]
    copies_b, crossing = [], []

    def onward(src, index):
        copies_b.extend(go(src, all_ref.at[index], place) for place in along_b)
        crossing.append(go(src, all_ref.at[index], sibling))

    onward(own_ref, me)
    yield begin + 3.0
    for k in range(3):
        index = plane_index(a - OFFSETS[k], b, core)
        copies_a[k].wait_recv()
        onward(all_ref.at[index], index)
    yield begin + 6.0
    for k, offset in enumerate((0, 2, 1, -1)):
        for j in range(3):
            index = plane_index(a - offset, b - OFFSETS[j], core)
            copies_b[3 * k + j].wait_recv()
            crossing.append(go(all_ref.at[index], all_ref.at[index], sibling))
    yield begin + 9.0
    for copy in crossing:
        copy.wait_recv()


LINE_COPIES = 4


def line_gather_steps(post, own_ref, all_ref, clock, near_time, far_time, arrived=None):
    tp = lax.axis_index("tp")
    ahead, behind = line_partners()
    top, bottom = halves(own_ref)
    before, after, far = wrap(tp - 1), wrap(tp + 1), wrap(tp + 2)
    begin = clock.now
    first = post.go(own_ref, all_ref.at[tp], ahead)
    second = post.go(own_ref, all_ref.at[tp], behind)
    if arrived is not None:
        yield from arrived(tp)
    yield clock.until(begin + near_time)
    first.wait_recv()
    third = post.go(all_ref.at[before, top], all_ref.at[before, top], ahead)
    second.wait_recv()
    fourth = post.go(all_ref.at[after, bottom], all_ref.at[after, bottom], behind)
    if arrived is not None:
        yield from arrived(before)
        yield from arrived(after)
    yield clock.until(begin + far_time)
    third.wait_recv()
    fourth.wait_recv()
    if arrived is not None:
        yield from arrived(far)


def line_scatter_steps(post, make, far, near, finish, clock, far_time, near_time):
    ahead, behind = line_partners()
    top, bottom = halves(far)
    high = top.size
    rows = far.shape[0]
    block = yield from make(2)
    begin = clock.now
    first = post.go(block.at[top], far.at[top], ahead)
    second = post.go(block.at[bottom], far.at[bottom], behind)
    block = yield from make(1)
    yield clock.until(begin + far_time)
    first.wait_recv()
    add_rows(block, [(block, 0), (far, 0)], 0, high)
    third = post.go(block, near.at[0], ahead)
    other = yield from make(-1)
    second.wait_recv()
    add_rows(other, [(other, high), (far, high)], high, rows - high)
    fourth = post.go(other, near.at[1], behind)
    begin = clock.now
    own = yield from make(0)
    yield clock.until(begin + near_time)
    third.wait_recv()
    fourth.wait_recv()
    finish(own, near.at[0], near.at[1])


def split_float(values):
    high = values.astype(BF16)
    return (high, (values - high.astype(F32)).astype(BF16))


def split_three(values):
    high = values.astype(BF16)
    rest = values - high.astype(F32)
    middle = rest.astype(BF16)
    return (high, middle, (rest - middle.astype(F32)).astype(BF16))


def head_mean(values):
    same = (
        lax.broadcasted_iota(jnp.int32, (128, 128), 0) // 64
        == lax.broadcasted_iota(jnp.int32, (128, 128), 1) // 64
    ).astype(BF16)
    high, low = split_float(values)
    total = jnp.dot(high, same, preferred_element_type=F32)
    total = total + jnp.dot(low, same, preferred_element_type=F32)
    return total * (1.0 / 64.0)


def other_half(values):
    lane = lax.broadcasted_iota(jnp.int32, values.shape, 1)
    return jnp.where(
        lax.rem(lane, 64) < 32, pltpu.roll(values, 96, 1), pltpu.roll(values, 32, 1)
    )


def head_ready(raw, gain, cosine, sine):
    normed = raw * lax.rsqrt(head_mean(raw * raw) + 1e-06) * gain
    return normed * cosine + other_half(normed) * sine


def head_back(grad, raw, gain, cosine, sine):
    grad = grad * cosine + other_half(grad * sine)
    scale = lax.rsqrt(head_mean(raw * raw) + 1e-06)
    plain = raw * scale
    grad_gain = jnp.sum(grad * plain, axis=0, keepdims=True)
    grad = grad * gain
    return (scale * (grad - plain * head_mean(grad * plain)), grad_gain)


def row_scale(values):
    return lax.rsqrt(jnp.mean(values * values, axis=1, keepdims=True) + 1e-05)


def exchange(values):
    return jnp.concatenate([values[:, 64:], values[:, :64]], axis=1)


def head_pairs(block):
    rows = block.shape[0]
    low = lax.broadcasted_iota(jnp.int32, (rows, 128), 1) < 64
    left, right = block[:, :128], block[:, 128:]
    zero = jnp.zeros_like(left)
    straight = jnp.concatenate([jnp.where(low, left, zero), jnp.where(low, zero, right)], axis=0)
    crossed = jnp.concatenate([jnp.where(low, zero, left), jnp.where(low, right, zero)], axis=0)
    return (straight, crossed)


def heads_back(straight, crossed):
    rows = straight.shape[0] // 2
    low = lax.broadcasted_iota(jnp.int32, (rows, 128), 1) < 64
    left = jnp.where(low, straight[:rows], crossed[:rows])
    right = jnp.where(low, crossed[rows:], straight[rows:])
    return jnp.concatenate([left, right], axis=1)


def attend_block(query, keys, values, bias, clock):
    rows = query.shape[0]
    outs = []
    for pair, key_part, value_part in zip(
        head_pairs(query), (keys, exchange(keys)), (values, exchange(values)), strict=True
    ):
        halves_out = []
        for number in range(2):
            part = pair[number * rows : (number + 1) * rows]
            scores = lax.dot_general(part, key_part, CONTRACT_LAST, preferred_element_type=F32)
            weights = jnp.exp(scores * 0.125 + bias)
            total_weight = jnp.sum(weights, axis=1, keepdims=True)
            out = jnp.dot(weights.astype(BF16), value_part, preferred_element_type=F32)
            halves_out.append(out / total_weight)
            yield clock.spend(0.45)
        outs.append(jnp.concatenate(halves_out, axis=0))
    return heads_back(*outs).astype(BF16)


def document_bounds(segments, live_mask):
    one = jnp.ones_like(segments)
    zero = jnp.zeros_like(segments)

    def count(chosen):
        return jnp.sum(jnp.where(chosen, one, zero), axis=1, keepdims=True)

    return (count(segments < 1), count(segments < 2), count(live_mask == 1))


def score_bias(bounds, query, key):
    first, second, living = bounds

    def document(position):
        return (position >= first).astype(jnp.int32) + (position >= second).astype(jnp.int32)

    seen = jnp.where(key < living, 1, 0)
    same = document(query) == document(key)
    return jnp.where(same & ((seen == 1) | (query == key)), 0.0, -1e30).astype(F32)


def block_rows(block):
    return pl.ds(pl.multiple_of(block * 256, 256), 256)


def opening_kernel(
    inputs, gain_one, query_weight, key_weight, value_weight, query_gain, key_gain, cosine, sine,
    segments, live_mask, output_weight, gain_two, router, routes, cotangent,
    gate,
    normed, raw, query, keys, values, mixed, residual, block, gates, grad_all,
    gate_all,
    parts, far, near, hold, send_sems, recv_sems, local_sems,
):
    tp = lax.axis_index("tp")
    own_parts = (
        (cotangent, parts.at[0], grad_all.at[lax.axis_index("ep")]),
        (gate, hold, gate_all.at[tp]),
    )
    inward = [
        pltpu.make_async_copy(src, through, local_sems.at[number])
        for number, (src, through, _) in enumerate(own_parts)
    ]
    outward = [
        pltpu.make_async_copy(through, dst, local_sems.at[number])
        for number, (_, through, dst) in enumerate(own_parts)
    ]
    for copy in inward:
        copy.start()
    greet(plane_partners() + line_partners())
    post = Post(send_sems, recv_sems)
    clock = Clock()
    bounds = document_bounds(segments[...], live_mask[...])

    def project(place):
        rows = block_rows(place)
        part = normed[place]
        cos, sin = cosine[rows, :], sine[rows, :]
        both = jnp.dot(part, query_weight[...], preferred_element_type=F32)
        raw[rows, :256] = both
        for lanes in (slice(0, 128), slice(128, 256)):
            query[rows, lanes] = head_ready(both[:, lanes], query_gain[...], cos, sin).astype(BF16)
        one = jnp.dot(part, key_weight[...], preferred_element_type=F32)
        raw[rows, 256:] = one
        keys[rows, :] = head_ready(one, key_gain[...], cos, sin).astype(BF16)
        values[rows, :] = jnp.dot(part, value_weight[...], preferred_element_type=F32).astype(BF16)
        yield clock.spend(1.5)

    def make(offset):
        place = wrap(tp + offset)
        rows = block_rows(place)
        bias = score_bias(
            bounds,
            place * 256 + lax.broadcasted_iota(jnp.int32, (256, 1), 0),
            lax.broadcasted_iota(jnp.int32, (1, 1024), 1),
        )
        out = yield from attend_block(query[rows, :], keys[...], values[...], bias, clock)
        mixed[rows, :] = out
        part = parts.at[(2, 1, -1, 0).index(offset)]
        part[...] = jnp.dot(out, output_weight[...], preferred_element_type=F32).astype(BF16)
        yield clock.spend(0.4)
        return part

    def finish(own, first, second):
        total = own[...].astype(F32) + first[...].astype(F32) + second[...].astype(F32)
        total = inputs[...].astype(F32) + total
        residual[...] = total
        normed_two = total * row_scale(total) * gain_two[...]
        block[:256, :] = normed_two.astype(BF16)
        logits = jnp.zeros((32, 256), F32)
        for piece in split_three(normed_two):
            logits = logits + lax.dot_general(
                router[...], piece, CONTRACT_LAST, preferred_element_type=F32
            )
        expert = lax.broadcasted_iota(jnp.int32, (32, 256), 0)
        named = expert < 0
        for choice in range(8):
            named = named | (routes[choice : choice + 1, :] == expert)
        top_logit = jnp.max(jnp.where(named, logits, -1e30), axis=0, keepdims=True)
        raised = jnp.where(named, jnp.exp(jnp.where(named, logits - top_logit, 0.0)), 0.0)
        probs = raised / jnp.sum(raised, axis=0, keepdims=True)
        gates[...] = probs
        high, low = split_float(probs)
        block[256:, :] = jnp.concatenate([high[:16], low[:16], high[16:], low[16:]], axis=1)

    def attention_steps():
        hidden = inputs[...].astype(F32)
        normed[tp] = (hidden * row_scale(hidden) * gain_one[...]).astype(BF16)
        for copy, onward in zip(inward, outward, strict=True):
            copy.wait()
            onward.start()
        clock.spend(1.0)
        yield from line_gather_steps(post, normed.at[tp], normed, clock, 11.5, 17.5, project)
        for copy in outward:
            copy.wait()
        yield from line_scatter_steps(post, make, far, near, finish, clock, 3.0, 12.0)

    def weight_steps(own, everyone, begin, near_time, far_time):
        yield begin
        yield from line_gather_steps(post, own, everyone, Clock(begin), near_time, far_time)

    together(
        attention_steps(),
        plane_gather_steps(post, cotangent, grad_all),
        weight_steps(gate, gate_all, 20.5, 22.0, 32.0),
    )
    post.finish()


def opening(arguments, number):
    count = 3 * LINE_COPIES + PLANE_COPIES
    return pl.pallas_call(
        opening_kernel,
        out_shape=[
            jax.ShapeDtypeStruct((4, 256, 1024), BF16),
            jax.ShapeDtypeStruct((1024, 384), F32),
            jax.ShapeDtypeStruct((1024, 256), BF16),
            jax.ShapeDtypeStruct((1024, 128), BF16),
            jax.ShapeDtypeStruct((1024, 128), BF16),
            jax.ShapeDtypeStruct((1024, 256), BF16),
            jax.ShapeDtypeStruct((256, 1024), F32),
            jax.ShapeDtypeStruct((256 + EXTRA, 1024), BF16),
            jax.ShapeDtypeStruct((32, 256), F32),
            jax.ShapeDtypeStruct((32, 256, 1024), BF16),
            jax.ShapeDtypeStruct((4, 1024, 128), BF16),
        ],
        in_specs=[VMEM] * (len(arguments) - 2) + [ANY] * 2,
        out_specs=[VMEM] * 9 + [ANY] * 2,
        scratch_shapes=[
            pltpu.VMEM((4, 256, 1024), BF16),
            pltpu.VMEM((256, 1024), BF16),
            pltpu.VMEM((2, 256, 1024), BF16),
            pltpu.VMEM((1024, 128), BF16),
            pltpu.SemaphoreType.DMA((count,)),
            pltpu.SemaphoreType.DMA((count,)),
            pltpu.SemaphoreType.DMA((2,)),
        ],
        compiler_params=pltpu.CompilerParams(
            collective_id=number, has_side_effects=True, vmem_limit_bytes=56 << 20
        ),
        name="opening",
    )(*arguments)


def attend_back_block(query, grad, keys, values, bias, keys_sum, values_sum, clock):
    rows = query.shape[0]
    query_pairs = head_pairs(query)
    grad_pairs = head_pairs(grad)
    key_parts = (keys, exchange(keys))
    value_parts = (values, exchange(values))
    outs = []
    for side in range(2):
        halves_out = []
        for number in range(2):
            part = query_pairs[side][number * rows : (number + 1) * rows]
            grad_part = grad_pairs[side][number * rows : (number + 1) * rows]
            scores = lax.dot_general(
                key_parts[side], part, CONTRACT_LAST, preferred_element_type=F32
            )
            raised = jnp.exp(scores * 0.125 + bias)
            weights = raised * (1.0 / jnp.sum(raised, axis=0, keepdims=True))
            grad_weights = lax.dot_general(
                value_parts[side], grad_part, CONTRACT_LAST, preferred_element_type=F32
            )
            inner = jnp.sum(weights * grad_weights, axis=0, keepdims=True)
            grad_scores = (weights * (grad_weights - inner)).astype(BF16)
            halves_out.append(
                lax.dot_general(
                    grad_scores, key_parts[side], CONTRACT_ROWS, preferred_element_type=F32
                )
            )
            keys_sum[side] += jnp.dot(grad_scores, part, preferred_element_type=F32)
            values_sum[side] += jnp.dot(
                weights.astype(BF16), grad_part, preferred_element_type=F32
            )
            yield clock.spend(1.4)
        outs.append(jnp.concatenate(halves_out, axis=0))
    return heads_back(*outs) * 0.125


SMALL_ROWS = 16


def closing_kernel(
    back, residual, gates, cotangent, gain_two, router, query, keys, values, mixed,
    output_weight, query_weight, key_weight, value_weight, raw, normed, inputs, gain_one,
    query_gain, key_gain, cosine, sine, segments, live_mask, out_parts,
    grad_inputs, dense_all, small_all, combined,
    grad_all, grad_residual, low, keys_sum, values_sum, output_sum, parts, far, near,
    dense, dense_own, small, small_own, small_line, small_sum, query_gain_sum, gain_one_sum,
    *rest,
):
    out_scratch, dense_scratch, small_scratch = rest[:7], rest[7:10], rest[10:13]
    post = Post(rest[13], rest[14])
    me = lax.axis_index("ep")
    tp = lax.axis_index("tp")
    ahead, behind = line_partners()
    across = (me, wrap(tp + 2))
    greet(brief_partners() + (ahead, behind, across))
    clock = Clock()
    out_steps = plane_scatter_steps(post, out_parts, combined, out_scratch)
    out_due = next(out_steps)

    lines = back[256:, :]
    grad_gates = jnp.concatenate(
        [lines[:, :256] + lines[:, 256:512], lines[:, 512:768] + lines[:, 768:]], axis=0
    )
    probs = gates[...]
    grad_logits = probs * (grad_gates - jnp.sum(probs * grad_gates, axis=0, keepdims=True))
    grad_two = back[:256, :]
    logit_pieces = split_three(grad_logits)
    for piece in logit_pieces:
        grad_two = grad_two + lax.dot_general(
            piece, router[...], CONTRACT_ROWS, preferred_element_type=F32
        )
    total = residual[...]
    scale = row_scale(total)
    plain = total * scale
    grad_gain_two = jnp.sum(grad_two * plain, axis=0, keepdims=True)
    grad_two = grad_two * gain_two[...]
    grad_total = cotangent[...].astype(F32) + scale * (
        grad_two - plain * jnp.mean(grad_two * plain, axis=1, keepdims=True)
    )
    grad_residual[...] = grad_total
    grad_all[tp] = grad_total.astype(BF16)
    clock.spend(4.0)

    bounds = document_bounds(segments[...], live_mask[...])
    keys_sum[...] = jnp.zeros_like(keys_sum)
    values_sum[...] = jnp.zeros_like(values_sum)
    output_sum[...] = jnp.zeros_like(output_sum)
    query_gain_sum[...] = jnp.zeros_like(query_gain_sum)
    gain_one_sum[...] = jnp.zeros_like(gain_one_sum)

    def attention(place):
        rows = block_rows(place)
        grad = grad_all[place]
        output_sum[...] += lax.dot_general(
            mixed[rows, :], grad, CONTRACT_ROWS, preferred_element_type=F32
        )
        grad_mixed = lax.dot_general(
            grad, output_weight[...], CONTRACT_LAST, preferred_element_type=F32
        ).astype(BF16)
        bias = score_bias(
            bounds,
            place * 256 + lax.broadcasted_iota(jnp.int32, (1, 256), 1),
            lax.broadcasted_iota(jnp.int32, (1024, 1), 0),
        )
        clock.spend(0.8)
        grad_query = yield from attend_back_block(
            query[rows, :], grad_mixed, keys[...], values[...], bias, keys_sum, values_sum, clock
        )
        for lanes in (slice(0, 128), slice(128, 256)):
            grad_raw, grad_gain = head_back(
                grad_query[:, lanes],
                raw[rows, lanes],
                query_gain[...],
                cosine[rows, :],
                sine[rows, :],
            )
            low[rows, lanes] = grad_raw.astype(BF16)
            query_gain_sum[...] += grad_gain
        yield clock.spend(0.5)

    def make(offset):
        rows = block_rows(wrap(tp + offset))
        total = lax.dot_general(
            low[rows, :256], query_weight[...], CONTRACT_LAST, preferred_element_type=F32
        )
        total = total + lax.dot_general(
            low[rows, 256:384], key_weight[...], CONTRACT_LAST, preferred_element_type=F32
        )
        total = total + lax.dot_general(
            low[rows, 384:], value_weight[...], CONTRACT_LAST, preferred_element_type=F32
        )
        gain_one_sum[...] += jnp.sum(
            total * normed[rows, :].astype(F32), axis=0, keepdims=True
        )
        part = parts.at[(2, 1, -1, 0).index(offset)]
        part[...] = total.astype(BF16)
        yield clock.spend(0.8)
        return part

    def finish(own, first, second):
        grad_one = own[...].astype(F32) + first[...].astype(F32) + second[...].astype(F32)
        hidden = inputs[...].astype(F32)
        scale = row_scale(hidden)
        plain = hidden * scale
        grad_one = grad_one * gain_one[...]
        grad_inputs[...] = (
            grad_residual[...]
            + scale * (grad_one - plain * jnp.mean(grad_one * plain, axis=1, keepdims=True))
        ).astype(BF16)

    def router_gradient():
        normed_pieces = split_three(plain * gain_two[...])
        total = jnp.zeros((32, 1024), F32)
        for first, second in ((0, 0), (0, 1), (1, 0), (1, 1), (0, 2), (2, 0)):
            total = total + jnp.dot(
                logit_pieces[first], normed_pieces[second], preferred_element_type=F32
            )
        return total

    def fill_small(grad_key_gain):
        grad_router = router_gradient()
        grad_gain_one = gain_one_sum[...] / gain_one[...]
        small[...] = jnp.zeros_like(small)
        for part in range(8):
            lanes = slice(part * 128, (part + 1) * 128)
            small[2 * part] = grad_router[:16, lanes]
            small[2 * part + 1] = grad_router[16:, lanes]
            small[16, part : part + 1, :] = grad_gain_one[:, lanes]
            small[16, 8 + part : 9 + part, :] = grad_gain_two[:, lanes]
        small[17, 0:1, :] = query_gain_sum[...]
        small[17, 1:2, :] = grad_key_gain

    def attention_steps():
        yield from line_gather_steps(
            post, grad_all.at[tp], grad_all, clock, 11.5, 17.5, attention
        )
        grad_raw, grad_key_gain = head_back(
            (keys_sum[0] + exchange(keys_sum[1])) * 0.125,
            raw[:, 256:],
            key_gain[...],
            cosine[...],
            sine[...],
        )
        low[:, 256:384] = grad_raw.astype(BF16)
        low[:, 384:] = (values_sum[0] + exchange(values_sum[1])).astype(BF16)
        yield clock.spend(2.0)
        line_steps = line_scatter_steps(post, make, far, near, finish, clock, 3.5, 11.5)
        last = yield from until_count(line_steps, 6)
        fill_small(grad_key_gain)
        now = clock.now
        yield from side_by_side(
            (last, line_steps), (now, dense_steps(now)), (now, small_steps(now))
        )

    def dense_steps(begin):
        weights = lax.dot_general(
            normed[...], low[...], CONTRACT_ROWS, preferred_element_type=F32
        ).astype(BF16)
        for part in range(32):
            dense[part, :, :512] = weights[part * 32 : (part + 1) * 32]
        for part in range(4):
            block = output_sum[:, part * 256 : (part + 1) * 256].astype(BF16)
            for piece in range(8):
                dense[part * 8 + piece, :, 512:] = block[piece * 32 : (piece + 1) * 32]
        yield from brief_scatter_steps(post, dense, dense_own, dense_scratch, begin + 3.0)
        dense_all[me] = dense_own[...]
        yield from brief_gather_steps(post, dense_own, dense_all, begin + 16.0)

    def small_steps(begin):
        yield from brief_scatter_steps(post, small, small_own, small_scratch, begin)
        line = [
            post.go(small_own, small_line.at[0], ahead),
            post.go(small_own, small_line.at[1], behind),
            post.go(small_own, small_line.at[2], across),
        ]
        yield begin + 12.0
        for copy in line:
            copy.wait_recv()
        small_sum[...] = small_own[...] + small_line[0] + small_line[1] + small_line[2]
        small_all[me] = small_sum[...]
        yield from brief_gather_steps(post, small_sum, small_all, begin + 14.0)

    together(attention_steps(), resumed(out_due, out_steps))
    post.finish()


def closing(arguments, number):
    count = 2 * LINE_COPIES + PLANE_COPIES + 4 * BRIEF_COPIES + 3
    return pl.pallas_call(
        closing_kernel,
        out_shape=[
            jax.ShapeDtypeStruct((256, 1024), BF16),
            jax.ShapeDtypeStruct((32, 32, 768), BF16),
            jax.ShapeDtypeStruct((32, SMALL_ROWS, 128), F32),
            jax.ShapeDtypeStruct((256, 1024), F32),
        ],
        in_specs=[VMEM] * (len(arguments) - 1) + [ANY],
        out_specs=[VMEM] * 4,
        scratch_shapes=[
            pltpu.VMEM((4, 256, 1024), BF16),
            pltpu.VMEM((256, 1024), F32),
            pltpu.VMEM((1024, 512), BF16),
            pltpu.VMEM((2, 1024, 128), F32),
            pltpu.VMEM((2, 1024, 128), F32),
            pltpu.VMEM((256, 1024), F32),
            pltpu.VMEM((4, 256, 1024), BF16),
            pltpu.VMEM((256, 1024), BF16),
            pltpu.VMEM((2, 256, 1024), BF16),
            pltpu.VMEM((32, 32, 768), BF16),
            pltpu.VMEM((32, 768), BF16),
            pltpu.VMEM((32, SMALL_ROWS, 128), F32),
            pltpu.VMEM((SMALL_ROWS, 128), F32),
            pltpu.VMEM((3, SMALL_ROWS, 128), F32),
            pltpu.VMEM((SMALL_ROWS, 128), F32),
            pltpu.VMEM((1, 128), F32),
            pltpu.VMEM((1, 1024), F32),
        ]
        + plane_scatter_scratch(256, 1024, BF16)
        + brief_scatter_scratch(32, 768, BF16)
        + brief_scatter_scratch(SMALL_ROWS, 128, F32)
        + [pltpu.SemaphoreType.DMA((count,)), pltpu.SemaphoreType.DMA((count,))],
        compiler_params=pltpu.CompilerParams(
            collective_id=number, has_side_effects=True, vmem_limit_bytes=63 << 20
        ),
        name="closing",
    )(*arguments)


def finish_kernel(
    dense, weights, residual, combined,
    result, grad_query, grad_key, grad_value, grad_output, grad_gate, grad_up, grad_down,
):
    result[...] = (residual[...] + combined[...]).astype(BF16)
    grad_query[...] = dense[:, :256].astype(F32)
    grad_key[...] = dense[:, 256:384].astype(F32)
    grad_value[...] = dense[:, 384:512].astype(F32)
    for part in range(4):
        grad_output[:, part * 256 : (part + 1) * 256] = dense[
            part * 256 : (part + 1) * 256, 512:
        ].astype(F32)
    grad_gate[0] = weights[:1024, :]
    grad_up[0] = weights[1024:2048, :]
    grad_down[0] = weights[2048:, :].T


def finish_all(dense, weights, residual, combined):
    return pl.pallas_call(
        finish_kernel,
        out_shape=[
            jax.ShapeDtypeStruct((256, 1024), BF16),
            jax.ShapeDtypeStruct((1024, 256), F32),
            jax.ShapeDtypeStruct((1024, 128), F32),
            jax.ShapeDtypeStruct((1024, 128), F32),
            jax.ShapeDtypeStruct((256, 1024), F32),
            jax.ShapeDtypeStruct((1, 1024, 128), F32),
            jax.ShapeDtypeStruct((1, 1024, 128), F32),
            jax.ShapeDtypeStruct((1, 128, 1024), F32),
        ],
        in_specs=[VMEM] * 4,
        out_specs=[VMEM] * 8,
        compiler_params=pltpu.CompilerParams(vmem_limit_bytes=40 << 20),
        name="finish_all",
    )(dense, weights, residual, combined)


STEPS = ((0, 1), (3, 4), (6, 7), (12, 13), (14, 15), (10, 11), (8, 9), (2, 5))
GROUP = 4


def experts_kernel(
    block, grads, gate_all, up, down,
    rows_all, out_parts, back_sum, weight_sum,
    rows_in, grads_in, both_full, down_full, both_sum, down_sum, rows_own, grads_own, gates_own,
    select, weighted, grad_rows, grad_gates, mine, other, stage, out_stage,
    b_far, b_near, a_far, a_near, line, line_far, line_near, send_sems, recv_sems, credit, load_sems, store_sems, weight_sems, own_sem,
):
    a, b, core = plane_place()
    me = lax.axis_index("ep")
    ahead_a, behind_a, ahead_b, behind_b, sibling = plane_partners()
    here = [plane_index(a + place[0], b + place[1], core) for place in ARRIVAL]
    there = [plane_index(b + place[0], a + place[1], 1 - core) for place in ARRIVAL]
    lane_row = lax.rem(me, 16)
    upper = me >= 16
    tp = lax.axis_index("tp")
    ahead, behind = line_partners()
    greet(plane_partners() + (ahead, behind))
    post = Post(send_sems, recv_sems)
    go = post.go
    events, held = plane_gather_events(post, block, rows_all)
    events[0][1]()
    own_copy = pltpu.make_async_copy(block, stage.at[0], own_sem)
    own_copy.start()
    before_me, after_me = wrap(tp - 1), wrap(tp + 1)

    def up_part(place, rows=slice(None)):
        return at(both_full, rows, pl.ds(pl.multiple_of(512 + place * 128, 128), 128))

    def down_part(place, first=0, count=128):
        return at(down_full, pl.ds(pl.multiple_of(place * 128 + first, 64), count))

    up_near = (
        post.go(up, up_part(tp), ahead), post.go(up, up_part(tp), behind)
    )
    down_near = (
        post.go(down, down_part(tp), ahead), post.go(down, down_part(tp), behind)
    )
    up_top, up_bottom = up_part(before_me, pl.ds(0, 512)), up_part(after_me, pl.ds(512, 512))
    up_far = (
        post.prepare(up_top, up_top, ahead), post.prepare(up_bottom, up_bottom, behind)
    )
    down_top, down_bottom = down_part(before_me, 0, 64), down_part(after_me, 64, 64)
    down_far = (
        post.prepare(down_top, down_top, ahead), post.prepare(down_bottom, down_bottom, behind)
    )

    def relay(near, far):
        for one, other_one in zip(near, far, strict=True):
            one.wait_recv()
            other_one.start()

    weight_loads = [
        pltpu.make_async_copy(
            gate_all.at[part], both_full.at[:, part * 128 : (part + 1) * 128], weight_sems.at[part]
        )
        for part in range(4)
    ]
    weight_loads.append(pltpu.make_async_copy(up, up_part(tp)(), weight_sems.at[4]))
    weight_loads.append(pltpu.make_async_copy(down, down_part(tp)(), weight_sems.at[5]))
    for copy in weight_loads:
        copy.start()
    both_sum[...] = jnp.zeros_like(both_sum)
    down_sum[...] = jnp.zeros_like(down_sum)

    def blocks(step):
        first, second = STEPS[step]
        return (here[first], here[second], there[first], there[second])

    loads, crossing, stores = {}, {}, {}
    for step in range(len(STEPS)):
        slot = step % 2
        loads[step], stores[step] = [], []
        crossing[step] = [
            post.prepare(at(stage, part), at(other, slot, part), sibling) for part in range(2)
        ]
        for part, index in enumerate(blocks(step)):
            loads[step] += [
                Local(
                    at(rows_all, index), at(rows_in, slot, part), at(load_sems, slot, 0, part)
                ),
                Local(at(grads, index), at(grads_in, slot, part), at(load_sems, slot, 1, part)),
            ]
            stores[step].append(
                Local(at(out_stage, part), at(out_parts, index), at(store_sems, part))
            )

    def load(step):
        for place in STEPS[step]:
            held[place].wait_recv()
        for copy in loads[step]:
            copy.start()

    def take(step):
        for part, place in enumerate(STEPS[step]):
            crossing[step][part].wait_recv()
            add_rows(
                mine.at[place], [(mine.at[place], 0), (other.at[step % 2, part], 0)], 0, rows
            )
        if step + 2 < len(STEPS):
            pl.semaphore_signal(credit, inc=1, device_id=sibling, device_id_type=MESH)

    rows = a_far.shape[0]
    top, bottom = halves(a_far)
    high = top.size
    low = rows - high
    far_b, near_b = {}, {}

    def number_of(k, j):
        return ARRIVAL.index((OFFSETS[k], OFFSETS[j]))

    def slot_of(k, j):
        return mine.at[number_of(k, j)]

    def far_step(k):
        part = number_of(k, 0)
        far_b[k] = (
            go(at(mine, part, top), at(b_far, k, top), ahead_b),
            go(at(mine, part, bottom), at(b_far, k, bottom), behind_b),
        )

    def near_step(k):
        far = b_far.at[k]
        far_b[k][0].wait_recv()
        part = slot_of(k, 1)
        add_rows(part, [(part, 0), (far, 0)], 0, high)
        first = go(at(mine, number_of(k, 1)), at(b_near, 0, k), ahead_b)
        far_b[k][1].wait_recv()
        part = slot_of(k, 2)
        add_rows(part, [(part, high), (far, high)], high, low)
        near_b[k] = (first, go(at(mine, number_of(k, 2)), at(b_near, 1, k), behind_b))

    def before(step):
        for copy in loads[step]:
            copy.wait()

    def between(step):
        if step > 0:
            for copy in crossing[step - 1]:
                copy.wait_send()
            for copy in stores[step - 1]:
                copy.wait()
        onward({0: (4,), 1: (6,), 2: (7, 8, 9), 3: (10, 11)}.get(step, ()))
        if step + 1 < len(STEPS):
            load(step + 1)
        if step > 0:
            take(step - 1)
        if step == 4:
            far_step(2)
            far_step(3)
        if step == 5:
            far_step(0)
            far_step(1)
            near_step(3)
            near_step(2)
        if step == 6:
            near_step(0)
        if step == 7:
            near_step(1)

    def onward(numbers):
        for number in numbers:
            events[number][1]()

    def early(step):
        if step == 0:
            for copy in down_far:
                copy.wait_recv()

    def after(step):
        onward({0: (5,)}.get(step, ()))
        if step >= 2:
            pl.semaphore_wait(credit, 1)
        for copy in crossing[step] + stores[step]:
            copy.start()

    def at_step(step, task):
        for number in range(len(STEPS)):

            @pl.when(step == number)
            def _(number=number):
                task(number)

    def from_table(step, table):
        value = step * 0 + table[0]
        for number in range(1, len(table)):
            value = jnp.where(step == number, table[number], value)
        return value

    own_copy.wait()
    own_copy = pltpu.make_async_copy(stage.at[0], rows_all.at[me], own_sem)
    own_copy.start()
    onward((1, 2))
    own_copy.wait()
    load(0)
    relay(up_near, up_far)
    onward((3,))
    relay(down_near, down_far)
    for copy in weight_loads:
        copy.wait()
    for copy in up_far:
        copy.wait_recv()
    extra_row = lax.broadcasted_iota(jnp.int32, (EXTRA, 1024), 0) == lane_row

    def one_step(step, carry):
        slot = lax.rem(step, 2)
        at_step(step, before)
        earlier = (
            lax.broadcasted_iota(jnp.int32, (256, 256), 0)
            <= lax.broadcasted_iota(jnp.int32, (256, 256), 1)
        ).astype(BF16)
        place = lax.broadcasted_iota(jnp.int32, (SLOTS, 256), 0).astype(F32)
        for part in range(GROUP):
            extras = jnp.where(extra_row, rows_in[slot, part, 256:, :].astype(F32), 0.0)
            extras = jnp.sum(extras, axis=0, keepdims=True)
            gates = jnp.where(
                upper, extras[:, 512:768] + extras[:, 768:], extras[:, :256] + extras[:, 256:512]
            )
            named = jnp.broadcast_to(gates, (16, 256)) > 0.0
            rank = jnp.dot(named.astype(BF16), earlier, preferred_element_type=F32)[:1] - 1.0
            chosen = (place == rank) & (gates > 0.0)
            chosen_low = chosen.astype(BF16)
            at = slice(part * SLOTS, (part + 1) * SLOTS)
            select[at, :] = chosen_low
            rows_own[at, :] = jnp.dot(
                chosen_low, rows_in[slot, part, :256, :], preferred_element_type=F32
            ).astype(BF16)
            grads_own[at, :] = jnp.dot(
                chosen_low, grads_in[slot, part], preferred_element_type=F32
            ).astype(BF16)
            gates_own[at, :] = jnp.sum(jnp.where(chosen, gates, 0.0), axis=1, keepdims=True)

        at_step(step, early)
        both_pre = jnp.dot(rows_own[...], both_full[...], preferred_element_type=F32)
        gate_pre, up_pre = both_pre[:, :512], both_pre[:, 512:]
        sigmoid = 1.0 / (1.0 + jnp.exp(-gate_pre))
        silu = gate_pre * sigmoid
        act = (silu * up_pre).astype(BF16)
        out = jnp.dot(act, down_full[...], preferred_element_type=F32).astype(BF16).astype(F32)
        gate_factor = gates_own[...]
        grads_float = grads_own[...].astype(F32)
        grad_gates[...] = jnp.sum(grads_float * out, axis=1, keepdims=True)
        weighted[...] = (gate_factor * out).astype(BF16)
        grad_out = (gate_factor * grads_float).astype(BF16)
        grad_act = lax.dot_general(
            grad_out, down_full[...], CONTRACT_LAST, preferred_element_type=F32
        )
        down_sum[...] += lax.dot_general(
            grad_out, act, CONTRACT_ROWS, preferred_element_type=F32
        )
        grad_gate_pre = grad_act * up_pre * sigmoid * (1.0 + gate_pre * (1.0 - sigmoid))
        grad_up_pre = grad_act * silu
        grad_pre = jnp.concatenate(
            [grad_gate_pre.astype(BF16), grad_up_pre.astype(BF16)], axis=1
        )
        both_sum[...] += lax.dot_general(
            rows_own[...], grad_pre, CONTRACT_ROWS, preferred_element_type=F32
        )
        grad_rows[...] = lax.dot_general(
            grad_pre, both_full[...], CONTRACT_LAST, preferred_element_type=F32
        ).astype(BF16)
        at_step(step, between)
        nothing = jnp.zeros((1, 512), F32)
        slots = [from_table(step, [pair[part] for pair in STEPS]) for part in range(2)]
        for part in range(GROUP):
            at = slice(part * SLOTS, (part + 1) * SLOTS)
            chosen_low = select[at, :]
            out_stage[part] = lax.dot_general(
                chosen_low, weighted[at], CONTRACT_ROWS, preferred_element_type=F32
            ).astype(BF16)
            target = mine.at[slots[part]] if part < 2 else stage.at[part - 2]
            target[:256, :] = lax.dot_general(
                chosen_low, grad_rows[at], CONTRACT_ROWS, preferred_element_type=F32
            ).astype(BF16)
            spread = jnp.sum(chosen_low.astype(F32) * grad_gates[at], axis=0, keepdims=True)
            upper_bits = spread.astype(BF16).astype(F32)
            both = jnp.concatenate([upper_bits, spread - upper_bits], axis=1)
            line_now = jnp.concatenate(
                [jnp.where(upper, nothing, both), jnp.where(upper, both, nothing)], axis=1
            )
            target[256:, :] = jnp.where(extra_row, line_now, 0.0).astype(BF16)
        at_step(step, after)
        return carry

    lax.fori_loop(0, len(STEPS), one_step, 0)
    last = len(STEPS) - 1

    def make_weights(offset):
        place = wrap(tp + offset)
        lanes = pl.ds(pl.multiple_of(place * 128, 128), 128)
        upper_lanes = pl.ds(pl.multiple_of(512 + place * 128, 128), 128)
        part = line.at[OFFSETS.index(offset)]
        part[:1024, :] = both_sum[:, lanes].astype(BF16)
        part[1024:2048, :] = both_sum[:, upper_lanes].astype(BF16)
        part[2048:, :] = down_sum[:, lanes].astype(BF16)
        yield 1.0
        return part

    def finish_weights(own, first, second):
        add_rows(weight_sum, [(own, 0), (first, 0), (second, 0)], 0, own.shape[0])

    def back_steps():
        yield 0.0
        take(last)
        far_a, near_a = [], []
        for k in range(4):
            yield (2.0, 4.0, 8.0, 12.0)[k]
            part = slot_of(k, 3)
            near_b[k][0].wait_recv()
            near_b[k][1].wait_recv()
            base = [part, b_near.at[0, k], b_near.at[1, k]]
            first_rows = [(ref, 0) for ref in base]
            last_rows = [(ref, high) for ref in base]
            if k == 0:
                add_rows(part, first_rows, 0, high)
                add_rows(part, last_rows, high, low)
                far_a = [
                    go(part.at[top], a_far.at[top], ahead_a),
                    go(part.at[bottom], a_far.at[bottom], behind_a),
                ]
            elif k == 1:
                far_a[0].wait_recv()
                add_rows(part, first_rows + [(a_far, 0)], 0, high)
                add_rows(part, last_rows, high, low)
                near_a.append(go(part, a_near.at[0], ahead_a))
            elif k == 2:
                far_a[1].wait_recv()
                add_rows(part, first_rows, 0, high)
                add_rows(part, last_rows + [(a_far, high)], high, low)
                near_a.append(go(part, a_near.at[1], behind_a))
            else:
                near_a[0].wait_recv()
                near_a[1].wait_recv()
                add_rows(
                    back_sum, first_rows + [(a_near.at[0], 0), (a_near.at[1], 0)], 0, rows
                )

    together(
        line_scatter_steps(post, make_weights, line_far, line_near, finish_weights, Clock(), 7.0, 24.0),
        back_steps(),
    )
    for copy in stores[last]:
        copy.wait()
    waited = [copy for step in range(last) for copy in crossing[step]]
    for copy in post.started:
        if not any(copy is other_copy for other_copy in waited):
            copy.wait_send()


def run_experts(block, grads, gate_all, up, down, number):
    rows, columns = block.shape
    sources = grads.shape[0]
    count = GROUP * SLOTS
    copies = PLANE_COPIES + 16 + 8 + 8 + 4 + 3 * LINE_COPIES
    whole = (rows, columns)
    return pl.pallas_call(
        experts_kernel,
        out_shape=[
            jax.ShapeDtypeStruct((sources,) + whole, BF16),
            jax.ShapeDtypeStruct((sources, 256, columns), BF16),
            jax.ShapeDtypeStruct(whole, F32),
            jax.ShapeDtypeStruct((3072, 128), F32),
        ],
        in_specs=[ANY] * 5,
        out_specs=[ANY, ANY, VMEM, VMEM],
        scratch_shapes=[
            pltpu.VMEM((2, GROUP) + whole, BF16),
            pltpu.VMEM((2, GROUP, 256, columns), BF16),
            pltpu.VMEM((1024, 1024), BF16),
            pltpu.VMEM((512, 1024), BF16),
            pltpu.VMEM((1024, 1024), F32),
            pltpu.VMEM((1024, 512), F32),
            pltpu.VMEM((count, 1024), BF16),
            pltpu.VMEM((count, 1024), BF16),
            pltpu.VMEM((count, 1), F32),
            pltpu.VMEM((count, 256), BF16),
            pltpu.VMEM((count, 1024), BF16),
            pltpu.VMEM((count, 1024), BF16),
            pltpu.VMEM((count, 1), F32),
            pltpu.VMEM((16,) + whole, BF16),
            pltpu.VMEM((2, 2) + whole, BF16),
            pltpu.VMEM((2,) + whole, BF16),
            pltpu.VMEM((GROUP, 256, columns), BF16),
            pltpu.VMEM((4,) + whole, BF16),
            pltpu.VMEM((2, 4) + whole, BF16),
            pltpu.VMEM(whole, BF16),
            pltpu.VMEM((2,) + whole, BF16),
            pltpu.VMEM((4, 3072, 128), BF16),
            pltpu.VMEM((3072, 128), BF16),
            pltpu.VMEM((2, 3072, 128), BF16),
            pltpu.SemaphoreType.DMA((copies,)),
            pltpu.SemaphoreType.DMA((copies,)),
            pltpu.SemaphoreType.REGULAR,
            pltpu.SemaphoreType.DMA((2, 2, GROUP)),
            pltpu.SemaphoreType.DMA((GROUP,)),
            pltpu.SemaphoreType.DMA((12,)),
            pltpu.SemaphoreType.DMA,
        ],
        compiler_params=pltpu.CompilerParams(
            collective_id=number, has_side_effects=True, vmem_limit_bytes=63 << 20
        ),
        name="run_experts",
    )(block, grads, gate_all, up, down)


def rotary_constants():
    position = np.arange(SEQ_LEN, dtype=np.float32)
    power = -(np.arange(32, dtype=np.float32) * np.float32(2.0)) / np.float32(64.0)
    frequency = np.float32(10000.0) ** power
    angles = position[:, None] * frequency[None, :]
    cosine, sine = np.cos(angles), np.sin(angles)
    return (np.tile(cosine, (1, 4)), np.concatenate([-sine, sine, -sine, sine], axis=1))


def shards(
    inputs,
    first_gain,
    query_weight,
    key_weight,
    value_weight,
    query_gain,
    key_gain,
    output_weight,
    second_gain,
    router_weight,
    gate_weight,
    up_weight,
    down_weight,
    segments,
    live_mask,
    routes,
    cotangent,
):
    gain_one = first_gain.astype(F32).reshape(1, -1)
    gain_two = second_gain.astype(F32).reshape(1, -1)
    query_scale = jnp.tile(query_gain.astype(F32), 2).reshape(1, -1)
    key_scale = jnp.tile(key_gain.astype(F32), 2).reshape(1, -1)
    cosine, sine = rotary_constants()
    seg_row, live_row = segments.reshape(1, -1), live_mask.reshape(1, -1)
    router = router_weight.T
    (
        normed, raw, query, keys, values, mixed, residual, block, gates, grad_all, gate_all,
    ) = opening(
        (
            inputs, gain_one, query_weight, key_weight, value_weight, query_scale, key_scale,
            cosine, sine, seg_row, live_row, output_weight, gain_two, router, routes.T,
            cotangent, gate_weight[0],
        ),
        1,
    )
    rows_all, out_parts, back, weight_sums = run_experts(
        block, grad_all, gate_all, up_weight[0], down_weight[0], 2
    )
    grad_inputs, dense, small, combined = closing(
        (
            back, residual, gates, cotangent, gain_two, router, query, keys, values, mixed,
            output_weight, query_weight, key_weight, value_weight, raw, normed.reshape(1024, 1024),
            inputs, gain_one, query_scale, key_scale, cosine, sine, seg_row,
            live_row, out_parts,
        ),
        4,
    )
    result, grad_query, grad_key, grad_value, grad_output, grad_gate, grad_up, grad_down = (
        finish_all(dense.reshape(1024, 768), weight_sums, residual, combined)
    )
    grad_router = small[:16].reshape(8, 32, 128).transpose(0, 2, 1).reshape(1024, 32)
    query_gain_sum, key_gain_sum = small[17, 0], small[17, 1]
    return (
        result,
        grad_inputs,
        small[16, :8].reshape(-1),
        grad_query,
        grad_key,
        grad_value,
        query_gain_sum[:64] + query_gain_sum[64:],
        key_gain_sum[:64] + key_gain_sum[64:],
        grad_output,
        small[16, 8:].reshape(-1),
        grad_router,
        grad_gate,
        grad_up,
        grad_down,
    )


def solution(mesh):
    return jax.shard_map(
        shards,
        mesh=mesh,
        in_specs=(
            P(("ep", "tp"), None),
            P(),
            P(None, "tp"),
            P(None, "tp"),
            P(None, "tp"),
            P(),
            P(),
            P("tp", None),
            P(),
            P(),
            P("ep", None, "tp"),
            P("ep", None, "tp"),
            P("ep", "tp", None),
            P("ep"),
            P("ep"),
            P(("ep", "tp"), None),
            P(("ep", "tp"), None),
        ),
        out_specs=(
            P(("ep", "tp"), None),
            P(("ep", "tp"), None),
            P(),
            P(None, "tp"),
            P(None, "tp"),
            P(None, "tp"),
            P(),
            P(),
            P("tp", None),
            P(),
            P(),
            P("ep", None, "tp"),
            P("ep", None, "tp"),
            P("ep", "tp", None),
        ),
        check_vma=False,
    )
```

```python
import jax
import jax.numpy as jnp
import numpy as np
from jax import lax
from jax.experimental import pallas as pl
from jax.experimental.pallas import tpu as pltpu
from jax.sharding import PartitionSpec as P

SEQ_LEN = 1024
HIGHEST_PRECISION = lax.Precision.HIGHEST
CONTRACT_ROWS = (((0,), (0,)), ((), ()))
CONTRACT_LAST = (((1,), (1,)), ((), ()))
MESH = pl.DeviceIdType.MESH
ANY = pl.BlockSpec(memory_space=pl.ANY)
VMEM = pl.BlockSpec(memory_space=pltpu.VMEM)
F32 = jnp.float32
BF16 = jnp.bfloat16
SLOTS = 96
EXTRA = 16


def wrap(value):
    return lax.rem(value + 4, 4)


def pick(core, first, second):
    return first * (1 - core) + second * core


def plane_place():
    ep = lax.axis_index("ep")
    core = lax.rem(ep, 2)
    z = lax.rem(lax.div(ep, 2), 4)
    x = lax.div(ep, 8)
    return (pick(core, x, z), pick(core, z, x), core)


def plane_index(a, b, core):
    a, b = wrap(a), wrap(b)
    return (pick(core, a, b) * 4 + pick(core, b, a)) * 2 + core


def plane_partners():
    a, b, core = plane_place()
    tp = lax.axis_index("tp")
    return (
        (plane_index(a + 1, b, core), tp),
        (plane_index(a - 1, b, core), tp),
        (plane_index(a, b + 1, core), tp),
        (plane_index(a, b - 1, core), tp),
        (plane_index(b, a, 1 - core), tp),
    )


def line_partners():
    ep, tp = lax.axis_index("ep"), lax.axis_index("tp")
    return ((ep, wrap(tp + 1)), (ep, wrap(tp - 1)))


def greet(partners):
    barrier = pltpu.get_barrier_semaphore()
    for partner in partners:
        pl.semaphore_signal(barrier, inc=1, device_id=partner, device_id_type=MESH)
    pl.semaphore_wait(barrier, len(partners))


def halves(ref):
    unit = 16 if ref.dtype == BF16 else 8
    rows = ref.shape[-2]
    top = (rows // 2 + unit - 1) // unit * unit
    return (pl.ds(0, top), pl.ds(top, rows - top))


def together(*tasks):
    waiting = [(0.0, number, task) for number, task in enumerate(tasks)]
    while waiting:
        waiting.sort(key=lambda entry: entry[:2])
        _, number, task = waiting.pop(0)
        due = next(task, None)
        if due is not None:
            waiting.append((due, number, task))


def resumed(due, task):
    yield due
    yield from task


def side_by_side(*tasks):
    waiting = [(due, number, task) for number, (due, task) in enumerate(tasks)]
    while waiting:
        waiting.sort(key=lambda entry: entry[:2])
        due, number, task = waiting.pop(0)
        yield due
        due = next(task, None)
        if due is not None:
            waiting.append((due, number, task))


class Clock:
    def __init__(self, now=0.0):
        self.now = now

    def spend(self, amount):
        self.now += amount
        return self.now

    def until(self, moment):
        self.now = max(self.now, moment)
        return self.now


def at(ref, *where):
    return lambda: ref.at[where]


def part_of(place):
    return place() if callable(place) else place


class Remote:
    def __init__(self, src, dst, send_sem, recv_sem, partner):
        self.all = (src, dst, send_sem, recv_sem, partner)

    def copy(self):
        src, dst, send_sem, recv_sem, partner = self.all
        return pltpu.make_async_remote_copy(
            src_ref=part_of(src),
            dst_ref=part_of(dst),
            send_sem=part_of(send_sem),
            recv_sem=part_of(recv_sem),
            device_id=partner,
            device_id_type=MESH,
        )

    def start(self):
        self.copy().start()

    def wait_send(self):
        self.copy().wait_send()

    def wait_recv(self):
        self.copy().wait_recv()


class Local:
    def __init__(self, src, dst, sem):
        self.all = (src, dst, sem)

    def start(self):
        pltpu.make_async_copy(*map(part_of, self.all)).start()

    def wait(self):
        pltpu.make_async_copy(*map(part_of, self.all)).wait()


class Post:
    def __init__(self, send_sems, recv_sems):
        self.send_sems, self.recv_sems, self.started = send_sems, recv_sems, []

    def go(self, src, dst, partner):
        copy = self.prepare(src, dst, partner)
        copy.start()
        return copy

    def prepare(self, src, dst, partner):
        number = len(self.started)
        copy = Remote(src, dst, at(self.send_sems, number), at(self.recv_sems, number), partner)
        self.started.append(copy)
        return copy

    def finish(self):
        for copy in self.started:
            copy.wait_send()


ARRIVAL = (
    (0, 0), (-1, 0), (1, 0), (0, -1), (0, 1), (2, 0), (-1, -1), (-1, 1),
    (1, -1), (1, 1), (2, -1), (2, 1), (0, 2), (-1, 2), (1, 2), (2, 2),
)


def plane_gather_events(post, own_ref, all_ref):
    a, b, core = plane_place()
    ahead_a, behind_a, ahead_b, behind_b, sibling = plane_partners()
    index = {place: plane_index(a + place[0], b + place[1], core) for place in ARRIVAL}
    top, bottom = halves(own_ref)

    def block(place):
        return own_ref if place == (0, 0) else at(all_ref, index[place])

    def copy(place, partner):
        return post.prepare(block(place), at(all_ref, index[place]), partner)

    def half_copy(place, half, partner):
        part = at(all_ref, index[place], half)
        return post.prepare(part, part, partner)

    a_copies = (copy((0, 0), ahead_a), copy((0, 0), behind_a))
    a_halves = (half_copy((-1, 0), top, ahead_a), half_copy((1, 0), bottom, behind_a))
    column = (0, -1, 1, 2)
    b_copies = [(copy((k, 0), ahead_b), copy((k, 0), behind_b)) for k in column]
    b_halves = [
        (half_copy((k, -1), top, ahead_b), half_copy((k, 1), bottom, behind_b)) for k in column
    ]
    crossing = [copy(place, sibling) for place in ARRIVAL]

    def start(*copies):
        for one in copies:
            one.start()

    def begin():
        start(*a_copies, *b_copies[0], crossing[0])

    def near_a(number):
        a_copies[number].wait_recv()
        start(a_halves[number], *b_copies[1 + number], crossing[1 + number])

    def far_a():
        a_halves[0].wait_recv()
        a_halves[1].wait_recv()
        start(*b_copies[3], crossing[5])

    def near_b(k):
        first = ARRIVAL.index((column[k], -1))
        for number in range(2):
            b_copies[k][number].wait_recv()
            start(b_halves[k][number], crossing[first + number])

    def far_b(k):
        b_halves[k][0].wait_recv()
        b_halves[k][1].wait_recv()
        start(crossing[12 + k])

    events = [
        (0.0, begin),
        (6.5, lambda: near_a(0)),
        (6.5, lambda: near_a(1)),
        (7.5, lambda: near_b(0)),
        (11.0, far_a),
        (15.0, lambda: near_b(1)),
        (21.0, lambda: near_b(2)),
        (24.0, lambda: far_b(0)),
        (28.0, lambda: near_b(3)),
        (32.0, lambda: far_b(1)),
        (40.0, lambda: far_b(2)),
        (44.0, lambda: far_b(3)),
    ]
    return (events, crossing)


def plane_gather_steps(post, own_ref, all_ref):
    events, crossing = plane_gather_events(post, own_ref, all_ref)
    for due, event in events:
        if due > 0.0:
            yield due
        event()
    yield 46.0
    for copy in crossing:
        copy.wait_recv()


PLANE_COPIES = 36


def add_rows(dst, sources, start, rows):
    step = 16 if rows % 16 == 0 else 8

    @pl.loop(0, rows // step)
    def _(i):
        at = pl.multiple_of(i * step, step)
        total = None
        for ref, first in sources:
            part = ref[pl.ds(first + at, step), :].astype(F32)
            total = part if total is None else total + part
        dst[pl.ds(start + at, step), :] = total.astype(dst.dtype)


def plane_scatter_steps(post, parts_ref, sum_ref, scratch, begin=0.0):
    mine, other, b_far, b_near, a_far, a_near, local_sems = scratch
    a, b, core = plane_place()
    ahead_a, behind_a, ahead_b, behind_b, sibling = plane_partners()
    rows = a_far.shape[0]
    top, bottom = halves(a_far)
    high = top.size
    low = rows - high
    offsets = (2, 1, -1, 0)
    go = post.go
    crossing = {}
    order = [(k, 0) for k in range(4)] + [(k, j) for k in range(4) for j in (1, 2)]
    order += [(k, 3) for k in range(4)]
    for k, j in order:
        there = plane_index(b + offsets[k], a + offsets[j], 1 - core)
        crossing[k, j] = go(parts_ref.at[there], other.at[k, j], sibling)
    slots = mine.shape[0]
    loads = []

    def load():
        number = len(loads)
        if number < len(order):
            k, j = order[number]
            here = plane_index(a + offsets[k], b + offsets[j], core)
            slot = number % slots
            copy = pltpu.make_async_copy(
                parts_ref.at[here], mine.at[slot], local_sems.at[slot]
            )
            copy.start()
            loads.append(copy)

    for _ in range(slots - 1):
        load()

    def ready(k, j):
        number = order.index((k, j))
        load()
        crossing[k, j].wait_recv()
        loads[number].wait()
        return (other.at[k, j], mine.at[number % slots])

    far_b, near_b = {}, {}
    for k in range(4):
        yield begin + 2.0 + 1.5 * k
        block, extra = ready(k, 0)
        add_rows(block, [(block, 0), (extra, 0)], 0, rows)
        far_b[k] = (
            go(block.at[top], b_far.at[k, top], ahead_b),
            go(block.at[bottom], b_far.at[k, bottom], behind_b),
        )
    for k in range(4):
        far = b_far.at[k]
        yield begin + 9.0 + 3.0 * k
        block, extra = ready(k, 1)
        far_b[k][0].wait_recv()
        add_rows(block, [(block, 0), (extra, 0), (far, 0)], 0, high)
        add_rows(block, [(block, high), (extra, high)], high, low)
        first = go(block, b_near.at[0, k], ahead_b)
        block, extra = ready(k, 2)
        far_b[k][1].wait_recv()
        add_rows(block, [(block, 0), (extra, 0)], 0, high)
        add_rows(block, [(block, high), (extra, high), (far, high)], high, low)
        near_b[k] = (first, go(block, b_near.at[1, k], behind_b))
    far_a, near_a = [], []
    for k in range(4):
        yield begin + (25.0, 31.0, 37.0, 45.0)[k]
        block, extra = ready(k, 3)
        near_b[k][0].wait_recv()
        near_b[k][1].wait_recv()
        base = [block, extra, b_near.at[0, k], b_near.at[1, k]]
        upper = [(ref, 0) for ref in base]
        lower = [(ref, high) for ref in base]
        if k == 0:
            add_rows(block, upper, 0, high)
            add_rows(block, lower, high, low)
            far_a = [
                go(block.at[top], a_far.at[top], ahead_a),
                go(block.at[bottom], a_far.at[bottom], behind_a),
            ]
        elif k == 1:
            far_a[0].wait_recv()
            add_rows(block, upper + [(a_far, 0)], 0, high)
            add_rows(block, lower, high, low)
            near_a.append(go(block, a_near.at[0], ahead_a))
        elif k == 2:
            far_a[1].wait_recv()
            add_rows(block, upper, 0, high)
            add_rows(block, lower + [(a_far, high)], high, low)
            near_a.append(go(block, a_near.at[1], behind_a))
        else:
            near_a[0].wait_recv()
            near_a[1].wait_recv()
            add_rows(sum_ref, upper + [(a_near.at[0], 0), (a_near.at[1], 0)], 0, rows)


def plane_scatter_scratch(rows, columns, kind):
    return [
        pltpu.VMEM((4, rows, columns), kind),
        pltpu.VMEM((4, 4, rows, columns), kind),
        pltpu.VMEM((4, rows, columns), kind),
        pltpu.VMEM((2, 4, rows, columns), kind),
        pltpu.VMEM((rows, columns), kind),
        pltpu.VMEM((2, rows, columns), kind),
        pltpu.SemaphoreType.DMA((4,)),
    ]


OFFSETS = (2, 1, -1, 0)


def ring_places(a, b, core, tp):
    along_a = [(plane_index(a + offset, b, core), tp) for offset in OFFSETS[:3]]
    along_b = [(plane_index(a, b + offset, core), tp) for offset in OFFSETS[:3]]
    return (along_a, along_b, (plane_index(b, a, 1 - core), tp))


def brief_partners():
    along_a, along_b, sibling = ring_places(*plane_place(), lax.axis_index("tp"))
    return tuple(along_a + along_b + [sibling])


BRIEF_COPIES = 1 + 3 + 3


def brief_number(number):
    return (number // 16, number // 4 % 4, number % 4)


def brief_scatter_steps(post, parts_ref, sum_ref, scratch, begin=0.0):
    other, from_b, total, from_a = scratch
    a, b, core = plane_place()
    along_a, along_b, sibling = ring_places(a, b, core, lax.axis_index("tp"))
    crossing = post.go(at(parts_ref, 1 - core), other, sibling)
    yield begin + 3.0
    crossing.wait_recv()
    for i in range(4):
        other[i] = (other[i].astype(F32) + parts_ref[core, i].astype(F32)).astype(other.dtype)
    copies = [
        post.go(at(other, slice(None), wrap(b + OFFSETS[j])), at(from_b, j), along_b[j])
        for j in range(3)
    ]
    yield begin + 8.0
    for copy in copies:
        copy.wait_recv()
    for i in range(4):
        part = other[i, b].astype(F32)
        for j in range(3):
            part = part + from_b[j, i].astype(F32)
        total[i] = part.astype(total.dtype)
    copies = [
        post.go(at(total, wrap(a + OFFSETS[j])), at(from_a, j), along_a[j]) for j in range(3)
    ]
    yield begin + 11.0
    part = total[a].astype(F32)
    for j in range(3):
        copies[j].wait_recv()
        part = part + from_a[j].astype(F32)
    sum_ref[...] = part.astype(sum_ref.dtype)


def brief_scatter_scratch(rows, columns, kind):
    return [
        pltpu.VMEM((4, 4, rows, columns), kind),
        pltpu.VMEM((3, 4, rows, columns), kind),
        pltpu.VMEM((4, rows, columns), kind),
        pltpu.VMEM((3, rows, columns), kind),
    ]


def brief_gather_steps(post, own_ref, all_ref, begin=0.0):
    a, b, core = plane_place()
    along_a, along_b, sibling = ring_places(a, b, core, lax.axis_index("tp"))
    all_ref[core, a, b] = own_ref[...]
    copies = [post.go(own_ref, at(all_ref, core, a, b), place) for place in along_a]
    yield begin + 3.0
    for copy in copies:
        copy.wait_recv()
    line = at(all_ref, core, slice(None), b)
    copies = [post.go(line, line, place) for place in along_b]
    yield begin + 8.0
    for copy in copies:
        copy.wait_recv()
    crossing = post.go(at(all_ref, core), at(all_ref, core), sibling)
    yield begin + 11.0
    crossing.wait_recv()


LINE_COPIES = 4


def line_gather_steps(post, own_ref, all_ref, clock, near_time, far_time, arrived=None):
    tp = lax.axis_index("tp")
    ahead, behind = line_partners()
    top, bottom = halves(own_ref)
    before, after, far = wrap(tp - 1), wrap(tp + 1), wrap(tp + 2)
    begin = clock.now
    first = post.go(own_ref, all_ref.at[tp], ahead)
    second = post.go(own_ref, all_ref.at[tp], behind)
    if arrived is not None:
        yield from arrived(tp)
    yield clock.until(begin + near_time)
    first.wait_recv()
    third = post.go(all_ref.at[before, top], all_ref.at[before, top], ahead)
    second.wait_recv()
    fourth = post.go(all_ref.at[after, bottom], all_ref.at[after, bottom], behind)
    if arrived is not None:
        yield from arrived(before)
        yield from arrived(after)
    yield clock.until(begin + far_time)
    third.wait_recv()
    fourth.wait_recv()
    if arrived is not None:
        yield from arrived(far)


def line_scatter_steps(post, make, far, near, finish, clock, far_time, near_time):
    ahead, behind = line_partners()
    top, bottom = halves(far)
    high = top.size
    rows = far.shape[0]
    block = yield from make(2)
    begin = clock.now
    first = post.go(block.at[top], far.at[top], ahead)
    second = post.go(block.at[bottom], far.at[bottom], behind)
    block = yield from make(1)
    yield clock.until(begin + far_time)
    first.wait_recv()
    add_rows(block, [(block, 0), (far, 0)], 0, high)
    third = post.go(block, near.at[0], ahead)
    other = yield from make(-1)
    second.wait_recv()
    add_rows(other, [(other, high), (far, high)], high, rows - high)
    fourth = post.go(other, near.at[1], behind)
    begin = clock.now
    own = yield from make(0)
    yield clock.until(begin + near_time)
    third.wait_recv()
    fourth.wait_recv()
    finish(own, near.at[0], near.at[1])


def split_float(values):
    high = values.astype(BF16)
    return (high, (values - high.astype(F32)).astype(BF16))


def split_three(values):
    high = values.astype(BF16)
    rest = values - high.astype(F32)
    middle = rest.astype(BF16)
    return (high, middle, (rest - middle.astype(F32)).astype(BF16))


def head_mean(values):
    same = (
        lax.broadcasted_iota(jnp.int32, (128, 128), 0) // 64
        == lax.broadcasted_iota(jnp.int32, (128, 128), 1) // 64
    ).astype(BF16)
    high, low = split_float(values)
    total = jnp.dot(high, same, preferred_element_type=F32)
    total = total + jnp.dot(low, same, preferred_element_type=F32)
    return total * (1.0 / 64.0)


def other_half(values):
    lane = lax.broadcasted_iota(jnp.int32, values.shape, 1)
    return jnp.where(
        lax.rem(lane, 64) < 32, pltpu.roll(values, 96, 1), pltpu.roll(values, 32, 1)
    )


def head_ready(raw, gain, cosine, sine):
    normed = raw * lax.rsqrt(head_mean(raw * raw) + 1e-06) * gain
    return normed * cosine + other_half(normed) * sine


def head_back(grad, raw, gain, cosine, sine):
    grad = grad * cosine + other_half(grad * sine)
    scale = lax.rsqrt(head_mean(raw * raw) + 1e-06)
    plain = raw * scale
    grad_gain = jnp.sum(grad * plain, axis=0, keepdims=True)
    grad = grad * gain
    return (scale * (grad - plain * head_mean(grad * plain)), grad_gain)


def wide(gain):
    gain = gain.astype(F32)
    return jnp.concatenate([gain[part : part + 1] for part in range(8)], axis=1)


def both_heads(gain):
    gain = gain.astype(F32)
    return jnp.concatenate([gain, gain], axis=1)


def row_scale(values):
    return lax.rsqrt(jnp.mean(values * values, axis=1, keepdims=True) + 1e-05)


def exchange(values):
    return jnp.concatenate([values[:, 64:], values[:, :64]], axis=1)


def head_pairs(block):
    rows = block.shape[0]
    low = lax.broadcasted_iota(jnp.int32, (rows, 128), 1) < 64
    left, right = block[:, :128], block[:, 128:]
    zero = jnp.zeros_like(left)
    straight = jnp.concatenate([jnp.where(low, left, zero), jnp.where(low, zero, right)], axis=0)
    crossed = jnp.concatenate([jnp.where(low, zero, left), jnp.where(low, right, zero)], axis=0)
    return (straight, crossed)


def heads_back(straight, crossed):
    rows = straight.shape[0] // 2
    low = lax.broadcasted_iota(jnp.int32, (rows, 128), 1) < 64
    left = jnp.where(low, straight[:rows], crossed[:rows])
    right = jnp.where(low, crossed[rows:], straight[rows:])
    return jnp.concatenate([left, right], axis=1)


def attend_block(query, keys, values, bias, clock):
    rows = query.shape[0]
    outs = []
    for pair, key_part, value_part in zip(
        head_pairs(query), (keys, exchange(keys)), (values, exchange(values)), strict=True
    ):
        halves_out = []
        for number in range(2):
            part = pair[number * rows : (number + 1) * rows]
            scores = lax.dot_general(part, key_part, CONTRACT_LAST, preferred_element_type=F32)
            weights = jnp.exp(scores * 0.125 + bias)
            total_weight = jnp.sum(weights, axis=1, keepdims=True)
            out = jnp.dot(weights.astype(BF16), value_part, preferred_element_type=F32)
            halves_out.append(out / total_weight)
            yield clock.spend(0.45)
        outs.append(jnp.concatenate(halves_out, axis=0))
    return heads_back(*outs).astype(BF16)


def document_bounds(segments, live_mask):
    one = jnp.ones_like(segments)
    zero = jnp.zeros_like(segments)

    def count(chosen):
        return jnp.sum(jnp.where(chosen, one, zero), axis=1, keepdims=True)

    return (count(segments < 1), count(segments < 2), count(live_mask == 1))


def score_bias(bounds, query, key):
    first, second, living = bounds

    def document(position):
        return (position >= first).astype(jnp.int32) + (position >= second).astype(jnp.int32)

    seen = jnp.where(key < living, 1, 0)
    same = document(query) == document(key)
    return jnp.where(same & ((seen == 1) | (query == key)), 0.0, -1e30).astype(F32)


def block_rows(block):
    return pl.ds(pl.multiple_of(block * 256, 256), 256)


def opening_kernel(
    inputs, gain_one, query_weight, key_weight, value_weight, query_gain, key_gain, cosine, sine,
    segments, live_mask, output_weight, gain_two, router, routes, cotangent,
    gate,
    normed_out, raw_out, query_out, keys_out, values_out, mixed_out,
    residual, block, gates, grad_all, gate_all,
    normed, raw, query, keys, values, mixed,
    parts, far, near, hold, send_sems, recv_sems, local_sems, out_sems,
):
    tp = lax.axis_index("tp")
    own_parts = (
        (cotangent, parts.at[0], grad_all.at[lax.axis_index("ep")]),
        (gate, hold, gate_all.at[tp]),
    )
    inward = [
        pltpu.make_async_copy(src, through, local_sems.at[number])
        for number, (src, through, _) in enumerate(own_parts)
    ]
    outward = [
        pltpu.make_async_copy(through, dst, local_sems.at[number])
        for number, (_, through, dst) in enumerate(own_parts)
    ]
    for copy in inward:
        copy.start()
    greet(plane_partners() + line_partners())
    post = Post(send_sems, recv_sems)
    clock = Clock()
    bounds = document_bounds(segments[...], live_mask[...])

    def project(place):
        rows = block_rows(place)
        part = normed[place]
        cos, sin = cosine[rows, :], sine[rows, :]
        both = jnp.dot(part, query_weight[...], preferred_element_type=F32)
        raw[rows, :256] = both
        for lanes in (slice(0, 128), slice(128, 256)):
            query[rows, lanes] = head_ready(both[:, lanes], both_heads(query_gain[...]), cos, sin).astype(BF16)
        one = jnp.dot(part, key_weight[...], preferred_element_type=F32)
        raw[rows, 256:] = one
        keys[rows, :] = head_ready(one, both_heads(key_gain[...]), cos, sin).astype(BF16)
        values[rows, :] = jnp.dot(part, value_weight[...], preferred_element_type=F32).astype(BF16)
        yield clock.spend(1.5)

    def make(offset):
        place = wrap(tp + offset)
        rows = block_rows(place)
        bias = score_bias(
            bounds,
            place * 256 + lax.broadcasted_iota(jnp.int32, (256, 1), 0),
            lax.broadcasted_iota(jnp.int32, (1, 1024), 1),
        )
        out = yield from attend_block(query[rows, :], keys[...], values[...], bias, clock)
        mixed[rows, :] = out
        part = parts.at[(2, 1, -1, 0).index(offset)]
        part[...] = jnp.dot(out, output_weight[...], preferred_element_type=F32).astype(BF16)
        yield clock.spend(0.4)
        return part

    results = [
        pltpu.make_async_copy(src, dst, out_sems.at[number])
        for number, (src, dst) in enumerate(
            (
                (normed, normed_out), (raw, raw_out), (query, query_out), (keys, keys_out),
                (values, values_out), (mixed, mixed_out),
            )
        )
    ]

    def finish(own, first, second):
        results[5].start()
        total = own[...].astype(F32) + first[...].astype(F32) + second[...].astype(F32)
        total = inputs[...].astype(F32) + total
        residual[...] = total
        normed_two = total * row_scale(total) * wide(gain_two[...])
        block[:256, :] = normed_two.astype(BF16)
        logits = jnp.zeros((32, 256), F32)
        for piece in split_three(normed_two):
            logits = logits + lax.dot_general(
                router[...], piece, CONTRACT_LAST, preferred_element_type=F32
            )
        expert = lax.broadcasted_iota(jnp.int32, (32, 256), 0)
        named = expert < 0
        for choice in range(8):
            named = named | (routes[choice : choice + 1, :] == expert)
        top_logit = jnp.max(jnp.where(named, logits, -1e30), axis=0, keepdims=True)
        raised = jnp.where(named, jnp.exp(jnp.where(named, logits - top_logit, 0.0)), 0.0)
        probs = raised / jnp.sum(raised, axis=0, keepdims=True)
        gates[...] = probs
        high, low = split_float(probs)
        block[256:, :] = jnp.concatenate([high[:16], low[:16], high[16:], low[16:]], axis=1)

    def attention_steps():
        hidden = inputs[...].astype(F32)
        normed[tp] = (hidden * row_scale(hidden) * wide(gain_one[...])).astype(BF16)
        for copy, onward in zip(inward, outward, strict=True):
            copy.wait()
            onward.start()
        clock.spend(1.0)
        yield from line_gather_steps(post, normed.at[tp], normed, clock, 11.5, 17.5, project)
        for copy in outward:
            copy.wait()
        for copy in results[:5]:
            copy.start()
        yield from line_scatter_steps(post, make, far, near, finish, clock, 3.0, 12.0)

    def weight_steps(own, everyone, begin, near_time, far_time):
        yield begin
        yield from line_gather_steps(post, own, everyone, Clock(begin), near_time, far_time)

    together(
        attention_steps(),
        plane_gather_steps(post, cotangent, grad_all),
        weight_steps(gate, gate_all, 20.5, 22.0, 32.0),
    )
    post.finish()
    for copy in results:
        copy.wait()


def opening(arguments, number):
    count = 3 * LINE_COPIES + PLANE_COPIES
    return pl.pallas_call(
        opening_kernel,
        out_shape=[
            jax.ShapeDtypeStruct((4, 256, 1024), BF16),
            jax.ShapeDtypeStruct((1024, 384), F32),
            jax.ShapeDtypeStruct((1024, 256), BF16),
            jax.ShapeDtypeStruct((1024, 128), BF16),
            jax.ShapeDtypeStruct((1024, 128), BF16),
            jax.ShapeDtypeStruct((1024, 256), BF16),
            jax.ShapeDtypeStruct((256, 1024), F32),
            jax.ShapeDtypeStruct((256 + EXTRA, 1024), BF16),
            jax.ShapeDtypeStruct((32, 256), F32),
            jax.ShapeDtypeStruct((32, 256, 1024), BF16),
            jax.ShapeDtypeStruct((4, 1024, 128), BF16),
        ],
        in_specs=[VMEM] * (len(arguments) - 2) + [ANY] * 2,
        out_specs=[ANY] * 6 + [VMEM] * 3 + [ANY] * 2,
        scratch_shapes=[
            pltpu.VMEM((4, 256, 1024), BF16),
            pltpu.VMEM((1024, 384), F32),
            pltpu.VMEM((1024, 256), BF16),
            pltpu.VMEM((1024, 128), BF16),
            pltpu.VMEM((1024, 128), BF16),
            pltpu.VMEM((1024, 256), BF16),
            pltpu.VMEM((4, 256, 1024), BF16),
            pltpu.VMEM((256, 1024), BF16),
            pltpu.VMEM((2, 256, 1024), BF16),
            pltpu.VMEM((1024, 128), BF16),
            pltpu.SemaphoreType.DMA((count,)),
            pltpu.SemaphoreType.DMA((count,)),
            pltpu.SemaphoreType.DMA((2,)),
            pltpu.SemaphoreType.DMA((6,)),
        ],
        compiler_params=pltpu.CompilerParams(
            collective_id=number, has_side_effects=True, vmem_limit_bytes=56 << 20
        ),
        name="opening",
    )(*arguments)


def attend_back_block(query, grad, keys, values, bias, keys_sum, values_sum, clock):
    rows = query.shape[0]
    query_pairs = head_pairs(query)
    grad_pairs = head_pairs(grad)
    key_parts = (keys, exchange(keys))
    value_parts = (values, exchange(values))
    outs = []
    for side in range(2):
        halves_out = []
        for number in range(2):
            part = query_pairs[side][number * rows : (number + 1) * rows]
            grad_part = grad_pairs[side][number * rows : (number + 1) * rows]
            scores = lax.dot_general(
                key_parts[side], part, CONTRACT_LAST, preferred_element_type=F32
            )
            raised = jnp.exp(scores * 0.125 + bias)
            weights = raised * (1.0 / jnp.sum(raised, axis=0, keepdims=True))
            grad_weights = lax.dot_general(
                value_parts[side], grad_part, CONTRACT_LAST, preferred_element_type=F32
            )
            inner = jnp.sum(weights * grad_weights, axis=0, keepdims=True)
            grad_scores = (weights * (grad_weights - inner)).astype(BF16)
            halves_out.append(
                lax.dot_general(
                    grad_scores, key_parts[side], CONTRACT_ROWS, preferred_element_type=F32
                )
            )
            keys_sum[side] += jnp.dot(grad_scores, part, preferred_element_type=F32)
            values_sum[side] += jnp.dot(
                weights.astype(BF16), grad_part, preferred_element_type=F32
            )
            yield clock.spend(1.4)
        outs.append(jnp.concatenate(halves_out, axis=0))
    return heads_back(*outs) * 0.125


SMALL_ROWS = 16
WEIGHTS_AT = 20.0


def closing_kernel(
    back, residual, gates, cotangent, gain_two, router, query_far, keys_far, values_far, mixed_far,
    output_weight, query_weight_far, key_weight_far, value_weight_far, raw_far, normed_far,
    inputs_far, gain_one, query_gain, key_gain, cosine, sine, segments, live_mask, out_parts,
    weight_parts, grad_inputs, dense_all, small_all, combined, weight_sum,
    grad_all, grad_residual, low, keys_sum, values_sum, output_sum, parts, far, near,
    dense, dense_own, small, small_own, small_early, small_late, small_total, query_gain_sum,
    weights, weights_far, weights_near, query, keys, values, mixed, query_weight, key_weight, value_weight, raw, normed, inputs,
    late_sems, *rest,
):
    out_scratch, dense_scratch, small_scratch = rest[:7], rest[7:11], rest[11:15]
    post = Post(rest[15], rest[16])
    me = lax.axis_index("ep")
    tp = lax.axis_index("tp")
    ahead, behind = line_partners()
    across = (me, wrap(tp + 2))
    late = [
        pltpu.make_async_copy(src, dst, late_sems.at[number])
        for number, (src, dst) in enumerate(
            (
                (query_far, query), (keys_far, keys), (values_far, values), (mixed_far, mixed),
                (query_weight_far, query_weight), (key_weight_far, key_weight),
                (value_weight_far, value_weight), (raw_far, raw), (normed_far, normed),
                (inputs_far, inputs),
                (weight_parts.at[wrap(tp + 1)], weights.at[0]),
                (weight_parts.at[wrap(tp - 1)], weights.at[1]),
                (weight_parts.at[tp], weights.at[2]),
            )
        )
    ]
    for copy in late:
        copy.start()
    greet(brief_partners() + (ahead, behind, across))
    clock = Clock()
    out_steps = plane_scatter_steps(post, out_parts, combined, out_scratch)
    out_due = next(out_steps)

    lines = back[256:, :]
    grad_gates = jnp.concatenate(
        [lines[:, :256] + lines[:, 256:512], lines[:, 512:768] + lines[:, 768:]], axis=0
    )
    probs = gates[...]
    grad_logits = probs * (grad_gates - jnp.sum(probs * grad_gates, axis=0, keepdims=True))
    grad_two = back[:256, :]
    logit_pieces = split_three(grad_logits)
    for piece in logit_pieces:
        grad_two = grad_two + lax.dot_general(
            piece, router[...], CONTRACT_ROWS, preferred_element_type=F32
        )
    total = residual[...]
    scale = row_scale(total)
    plain = total * scale
    grad_gain_two = jnp.sum(grad_two * plain, axis=0, keepdims=True)
    grad_two = grad_two * wide(gain_two[...])
    grad_total = cotangent[...].astype(F32) + scale * (
        grad_two - plain * jnp.mean(grad_two * plain, axis=1, keepdims=True)
    )
    grad_residual[...] = grad_total
    grad_all[tp] = grad_total.astype(BF16)
    clock.spend(4.0)

    bounds = document_bounds(segments[...], live_mask[...])
    keys_sum[...] = jnp.zeros_like(keys_sum)
    values_sum[...] = jnp.zeros_like(values_sum)
    output_sum[...] = jnp.zeros_like(output_sum)
    query_gain_sum[...] = jnp.zeros_like(query_gain_sum)

    def attention(place):
        rows = block_rows(place)
        grad = grad_all[place]
        output_sum[...] += lax.dot_general(
            mixed[rows, :], grad, CONTRACT_ROWS, preferred_element_type=F32
        )
        grad_mixed = lax.dot_general(
            grad, output_weight[...], CONTRACT_LAST, preferred_element_type=F32
        ).astype(BF16)
        bias = score_bias(
            bounds,
            place * 256 + lax.broadcasted_iota(jnp.int32, (1, 256), 1),
            lax.broadcasted_iota(jnp.int32, (1024, 1), 0),
        )
        clock.spend(0.8)
        grad_query = yield from attend_back_block(
            query[rows, :], grad_mixed, keys[...], values[...], bias, keys_sum, values_sum, clock
        )
        for lanes in (slice(0, 128), slice(128, 256)):
            grad_raw, grad_gain = head_back(
                grad_query[:, lanes],
                raw[rows, lanes],
                both_heads(query_gain[...]),
                cosine[rows, :],
                sine[rows, :],
            )
            low[rows, lanes] = grad_raw.astype(BF16)
            query_gain_sum[...] += grad_gain
        yield clock.spend(0.5)

    def make(offset):
        rows = block_rows(wrap(tp + offset))
        total = lax.dot_general(
            low[rows, :256], query_weight[...], CONTRACT_LAST, preferred_element_type=F32
        )
        total = total + lax.dot_general(
            low[rows, 256:384], key_weight[...], CONTRACT_LAST, preferred_element_type=F32
        )
        total = total + lax.dot_general(
            low[rows, 384:], value_weight[...], CONTRACT_LAST, preferred_element_type=F32
        )
        part = parts.at[(2, 1, -1, 0).index(offset)]
        part[...] = total.astype(BF16)
        yield clock.spend(0.8)
        return part

    def finish(own, first, second):
        grad_one = own[...].astype(F32) + first[...].astype(F32) + second[...].astype(F32)
        hidden = inputs[...].astype(F32)
        scale = row_scale(hidden)
        plain = hidden * scale
        grad_one = grad_one * wide(gain_one[...])
        grad_inputs[...] = (
            grad_residual[...]
            + scale * (grad_one - plain * jnp.mean(grad_one * plain, axis=1, keepdims=True))
        ).astype(BF16)

    def router_gradient():
        normed_pieces = split_three(plain * wide(gain_two[...]))
        total = jnp.zeros((32, 1024), F32)
        for first, second in ((0, 0), (0, 1), (1, 0), (1, 1), (0, 2), (2, 0)):
            total = total + jnp.dot(
                logit_pieces[first], normed_pieces[second], preferred_element_type=F32
            )
        return total

    gain_rows = small.at[brief_number(16)]
    head_rows = small.at[brief_number(17)]

    def fill_router():
        grad_router = router_gradient()
        small[...] = jnp.zeros_like(small)
        for part in range(8):
            lanes = slice(part * 128, (part + 1) * 128)
            small[brief_number(2 * part)] = grad_router[:16, lanes]
            small[brief_number(2 * part + 1)] = grad_router[16:, lanes]
            gain_rows[8 + part : 9 + part, :] = grad_gain_two[:, lanes]

    def fill_small(weights, grad_key_gain):
        grad_gain_one = jnp.zeros((8, 1024), F32)
        ones = jnp.ones((8, 128), BF16)
        parts = [query_weight[:, :128], query_weight[:, 128:], key_weight[...], value_weight[...]]
        for number, part in enumerate(parts):
            product = weights[:, number * 128 : (number + 1) * 128] * part.astype(F32)
            for piece in split_float(product):
                grad_gain_one = grad_gain_one + lax.dot_general(
                    ones, piece, CONTRACT_LAST, preferred_element_type=F32
                )
        grad_gain_one = grad_gain_one[:1] / wide(gain_one[...])
        for part in range(8):
            gain_rows[part : part + 1, :] = grad_gain_one[:, part * 128 : (part + 1) * 128]
        head_rows[0:1, :] = query_gain_sum[...]
        head_rows[1:2, :] = grad_key_gain

    def attention_steps():
        filled, early_line = [], []

        def send_line(part, slots):
            return [
                post.go(part, at(slots, number), partner)
                for number, partner in enumerate((ahead, behind, across))
            ]

        def arrived(place):
            if not filled:
                filled.append(place)
                fill_router()
                early_line.extend(send_line(at(small, 0), small_early))
                for copy in late:
                    copy.wait()
            yield from attention(place)

        yield from line_gather_steps(
            post, grad_all.at[tp], grad_all, clock, 11.5, 17.5, arrived
        )
        grad_raw, grad_key_gain = head_back(
            (keys_sum[0] + exchange(keys_sum[1])) * 0.125,
            raw[:, 256:],
            both_heads(key_gain[...]),
            cosine[...],
            sine[...],
        )
        low[:, 256:384] = grad_raw.astype(BF16)
        low[:, 384:] = (values_sum[0] + exchange(values_sum[1])).astype(BF16)
        weights = lax.dot_general(
            normed[...], low[...], CONTRACT_ROWS, preferred_element_type=F32
        )
        fill_small(weights, grad_key_gain)
        line = early_line + send_line(at(small, 1, 0, pl.ds(0, 2)), small_late)
        fill_dense(weights)
        now = clock.spend(8.0)
        yield from side_by_side(
            (now, dense_steps(now)),
            (now, small_steps(now, line)),
            (now, line_scatter_steps(post, make, far, near, finish, clock, 3.5, 11.5)),
        )

    def fill_dense(weights):
        weights = weights.astype(BF16)
        for part in range(32):
            dense[(*brief_number(part), slice(None), slice(0, 512))] = weights[
                part * 32 : (part + 1) * 32
            ]
        for part in range(4):
            block = output_sum[:, part * 256 : (part + 1) * 256].astype(BF16)
            for piece in range(8):
                dense[(*brief_number(part * 8 + piece), slice(None), slice(512, 768))] = block[
                    piece * 32 : (piece + 1) * 32
                ]

    def dense_steps(begin):
        yield from brief_scatter_steps(post, dense, dense_own, dense_scratch, begin)
        yield from brief_gather_steps(post, dense_own, dense_all, begin + 12.0)

    def small_steps(begin, line):
        for copy in line:
            copy.wait_recv()
        small_total[...] = jnp.zeros_like(small_total)
        for place in range(4):
            small_total[0, place] = small[0, place] + (
                small_early[0, place] + small_early[1, place] + small_early[2, place]
            )
        small_total[1, 0, :2] = small[1, 0, :2] + small_late[0] + small_late[1] + small_late[2]
        yield from brief_scatter_steps(post, small_total, small_own, small_scratch, begin)
        yield from brief_gather_steps(post, small_own, small_all, begin + 12.0)

    def make_weights(offset):
        yield 0.0
        if offset == 2:
            return weight_parts.at[wrap(tp + 2)]
        return weights.at[(1, -1, 0).index(offset)]

    def finish_weights(own, first, second):
        add_rows(weight_sum, [(own, 0), (first, 0), (second, 0)], 0, own.shape[0])

    def weight_steps():
        yield WEIGHTS_AT
        yield from line_scatter_steps(
            post, make_weights, weights_far, weights_near, finish_weights, Clock(WEIGHTS_AT), 14.0, 60.0
        )

    together(attention_steps(), resumed(out_due, out_steps), weight_steps())
    post.finish()


def closing(arguments, number):
    count = 3 * LINE_COPIES + PLANE_COPIES + 4 * BRIEF_COPIES + 6
    return pl.pallas_call(
        closing_kernel,
        out_shape=[
            jax.ShapeDtypeStruct((256, 1024), BF16),
            jax.ShapeDtypeStruct((2, 4, 4, 32, 768), BF16),
            jax.ShapeDtypeStruct((2, 4, 4, SMALL_ROWS, 128), F32),
            jax.ShapeDtypeStruct((256, 1024), F32),
            jax.ShapeDtypeStruct((3072, 128), F32),
        ],
        in_specs=[VMEM] * 6 + [ANY] * 4 + [VMEM] + [ANY] * 6 + [VMEM] * 7 + [ANY] * 2,
        out_specs=[VMEM] * 5,
        scratch_shapes=[
            pltpu.VMEM((4, 256, 1024), BF16),
            pltpu.VMEM((256, 1024), F32),
            pltpu.VMEM((1024, 512), BF16),
            pltpu.VMEM((2, 1024, 128), F32),
            pltpu.VMEM((2, 1024, 128), F32),
            pltpu.VMEM((256, 1024), F32),
            pltpu.VMEM((4, 256, 1024), BF16),
            pltpu.VMEM((256, 1024), BF16),
            pltpu.VMEM((2, 256, 1024), BF16),
            pltpu.VMEM((2, 4, 4, 32, 768), BF16),
            pltpu.VMEM((32, 768), BF16),
            pltpu.VMEM((2, 4, 4, SMALL_ROWS, 128), F32),
            pltpu.VMEM((SMALL_ROWS, 128), F32),
            pltpu.VMEM((3, 4, 4, SMALL_ROWS, 128), F32),
            pltpu.VMEM((3, 2, SMALL_ROWS, 128), F32),
            pltpu.VMEM((2, 4, 4, SMALL_ROWS, 128), F32),
            pltpu.VMEM((1, 128), F32),
            pltpu.VMEM((3, 3072, 128), BF16),
            pltpu.VMEM((3072, 128), BF16),
            pltpu.VMEM((2, 3072, 128), BF16),
            pltpu.VMEM((1024, 256), BF16),
            pltpu.VMEM((1024, 128), BF16),
            pltpu.VMEM((1024, 128), BF16),
            pltpu.VMEM((1024, 256), BF16),
            pltpu.VMEM((1024, 256), BF16),
            pltpu.VMEM((1024, 128), BF16),
            pltpu.VMEM((1024, 128), BF16),
            pltpu.VMEM((1024, 384), F32),
            pltpu.VMEM((1024, 1024), BF16),
            pltpu.VMEM((256, 1024), BF16),
            pltpu.SemaphoreType.DMA((13,)),
        ]
        + plane_scatter_scratch(256, 1024, BF16)
        + brief_scatter_scratch(32, 768, BF16)
        + brief_scatter_scratch(SMALL_ROWS, 128, F32)
        + [pltpu.SemaphoreType.DMA((count,)), pltpu.SemaphoreType.DMA((count,))],
        compiler_params=pltpu.CompilerParams(
            collective_id=number, has_side_effects=True, vmem_limit_bytes=63 << 20
        ),
        name="closing",
    )(*arguments)


def finish_kernel(
    dense_far, weights_far, residual_far, combined_far, small_far, inputs_far,
    result, grad_inputs, grad_query, grad_key, grad_value, grad_output, grad_gate, grad_up,
    grad_down, gain_one, gain_two, query_gain, key_gain, router,
    dense, weights, residual, combined, small, sems,
):
    copies = [
        pltpu.make_async_copy(src, dst, sems.at[number])
        for number, (src, dst) in enumerate(
            (
                (weights_far, weights), (dense_far, dense), (residual_far, residual),
                (combined_far, combined), (small_far, small), (inputs_far, grad_inputs),
            )
        )
    ]
    for copy in copies:
        copy.start()
    copies[0].wait()
    grad_gate[0] = weights[:1024, :]
    grad_up[0] = weights[1024:2048, :]
    grad_down[0] = weights[2048:, :].T
    copies[1].wait()
    grad_query[...] = dense[:, :256].astype(F32)
    grad_key[...] = dense[:, 256:384].astype(F32)
    grad_value[...] = dense[:, 384:512].astype(F32)
    for part in range(4):
        grad_output[:, part * 256 : (part + 1) * 256] = dense[
            part * 256 : (part + 1) * 256, 512:
        ].astype(F32)
    copies[2].wait()
    copies[3].wait()
    result[...] = (residual[...] + combined[...]).astype(BF16)
    copies[4].wait()
    for part in range(8):
        lanes = slice(part * 128, (part + 1) * 128)
        router[:16, lanes] = small[2 * part]
        router[16:, lanes] = small[2 * part + 1]
        gain_one[:, lanes] = small[16, part : part + 1, :]
        gain_two[:, lanes] = small[16, 8 + part : 9 + part, :]
    heads = small[17]
    heads = heads[:, :64] + heads[:, 64:]
    query_gain[...] = heads[0:1]
    key_gain[...] = heads[1:2]
    copies[5].wait()


def finish_all(arguments):
    return pl.pallas_call(
        finish_kernel,
        out_shape=[
            jax.ShapeDtypeStruct((256, 1024), BF16),
            jax.ShapeDtypeStruct((256, 1024), BF16),
            jax.ShapeDtypeStruct((1024, 256), F32),
            jax.ShapeDtypeStruct((1024, 128), F32),
            jax.ShapeDtypeStruct((1024, 128), F32),
            jax.ShapeDtypeStruct((256, 1024), F32),
            jax.ShapeDtypeStruct((1, 1024, 128), F32),
            jax.ShapeDtypeStruct((1, 1024, 128), F32),
            jax.ShapeDtypeStruct((1, 128, 1024), F32),
            jax.ShapeDtypeStruct((1, 1024), F32),
            jax.ShapeDtypeStruct((1, 1024), F32),
            jax.ShapeDtypeStruct((1, 64), F32),
            jax.ShapeDtypeStruct((1, 64), F32),
            jax.ShapeDtypeStruct((32, 1024), F32),
        ],
        in_specs=[ANY] * 6,
        out_specs=[VMEM] * 14,
        scratch_shapes=[
            pltpu.VMEM((1024, 768), BF16),
            pltpu.VMEM((3072, 128), F32),
            pltpu.VMEM((256, 1024), F32),
            pltpu.VMEM((256, 1024), F32),
            pltpu.VMEM((32, SMALL_ROWS, 128), F32),
            pltpu.SemaphoreType.DMA((6,)),
        ],
        compiler_params=pltpu.CompilerParams(vmem_limit_bytes=60 << 20),
        name="finish_all",
    )(*arguments)


STEPS = ((0, 1), (3, 4), (6, 7), (12, 13), (14, 15), (10, 11), (8, 9), (2, 5))
GROUP = 4


def experts_kernel(
    block, grads, gate_all, up, down,
    rows_all, out_parts, back_sum, weight_parts,
    rows_in, grads_in, both_full, down_full, both_sum, down_sum, rows_own, grads_own, gates_own,
    select, weighted, grad_rows, grad_gates, mine, other, stage, out_stage,
    b_far, b_near, a_far, a_near, line, send_sems, recv_sems, credit, load_sems, store_sems, weight_sems, own_sem,
):
    a, b, core = plane_place()
    me = lax.axis_index("ep")
    ahead_a, behind_a, ahead_b, behind_b, sibling = plane_partners()
    here = [plane_index(a + place[0], b + place[1], core) for place in ARRIVAL]
    there = [plane_index(b + place[0], a + place[1], 1 - core) for place in ARRIVAL]
    lane_row = lax.rem(me, 16)
    upper = me >= 16
    tp = lax.axis_index("tp")
    ahead, behind = line_partners()
    greet(plane_partners() + (ahead, behind))
    post = Post(send_sems, recv_sems)
    go = post.go
    events, held = plane_gather_events(post, block, rows_all)
    events[0][1]()
    own_copy = pltpu.make_async_copy(block, stage.at[0], own_sem)
    own_copy.start()
    before_me, after_me = wrap(tp - 1), wrap(tp + 1)

    def up_part(place, rows=slice(None)):
        return at(both_full, rows, pl.ds(pl.multiple_of(512 + place * 128, 128), 128))

    def down_part(place, first=0, count=128):
        return at(down_full, pl.ds(pl.multiple_of(place * 128 + first, 64), count))

    up_near = (
        post.go(up, up_part(tp), ahead), post.go(up, up_part(tp), behind)
    )
    down_near = (
        post.go(down, down_part(tp), ahead), post.go(down, down_part(tp), behind)
    )
    up_top, up_bottom = up_part(before_me, pl.ds(0, 512)), up_part(after_me, pl.ds(512, 512))
    up_far = (
        post.prepare(up_top, up_top, ahead), post.prepare(up_bottom, up_bottom, behind)
    )
    down_top, down_bottom = down_part(before_me, 0, 64), down_part(after_me, 64, 64)
    down_far = (
        post.prepare(down_top, down_top, ahead), post.prepare(down_bottom, down_bottom, behind)
    )

    def relay(near, far):
        for one, other_one in zip(near, far, strict=True):
            one.wait_recv()
            other_one.start()

    weight_loads = [
        pltpu.make_async_copy(
            gate_all.at[part], both_full.at[:, part * 128 : (part + 1) * 128], weight_sems.at[part]
        )
        for part in range(4)
    ]
    weight_loads.append(pltpu.make_async_copy(up, up_part(tp)(), weight_sems.at[4]))
    weight_loads.append(pltpu.make_async_copy(down, down_part(tp)(), weight_sems.at[5]))
    for copy in weight_loads:
        copy.start()
    both_sum[...] = jnp.zeros_like(both_sum)
    down_sum[...] = jnp.zeros_like(down_sum)

    def blocks(step):
        first, second = STEPS[step]
        return (here[first], here[second], there[first], there[second])

    loads, crossing, stores = {}, {}, {}
    for step in range(len(STEPS)):
        slot = step % 2
        loads[step], stores[step] = [], []
        crossing[step] = [
            post.prepare(at(stage, part), at(other, slot, part), sibling) for part in range(2)
        ]
        for part, index in enumerate(blocks(step)):
            loads[step] += [
                Local(
                    at(rows_all, index), at(rows_in, slot, part), at(load_sems, slot, 0, part)
                ),
                Local(at(grads, index), at(grads_in, slot, part), at(load_sems, slot, 1, part)),
            ]
            stores[step].append(
                Local(at(out_stage, part), at(out_parts, index), at(store_sems, part))
            )

    def load(step):
        for place in STEPS[step]:
            held[place].wait_recv()
        for copy in loads[step]:
            copy.start()

    def take(step):
        for part, place in enumerate(STEPS[step]):
            crossing[step][part].wait_recv()
            add_rows(
                mine.at[place], [(mine.at[place], 0), (other.at[step % 2, part], 0)], 0, rows
            )
        if step + 2 < len(STEPS):
            pl.semaphore_signal(credit, inc=1, device_id=sibling, device_id_type=MESH)

    rows = a_far.shape[0]
    top, bottom = halves(a_far)
    high = top.size
    low = rows - high
    far_b, near_b = {}, {}

    def number_of(k, j):
        return ARRIVAL.index((OFFSETS[k], OFFSETS[j]))

    def slot_of(k, j):
        return mine.at[number_of(k, j)]

    def far_step(k):
        part = number_of(k, 0)
        far_b[k] = (
            go(at(mine, part, top), at(b_far, k, top), ahead_b),
            go(at(mine, part, bottom), at(b_far, k, bottom), behind_b),
        )

    def near_step(k):
        far = b_far.at[k]
        far_b[k][0].wait_recv()
        part = slot_of(k, 1)
        add_rows(part, [(part, 0), (far, 0)], 0, high)
        first = go(at(mine, number_of(k, 1)), at(b_near, 0, k), ahead_b)
        far_b[k][1].wait_recv()
        part = slot_of(k, 2)
        add_rows(part, [(part, high), (far, high)], high, low)
        near_b[k] = (first, go(at(mine, number_of(k, 2)), at(b_near, 1, k), behind_b))

    def before(step):
        for copy in loads[step]:
            copy.wait()

    def between(step):
        if step > 0:
            for copy in crossing[step - 1]:
                copy.wait_send()
            for copy in stores[step - 1]:
                copy.wait()
        onward({0: (4,), 1: (6,), 2: (7, 8, 9), 3: (10, 11)}.get(step, ()))
        if step + 1 < len(STEPS):
            load(step + 1)
        if step > 0:
            take(step - 1)
        if step == 4:
            far_step(2)
            far_step(3)
        if step == 5:
            far_step(0)
            far_step(1)
            near_step(3)
            near_step(2)
        if step == 6:
            near_step(0)
        if step == 7:
            near_step(1)

    def onward(numbers):
        for number in numbers:
            events[number][1]()

    def early(step):
        if step == 0:
            for copy in up_far + down_far:
                copy.wait_recv()

    def after(step):
        onward({0: (5,)}.get(step, ()))
        if step >= 2:
            pl.semaphore_wait(credit, 1)
        for copy in crossing[step] + stores[step]:
            copy.start()

    def at_step(step, task):
        for number in range(len(STEPS)):

            @pl.when(step == number)
            def _(number=number):
                task(number)

    def from_table(step, table):
        value = step * 0 + table[0]
        for number in range(1, len(table)):
            value = jnp.where(step == number, table[number], value)
        return value

    own_copy.wait()
    own_copy = pltpu.make_async_copy(stage.at[0], rows_all.at[me], own_sem)
    own_copy.start()
    onward((1, 2))
    own_copy.wait()
    load(0)
    relay(up_near, up_far)
    onward((3,))
    relay(down_near, down_far)
    for copy in weight_loads:
        copy.wait()
    extra_row = lax.broadcasted_iota(jnp.int32, (EXTRA, 1024), 0) == lane_row

    def one_step(step, carry):
        slot = lax.rem(step, 2)
        at_step(step, before)
        earlier = (
            lax.broadcasted_iota(jnp.int32, (256, 256), 0)
            <= lax.broadcasted_iota(jnp.int32, (256, 256), 1)
        ).astype(BF16)
        place = lax.broadcasted_iota(jnp.int32, (SLOTS, 256), 0).astype(F32)
        for part in range(GROUP):
            extras = jnp.where(extra_row, rows_in[slot, part, 256:, :].astype(F32), 0.0)
            extras = jnp.sum(extras, axis=0, keepdims=True)
            gates = jnp.where(
                upper, extras[:, 512:768] + extras[:, 768:], extras[:, :256] + extras[:, 256:512]
            )
            named = jnp.broadcast_to(gates, (16, 256)) > 0.0
            rank = jnp.dot(named.astype(BF16), earlier, preferred_element_type=F32)[:1] - 1.0
            chosen = (place == rank) & (gates > 0.0)
            chosen_low = chosen.astype(BF16)
            at = slice(part * SLOTS, (part + 1) * SLOTS)
            select[at, :] = chosen_low
            rows_own[at, :] = jnp.dot(
                chosen_low, rows_in[slot, part, :256, :], preferred_element_type=F32
            ).astype(BF16)
            grads_own[at, :] = jnp.dot(
                chosen_low, grads_in[slot, part], preferred_element_type=F32
            ).astype(BF16)
            gates_own[at, :] = jnp.sum(jnp.where(chosen, gates, 0.0), axis=1, keepdims=True)

        at_step(step, early)
        both_pre = jnp.dot(rows_own[...], both_full[...], preferred_element_type=F32)
        gate_pre, up_pre = both_pre[:, :512], both_pre[:, 512:]
        sigmoid = 1.0 / (1.0 + jnp.exp(-gate_pre))
        silu = gate_pre * sigmoid
        act = (silu * up_pre).astype(BF16)
        out = jnp.dot(act, down_full[...], preferred_element_type=F32).astype(BF16).astype(F32)
        gate_factor = gates_own[...]
        grads_float = grads_own[...].astype(F32)
        grad_gates[...] = jnp.sum(grads_float * out, axis=1, keepdims=True)
        weighted[...] = (gate_factor * out).astype(BF16)
        grad_out = (gate_factor * grads_float).astype(BF16)
        grad_act = lax.dot_general(
            grad_out, down_full[...], CONTRACT_LAST, preferred_element_type=F32
        )
        down_sum[...] += lax.dot_general(
            grad_out, act, CONTRACT_ROWS, preferred_element_type=F32
        )
        grad_gate_pre = grad_act * up_pre * sigmoid * (1.0 + gate_pre * (1.0 - sigmoid))
        grad_up_pre = grad_act * silu
        grad_pre = jnp.concatenate(
            [grad_gate_pre.astype(BF16), grad_up_pre.astype(BF16)], axis=1
        )
        both_sum[...] += lax.dot_general(
            rows_own[...], grad_pre, CONTRACT_ROWS, preferred_element_type=F32
        )
        grad_rows[...] = lax.dot_general(
            grad_pre, both_full[...], CONTRACT_LAST, preferred_element_type=F32
        ).astype(BF16)
        at_step(step, between)
        nothing = jnp.zeros((1, 512), F32)
        slots = [from_table(step, [pair[part] for pair in STEPS]) for part in range(2)]
        for part in range(GROUP):
            at = slice(part * SLOTS, (part + 1) * SLOTS)
            chosen_low = select[at, :]
            out_stage[part] = lax.dot_general(
                chosen_low, weighted[at], CONTRACT_ROWS, preferred_element_type=F32
            ).astype(BF16)
            target = mine.at[slots[part]] if part < 2 else stage.at[part - 2]
            target[:256, :] = lax.dot_general(
                chosen_low, grad_rows[at], CONTRACT_ROWS, preferred_element_type=F32
            ).astype(BF16)
            spread = jnp.sum(chosen_low.astype(F32) * grad_gates[at], axis=0, keepdims=True)
            upper_bits = spread.astype(BF16).astype(F32)
            both = jnp.concatenate([upper_bits, spread - upper_bits], axis=1)
            line_now = jnp.concatenate(
                [jnp.where(upper, nothing, both), jnp.where(upper, both, nothing)], axis=1
            )
            target[256:, :] = jnp.where(extra_row, line_now, 0.0).astype(BF16)
        at_step(step, after)
        return carry

    lax.fori_loop(0, len(STEPS), one_step, 0)
    last = len(STEPS) - 1

    def weight_steps():
        for part in range(4):
            yield 2.5 + part
            lanes = slice(part * 128, (part + 1) * 128)
            upper_lanes = slice(512 + part * 128, 512 + (part + 1) * 128)
            line[part, :1024, :] = both_sum[:, lanes].astype(BF16)
            line[part, 1024:2048, :] = both_sum[:, upper_lanes].astype(BF16)
            line[part, 2048:, :] = down_sum[:, lanes].astype(BF16)
            Local(at(line, part), at(weight_parts, part), at(weight_sems, part)).start()
        yield 100.0
        for part in range(4):
            Local(at(line, part), at(weight_parts, part), at(weight_sems, part)).wait()

    def back_steps():
        yield 0.0
        take(last)
        far_a, near_a = [], []
        for k in range(4):
            yield (2.0, 4.0, 8.0, 12.0)[k]
            part = slot_of(k, 3)
            near_b[k][0].wait_recv()
            near_b[k][1].wait_recv()
            base = [part, b_near.at[0, k], b_near.at[1, k]]
            first_rows = [(ref, 0) for ref in base]
            last_rows = [(ref, high) for ref in base]
            if k == 0:
                add_rows(part, first_rows, 0, high)
                add_rows(part, last_rows, high, low)
                far_a = [
                    go(part.at[top], a_far.at[top], ahead_a),
                    go(part.at[bottom], a_far.at[bottom], behind_a),
                ]
            elif k == 1:
                far_a[0].wait_recv()
                add_rows(part, first_rows + [(a_far, 0)], 0, high)
                add_rows(part, last_rows, high, low)
                near_a.append(go(part, a_near.at[0], ahead_a))
            elif k == 2:
                far_a[1].wait_recv()
                add_rows(part, first_rows, 0, high)
                add_rows(part, last_rows + [(a_far, high)], high, low)
                near_a.append(go(part, a_near.at[1], behind_a))
            else:
                near_a[0].wait_recv()
                near_a[1].wait_recv()
                add_rows(
                    back_sum, first_rows + [(a_near.at[0], 0), (a_near.at[1], 0)], 0, rows
                )

    together(back_steps(), weight_steps())
    for copy in stores[last]:
        copy.wait()
    waited = [copy for step in range(last) for copy in crossing[step]]
    for copy in post.started:
        if not any(copy is other_copy for other_copy in waited):
            copy.wait_send()


def run_experts(block, grads, gate_all, up, down, number):
    rows, columns = block.shape
    sources = grads.shape[0]
    count = GROUP * SLOTS
    copies = PLANE_COPIES + 16 + 8 + 8 + 4 + 2 * LINE_COPIES
    whole = (rows, columns)
    return pl.pallas_call(
        experts_kernel,
        out_shape=[
            jax.ShapeDtypeStruct((sources,) + whole, BF16),
            jax.ShapeDtypeStruct((sources, 256, columns), BF16),
            jax.ShapeDtypeStruct(whole, F32),
            jax.ShapeDtypeStruct((4, 3072, 128), BF16),
        ],
        in_specs=[ANY] * 5,
        out_specs=[ANY, ANY, VMEM, ANY],
        scratch_shapes=[
            pltpu.VMEM((2, GROUP) + whole, BF16),
            pltpu.VMEM((2, GROUP, 256, columns), BF16),
            pltpu.VMEM((1024, 1024), BF16),
            pltpu.VMEM((512, 1024), BF16),
            pltpu.VMEM((1024, 1024), F32),
            pltpu.VMEM((1024, 512), F32),
            pltpu.VMEM((count, 1024), BF16),
            pltpu.VMEM((count, 1024), BF16),
            pltpu.VMEM((count, 1), F32),
            pltpu.VMEM((count, 256), BF16),
            pltpu.VMEM((count, 1024), BF16),
            pltpu.VMEM((count, 1024), BF16),
            pltpu.VMEM((count, 1), F32),
            pltpu.VMEM((16,) + whole, BF16),
            pltpu.VMEM((2, 2) + whole, BF16),
            pltpu.VMEM((2,) + whole, BF16),
            pltpu.VMEM((GROUP, 256, columns), BF16),
            pltpu.VMEM((4,) + whole, BF16),
            pltpu.VMEM((2, 4) + whole, BF16),
            pltpu.VMEM(whole, BF16),
            pltpu.VMEM((2,) + whole, BF16),
            pltpu.VMEM((4, 3072, 128), BF16),
            pltpu.SemaphoreType.DMA((copies,)),
            pltpu.SemaphoreType.DMA((copies,)),
            pltpu.SemaphoreType.REGULAR,
            pltpu.SemaphoreType.DMA((2, 2, GROUP)),
            pltpu.SemaphoreType.DMA((GROUP,)),
            pltpu.SemaphoreType.DMA((12,)),
            pltpu.SemaphoreType.DMA,
        ],
        compiler_params=pltpu.CompilerParams(
            collective_id=number, has_side_effects=True, vmem_limit_bytes=63 << 20
        ),
        name="run_experts",
    )(block, grads, gate_all, up, down)


def rotary_constants():
    position = np.arange(SEQ_LEN, dtype=np.float32)
    power = -(np.arange(32, dtype=np.float32) * np.float32(2.0)) / np.float32(64.0)
    frequency = np.float32(10000.0) ** power
    angles = position[:, None] * frequency[None, :]
    cosine, sine = np.cos(angles), np.sin(angles)
    return (np.tile(cosine, (1, 4)), np.concatenate([-sine, sine, -sine, sine], axis=1))


def shards(
    inputs,
    first_gain,
    query_weight,
    key_weight,
    value_weight,
    query_gain,
    key_gain,
    output_weight,
    second_gain,
    router_weight,
    gate_weight,
    up_weight,
    down_weight,
    segments,
    live_mask,
    routes,
    cotangent,
):
    gain_one, gain_two = first_gain.reshape(8, 128), second_gain.reshape(8, 128)
    query_scale, key_scale = query_gain.reshape(1, -1), key_gain.reshape(1, -1)
    cosine, sine = rotary_constants()
    seg_row, live_row = segments.reshape(1, -1), live_mask.reshape(1, -1)
    router = router_weight.T
    (
        normed, raw, query, keys, values, mixed, residual, block, gates, grad_all, gate_all,
    ) = opening(
        (
            inputs, gain_one, query_weight, key_weight, value_weight, query_scale, key_scale,
            cosine, sine, seg_row, live_row, output_weight, gain_two, router, routes.T,
            cotangent, gate_weight[0],
        ),
        1,
    )
    rows_all, out_parts, back, weight_parts = run_experts(
        block, grad_all, gate_all, up_weight[0], down_weight[0], 2
    )
    grad_inputs, dense, small, combined, weight_sums = closing(
        (
            back, residual, gates, cotangent, gain_two, router, query, keys, values, mixed,
            output_weight, query_weight, key_weight, value_weight, raw, normed.reshape(1024, 1024),
            inputs, gain_one, query_scale, key_scale, cosine, sine, seg_row,
            live_row, out_parts, weight_parts,
        ),
        4,
    )
    (
        result, grad_inputs, grad_query, grad_key, grad_value, grad_output, grad_gate, grad_up,
        grad_down, grad_gain_one, grad_gain_two, grad_query_gain, grad_key_gain, grad_router,
    ) = finish_all(
        (
            dense.reshape(1024, 768), weight_sums, residual, combined,
            small.reshape(32, SMALL_ROWS, 128), grad_inputs,
        )
    )
    return (
        result,
        grad_inputs,
        grad_gain_one.reshape(-1),
        grad_query,
        grad_key,
        grad_value,
        grad_query_gain.reshape(-1),
        grad_key_gain.reshape(-1),
        grad_output,
        grad_gain_two.reshape(-1),
        grad_router.T,
        grad_gate,
        grad_up,
        grad_down,
    )


def solution(mesh):
    return jax.shard_map(
        shards,
        mesh=mesh,
        in_specs=(
            P(("ep", "tp"), None),
            P(),
            P(None, "tp"),
            P(None, "tp"),
            P(None, "tp"),
            P(),
            P(),
            P("tp", None),
            P(),
            P(),
            P("ep", None, "tp"),
            P("ep", None, "tp"),
            P("ep", "tp", None),
            P("ep"),
            P("ep"),
            P(("ep", "tp"), None),
            P(("ep", "tp"), None),
        ),
        out_specs=(
            P(("ep", "tp"), None),
            P(("ep", "tp"), None),
            P(),
            P(None, "tp"),
            P(None, "tp"),
            P(None, "tp"),
            P(),
            P(),
            P("tp", None),
            P(),
            P(),
            P("ep", None, "tp"),
            P("ep", None, "tp"),
            P("ep", "tp", None),
        ),
        check_vma=False,
    )
```

```python
import jax
import jax.numpy as jnp
import numpy as np
from jax import lax
from jax.experimental import pallas as pl
from jax.experimental.pallas import tpu as pltpu
from jax.sharding import PartitionSpec as P

SEQ_LEN = 1024
HIGHEST_PRECISION = lax.Precision.HIGHEST
CONTRACT_ROWS = (((0,), (0,)), ((), ()))
CONTRACT_LAST = (((1,), (1,)), ((), ()))
MESH = pl.DeviceIdType.MESH
ANY = pl.BlockSpec(memory_space=pl.ANY)
VMEM = pl.BlockSpec(memory_space=pltpu.VMEM)
F32 = jnp.float32
BF16 = jnp.bfloat16
SLOTS = 96
EXTRA = 16


def wrap(value):
    return lax.rem(value + 4, 4)


def pick(core, first, second):
    return first * (1 - core) + second * core


def plane_place():
    ep = lax.axis_index("ep")
    core = lax.rem(ep, 2)
    z = lax.rem(lax.div(ep, 2), 4)
    x = lax.div(ep, 8)
    return (pick(core, x, z), pick(core, z, x), core)


def plane_index(a, b, core):
    a, b = wrap(a), wrap(b)
    return (pick(core, a, b) * 4 + pick(core, b, a)) * 2 + core


def plane_partners():
    a, b, core = plane_place()
    tp = lax.axis_index("tp")
    return (
        (plane_index(a + 1, b, core), tp),
        (plane_index(a - 1, b, core), tp),
        (plane_index(a, b + 1, core), tp),
        (plane_index(a, b - 1, core), tp),
        (plane_index(b, a, 1 - core), tp),
    )


def line_partners():
    ep, tp = lax.axis_index("ep"), lax.axis_index("tp")
    return ((ep, wrap(tp + 1)), (ep, wrap(tp - 1)))


def greet(partners):
    barrier = pltpu.get_barrier_semaphore()
    for partner in partners:
        pl.semaphore_signal(barrier, inc=1, device_id=partner, device_id_type=MESH)
    pl.semaphore_wait(barrier, len(partners))


def halves(ref):
    unit = 16 if ref.dtype == BF16 else 8
    rows = ref.shape[-2]
    top = (rows // 2 + unit - 1) // unit * unit
    return (pl.ds(0, top), pl.ds(top, rows - top))


def together(*tasks):
    waiting = [(0.0, number, task) for number, task in enumerate(tasks)]
    while waiting:
        waiting.sort(key=lambda entry: entry[:2])
        _, number, task = waiting.pop(0)
        due = next(task, None)
        if due is not None:
            waiting.append((due, number, task))


def resumed(due, task):
    yield due
    yield from task


def side_by_side(*tasks):
    waiting = [(due, number, task) for number, (due, task) in enumerate(tasks)]
    while waiting:
        waiting.sort(key=lambda entry: entry[:2])
        due, number, task = waiting.pop(0)
        yield due
        due = next(task, None)
        if due is not None:
            waiting.append((due, number, task))


class Clock:
    def __init__(self, now=0.0):
        self.now = now

    def spend(self, amount):
        self.now += amount
        return self.now

    def until(self, moment):
        self.now = max(self.now, moment)
        return self.now


def at(ref, *where):
    return lambda: ref.at[where]


def part_of(place):
    return place() if callable(place) else place


class Remote:
    def __init__(self, src, dst, send_sem, recv_sem, partner):
        self.all = (src, dst, send_sem, recv_sem, partner)

    def copy(self):
        src, dst, send_sem, recv_sem, partner = self.all
        return pltpu.make_async_remote_copy(
            src_ref=part_of(src),
            dst_ref=part_of(dst),
            send_sem=part_of(send_sem),
            recv_sem=part_of(recv_sem),
            device_id=partner,
            device_id_type=MESH,
        )

    def start(self):
        self.copy().start()

    def wait_send(self):
        self.copy().wait_send()

    def wait_recv(self):
        self.copy().wait_recv()


class Local:
    def __init__(self, src, dst, sem):
        self.all = (src, dst, sem)

    def start(self):
        pltpu.make_async_copy(*map(part_of, self.all)).start()

    def wait(self):
        pltpu.make_async_copy(*map(part_of, self.all)).wait()


class Post:
    def __init__(self, send_sems, recv_sems):
        self.send_sems, self.recv_sems, self.started = send_sems, recv_sems, []

    def go(self, src, dst, partner):
        copy = self.prepare(src, dst, partner)
        copy.start()
        return copy

    def prepare(self, src, dst, partner):
        number = len(self.started)
        copy = Remote(src, dst, at(self.send_sems, number), at(self.recv_sems, number), partner)
        self.started.append(copy)
        return copy

    def finish(self):
        for copy in self.started:
            copy.wait_send()


ARRIVAL = (
    (0, 0), (-1, 0), (1, 0), (0, -1), (0, 1), (2, 0), (-1, -1), (-1, 1),
    (1, -1), (1, 1), (2, -1), (2, 1), (0, 2), (-1, 2), (1, 2), (2, 2),
)


def plane_gather_events(post, own_ref, all_ref):
    a, b, core = plane_place()
    ahead_a, behind_a, ahead_b, behind_b, sibling = plane_partners()
    index = {place: plane_index(a + place[0], b + place[1], core) for place in ARRIVAL}
    top, bottom = halves(own_ref)

    def block(place):
        return own_ref if place == (0, 0) else at(all_ref, index[place])

    def copy(place, partner):
        return post.prepare(block(place), at(all_ref, index[place]), partner)

    def half_copy(place, half, partner):
        part = at(all_ref, index[place], half)
        return post.prepare(part, part, partner)

    a_copies = (copy((0, 0), ahead_a), copy((0, 0), behind_a))
    a_halves = (half_copy((-1, 0), top, ahead_a), half_copy((1, 0), bottom, behind_a))
    column = (0, -1, 1, 2)
    b_copies = [(copy((k, 0), ahead_b), copy((k, 0), behind_b)) for k in column]
    b_halves = [
        (half_copy((k, -1), top, ahead_b), half_copy((k, 1), bottom, behind_b)) for k in column
    ]
    crossing = [copy(place, sibling) for place in ARRIVAL]

    def start(*copies):
        for one in copies:
            one.start()

    def begin():
        start(*a_copies, *b_copies[0], crossing[0])

    def near_a(number):
        a_copies[number].wait_recv()
        start(a_halves[number], *b_copies[1 + number], crossing[1 + number])

    def far_a():
        a_halves[0].wait_recv()
        a_halves[1].wait_recv()
        start(*b_copies[3], crossing[5])

    def near_b(k):
        first = ARRIVAL.index((column[k], -1))
        for number in range(2):
            b_copies[k][number].wait_recv()
            start(b_halves[k][number], crossing[first + number])

    def far_b(k):
        b_halves[k][0].wait_recv()
        b_halves[k][1].wait_recv()
        start(crossing[12 + k])

    events = [
        (0.0, begin),
        (6.5, lambda: near_a(0)),
        (6.5, lambda: near_a(1)),
        (7.5, lambda: near_b(0)),
        (11.0, far_a),
        (15.0, lambda: near_b(1)),
        (21.0, lambda: near_b(2)),
        (24.0, lambda: far_b(0)),
        (28.0, lambda: near_b(3)),
        (32.0, lambda: far_b(1)),
        (40.0, lambda: far_b(2)),
        (44.0, lambda: far_b(3)),
    ]
    return (events, crossing)


def plane_gather_steps(post, own_ref, all_ref):
    events, crossing = plane_gather_events(post, own_ref, all_ref)
    for due, event in events:
        if due > 0.0:
            yield due
        event()
    yield 46.0
    for copy in crossing:
        copy.wait_recv()


PLANE_COPIES = 36


def add_rows(dst, sources, start, rows):
    step = 16 if rows % 16 == 0 else 8

    @pl.loop(0, rows // step)
    def _(i):
        at = pl.multiple_of(i * step, step)
        total = None
        for ref, first in sources:
            part = ref[pl.ds(first + at, step), :].astype(F32)
            total = part if total is None else total + part
        dst[pl.ds(start + at, step), :] = total.astype(dst.dtype)


def plane_scatter_steps(post, parts_ref, sum_ref, scratch, begin=0.0):
    mine, other, b_far, b_near, a_far, a_near, local_sems = scratch
    a, b, core = plane_place()
    ahead_a, behind_a, ahead_b, behind_b, sibling = plane_partners()
    rows = a_far.shape[0]
    top, bottom = halves(a_far)
    high = top.size
    low = rows - high
    offsets = (2, 1, -1, 0)
    go = post.go
    crossing = {}
    order = [(k, 0) for k in range(4)] + [(k, j) for k in range(4) for j in (1, 2)]
    order += [(k, 3) for k in range(4)]
    for k, j in order:
        there = plane_index(b + offsets[k], a + offsets[j], 1 - core)
        crossing[k, j] = go(parts_ref.at[there], other.at[k, j], sibling)
    slots = mine.shape[0]
    loads = []

    def load():
        number = len(loads)
        if number < len(order):
            k, j = order[number]
            here = plane_index(a + offsets[k], b + offsets[j], core)
            slot = number % slots
            copy = pltpu.make_async_copy(
                parts_ref.at[here], mine.at[slot], local_sems.at[slot]
            )
            copy.start()
            loads.append(copy)

    for _ in range(slots - 1):
        load()

    def ready(k, j):
        number = order.index((k, j))
        load()
        crossing[k, j].wait_recv()
        loads[number].wait()
        return (other.at[k, j], mine.at[number % slots])

    far_b, near_b = {}, {}
    for k in range(4):
        yield begin + 2.0 + 1.5 * k
        block, extra = ready(k, 0)
        add_rows(block, [(block, 0), (extra, 0)], 0, rows)
        far_b[k] = (
            go(block.at[top], b_far.at[k, top], ahead_b),
            go(block.at[bottom], b_far.at[k, bottom], behind_b),
        )
    for k in range(4):
        far = b_far.at[k]
        yield begin + 9.0 + 3.0 * k
        block, extra = ready(k, 1)
        far_b[k][0].wait_recv()
        add_rows(block, [(block, 0), (extra, 0), (far, 0)], 0, high)
        add_rows(block, [(block, high), (extra, high)], high, low)
        first = go(block, b_near.at[0, k], ahead_b)
        block, extra = ready(k, 2)
        far_b[k][1].wait_recv()
        add_rows(block, [(block, 0), (extra, 0)], 0, high)
        add_rows(block, [(block, high), (extra, high), (far, high)], high, low)
        near_b[k] = (first, go(block, b_near.at[1, k], behind_b))
    far_a, near_a = [], []
    for k in range(4):
        yield begin + (25.0, 31.0, 37.0, 45.0)[k]
        block, extra = ready(k, 3)
        near_b[k][0].wait_recv()
        near_b[k][1].wait_recv()
        base = [block, extra, b_near.at[0, k], b_near.at[1, k]]
        upper = [(ref, 0) for ref in base]
        lower = [(ref, high) for ref in base]
        if k == 0:
            add_rows(block, upper, 0, high)
            add_rows(block, lower, high, low)
            far_a = [
                go(block.at[top], a_far.at[top], ahead_a),
                go(block.at[bottom], a_far.at[bottom], behind_a),
            ]
        elif k == 1:
            far_a[0].wait_recv()
            add_rows(block, upper + [(a_far, 0)], 0, high)
            add_rows(block, lower, high, low)
            near_a.append(go(block, a_near.at[0], ahead_a))
        elif k == 2:
            far_a[1].wait_recv()
            add_rows(block, upper, 0, high)
            add_rows(block, lower + [(a_far, high)], high, low)
            near_a.append(go(block, a_near.at[1], behind_a))
        else:
            near_a[0].wait_recv()
            near_a[1].wait_recv()
            add_rows(sum_ref, upper + [(a_near.at[0], 0), (a_near.at[1], 0)], 0, rows)


def plane_scatter_scratch(rows, columns, kind):
    return [
        pltpu.VMEM((4, rows, columns), kind),
        pltpu.VMEM((4, 4, rows, columns), kind),
        pltpu.VMEM((4, rows, columns), kind),
        pltpu.VMEM((2, 4, rows, columns), kind),
        pltpu.VMEM((rows, columns), kind),
        pltpu.VMEM((2, rows, columns), kind),
        pltpu.SemaphoreType.DMA((4,)),
    ]


OFFSETS = (2, 1, -1, 0)


def ring_places(a, b, core, tp):
    along_a = [(plane_index(a + offset, b, core), tp) for offset in OFFSETS[:3]]
    along_b = [(plane_index(a, b + offset, core), tp) for offset in OFFSETS[:3]]
    return (along_a, along_b, (plane_index(b, a, 1 - core), tp))


def brief_partners():
    along_a, along_b, sibling = ring_places(*plane_place(), lax.axis_index("tp"))
    return tuple(along_a + along_b + [sibling])


BRIEF_COPIES = 1 + 3 + 3


def brief_number(number):
    return (number // 16, number // 4 % 4, number % 4)


def brief_scatter_steps(post, parts_ref, sum_ref, scratch, begin=0.0):
    other, from_b, total, from_a = scratch
    a, b, core = plane_place()
    along_a, along_b, sibling = ring_places(a, b, core, lax.axis_index("tp"))
    crossing = post.go(at(parts_ref, 1 - core), other, sibling)
    yield begin + 3.0
    crossing.wait_recv()
    for i in range(4):
        other[i] = (other[i].astype(F32) + parts_ref[core, i].astype(F32)).astype(other.dtype)
    copies = [
        post.go(at(other, slice(None), wrap(b + OFFSETS[j])), at(from_b, j), along_b[j])
        for j in range(3)
    ]
    yield begin + 8.0
    for copy in copies:
        copy.wait_recv()
    for i in range(4):
        part = other[i, b].astype(F32)
        for j in range(3):
            part = part + from_b[j, i].astype(F32)
        total[i] = part.astype(total.dtype)
    copies = [
        post.go(at(total, wrap(a + OFFSETS[j])), at(from_a, j), along_a[j]) for j in range(3)
    ]
    yield begin + 11.0
    part = total[a].astype(F32)
    for j in range(3):
        copies[j].wait_recv()
        part = part + from_a[j].astype(F32)
    sum_ref[...] = part.astype(sum_ref.dtype)


def brief_scatter_scratch(rows, columns, kind):
    return [
        pltpu.VMEM((4, 4, rows, columns), kind),
        pltpu.VMEM((3, 4, rows, columns), kind),
        pltpu.VMEM((4, rows, columns), kind),
        pltpu.VMEM((3, rows, columns), kind),
    ]


def brief_gather_steps(post, own_ref, all_ref, begin=0.0):
    a, b, core = plane_place()
    along_a, along_b, sibling = ring_places(a, b, core, lax.axis_index("tp"))
    all_ref[core, a, b] = own_ref[...]
    copies = [post.go(own_ref, at(all_ref, core, a, b), place) for place in along_a]
    yield begin + 3.0
    for copy in copies:
        copy.wait_recv()
    line = at(all_ref, core, slice(None), b)
    copies = [post.go(line, line, place) for place in along_b]
    yield begin + 8.0
    for copy in copies:
        copy.wait_recv()
    crossing = post.go(at(all_ref, core), at(all_ref, core), sibling)
    yield begin + 11.0
    crossing.wait_recv()


LINE_COPIES = 4


def line_gather_steps(post, own_ref, all_ref, clock, near_time, far_time, arrived=None):
    tp = lax.axis_index("tp")
    ahead, behind = line_partners()
    top, bottom = halves(own_ref)
    before, after, far = wrap(tp - 1), wrap(tp + 1), wrap(tp + 2)
    begin = clock.now
    first = post.go(own_ref, all_ref.at[tp], ahead)
    second = post.go(own_ref, all_ref.at[tp], behind)
    if arrived is not None:
        yield from arrived(tp)
    yield clock.until(begin + near_time)
    first.wait_recv()
    third = post.go(all_ref.at[before, top], all_ref.at[before, top], ahead)
    second.wait_recv()
    fourth = post.go(all_ref.at[after, bottom], all_ref.at[after, bottom], behind)
    if arrived is not None:
        yield from arrived(before)
        yield from arrived(after)
    yield clock.until(begin + far_time)
    third.wait_recv()
    fourth.wait_recv()
    if arrived is not None:
        yield from arrived(far)


def line_scatter_steps(post, make, far, near, finish, clock, far_time, near_time):
    ahead, behind = line_partners()
    top, bottom = halves(far)
    high = top.size
    rows = far.shape[0]
    block = yield from make(2)
    begin = clock.now
    first = post.go(block.at[top], far.at[top], ahead)
    second = post.go(block.at[bottom], far.at[bottom], behind)
    block = yield from make(1)
    yield clock.until(begin + far_time)
    first.wait_recv()
    add_rows(block, [(block, 0), (far, 0)], 0, high)
    third = post.go(block, near.at[0], ahead)
    other = yield from make(-1)
    second.wait_recv()
    add_rows(other, [(other, high), (far, high)], high, rows - high)
    fourth = post.go(other, near.at[1], behind)
    begin = clock.now
    own = yield from make(0)
    yield clock.until(begin + near_time)
    third.wait_recv()
    fourth.wait_recv()
    finish(own, near.at[0], near.at[1])


def split_float(values):
    high = values.astype(BF16)
    return (high, (values - high.astype(F32)).astype(BF16))


def split_three(values):
    high = values.astype(BF16)
    rest = values - high.astype(F32)
    middle = rest.astype(BF16)
    return (high, middle, (rest - middle.astype(F32)).astype(BF16))


def head_mean(values):
    same = (
        lax.broadcasted_iota(jnp.int32, (128, 128), 0) // 64
        == lax.broadcasted_iota(jnp.int32, (128, 128), 1) // 64
    ).astype(BF16)
    high, low = split_float(values)
    total = jnp.dot(high, same, preferred_element_type=F32)
    total = total + jnp.dot(low, same, preferred_element_type=F32)
    return total * (1.0 / 64.0)


def other_half(values):
    lane = lax.broadcasted_iota(jnp.int32, values.shape, 1)
    return jnp.where(
        lax.rem(lane, 64) < 32, pltpu.roll(values, 96, 1), pltpu.roll(values, 32, 1)
    )


def head_ready(raw, gain, cosine, sine):
    normed = raw * lax.rsqrt(head_mean(raw * raw) + 1e-06) * gain
    return normed * cosine + other_half(normed) * sine


def head_back(grad, raw, gain, cosine, sine):
    grad = grad * cosine + other_half(grad * sine)
    scale = lax.rsqrt(head_mean(raw * raw) + 1e-06)
    plain = raw * scale
    grad_gain = jnp.sum(grad * plain, axis=0, keepdims=True)
    grad = grad * gain
    return (scale * (grad - plain * head_mean(grad * plain)), grad_gain)


def wide(gain):
    gain = gain.astype(F32)
    return jnp.concatenate([gain[part : part + 1] for part in range(8)], axis=1)


def both_heads(gain):
    gain = gain.astype(F32)
    return jnp.concatenate([gain, gain], axis=1)


def row_scale(values):
    return lax.rsqrt(jnp.mean(values * values, axis=1, keepdims=True) + 1e-05)


def exchange(values):
    return jnp.concatenate([values[:, 64:], values[:, :64]], axis=1)


def head_pairs(block):
    rows = block.shape[0]
    low = lax.broadcasted_iota(jnp.int32, (rows, 128), 1) < 64
    left, right = block[:, :128], block[:, 128:]
    zero = jnp.zeros_like(left)
    straight = jnp.concatenate([jnp.where(low, left, zero), jnp.where(low, zero, right)], axis=0)
    crossed = jnp.concatenate([jnp.where(low, zero, left), jnp.where(low, right, zero)], axis=0)
    return (straight, crossed)


def heads_back(straight, crossed):
    rows = straight.shape[0] // 2
    low = lax.broadcasted_iota(jnp.int32, (rows, 128), 1) < 64
    left = jnp.where(low, straight[:rows], crossed[:rows])
    right = jnp.where(low, crossed[rows:], straight[rows:])
    return jnp.concatenate([left, right], axis=1)


def attend_block(query, keys, values, bias, clock):
    rows = query.shape[0]
    outs = []
    for pair, key_part, value_part in zip(
        head_pairs(query), (keys, exchange(keys)), (values, exchange(values)), strict=True
    ):
        halves_out = []
        for number in range(2):
            part = pair[number * rows : (number + 1) * rows]
            scores = lax.dot_general(part, key_part, CONTRACT_LAST, preferred_element_type=F32)
            weights = jnp.exp(scores * 0.125 + bias)
            total_weight = jnp.sum(weights, axis=1, keepdims=True)
            out = jnp.dot(weights.astype(BF16), value_part, preferred_element_type=F32)
            halves_out.append(out / total_weight)
            yield clock.spend(0.45)
        outs.append(jnp.concatenate(halves_out, axis=0))
    return heads_back(*outs).astype(BF16)


def document_bounds(segments, live_mask):
    one = jnp.ones_like(segments)
    zero = jnp.zeros_like(segments)

    def count(chosen):
        return jnp.sum(jnp.where(chosen, one, zero), axis=1, keepdims=True)

    return (count(segments < 1), count(segments < 2), count(live_mask == 1))


def score_bias(bounds, query, key):
    first, second, living = bounds

    def document(position):
        return (position >= first).astype(jnp.int32) + (position >= second).astype(jnp.int32)

    seen = jnp.where(key < living, 1, 0)
    same = document(query) == document(key)
    return jnp.where(same & ((seen == 1) | (query == key)), 0.0, -1e30).astype(F32)


def block_rows(block):
    return pl.ds(pl.multiple_of(block * 256, 256), 256)


def opening_kernel(
    inputs, gain_one, query_weight, key_weight, value_weight, query_gain, key_gain, cosine, sine,
    segments, live_mask, output_weight, gain_two, router, routes, cotangent,
    gate,
    normed_out, raw_out, query_out, keys_out, values_out, mixed_out,
    residual, block, gates, grad_all, gate_all,
    normed, raw, query, keys, values, mixed,
    parts, far, near, hold, send_sems, recv_sems, local_sems, out_sems,
):
    tp = lax.axis_index("tp")
    own_parts = (
        (cotangent, parts.at[0], grad_all.at[lax.axis_index("ep")]),
        (gate, hold, gate_all.at[tp]),
    )
    inward = [
        pltpu.make_async_copy(src, through, local_sems.at[number])
        for number, (src, through, _) in enumerate(own_parts)
    ]
    outward = [
        pltpu.make_async_copy(through, dst, local_sems.at[number])
        for number, (_, through, dst) in enumerate(own_parts)
    ]
    for copy in inward:
        copy.start()
    greet(plane_partners() + line_partners())
    post = Post(send_sems, recv_sems)
    clock = Clock()
    bounds = document_bounds(segments[...], live_mask[...])

    def project(place):
        rows = block_rows(place)
        part = normed[place]
        cos, sin = cosine[rows, :], sine[rows, :]
        both = jnp.dot(part, query_weight[...], preferred_element_type=F32)
        raw[rows, :256] = both
        for lanes in (slice(0, 128), slice(128, 256)):
            query[rows, lanes] = head_ready(both[:, lanes], both_heads(query_gain[...]), cos, sin).astype(BF16)
        one = jnp.dot(part, key_weight[...], preferred_element_type=F32)
        raw[rows, 256:] = one
        keys[rows, :] = head_ready(one, both_heads(key_gain[...]), cos, sin).astype(BF16)
        values[rows, :] = jnp.dot(part, value_weight[...], preferred_element_type=F32).astype(BF16)
        yield clock.spend(1.5)

    def make(offset):
        place = wrap(tp + offset)
        rows = block_rows(place)
        bias = score_bias(
            bounds,
            place * 256 + lax.broadcasted_iota(jnp.int32, (256, 1), 0),
            lax.broadcasted_iota(jnp.int32, (1, 1024), 1),
        )
        out = yield from attend_block(query[rows, :], keys[...], values[...], bias, clock)
        mixed[rows, :] = out
        part = parts.at[(2, 1, -1, 0).index(offset)]
        part[...] = jnp.dot(out, output_weight[...], preferred_element_type=F32).astype(BF16)
        yield clock.spend(0.4)
        return part

    results = [
        pltpu.make_async_copy(src, dst, out_sems.at[number])
        for number, (src, dst) in enumerate(
            (
                (normed, normed_out), (raw, raw_out), (query, query_out), (keys, keys_out),
                (values, values_out), (mixed, mixed_out),
            )
        )
    ]

    def finish(own, first, second):
        results[5].start()
        total = own[...].astype(F32) + first[...].astype(F32) + second[...].astype(F32)
        total = inputs[...].astype(F32) + total
        residual[...] = total
        normed_two = total * row_scale(total) * wide(gain_two[...])
        block[:256, :] = normed_two.astype(BF16)
        logits = jnp.zeros((32, 256), F32)
        for piece in split_three(normed_two):
            logits = logits + lax.dot_general(
                router[...], piece, CONTRACT_LAST, preferred_element_type=F32
            )
        expert = lax.broadcasted_iota(jnp.int32, (32, 256), 0)
        named = expert < 0
        for choice in range(8):
            named = named | (routes[choice : choice + 1, :] == expert)
        top_logit = jnp.max(jnp.where(named, logits, -1e30), axis=0, keepdims=True)
        raised = jnp.where(named, jnp.exp(jnp.where(named, logits - top_logit, 0.0)), 0.0)
        probs = raised / jnp.sum(raised, axis=0, keepdims=True)
        gates[...] = probs
        high, low = split_float(probs)
        block[256:, :] = jnp.concatenate([high[:16], low[:16], high[16:], low[16:]], axis=1)

    def attention_steps():
        hidden = inputs[...].astype(F32)
        normed[tp] = (hidden * row_scale(hidden) * wide(gain_one[...])).astype(BF16)
        for copy, onward in zip(inward, outward, strict=True):
            copy.wait()
            onward.start()
        clock.spend(1.0)
        yield from line_gather_steps(post, normed.at[tp], normed, clock, 11.5, 17.5, project)
        for copy in outward:
            copy.wait()
        for copy in results[:5]:
            copy.start()
        yield from line_scatter_steps(post, make, far, near, finish, clock, 5.0, 22.0)

    def weight_steps(own, everyone, begin, near_time, far_time):
        yield begin
        yield from line_gather_steps(post, own, everyone, Clock(begin), near_time, far_time)

    together(
        attention_steps(),
        plane_gather_steps(post, cotangent, grad_all),
        weight_steps(gate, gate_all, 20.5, 22.0, 32.0),
    )
    post.finish()
    for copy in results:
        copy.wait()


def opening(arguments, number):
    count = 3 * LINE_COPIES + PLANE_COPIES
    return pl.pallas_call(
        opening_kernel,
        out_shape=[
            jax.ShapeDtypeStruct((4, 256, 1024), BF16),
            jax.ShapeDtypeStruct((1024, 384), F32),
            jax.ShapeDtypeStruct((1024, 256), BF16),
            jax.ShapeDtypeStruct((1024, 128), BF16),
            jax.ShapeDtypeStruct((1024, 128), BF16),
            jax.ShapeDtypeStruct((1024, 256), BF16),
            jax.ShapeDtypeStruct((256, 1024), F32),
            jax.ShapeDtypeStruct((256 + EXTRA, 1024), BF16),
            jax.ShapeDtypeStruct((32, 256), F32),
            jax.ShapeDtypeStruct((32, 256, 1024), BF16),
            jax.ShapeDtypeStruct((4, 1024, 128), BF16),
        ],
        in_specs=[VMEM] * (len(arguments) - 2) + [ANY] * 2,
        out_specs=[ANY] * 6 + [VMEM] * 3 + [ANY] * 2,
        scratch_shapes=[
            pltpu.VMEM((4, 256, 1024), BF16),
            pltpu.VMEM((1024, 384), F32),
            pltpu.VMEM((1024, 256), BF16),
            pltpu.VMEM((1024, 128), BF16),
            pltpu.VMEM((1024, 128), BF16),
            pltpu.VMEM((1024, 256), BF16),
            pltpu.VMEM((4, 256, 1024), BF16),
            pltpu.VMEM((256, 1024), BF16),
            pltpu.VMEM((2, 256, 1024), BF16),
            pltpu.VMEM((1024, 128), BF16),
            pltpu.SemaphoreType.DMA((count,)),
            pltpu.SemaphoreType.DMA((count,)),
            pltpu.SemaphoreType.DMA((2,)),
            pltpu.SemaphoreType.DMA((6,)),
        ],
        compiler_params=pltpu.CompilerParams(
            collective_id=number, has_side_effects=True, vmem_limit_bytes=56 << 20
        ),
        name="opening",
    )(*arguments)


def attend_back_block(query, grad, keys, values, bias, keys_sum, values_sum, clock):
    query_pairs = head_pairs(query)
    grad_pairs = head_pairs(grad)
    key_parts = (keys, exchange(keys))
    value_parts = (values, exchange(values))
    outs = []
    bias = jnp.concatenate([bias, bias], axis=1)
    for side in range(2):
        part, grad_part = query_pairs[side], grad_pairs[side]
        scores = lax.dot_general(key_parts[side], part, CONTRACT_LAST, preferred_element_type=F32)
        raised = jnp.exp(scores * 0.125 + bias)
        weights = raised * (1.0 / jnp.sum(raised, axis=0, keepdims=True))
        grad_weights = lax.dot_general(
            value_parts[side], grad_part, CONTRACT_LAST, preferred_element_type=F32
        )
        inner = jnp.sum(weights * grad_weights, axis=0, keepdims=True)
        grad_scores = (weights * (grad_weights - inner)).astype(BF16)
        outs.append(
            lax.dot_general(
                grad_scores, key_parts[side], CONTRACT_ROWS, preferred_element_type=F32
            )
        )
        keys_sum[side] += jnp.dot(grad_scores, part, preferred_element_type=F32)
        values_sum[side] += jnp.dot(weights.astype(BF16), grad_part, preferred_element_type=F32)
        yield clock.spend(2.3)
    return heads_back(*outs) * 0.125


SMALL_ROWS = 16
WEIGHTS_AT = 20.0


def closing_kernel(
    back, residual, gates, cotangent, gain_two, router, query_far, keys_far, values_far, mixed_far,
    output_weight, query_weight_far, key_weight_far, value_weight_far, raw_far, normed_far,
    inputs_far, gain_one, query_gain, key_gain, cosine, sine, segments, live_mask, out_parts,
    weight_parts, grad_inputs, dense_all, small_all, combined, weight_sum,
    grad_all, grad_residual, low, keys_sum, values_sum, output_sum, parts, far, near,
    dense, dense_own, small, small_own, small_early, small_late, small_total, query_gain_sum,
    weights, weights_far, weights_near, query, keys, values, mixed, query_weight, key_weight, value_weight, raw, normed, inputs,
    late_sems, *rest,
):
    out_scratch, dense_scratch, small_scratch = rest[:7], rest[7:11], rest[11:15]
    post = Post(rest[15], rest[16])
    me = lax.axis_index("ep")
    tp = lax.axis_index("tp")
    ahead, behind = line_partners()
    across = (me, wrap(tp + 2))
    late = [
        pltpu.make_async_copy(src, dst, late_sems.at[number])
        for number, (src, dst) in enumerate(
            (
                (query_far, query), (keys_far, keys), (values_far, values), (mixed_far, mixed),
                (query_weight_far, query_weight), (key_weight_far, key_weight),
                (value_weight_far, value_weight), (raw_far, raw), (normed_far, normed),
                (inputs_far, inputs),
                (weight_parts.at[wrap(tp + 1)], weights.at[0]),
                (weight_parts.at[wrap(tp - 1)], weights.at[1]),
                (weight_parts.at[tp], weights.at[2]),
            )
        )
    ]
    for copy in late:
        copy.start()
    greet(brief_partners() + (ahead, behind, across))
    clock = Clock()
    out_steps = plane_scatter_steps(post, out_parts, combined, out_scratch)
    out_due = next(out_steps)

    lines = back[256:, :]
    grad_gates = jnp.concatenate(
        [lines[:, :256] + lines[:, 256:512], lines[:, 512:768] + lines[:, 768:]], axis=0
    )
    probs = gates[...]
    grad_logits = probs * (grad_gates - jnp.sum(probs * grad_gates, axis=0, keepdims=True))
    grad_two = back[:256, :]
    logit_pieces = split_three(grad_logits)
    for piece in logit_pieces:
        grad_two = grad_two + lax.dot_general(
            piece, router[...], CONTRACT_ROWS, preferred_element_type=F32
        )
    total = residual[...]
    scale = row_scale(total)
    plain = total * scale
    grad_gain_two = jnp.sum(grad_two * plain, axis=0, keepdims=True)
    grad_two = grad_two * wide(gain_two[...])
    grad_total = cotangent[...].astype(F32) + scale * (
        grad_two - plain * jnp.mean(grad_two * plain, axis=1, keepdims=True)
    )
    grad_residual[...] = grad_total
    grad_all[tp] = grad_total.astype(BF16)
    clock.spend(4.0)

    bounds = document_bounds(segments[...], live_mask[...])
    keys_sum[...] = jnp.zeros_like(keys_sum)
    values_sum[...] = jnp.zeros_like(values_sum)
    output_sum[...] = jnp.zeros_like(output_sum)
    query_gain_sum[...] = jnp.zeros_like(query_gain_sum)

    def attention(place):
        rows = block_rows(place)
        grad = grad_all[place]
        output_sum[...] += lax.dot_general(
            mixed[rows, :], grad, CONTRACT_ROWS, preferred_element_type=F32
        )
        grad_mixed = lax.dot_general(
            grad, output_weight[...], CONTRACT_LAST, preferred_element_type=F32
        ).astype(BF16)
        bias = score_bias(
            bounds,
            place * 256 + lax.broadcasted_iota(jnp.int32, (1, 256), 1),
            lax.broadcasted_iota(jnp.int32, (1024, 1), 0),
        )
        clock.spend(0.8)
        grad_query = yield from attend_back_block(
            query[rows, :], grad_mixed, keys[...], values[...], bias, keys_sum, values_sum, clock
        )
        for lanes in (slice(0, 128), slice(128, 256)):
            grad_raw, grad_gain = head_back(
                grad_query[:, lanes],
                raw[rows, lanes],
                both_heads(query_gain[...]),
                cosine[rows, :],
                sine[rows, :],
            )
            low[rows, lanes] = grad_raw.astype(BF16)
            query_gain_sum[...] += grad_gain
        yield clock.spend(0.5)

    def make(offset):
        rows = block_rows(wrap(tp + offset))
        total = lax.dot_general(
            low[rows, :256], query_weight[...], CONTRACT_LAST, preferred_element_type=F32
        )
        total = total + lax.dot_general(
            low[rows, 256:384], key_weight[...], CONTRACT_LAST, preferred_element_type=F32
        )
        total = total + lax.dot_general(
            low[rows, 384:], value_weight[...], CONTRACT_LAST, preferred_element_type=F32
        )
        part = parts.at[(2, 1, -1, 0).index(offset)]
        part[...] = total.astype(BF16)
        yield clock.spend(0.8)
        return part

    def finish(own, first, second):
        grad_one = own[...].astype(F32) + first[...].astype(F32) + second[...].astype(F32)
        hidden = inputs[...].astype(F32)
        scale = row_scale(hidden)
        plain = hidden * scale
        grad_one = grad_one * wide(gain_one[...])
        grad_inputs[...] = (
            grad_residual[...]
            + scale * (grad_one - plain * jnp.mean(grad_one * plain, axis=1, keepdims=True))
        ).astype(BF16)

    def router_gradient():
        normed_pieces = split_three(plain * wide(gain_two[...]))
        total = jnp.zeros((32, 1024), F32)
        for first, second in ((0, 0), (0, 1), (1, 0), (1, 1), (0, 2), (2, 0)):
            total = total + jnp.dot(
                logit_pieces[first], normed_pieces[second], preferred_element_type=F32
            )
        return total

    gain_rows = small.at[brief_number(16)]
    head_rows = small.at[brief_number(17)]

    def fill_router():
        grad_router = router_gradient()
        small[...] = jnp.zeros_like(small)
        for part in range(8):
            lanes = slice(part * 128, (part + 1) * 128)
            small[brief_number(2 * part)] = grad_router[:16, lanes]
            small[brief_number(2 * part + 1)] = grad_router[16:, lanes]
            gain_rows[8 + part : 9 + part, :] = grad_gain_two[:, lanes]

    def fill_small(weights, grad_key_gain):
        grad_gain_one = jnp.zeros((8, 1024), F32)
        ones = jnp.ones((8, 128), BF16)
        parts = [query_weight[:, :128], query_weight[:, 128:], key_weight[...], value_weight[...]]
        for number, part in enumerate(parts):
            product = weights[:, number * 128 : (number + 1) * 128] * part.astype(F32)
            for piece in split_float(product):
                grad_gain_one = grad_gain_one + lax.dot_general(
                    ones, piece, CONTRACT_LAST, preferred_element_type=F32
                )
        grad_gain_one = grad_gain_one[:1] / wide(gain_one[...])
        for part in range(8):
            gain_rows[part : part + 1, :] = grad_gain_one[:, part * 128 : (part + 1) * 128]
        head_rows[0:1, :] = query_gain_sum[...]
        head_rows[1:2, :] = grad_key_gain

    def attention_steps():
        filled, early_line = [], []

        def send_line(part, slots):
            return [
                post.go(part, at(slots, number), partner)
                for number, partner in enumerate((ahead, behind, across))
            ]

        def arrived(place):
            if not filled:
                filled.append(place)
                fill_router()
                early_line.extend(send_line(at(small, 0), small_early))
                for copy in late:
                    copy.wait()
            yield from attention(place)

        yield from line_gather_steps(
            post, grad_all.at[tp], grad_all, clock, 11.5, 17.5, arrived
        )
        grad_raw, grad_key_gain = head_back(
            (keys_sum[0] + exchange(keys_sum[1])) * 0.125,
            raw[:, 256:],
            both_heads(key_gain[...]),
            cosine[...],
            sine[...],
        )
        low[:, 256:384] = grad_raw.astype(BF16)
        low[:, 384:] = (values_sum[0] + exchange(values_sum[1])).astype(BF16)
        weights = lax.dot_general(
            normed[...], low[...], CONTRACT_ROWS, preferred_element_type=F32
        )
        fill_small(weights, grad_key_gain)
        line = early_line + send_line(at(small, 1, 0, pl.ds(0, 2)), small_late)
        fill_dense(weights)
        now = clock.spend(8.0)
        yield from side_by_side(
            (now, dense_steps(now)),
            (now, small_steps(now, line)),
            (now, line_scatter_steps(post, make, far, near, finish, clock, 3.5, 11.5)),
        )

    def fill_dense(weights):
        weights = weights.astype(BF16)
        for part in range(32):
            dense[(*brief_number(part), slice(None), slice(0, 512))] = weights[
                part * 32 : (part + 1) * 32
            ]
        for part in range(4):
            block = output_sum[:, part * 256 : (part + 1) * 256].astype(BF16)
            for piece in range(8):
                dense[(*brief_number(part * 8 + piece), slice(None), slice(512, 768))] = block[
                    piece * 32 : (piece + 1) * 32
                ]

    def dense_steps(begin):
        yield from brief_scatter_steps(post, dense, dense_own, dense_scratch, begin)
        yield from brief_gather_steps(post, dense_own, dense_all, begin + 12.0)

    def small_steps(begin, line):
        for copy in line:
            copy.wait_recv()
        small_total[...] = jnp.zeros_like(small_total)
        for place in range(4):
            small_total[0, place] = small[0, place] + (
                small_early[0, place] + small_early[1, place] + small_early[2, place]
            )
        small_total[1, 0, :2] = small[1, 0, :2] + small_late[0] + small_late[1] + small_late[2]
        yield from brief_scatter_steps(post, small_total, small_own, small_scratch, begin)
        yield from brief_gather_steps(post, small_own, small_all, begin + 12.0)

    def make_weights(offset):
        yield 0.0
        if offset == 2:
            return weight_parts.at[wrap(tp + 2)]
        return weights.at[(1, -1, 0).index(offset)]

    def finish_weights(own, first, second):
        add_rows(weight_sum, [(own, 0), (first, 0), (second, 0)], 0, own.shape[0])

    def weight_steps():
        yield WEIGHTS_AT
        yield from line_scatter_steps(
            post, make_weights, weights_far, weights_near, finish_weights, Clock(WEIGHTS_AT), 14.0, 60.0
        )

    together(attention_steps(), resumed(out_due, out_steps), weight_steps())
    post.finish()


def closing(arguments, number):
    count = 3 * LINE_COPIES + PLANE_COPIES + 4 * BRIEF_COPIES + 6
    return pl.pallas_call(
        closing_kernel,
        out_shape=[
            jax.ShapeDtypeStruct((256, 1024), BF16),
            jax.ShapeDtypeStruct((2, 4, 4, 32, 768), BF16),
            jax.ShapeDtypeStruct((2, 4, 4, SMALL_ROWS, 128), F32),
            jax.ShapeDtypeStruct((256, 1024), F32),
            jax.ShapeDtypeStruct((3072, 128), F32),
        ],
        in_specs=[VMEM] * 6 + [ANY] * 4 + [VMEM] + [ANY] * 6 + [VMEM] * 7 + [ANY] * 2,
        out_specs=[VMEM] * 5,
        scratch_shapes=[
            pltpu.VMEM((4, 256, 1024), BF16),
            pltpu.VMEM((256, 1024), F32),
            pltpu.VMEM((1024, 512), BF16),
            pltpu.VMEM((2, 1024, 128), F32),
            pltpu.VMEM((2, 1024, 128), F32),
            pltpu.VMEM((256, 1024), F32),
            pltpu.VMEM((4, 256, 1024), BF16),
            pltpu.VMEM((256, 1024), BF16),
            pltpu.VMEM((2, 256, 1024), BF16),
            pltpu.VMEM((2, 4, 4, 32, 768), BF16),
            pltpu.VMEM((32, 768), BF16),
            pltpu.VMEM((2, 4, 4, SMALL_ROWS, 128), F32),
            pltpu.VMEM((SMALL_ROWS, 128), F32),
            pltpu.VMEM((3, 4, 4, SMALL_ROWS, 128), F32),
            pltpu.VMEM((3, 2, SMALL_ROWS, 128), F32),
            pltpu.VMEM((2, 4, 4, SMALL_ROWS, 128), F32),
            pltpu.VMEM((1, 128), F32),
            pltpu.VMEM((3, 3072, 128), BF16),
            pltpu.VMEM((3072, 128), BF16),
            pltpu.VMEM((2, 3072, 128), BF16),
            pltpu.VMEM((1024, 256), BF16),
            pltpu.VMEM((1024, 128), BF16),
            pltpu.VMEM((1024, 128), BF16),
            pltpu.VMEM((1024, 256), BF16),
            pltpu.VMEM((1024, 256), BF16),
            pltpu.VMEM((1024, 128), BF16),
            pltpu.VMEM((1024, 128), BF16),
            pltpu.VMEM((1024, 384), F32),
            pltpu.VMEM((1024, 1024), BF16),
            pltpu.VMEM((256, 1024), BF16),
            pltpu.SemaphoreType.DMA((13,)),
        ]
        + plane_scatter_scratch(256, 1024, BF16)
        + brief_scatter_scratch(32, 768, BF16)
        + brief_scatter_scratch(SMALL_ROWS, 128, F32)
        + [pltpu.SemaphoreType.DMA((count,)), pltpu.SemaphoreType.DMA((count,))],
        compiler_params=pltpu.CompilerParams(
            collective_id=number, has_side_effects=True, vmem_limit_bytes=63 << 20
        ),
        name="closing",
    )(*arguments)


def finish_kernel(
    dense_far, weights_far, residual_far, combined_far, small_far, inputs_far,
    result, grad_inputs, grad_query, grad_key, grad_value, grad_output, grad_gate, grad_up,
    grad_down, gain_one, gain_two, query_gain, key_gain, router,
    dense, weights, residual, combined, small, sems,
):
    copies = [
        pltpu.make_async_copy(src, dst, sems.at[number])
        for number, (src, dst) in enumerate(
            (
                (weights_far, weights), (dense_far, dense), (residual_far, residual),
                (combined_far, combined), (small_far, small), (inputs_far, grad_inputs),
            )
        )
    ]
    for copy in copies:
        copy.start()
    copies[0].wait()
    grad_gate[0] = weights[:1024, :]
    grad_up[0] = weights[1024:2048, :]
    grad_down[0] = weights[2048:, :].T
    copies[1].wait()
    grad_query[...] = dense[:, :256].astype(F32)
    grad_key[...] = dense[:, 256:384].astype(F32)
    grad_value[...] = dense[:, 384:512].astype(F32)
    for part in range(4):
        grad_output[:, part * 256 : (part + 1) * 256] = dense[
            part * 256 : (part + 1) * 256, 512:
        ].astype(F32)
    copies[2].wait()
    copies[3].wait()
    result[...] = (residual[...] + combined[...]).astype(BF16)
    copies[4].wait()
    for part in range(8):
        lanes = slice(part * 128, (part + 1) * 128)
        router[:16, lanes] = small[2 * part]
        router[16:, lanes] = small[2 * part + 1]
        gain_one[:, lanes] = small[16, part : part + 1, :]
        gain_two[:, lanes] = small[16, 8 + part : 9 + part, :]
    heads = small[17]
    heads = heads[:, :64] + heads[:, 64:]
    query_gain[...] = heads[0:1]
    key_gain[...] = heads[1:2]
    copies[5].wait()


def finish_all(arguments):
    return pl.pallas_call(
        finish_kernel,
        out_shape=[
            jax.ShapeDtypeStruct((256, 1024), BF16),
            jax.ShapeDtypeStruct((256, 1024), BF16),
            jax.ShapeDtypeStruct((1024, 256), F32),
            jax.ShapeDtypeStruct((1024, 128), F32),
            jax.ShapeDtypeStruct((1024, 128), F32),
            jax.ShapeDtypeStruct((256, 1024), F32),
            jax.ShapeDtypeStruct((1, 1024, 128), F32),
            jax.ShapeDtypeStruct((1, 1024, 128), F32),
            jax.ShapeDtypeStruct((1, 128, 1024), F32),
            jax.ShapeDtypeStruct((1, 1024), F32),
            jax.ShapeDtypeStruct((1, 1024), F32),
            jax.ShapeDtypeStruct((1, 64), F32),
            jax.ShapeDtypeStruct((1, 64), F32),
            jax.ShapeDtypeStruct((32, 1024), F32),
        ],
        in_specs=[ANY] * 6,
        out_specs=[VMEM] * 14,
        scratch_shapes=[
            pltpu.VMEM((1024, 768), BF16),
            pltpu.VMEM((3072, 128), F32),
            pltpu.VMEM((256, 1024), F32),
            pltpu.VMEM((256, 1024), F32),
            pltpu.VMEM((32, SMALL_ROWS, 128), F32),
            pltpu.SemaphoreType.DMA((6,)),
        ],
        compiler_params=pltpu.CompilerParams(vmem_limit_bytes=60 << 20),
        name="finish_all",
    )(*arguments)


STEPS = ((0, 1), (3, 4), (6, 7), (12, 13), (14, 15), (10, 11), (8, 9), (2, 5))
GROUP = 4


def experts_kernel(
    block, grads, gate_all, up, down,
    rows_all, out_parts, back_sum, weight_parts,
    rows_in, grads_in, both_full, down_full, both_sum, down_sum, rows_own, grads_own, gates_own,
    select, weighted, grad_rows, grad_gates, mine, other, stage, out_stage,
    b_far, b_near, a_far, a_near, line, send_sems, recv_sems, credit, load_sems, store_sems, weight_sems, own_sem,
):
    a, b, core = plane_place()
    me = lax.axis_index("ep")
    ahead_a, behind_a, ahead_b, behind_b, sibling = plane_partners()
    here = [plane_index(a + place[0], b + place[1], core) for place in ARRIVAL]
    there = [plane_index(b + place[0], a + place[1], 1 - core) for place in ARRIVAL]
    lane_row = lax.rem(me, 16)
    upper = me >= 16
    tp = lax.axis_index("tp")
    ahead, behind = line_partners()
    greet(plane_partners() + (ahead, behind))
    post = Post(send_sems, recv_sems)
    go = post.go
    events, held = plane_gather_events(post, block, rows_all)
    events[0][1]()
    own_copy = pltpu.make_async_copy(block, stage.at[0], own_sem)
    own_copy.start()
    before_me, after_me = wrap(tp - 1), wrap(tp + 1)

    def up_part(place, rows=slice(None)):
        return at(both_full, rows, pl.ds(pl.multiple_of(512 + place * 128, 128), 128))

    def down_part(place, first=0, count=128):
        return at(down_full, pl.ds(pl.multiple_of(place * 128 + first, 64), count))

    up_near = (
        post.go(up, up_part(tp), ahead), post.go(up, up_part(tp), behind)
    )
    down_near = (
        post.go(down, down_part(tp), ahead), post.go(down, down_part(tp), behind)
    )
    up_top, up_bottom = up_part(before_me, pl.ds(0, 512)), up_part(after_me, pl.ds(512, 512))
    up_far = (
        post.prepare(up_top, up_top, ahead), post.prepare(up_bottom, up_bottom, behind)
    )
    down_top, down_bottom = down_part(before_me, 0, 64), down_part(after_me, 64, 64)
    down_far = (
        post.prepare(down_top, down_top, ahead), post.prepare(down_bottom, down_bottom, behind)
    )

    def relay(near, far):
        for one, other_one in zip(near, far, strict=True):
            one.wait_recv()
            other_one.start()

    weight_loads = [
        pltpu.make_async_copy(
            gate_all.at[part], both_full.at[:, part * 128 : (part + 1) * 128], weight_sems.at[part]
        )
        for part in range(4)
    ]
    weight_loads.append(pltpu.make_async_copy(up, up_part(tp)(), weight_sems.at[4]))
    weight_loads.append(pltpu.make_async_copy(down, down_part(tp)(), weight_sems.at[5]))
    for copy in weight_loads:
        copy.start()
    both_sum[...] = jnp.zeros_like(both_sum)
    down_sum[...] = jnp.zeros_like(down_sum)

    def blocks(step):
        first, second = STEPS[step]
        return (here[first], here[second], there[first], there[second])

    loads, crossing, stores = {}, {}, {}
    for step in range(len(STEPS)):
        slot = step % 2
        loads[step], stores[step] = [], []
        crossing[step] = [
            post.prepare(at(stage, part), at(other, slot, part), sibling) for part in range(2)
        ]
        for part, index in enumerate(blocks(step)):
            loads[step] += [
                Local(
                    at(rows_all, index), at(rows_in, slot, part), at(load_sems, slot, 0, part)
                ),
                Local(at(grads, index), at(grads_in, slot, part), at(load_sems, slot, 1, part)),
            ]
            stores[step].append(
                Local(at(out_stage, part), at(out_parts, index), at(store_sems, part))
            )

    def load(step):
        for place in STEPS[step]:
            held[place].wait_recv()
        for copy in loads[step]:
            copy.start()

    def take(step):
        for part, place in enumerate(STEPS[step]):
            crossing[step][part].wait_recv()
            add_rows(
                mine.at[place], [(mine.at[place], 0), (other.at[step % 2, part], 0)], 0, rows
            )
        if step + 2 < len(STEPS):
            pl.semaphore_signal(credit, inc=1, device_id=sibling, device_id_type=MESH)

    rows = a_far.shape[0]
    top, bottom = halves(a_far)
    high = top.size
    low = rows - high
    far_b, near_b = {}, {}

    def number_of(k, j):
        return ARRIVAL.index((OFFSETS[k], OFFSETS[j]))

    def slot_of(k, j):
        return mine.at[number_of(k, j)]

    def far_step(k):
        part = number_of(k, 0)
        far_b[k] = (
            go(at(mine, part, top), at(b_far, k, top), ahead_b),
            go(at(mine, part, bottom), at(b_far, k, bottom), behind_b),
        )

    def near_step(k):
        far = b_far.at[k]
        far_b[k][0].wait_recv()
        part = slot_of(k, 1)
        add_rows(part, [(part, 0), (far, 0)], 0, high)
        first = go(at(mine, number_of(k, 1)), at(b_near, 0, k), ahead_b)
        far_b[k][1].wait_recv()
        part = slot_of(k, 2)
        add_rows(part, [(part, high), (far, high)], high, low)
        near_b[k] = (first, go(at(mine, number_of(k, 2)), at(b_near, 1, k), behind_b))

    def before(step):
        for copy in loads[step]:
            copy.wait()

    def between(step):
        if step > 0:
            for copy in crossing[step - 1]:
                copy.wait_send()
            for copy in stores[step - 1]:
                copy.wait()
        onward({0: (4,), 1: (6,), 2: (7, 8, 9), 3: (10, 11)}.get(step, ()))
        if step + 1 < len(STEPS):
            load(step + 1)
        if step > 0:
            take(step - 1)
        if step == 4:
            far_step(2)
            far_step(3)
        if step == 5:
            far_step(0)
            far_step(1)
            near_step(3)
            near_step(2)
        if step == 6:
            near_step(0)
        if step == 7:
            near_step(1)

    def onward(numbers):
        for number in numbers:
            events[number][1]()

    def early(step):
        if step == 0:
            for copy in up_far + down_far:
                copy.wait_recv()

    def after(step):
        onward({0: (5,)}.get(step, ()))
        if step >= 2:
            pl.semaphore_wait(credit, 1)
        for copy in crossing[step] + stores[step]:
            copy.start()

    def at_step(step, task):
        for number in range(len(STEPS)):

            @pl.when(step == number)
            def _(number=number):
                task(number)

    def from_table(step, table):
        value = step * 0 + table[0]
        for number in range(1, len(table)):
            value = jnp.where(step == number, table[number], value)
        return value

    own_copy.wait()
    own_copy = pltpu.make_async_copy(stage.at[0], rows_all.at[me], own_sem)
    own_copy.start()
    onward((1, 2))
    own_copy.wait()
    load(0)
    relay(up_near, up_far)
    onward((3,))
    relay(down_near, down_far)
    for copy in weight_loads:
        copy.wait()
    extra_row = lax.broadcasted_iota(jnp.int32, (EXTRA, 1024), 0) == lane_row

    def one_step(step, carry):
        slot = lax.rem(step, 2)
        at_step(step, before)
        earlier = (
            lax.broadcasted_iota(jnp.int32, (256, 256), 0)
            <= lax.broadcasted_iota(jnp.int32, (256, 256), 1)
        ).astype(BF16)
        place = lax.broadcasted_iota(jnp.int32, (SLOTS, 256), 0).astype(F32)
        for part in range(GROUP):
            extras = jnp.where(extra_row, rows_in[slot, part, 256:, :].astype(F32), 0.0)
            extras = jnp.sum(extras, axis=0, keepdims=True)
            gates = jnp.where(
                upper, extras[:, 512:768] + extras[:, 768:], extras[:, :256] + extras[:, 256:512]
            )
            named = jnp.broadcast_to(gates, (16, 256)) > 0.0
            rank = jnp.dot(named.astype(BF16), earlier, preferred_element_type=F32)[:1] - 1.0
            chosen = (place == rank) & (gates > 0.0)
            chosen_low = chosen.astype(BF16)
            at = slice(part * SLOTS, (part + 1) * SLOTS)
            select[at, :] = chosen_low
            rows_own[at, :] = jnp.dot(
                chosen_low, rows_in[slot, part, :256, :], preferred_element_type=F32
            ).astype(BF16)
            grads_own[at, :] = jnp.dot(
                chosen_low, grads_in[slot, part], preferred_element_type=F32
            ).astype(BF16)
            gates_own[at, :] = jnp.sum(jnp.where(chosen, gates, 0.0), axis=1, keepdims=True)

        at_step(step, early)
        both_pre = jnp.dot(rows_own[...], both_full[...], preferred_element_type=F32)
        gate_pre, up_pre = both_pre[:, :512], both_pre[:, 512:]
        sigmoid = 1.0 / (1.0 + jnp.exp(-gate_pre))
        silu = gate_pre * sigmoid
        act = (silu * up_pre).astype(BF16)
        out = jnp.dot(act, down_full[...], preferred_element_type=F32).astype(BF16).astype(F32)
        gate_factor = gates_own[...]
        grads_float = grads_own[...].astype(F32)
        grad_gates[...] = jnp.sum(grads_float * out, axis=1, keepdims=True)
        weighted[...] = (gate_factor * out).astype(BF16)
        grad_out = (gate_factor * grads_float).astype(BF16)
        grad_act = lax.dot_general(
            grad_out, down_full[...], CONTRACT_LAST, preferred_element_type=F32
        )
        down_sum[...] += lax.dot_general(
            grad_out, act, CONTRACT_ROWS, preferred_element_type=F32
        )
        grad_gate_pre = grad_act * up_pre * sigmoid * (1.0 + gate_pre * (1.0 - sigmoid))
        grad_up_pre = grad_act * silu
        grad_pre = jnp.concatenate(
            [grad_gate_pre.astype(BF16), grad_up_pre.astype(BF16)], axis=1
        )
        both_sum[...] += lax.dot_general(
            rows_own[...], grad_pre, CONTRACT_ROWS, preferred_element_type=F32
        )
        grad_rows[...] = lax.dot_general(
            grad_pre, both_full[...], CONTRACT_LAST, preferred_element_type=F32
        ).astype(BF16)
        at_step(step, between)
        nothing = jnp.zeros((1, 512), F32)
        slots = [from_table(step, [pair[part] for pair in STEPS]) for part in range(2)]
        for part in range(GROUP):
            at = slice(part * SLOTS, (part + 1) * SLOTS)
            chosen_low = select[at, :]
            out_stage[part] = lax.dot_general(
                chosen_low, weighted[at], CONTRACT_ROWS, preferred_element_type=F32
            ).astype(BF16)
            target = mine.at[slots[part]] if part < 2 else stage.at[part - 2]
            target[:256, :] = lax.dot_general(
                chosen_low, grad_rows[at], CONTRACT_ROWS, preferred_element_type=F32
            ).astype(BF16)
            spread = jnp.sum(chosen_low.astype(F32) * grad_gates[at], axis=0, keepdims=True)
            upper_bits = spread.astype(BF16).astype(F32)
            both = jnp.concatenate([upper_bits, spread - upper_bits], axis=1)
            line_now = jnp.concatenate(
                [jnp.where(upper, nothing, both), jnp.where(upper, both, nothing)], axis=1
            )
            target[256:, :] = jnp.where(extra_row, line_now, 0.0).astype(BF16)
        at_step(step, after)
        return carry

    lax.fori_loop(0, len(STEPS), one_step, 0)
    last = len(STEPS) - 1

    def weight_steps():
        for part in range(4):
            yield 2.5 + part
            lanes = slice(part * 128, (part + 1) * 128)
            upper_lanes = slice(512 + part * 128, 512 + (part + 1) * 128)
            line[part, :1024, :] = both_sum[:, lanes].astype(BF16)
            line[part, 1024:2048, :] = both_sum[:, upper_lanes].astype(BF16)
            line[part, 2048:, :] = down_sum[:, lanes].astype(BF16)
            Local(at(line, part), at(weight_parts, part), at(weight_sems, part)).start()
        yield 100.0
        for part in range(4):
            Local(at(line, part), at(weight_parts, part), at(weight_sems, part)).wait()

    def back_steps():
        yield 0.0
        take(last)
        far_a, near_a = [], []
        for k in range(4):
            yield (2.0, 4.0, 8.0, 12.0)[k]
            part = slot_of(k, 3)
            near_b[k][0].wait_recv()
            near_b[k][1].wait_recv()
            base = [part, b_near.at[0, k], b_near.at[1, k]]
            first_rows = [(ref, 0) for ref in base]
            last_rows = [(ref, high) for ref in base]
            if k == 0:
                add_rows(part, first_rows, 0, high)
                add_rows(part, last_rows, high, low)
                far_a = [
                    go(part.at[top], a_far.at[top], ahead_a),
                    go(part.at[bottom], a_far.at[bottom], behind_a),
                ]
            elif k == 1:
                far_a[0].wait_recv()
                add_rows(part, first_rows + [(a_far, 0)], 0, high)
                add_rows(part, last_rows, high, low)
                near_a.append(go(part, a_near.at[0], ahead_a))
            elif k == 2:
                far_a[1].wait_recv()
                add_rows(part, first_rows, 0, high)
                add_rows(part, last_rows + [(a_far, high)], high, low)
                near_a.append(go(part, a_near.at[1], behind_a))
            else:
                near_a[0].wait_recv()
                near_a[1].wait_recv()
                add_rows(
                    back_sum, first_rows + [(a_near.at[0], 0), (a_near.at[1], 0)], 0, rows
                )

    together(back_steps(), weight_steps())
    for copy in stores[last]:
        copy.wait()
    waited = [copy for step in range(last) for copy in crossing[step]]
    for copy in post.started:
        if not any(copy is other_copy for other_copy in waited):
            copy.wait_send()


def run_experts(block, grads, gate_all, up, down, number):
    rows, columns = block.shape
    sources = grads.shape[0]
    count = GROUP * SLOTS
    copies = PLANE_COPIES + 16 + 8 + 8 + 4 + 2 * LINE_COPIES
    whole = (rows, columns)
    return pl.pallas_call(
        experts_kernel,
        out_shape=[
            jax.ShapeDtypeStruct((sources,) + whole, BF16),
            jax.ShapeDtypeStruct((sources, 256, columns), BF16),
            jax.ShapeDtypeStruct(whole, F32),
            jax.ShapeDtypeStruct((4, 3072, 128), BF16),
        ],
        in_specs=[ANY] * 5,
        out_specs=[ANY, ANY, VMEM, ANY],
        scratch_shapes=[
            pltpu.VMEM((2, GROUP) + whole, BF16),
            pltpu.VMEM((2, GROUP, 256, columns), BF16),
            pltpu.VMEM((1024, 1024), BF16),
            pltpu.VMEM((512, 1024), BF16),
            pltpu.VMEM((1024, 1024), F32),
            pltpu.VMEM((1024, 512), F32),
            pltpu.VMEM((count, 1024), BF16),
            pltpu.VMEM((count, 1024), BF16),
            pltpu.VMEM((count, 1), F32),
            pltpu.VMEM((count, 256), BF16),
            pltpu.VMEM((count, 1024), BF16),
            pltpu.VMEM((count, 1024), BF16),
            pltpu.VMEM((count, 1), F32),
            pltpu.VMEM((16,) + whole, BF16),
            pltpu.VMEM((2, 2) + whole, BF16),
            pltpu.VMEM((2,) + whole, BF16),
            pltpu.VMEM((GROUP, 256, columns), BF16),
            pltpu.VMEM((4,) + whole, BF16),
            pltpu.VMEM((2, 4) + whole, BF16),
            pltpu.VMEM(whole, BF16),
            pltpu.VMEM((2,) + whole, BF16),
            pltpu.VMEM((4, 3072, 128), BF16),
            pltpu.SemaphoreType.DMA((copies,)),
            pltpu.SemaphoreType.DMA((copies,)),
            pltpu.SemaphoreType.REGULAR,
            pltpu.SemaphoreType.DMA((2, 2, GROUP)),
            pltpu.SemaphoreType.DMA((GROUP,)),
            pltpu.SemaphoreType.DMA((12,)),
            pltpu.SemaphoreType.DMA,
        ],
        compiler_params=pltpu.CompilerParams(
            collective_id=number, has_side_effects=True, vmem_limit_bytes=63 << 20
        ),
        name="run_experts",
    )(block, grads, gate_all, up, down)


def rotary_constants():
    position = np.arange(SEQ_LEN, dtype=np.float32)
    power = -(np.arange(32, dtype=np.float32) * np.float32(2.0)) / np.float32(64.0)
    frequency = np.float32(10000.0) ** power
    angles = position[:, None] * frequency[None, :]
    cosine, sine = np.cos(angles), np.sin(angles)
    return (np.tile(cosine, (1, 4)), np.concatenate([-sine, sine, -sine, sine], axis=1))


def shards(
    inputs,
    first_gain,
    query_weight,
    key_weight,
    value_weight,
    query_gain,
    key_gain,
    output_weight,
    second_gain,
    router_weight,
    gate_weight,
    up_weight,
    down_weight,
    segments,
    live_mask,
    routes,
    cotangent,
):
    gain_one, gain_two = first_gain.reshape(8, 128), second_gain.reshape(8, 128)
    query_scale, key_scale = query_gain.reshape(1, -1), key_gain.reshape(1, -1)
    cosine, sine = rotary_constants()
    seg_row, live_row = segments.reshape(1, -1), live_mask.reshape(1, -1)
    router = router_weight.T
    (
        normed, raw, query, keys, values, mixed, residual, block, gates, grad_all, gate_all,
    ) = opening(
        (
            inputs, gain_one, query_weight, key_weight, value_weight, query_scale, key_scale,
            cosine, sine, seg_row, live_row, output_weight, gain_two, router, routes.T,
            cotangent, gate_weight[0],
        ),
        1,
    )
    rows_all, out_parts, back, weight_parts = run_experts(
        block, grad_all, gate_all, up_weight[0], down_weight[0], 2
    )
    grad_inputs, dense, small, combined, weight_sums = closing(
        (
            back, residual, gates, cotangent, gain_two, router, query, keys, values, mixed,
            output_weight, query_weight, key_weight, value_weight, raw, normed.reshape(1024, 1024),
            inputs, gain_one, query_scale, key_scale, cosine, sine, seg_row,
            live_row, out_parts, weight_parts,
        ),
        4,
    )
    (
        result, grad_inputs, grad_query, grad_key, grad_value, grad_output, grad_gate, grad_up,
        grad_down, grad_gain_one, grad_gain_two, grad_query_gain, grad_key_gain, grad_router,
    ) = finish_all(
        (
            dense.reshape(1024, 768), weight_sums, residual, combined,
            small.reshape(32, SMALL_ROWS, 128), grad_inputs,
        )
    )
    return (
        result,
        grad_inputs,
        grad_gain_one.reshape(-1),
        grad_query,
        grad_key,
        grad_value,
        grad_query_gain.reshape(-1),
        grad_key_gain.reshape(-1),
        grad_output,
        grad_gain_two.reshape(-1),
        grad_router.T,
        grad_gate,
        grad_up,
        grad_down,
    )


def solution(mesh):
    return jax.shard_map(
        shards,
        mesh=mesh,
        in_specs=(
            P(("ep", "tp"), None),
            P(),
            P(None, "tp"),
            P(None, "tp"),
            P(None, "tp"),
            P(),
            P(),
            P("tp", None),
            P(),
            P(),
            P("ep", None, "tp"),
            P("ep", None, "tp"),
            P("ep", "tp", None),
            P("ep"),
            P("ep"),
            P(("ep", "tp"), None),
            P(("ep", "tp"), None),
        ),
        out_specs=(
            P(("ep", "tp"), None),
            P(("ep", "tp"), None),
            P(),
            P(None, "tp"),
            P(None, "tp"),
            P(None, "tp"),
            P(),
            P(),
            P("tp", None),
            P(),
            P(),
            P("ep", None, "tp"),
            P("ep", None, "tp"),
            P("ep", "tp", None),
        ),
        check_vma=False,
    )
```

```python
import jax
import jax.numpy as jnp
import numpy as np
from jax import lax
from jax.experimental import pallas as pl
from jax.experimental.pallas import tpu as pltpu
from jax.sharding import PartitionSpec as P

SEQ_LEN = 1024
HIGHEST_PRECISION = lax.Precision.HIGHEST
CONTRACT_ROWS = (((0,), (0,)), ((), ()))
CONTRACT_LAST = (((1,), (1,)), ((), ()))
MESH = pl.DeviceIdType.MESH
ANY = pl.BlockSpec(memory_space=pl.ANY)
VMEM = pl.BlockSpec(memory_space=pltpu.VMEM)
F32 = jnp.float32
BF16 = jnp.bfloat16
SLOTS = 96
EXTRA = 16


def wrap(value):
    return lax.rem(value + 4, 4)


def pick(core, first, second):
    return first * (1 - core) + second * core


def plane_place():
    ep = lax.axis_index("ep")
    core = lax.rem(ep, 2)
    z = lax.rem(lax.div(ep, 2), 4)
    x = lax.div(ep, 8)
    return (pick(core, x, z), pick(core, z, x), core)


def plane_index(a, b, core):
    a, b = wrap(a), wrap(b)
    return (pick(core, a, b) * 4 + pick(core, b, a)) * 2 + core


def plane_partners():
    a, b, core = plane_place()
    tp = lax.axis_index("tp")
    return (
        (plane_index(a + 1, b, core), tp),
        (plane_index(a - 1, b, core), tp),
        (plane_index(a, b + 1, core), tp),
        (plane_index(a, b - 1, core), tp),
        (plane_index(b, a, 1 - core), tp),
    )


def line_partners():
    ep, tp = lax.axis_index("ep"), lax.axis_index("tp")
    return ((ep, wrap(tp + 1)), (ep, wrap(tp - 1)))


def greet(partners):
    barrier = pltpu.get_barrier_semaphore()
    for partner in partners:
        pl.semaphore_signal(barrier, inc=1, device_id=partner, device_id_type=MESH)
    pl.semaphore_wait(barrier, len(partners))


def halves(ref):
    unit = 16 if ref.dtype == BF16 else 8
    rows = ref.shape[-2]
    top = (rows // 2 + unit - 1) // unit * unit
    return (pl.ds(0, top), pl.ds(top, rows - top))


def together(*tasks):
    waiting = [(0.0, number, task) for number, task in enumerate(tasks)]
    while waiting:
        waiting.sort(key=lambda entry: entry[:2])
        _, number, task = waiting.pop(0)
        due = next(task, None)
        if due is not None:
            waiting.append((due, number, task))


def resumed(due, task):
    yield due
    yield from task


def side_by_side(*tasks):
    waiting = [(due, number, task) for number, (due, task) in enumerate(tasks)]
    while waiting:
        waiting.sort(key=lambda entry: entry[:2])
        due, number, task = waiting.pop(0)
        yield due
        due = next(task, None)
        if due is not None:
            waiting.append((due, number, task))


class Clock:
    def __init__(self, now=0.0):
        self.now = now

    def spend(self, amount):
        self.now += amount
        return self.now

    def until(self, moment):
        self.now = max(self.now, moment)
        return self.now


def at(ref, *where):
    return lambda: ref.at[where]


def part_of(place):
    return place() if callable(place) else place


class Remote:
    def __init__(self, src, dst, send_sem, recv_sem, partner):
        self.all = (src, dst, send_sem, recv_sem, partner)

    def copy(self):
        src, dst, send_sem, recv_sem, partner = self.all
        return pltpu.make_async_remote_copy(
            src_ref=part_of(src),
            dst_ref=part_of(dst),
            send_sem=part_of(send_sem),
            recv_sem=part_of(recv_sem),
            device_id=partner,
            device_id_type=MESH,
        )

    def start(self):
        self.copy().start()

    def wait_send(self):
        self.copy().wait_send()

    def wait_recv(self):
        self.copy().wait_recv()


class Local:
    def __init__(self, src, dst, sem):
        self.all = (src, dst, sem)

    def start(self):
        pltpu.make_async_copy(*map(part_of, self.all)).start()

    def wait(self):
        pltpu.make_async_copy(*map(part_of, self.all)).wait()


class Post:
    def __init__(self, send_sems, recv_sems):
        self.send_sems, self.recv_sems, self.started = send_sems, recv_sems, []

    def go(self, src, dst, partner):
        copy = self.prepare(src, dst, partner)
        copy.start()
        return copy

    def prepare(self, src, dst, partner):
        number = len(self.started)
        copy = Remote(src, dst, at(self.send_sems, number), at(self.recv_sems, number), partner)
        self.started.append(copy)
        return copy

    def finish(self):
        for copy in self.started:
            copy.wait_send()


ARRIVAL = (
    (0, 0), (-1, 0), (1, 0), (0, -1), (0, 1), (2, 0), (-1, -1), (-1, 1),
    (1, -1), (1, 1), (2, -1), (2, 1), (0, 2), (-1, 2), (1, 2), (2, 2),
)


def plane_gather_events(post, own_ref, all_ref):
    a, b, core = plane_place()
    ahead_a, behind_a, ahead_b, behind_b, sibling = plane_partners()
    index = {place: plane_index(a + place[0], b + place[1], core) for place in ARRIVAL}
    top, bottom = halves(own_ref)

    def block(place):
        return own_ref if place == (0, 0) else at(all_ref, index[place])

    def copy(place, partner):
        return post.prepare(block(place), at(all_ref, index[place]), partner)

    def half_copy(place, half, partner):
        part = at(all_ref, index[place], half)
        return post.prepare(part, part, partner)

    a_copies = (copy((0, 0), ahead_a), copy((0, 0), behind_a))
    a_halves = (half_copy((-1, 0), top, ahead_a), half_copy((1, 0), bottom, behind_a))
    column = (0, -1, 1, 2)
    b_copies = [(copy((k, 0), ahead_b), copy((k, 0), behind_b)) for k in column]
    b_halves = [
        (half_copy((k, -1), top, ahead_b), half_copy((k, 1), bottom, behind_b)) for k in column
    ]
    crossing = [copy(place, sibling) for place in ARRIVAL]

    def start(*copies):
        for one in copies:
            one.start()

    def begin():
        start(*a_copies, *b_copies[0], crossing[0])

    def near_a(number):
        a_copies[number].wait_recv()
        start(a_halves[number], *b_copies[1 + number], crossing[1 + number])

    def far_a():
        a_halves[0].wait_recv()
        a_halves[1].wait_recv()
        start(*b_copies[3], crossing[5])

    def near_b(k):
        first = ARRIVAL.index((column[k], -1))
        for number in range(2):
            b_copies[k][number].wait_recv()
            start(b_halves[k][number], crossing[first + number])

    def far_b(k):
        b_halves[k][0].wait_recv()
        b_halves[k][1].wait_recv()
        start(crossing[12 + k])

    events = [
        (0.0, begin),
        (6.5, lambda: near_a(0)),
        (6.5, lambda: near_a(1)),
        (7.5, lambda: near_b(0)),
        (11.0, far_a),
        (15.0, lambda: near_b(1)),
        (21.0, lambda: near_b(2)),
        (24.0, lambda: far_b(0)),
        (28.0, lambda: near_b(3)),
        (32.0, lambda: far_b(1)),
        (40.0, lambda: far_b(2)),
        (44.0, lambda: far_b(3)),
    ]
    return (events, crossing)


def plane_gather_steps(post, own_ref, all_ref):
    events, crossing = plane_gather_events(post, own_ref, all_ref)
    for due, event in events:
        if due > 0.0:
            yield due
        event()
    yield 46.0
    for copy in crossing:
        copy.wait_recv()


PLANE_COPIES = 36


def add_rows(dst, sources, start, rows):
    step = 16 if rows % 16 == 0 else 8

    @pl.loop(0, rows // step)
    def _(i):
        at = pl.multiple_of(i * step, step)
        total = None
        for ref, first in sources:
            part = ref[pl.ds(first + at, step), :].astype(F32)
            total = part if total is None else total + part
        dst[pl.ds(start + at, step), :] = total.astype(dst.dtype)


def plane_scatter_steps(post, parts_ref, sum_ref, scratch, begin=0.0):
    mine, other, b_far, b_near, a_far, a_near, local_sems = scratch
    a, b, core = plane_place()
    ahead_a, behind_a, ahead_b, behind_b, sibling = plane_partners()
    rows = a_far.shape[0]
    top, bottom = halves(a_far)
    high = top.size
    low = rows - high
    offsets = (2, 1, -1, 0)
    go = post.go
    crossing = {}
    order = [(k, 0) for k in range(4)] + [(k, j) for k in range(4) for j in (1, 2)]
    order += [(k, 3) for k in range(4)]
    for k, j in order:
        there = plane_index(b + offsets[k], a + offsets[j], 1 - core)
        crossing[k, j] = go(parts_ref.at[there], other.at[k, j], sibling)
    slots = mine.shape[0]
    loads = []

    def load():
        number = len(loads)
        if number < len(order):
            k, j = order[number]
            here = plane_index(a + offsets[k], b + offsets[j], core)
            slot = number % slots
            copy = pltpu.make_async_copy(
                parts_ref.at[here], mine.at[slot], local_sems.at[slot]
            )
            copy.start()
            loads.append(copy)

    for _ in range(slots - 1):
        load()

    def ready(k, j):
        number = order.index((k, j))
        load()
        crossing[k, j].wait_recv()
        loads[number].wait()
        return (other.at[k, j], mine.at[number % slots])

    far_b, near_b = {}, {}
    for k in range(4):
        yield begin + 2.0 + 1.5 * k
        block, extra = ready(k, 0)
        add_rows(block, [(block, 0), (extra, 0)], 0, rows)
        far_b[k] = (
            go(block.at[top], b_far.at[k, top], ahead_b),
            go(block.at[bottom], b_far.at[k, bottom], behind_b),
        )
    for k in range(4):
        far = b_far.at[k]
        yield begin + 9.0 + 3.0 * k
        block, extra = ready(k, 1)
        far_b[k][0].wait_recv()
        add_rows(block, [(block, 0), (extra, 0), (far, 0)], 0, high)
        add_rows(block, [(block, high), (extra, high)], high, low)
        first = go(block, b_near.at[0, k], ahead_b)
        block, extra = ready(k, 2)
        far_b[k][1].wait_recv()
        add_rows(block, [(block, 0), (extra, 0)], 0, high)
        add_rows(block, [(block, high), (extra, high), (far, high)], high, low)
        near_b[k] = (first, go(block, b_near.at[1, k], behind_b))
    far_a, near_a = [], []
    for k in range(4):
        yield begin + (25.0, 31.0, 37.0, 45.0)[k]
        block, extra = ready(k, 3)
        near_b[k][0].wait_recv()
        near_b[k][1].wait_recv()
        base = [block, extra, b_near.at[0, k], b_near.at[1, k]]
        upper = [(ref, 0) for ref in base]
        lower = [(ref, high) for ref in base]
        if k == 0:
            add_rows(block, upper, 0, high)
            add_rows(block, lower, high, low)
            far_a = [
                go(block.at[top], a_far.at[top], ahead_a),
                go(block.at[bottom], a_far.at[bottom], behind_a),
            ]
        elif k == 1:
            far_a[0].wait_recv()
            add_rows(block, upper + [(a_far, 0)], 0, high)
            add_rows(block, lower, high, low)
            near_a.append(go(block, a_near.at[0], ahead_a))
        elif k == 2:
            far_a[1].wait_recv()
            add_rows(block, upper, 0, high)
            add_rows(block, lower + [(a_far, high)], high, low)
            near_a.append(go(block, a_near.at[1], behind_a))
        else:
            near_a[0].wait_recv()
            near_a[1].wait_recv()
            add_rows(sum_ref, upper + [(a_near.at[0], 0), (a_near.at[1], 0)], 0, rows)


def plane_scatter_scratch(rows, columns, kind):
    return [
        pltpu.VMEM((4, rows, columns), kind),
        pltpu.VMEM((4, 4, rows, columns), kind),
        pltpu.VMEM((4, rows, columns), kind),
        pltpu.VMEM((2, 4, rows, columns), kind),
        pltpu.VMEM((rows, columns), kind),
        pltpu.VMEM((2, rows, columns), kind),
        pltpu.SemaphoreType.DMA((4,)),
    ]


OFFSETS = (2, 1, -1, 0)


def ring_places(a, b, core, tp):
    along_a = [(plane_index(a + offset, b, core), tp) for offset in OFFSETS[:3]]
    along_b = [(plane_index(a, b + offset, core), tp) for offset in OFFSETS[:3]]
    return (along_a, along_b, (plane_index(b, a, 1 - core), tp))


def brief_partners():
    along_a, along_b, sibling = ring_places(*plane_place(), lax.axis_index("tp"))
    return tuple(along_a + along_b + [sibling])


BRIEF_COPIES = 1 + 3 + 3


def brief_number(number):
    return (number // 16, number // 4 % 4, number % 4)


def brief_scatter_steps(post, parts_ref, sum_ref, scratch, begin=0.0):
    other, from_b, total, from_a = scratch
    a, b, core = plane_place()
    along_a, along_b, sibling = ring_places(a, b, core, lax.axis_index("tp"))
    crossing = post.go(at(parts_ref, 1 - core), other, sibling)
    yield begin + 3.0
    crossing.wait_recv()
    for i in range(4):
        other[i] = (other[i].astype(F32) + parts_ref[core, i].astype(F32)).astype(other.dtype)
    copies = [
        post.go(at(other, slice(None), wrap(b + OFFSETS[j])), at(from_b, j), along_b[j])
        for j in range(3)
    ]
    yield begin + 8.0
    for copy in copies:
        copy.wait_recv()
    for i in range(4):
        part = other[i, b].astype(F32)
        for j in range(3):
            part = part + from_b[j, i].astype(F32)
        total[i] = part.astype(total.dtype)
    copies = [
        post.go(at(total, wrap(a + OFFSETS[j])), at(from_a, j), along_a[j]) for j in range(3)
    ]
    yield begin + 11.0
    part = total[a].astype(F32)
    for j in range(3):
        copies[j].wait_recv()
        part = part + from_a[j].astype(F32)
    sum_ref[...] = part.astype(sum_ref.dtype)


def brief_scatter_scratch(rows, columns, kind):
    return [
        pltpu.VMEM((4, 4, rows, columns), kind),
        pltpu.VMEM((3, 4, rows, columns), kind),
        pltpu.VMEM((4, rows, columns), kind),
        pltpu.VMEM((3, rows, columns), kind),
    ]


def brief_gather_steps(post, own_ref, all_ref, begin=0.0):
    a, b, core = plane_place()
    along_a, along_b, sibling = ring_places(a, b, core, lax.axis_index("tp"))
    all_ref[core, a, b] = own_ref[...]
    copies = [post.go(own_ref, at(all_ref, core, a, b), place) for place in along_a]
    yield begin + 3.0
    for copy in copies:
        copy.wait_recv()
    line = at(all_ref, core, slice(None), b)
    copies = [post.go(line, line, place) for place in along_b]
    yield begin + 8.0
    for copy in copies:
        copy.wait_recv()
    crossing = post.go(at(all_ref, core), at(all_ref, core), sibling)
    yield begin + 11.0
    crossing.wait_recv()


LINE_COPIES = 4


def line_gather_steps(post, own_ref, all_ref, clock, near_time, far_time, arrived=None):
    tp = lax.axis_index("tp")
    ahead, behind = line_partners()
    top, bottom = halves(own_ref)
    before, after, far = wrap(tp - 1), wrap(tp + 1), wrap(tp + 2)
    begin = clock.now
    first = post.go(own_ref, all_ref.at[tp], ahead)
    second = post.go(own_ref, all_ref.at[tp], behind)
    if arrived is not None:
        yield from arrived(tp)
    yield clock.until(begin + near_time)
    first.wait_recv()
    third = post.go(all_ref.at[before, top], all_ref.at[before, top], ahead)
    second.wait_recv()
    fourth = post.go(all_ref.at[after, bottom], all_ref.at[after, bottom], behind)
    if arrived is not None:
        yield from arrived(before)
        yield from arrived(after)
    yield clock.until(begin + far_time)
    third.wait_recv()
    fourth.wait_recv()
    if arrived is not None:
        yield from arrived(far)


def line_scatter_steps(post, make, far, near, finish, clock, far_time, near_time):
    ahead, behind = line_partners()
    top, bottom = halves(far)
    high = top.size
    rows = far.shape[0]
    block = yield from make(2)
    begin = clock.now
    first = post.go(block.at[top], far.at[top], ahead)
    second = post.go(block.at[bottom], far.at[bottom], behind)
    block = yield from make(1)
    yield clock.until(begin + far_time)
    first.wait_recv()
    add_rows(block, [(block, 0), (far, 0)], 0, high)
    third = post.go(block, near.at[0], ahead)
    other = yield from make(-1)
    second.wait_recv()
    add_rows(other, [(other, high), (far, high)], high, rows - high)
    fourth = post.go(other, near.at[1], behind)
    begin = clock.now
    own = yield from make(0)
    yield clock.until(begin + near_time)
    third.wait_recv()
    fourth.wait_recv()
    finish(own, near.at[0], near.at[1])


def split_float(values):
    high = values.astype(BF16)
    return (high, (values - high.astype(F32)).astype(BF16))


def split_three(values):
    high = values.astype(BF16)
    rest = values - high.astype(F32)
    middle = rest.astype(BF16)
    return (high, middle, (rest - middle.astype(F32)).astype(BF16))


def head_mean(values):
    same = (
        lax.broadcasted_iota(jnp.int32, (128, 128), 0) // 64
        == lax.broadcasted_iota(jnp.int32, (128, 128), 1) // 64
    ).astype(BF16)
    high, low = split_float(values)
    total = jnp.dot(high, same, preferred_element_type=F32)
    total = total + jnp.dot(low, same, preferred_element_type=F32)
    return total * (1.0 / 64.0)


def other_half(values):
    lane = lax.broadcasted_iota(jnp.int32, values.shape, 1)
    return jnp.where(
        lax.rem(lane, 64) < 32, pltpu.roll(values, 96, 1), pltpu.roll(values, 32, 1)
    )


def head_ready(raw, gain, cosine, sine):
    normed = raw * lax.rsqrt(head_mean(raw * raw) + 1e-06) * gain
    return normed * cosine + other_half(normed) * sine


def head_back(grad, raw, gain, cosine, sine):
    grad = grad * cosine + other_half(grad * sine)
    scale = lax.rsqrt(head_mean(raw * raw) + 1e-06)
    plain = raw * scale
    grad_gain = jnp.sum(grad * plain, axis=0, keepdims=True)
    grad = grad * gain
    return (scale * (grad - plain * head_mean(grad * plain)), grad_gain)


def wide(gain):
    gain = gain.astype(F32)
    return jnp.concatenate([gain[part : part + 1] for part in range(8)], axis=1)


def both_heads(gain):
    gain = gain.astype(F32)
    return jnp.concatenate([gain, gain], axis=1)


def row_scale(values):
    return lax.rsqrt(jnp.mean(values * values, axis=1, keepdims=True) + 1e-05)


def exchange(values):
    return jnp.concatenate([values[:, 64:], values[:, :64]], axis=1)


def head_pairs(block):
    rows = block.shape[0]
    low = lax.broadcasted_iota(jnp.int32, (rows, 128), 1) < 64
    left, right = block[:, :128], block[:, 128:]
    zero = jnp.zeros_like(left)
    straight = jnp.concatenate([jnp.where(low, left, zero), jnp.where(low, zero, right)], axis=0)
    crossed = jnp.concatenate([jnp.where(low, zero, left), jnp.where(low, right, zero)], axis=0)
    return (straight, crossed)


def heads_back(straight, crossed):
    rows = straight.shape[0] // 2
    low = lax.broadcasted_iota(jnp.int32, (rows, 128), 1) < 64
    left = jnp.where(low, straight[:rows], crossed[:rows])
    right = jnp.where(low, crossed[rows:], straight[rows:])
    return jnp.concatenate([left, right], axis=1)


def attend_block(query, keys, values, bias, clock):
    bias = jnp.concatenate([bias, bias], axis=0)
    outs = []
    for pair, key_part, value_part in zip(
        head_pairs(query), (keys, exchange(keys)), (values, exchange(values)), strict=True
    ):
        scores = lax.dot_general(pair, key_part, CONTRACT_LAST, preferred_element_type=F32)
        weights = jnp.exp(scores * 0.125 + bias)
        total_weight = jnp.sum(weights, axis=1, keepdims=True)
        out = jnp.dot(weights.astype(BF16), value_part, preferred_element_type=F32)
        outs.append(out / total_weight)
        yield clock.spend(0.8)
    return heads_back(*outs).astype(BF16)


def document_bounds(segments, live_mask):
    one = jnp.ones_like(segments)
    zero = jnp.zeros_like(segments)

    def count(chosen):
        return jnp.sum(jnp.where(chosen, one, zero), axis=1, keepdims=True)

    return (count(segments < 1), count(segments < 2), count(live_mask == 1))


def score_bias(bounds, query, key):
    first, second, living = bounds

    def document(position):
        return (position >= first).astype(jnp.int32) + (position >= second).astype(jnp.int32)

    seen = jnp.where(key < living, 1, 0)
    same = document(query) == document(key)
    return jnp.where(same & ((seen == 1) | (query == key)), 0.0, -1e30).astype(F32)


def block_rows(block):
    return pl.ds(pl.multiple_of(block * 256, 256), 256)


def opening_kernel(
    inputs, gain_one, query_weight, key_weight, value_weight, query_gain, key_gain, cosine, sine,
    segments, live_mask, output_weight, gain_two, router, routes, cotangent,
    gate,
    normed_out, raw_out, query_out, keys_out, values_out, mixed_out,
    residual, block, gates, grad_all, gate_all,
    normed, raw, query, keys, values, mixed,
    parts, far, near, hold, send_sems, recv_sems, local_sems, out_sems,
):
    tp = lax.axis_index("tp")
    own_parts = (
        (cotangent, parts.at[0], grad_all.at[lax.axis_index("ep")]),
        (gate, hold, gate_all.at[tp]),
    )
    inward = [
        pltpu.make_async_copy(src, through, local_sems.at[number])
        for number, (src, through, _) in enumerate(own_parts)
    ]
    outward = [
        pltpu.make_async_copy(through, dst, local_sems.at[number])
        for number, (_, through, dst) in enumerate(own_parts)
    ]
    for copy in inward:
        copy.start()
    greet(plane_partners() + line_partners())
    post = Post(send_sems, recv_sems)
    clock = Clock()
    bounds = document_bounds(segments[...], live_mask[...])

    def project(place):
        rows = block_rows(place)
        part = normed[place]
        cos, sin = cosine[rows, :], sine[rows, :]
        both = jnp.dot(part, query_weight[...], preferred_element_type=F32)
        raw[rows, :256] = both
        for lanes in (slice(0, 128), slice(128, 256)):
            query[rows, lanes] = head_ready(both[:, lanes], both_heads(query_gain[...]), cos, sin).astype(BF16)
        one = jnp.dot(part, key_weight[...], preferred_element_type=F32)
        raw[rows, 256:] = one
        keys[rows, :] = head_ready(one, both_heads(key_gain[...]), cos, sin).astype(BF16)
        values[rows, :] = jnp.dot(part, value_weight[...], preferred_element_type=F32).astype(BF16)
        yield clock.spend(1.5)

    def make(offset):
        place = wrap(tp + offset)
        rows = block_rows(place)
        bias = score_bias(
            bounds,
            place * 256 + lax.broadcasted_iota(jnp.int32, (256, 1), 0),
            lax.broadcasted_iota(jnp.int32, (1, 1024), 1),
        )
        out = yield from attend_block(query[rows, :], keys[...], values[...], bias, clock)
        mixed[rows, :] = out
        part = parts.at[(2, 1, -1, 0).index(offset)]
        part[...] = jnp.dot(out, output_weight[...], preferred_element_type=F32).astype(BF16)
        yield clock.spend(0.4)
        return part

    results = [
        pltpu.make_async_copy(src, dst, out_sems.at[number])
        for number, (src, dst) in enumerate(
            (
                (normed, normed_out), (raw, raw_out), (query, query_out), (keys, keys_out),
                (values, values_out), (mixed, mixed_out),
            )
        )
    ]

    def finish(own, first, second):
        results[5].start()
        total = own[...].astype(F32) + first[...].astype(F32) + second[...].astype(F32)
        total = inputs[...].astype(F32) + total
        residual[...] = total
        normed_two = total * row_scale(total) * wide(gain_two[...])
        block[:256, :] = normed_two.astype(BF16)
        logits = jnp.zeros((32, 256), F32)
        for piece in split_three(normed_two):
            logits = logits + lax.dot_general(
                router[...], piece, CONTRACT_LAST, preferred_element_type=F32
            )
        expert = lax.broadcasted_iota(jnp.int32, (32, 256), 0)
        named = expert < 0
        for choice in range(8):
            named = named | (routes[choice : choice + 1, :] == expert)
        top_logit = jnp.max(jnp.where(named, logits, -1e30), axis=0, keepdims=True)
        raised = jnp.where(named, jnp.exp(jnp.where(named, logits - top_logit, 0.0)), 0.0)
        probs = raised / jnp.sum(raised, axis=0, keepdims=True)
        gates[...] = probs
        high, low = split_float(probs)
        block[256:, :] = jnp.concatenate([high[:16], low[:16], high[16:], low[16:]], axis=1)

    def attention_steps():
        hidden = inputs[...].astype(F32)
        normed[tp] = (hidden * row_scale(hidden) * wide(gain_one[...])).astype(BF16)
        for copy, onward in zip(inward, outward, strict=True):
            copy.wait()
            onward.start()
        clock.spend(1.0)
        yield from line_gather_steps(post, normed.at[tp], normed, clock, 11.5, 17.5, project)
        for copy in outward:
            copy.wait()
        for copy in results[:5]:
            copy.start()
        yield from line_scatter_steps(post, make, far, near, finish, clock, 5.0, 22.0)

    def weight_steps(own, everyone, begin, near_time, far_time):
        yield begin
        yield from line_gather_steps(post, own, everyone, Clock(begin), near_time, far_time)

    together(
        attention_steps(),
        plane_gather_steps(post, cotangent, grad_all),
        weight_steps(gate, gate_all, 20.5, 22.0, 32.0),
    )
    post.finish()
    for copy in results:
        copy.wait()


def opening(arguments, number):
    count = 3 * LINE_COPIES + PLANE_COPIES
    return pl.pallas_call(
        opening_kernel,
        out_shape=[
            jax.ShapeDtypeStruct((4, 256, 1024), BF16),
            jax.ShapeDtypeStruct((1024, 384), F32),
            jax.ShapeDtypeStruct((1024, 256), BF16),
            jax.ShapeDtypeStruct((1024, 128), BF16),
            jax.ShapeDtypeStruct((1024, 128), BF16),
            jax.ShapeDtypeStruct((1024, 256), BF16),
            jax.ShapeDtypeStruct((256, 1024), F32),
            jax.ShapeDtypeStruct((256 + EXTRA, 1024), BF16),
            jax.ShapeDtypeStruct((32, 256), F32),
            jax.ShapeDtypeStruct((32, 256, 1024), BF16),
            jax.ShapeDtypeStruct((4, 1024, 128), BF16),
        ],
        in_specs=[VMEM] * (len(arguments) - 2) + [ANY] * 2,
        out_specs=[ANY] * 6 + [VMEM] * 3 + [ANY] * 2,
        scratch_shapes=[
            pltpu.VMEM((4, 256, 1024), BF16),
            pltpu.VMEM((1024, 384), F32),
            pltpu.VMEM((1024, 256), BF16),
            pltpu.VMEM((1024, 128), BF16),
            pltpu.VMEM((1024, 128), BF16),
            pltpu.VMEM((1024, 256), BF16),
            pltpu.VMEM((4, 256, 1024), BF16),
            pltpu.VMEM((256, 1024), BF16),
            pltpu.VMEM((2, 256, 1024), BF16),
            pltpu.VMEM((1024, 128), BF16),
            pltpu.SemaphoreType.DMA((count,)),
            pltpu.SemaphoreType.DMA((count,)),
            pltpu.SemaphoreType.DMA((2,)),
            pltpu.SemaphoreType.DMA((6,)),
        ],
        compiler_params=pltpu.CompilerParams(
            collective_id=number, has_side_effects=True, vmem_limit_bytes=56 << 20
        ),
        name="opening",
    )(*arguments)


def attend_back_block(query, grad, keys, values, bias, keys_sum, values_sum, clock):
    query_pairs = head_pairs(query)
    grad_pairs = head_pairs(grad)
    key_parts = (keys, exchange(keys))
    value_parts = (values, exchange(values))
    outs = []
    bias = jnp.concatenate([bias, bias], axis=1)
    for side in range(2):
        part, grad_part = query_pairs[side], grad_pairs[side]
        scores = lax.dot_general(key_parts[side], part, CONTRACT_LAST, preferred_element_type=F32)
        raised = jnp.exp(scores * 0.125 + bias)
        weights = raised * (1.0 / jnp.sum(raised, axis=0, keepdims=True))
        grad_weights = lax.dot_general(
            value_parts[side], grad_part, CONTRACT_LAST, preferred_element_type=F32
        )
        inner = jnp.sum(weights * grad_weights, axis=0, keepdims=True)
        grad_scores = (weights * (grad_weights - inner)).astype(BF16)
        outs.append(
            lax.dot_general(
                grad_scores, key_parts[side], CONTRACT_ROWS, preferred_element_type=F32
            )
        )
        keys_sum[side] += jnp.dot(grad_scores, part, preferred_element_type=F32)
        values_sum[side] += jnp.dot(weights.astype(BF16), grad_part, preferred_element_type=F32)
        yield clock.spend(2.3)
    return heads_back(*outs) * 0.125


SMALL_ROWS = 16
WEIGHTS_AT = 20.0


def closing_kernel(
    back, residual, gates, cotangent, gain_two, router, query_far, keys_far, values_far, mixed_far,
    output_weight, query_weight_far, key_weight_far, value_weight_far, raw_far, normed_far,
    inputs_far, gain_one, query_gain, key_gain, cosine, sine, segments, live_mask, out_parts,
    weight_parts, grad_inputs, dense_all, small_all, combined, weight_sum,
    grad_all, grad_residual, low, keys_sum, values_sum, output_sum, parts, far, near,
    dense, dense_own, small, small_own, small_early, small_late, small_total, query_gain_sum,
    weights, weights_far, weights_near, query, keys, values, mixed, query_weight, key_weight, value_weight, raw, normed, inputs,
    late_sems, *rest,
):
    out_scratch, dense_scratch, small_scratch = rest[:7], rest[7:11], rest[11:15]
    post = Post(rest[15], rest[16])
    me = lax.axis_index("ep")
    tp = lax.axis_index("tp")
    ahead, behind = line_partners()
    across = (me, wrap(tp + 2))
    late = [
        pltpu.make_async_copy(src, dst, late_sems.at[number])
        for number, (src, dst) in enumerate(
            (
                (query_far, query), (keys_far, keys), (values_far, values), (mixed_far, mixed),
                (query_weight_far, query_weight), (key_weight_far, key_weight),
                (value_weight_far, value_weight), (raw_far, raw), (normed_far, normed),
                (inputs_far, inputs),
                (weight_parts.at[wrap(tp + 1)], weights.at[0]),
                (weight_parts.at[wrap(tp - 1)], weights.at[1]),
                (weight_parts.at[tp], weights.at[2]),
            )
        )
    ]
    for copy in late:
        copy.start()
    greet(brief_partners() + (ahead, behind, across))
    clock = Clock()
    out_steps = plane_scatter_steps(post, out_parts, combined, out_scratch)
    out_due = next(out_steps)

    lines = back[256:, :]
    grad_gates = jnp.concatenate(
        [lines[:, :256] + lines[:, 256:512], lines[:, 512:768] + lines[:, 768:]], axis=0
    )
    probs = gates[...]
    grad_logits = probs * (grad_gates - jnp.sum(probs * grad_gates, axis=0, keepdims=True))
    grad_two = back[:256, :]
    logit_pieces = split_three(grad_logits)
    for piece in logit_pieces:
        grad_two = grad_two + lax.dot_general(
            piece, router[...], CONTRACT_ROWS, preferred_element_type=F32
        )
    total = residual[...]
    scale = row_scale(total)
    plain = total * scale
    grad_gain_two = jnp.sum(grad_two * plain, axis=0, keepdims=True)
    grad_two = grad_two * wide(gain_two[...])
    grad_total = cotangent[...].astype(F32) + scale * (
        grad_two - plain * jnp.mean(grad_two * plain, axis=1, keepdims=True)
    )
    grad_residual[...] = grad_total
    grad_all[tp] = grad_total.astype(BF16)
    clock.spend(4.0)

    bounds = document_bounds(segments[...], live_mask[...])
    keys_sum[...] = jnp.zeros_like(keys_sum)
    values_sum[...] = jnp.zeros_like(values_sum)
    output_sum[...] = jnp.zeros_like(output_sum)
    query_gain_sum[...] = jnp.zeros_like(query_gain_sum)

    def attention(place):
        rows = block_rows(place)
        grad = grad_all[place]
        output_sum[...] += lax.dot_general(
            mixed[rows, :], grad, CONTRACT_ROWS, preferred_element_type=F32
        )
        grad_mixed = lax.dot_general(
            grad, output_weight[...], CONTRACT_LAST, preferred_element_type=F32
        ).astype(BF16)
        bias = score_bias(
            bounds,
            place * 256 + lax.broadcasted_iota(jnp.int32, (1, 256), 1),
            lax.broadcasted_iota(jnp.int32, (1024, 1), 0),
        )
        clock.spend(0.8)
        grad_query = yield from attend_back_block(
            query[rows, :], grad_mixed, keys[...], values[...], bias, keys_sum, values_sum, clock
        )
        for lanes in (slice(0, 128), slice(128, 256)):
            grad_raw, grad_gain = head_back(
                grad_query[:, lanes],
                raw[rows, lanes],
                both_heads(query_gain[...]),
                cosine[rows, :],
                sine[rows, :],
            )
            low[rows, lanes] = grad_raw.astype(BF16)
            query_gain_sum[...] += grad_gain
        yield clock.spend(0.5)

    def make(offset):
        rows = block_rows(wrap(tp + offset))
        total = lax.dot_general(
            low[rows, :256], query_weight[...], CONTRACT_LAST, preferred_element_type=F32
        )
        total = total + lax.dot_general(
            low[rows, 256:384], key_weight[...], CONTRACT_LAST, preferred_element_type=F32
        )
        total = total + lax.dot_general(
            low[rows, 384:], value_weight[...], CONTRACT_LAST, preferred_element_type=F32
        )
        part = parts.at[(2, 1, -1, 0).index(offset)]
        part[...] = total.astype(BF16)
        yield clock.spend(0.8)
        return part

    def finish(own, first, second):
        grad_one = own[...].astype(F32) + first[...].astype(F32) + second[...].astype(F32)
        hidden = inputs[...].astype(F32)
        scale = row_scale(hidden)
        plain = hidden * scale
        grad_one = grad_one * wide(gain_one[...])
        grad_inputs[...] = (
            grad_residual[...]
            + scale * (grad_one - plain * jnp.mean(grad_one * plain, axis=1, keepdims=True))
        ).astype(BF16)

    def router_gradient():
        normed_pieces = split_three(plain * wide(gain_two[...]))
        total = jnp.zeros((32, 1024), F32)
        for first, second in ((0, 0), (0, 1), (1, 0), (1, 1), (0, 2), (2, 0)):
            total = total + jnp.dot(
                logit_pieces[first], normed_pieces[second], preferred_element_type=F32
            )
        return total

    gain_rows = small.at[brief_number(16)]
    head_rows = small.at[brief_number(17)]

    def fill_router():
        grad_router = router_gradient()
        small[...] = jnp.zeros_like(small)
        for part in range(8):
            lanes = slice(part * 128, (part + 1) * 128)
            small[brief_number(2 * part)] = grad_router[:16, lanes]
            small[brief_number(2 * part + 1)] = grad_router[16:, lanes]
            gain_rows[8 + part : 9 + part, :] = grad_gain_two[:, lanes]

    def fill_small(weights, grad_key_gain):
        grad_gain_one = jnp.zeros((8, 1024), F32)
        ones = jnp.ones((8, 128), BF16)
        parts = [query_weight[:, :128], query_weight[:, 128:], key_weight[...], value_weight[...]]
        for number, part in enumerate(parts):
            product = weights[:, number * 128 : (number + 1) * 128] * part.astype(F32)
            for piece in split_float(product):
                grad_gain_one = grad_gain_one + lax.dot_general(
                    ones, piece, CONTRACT_LAST, preferred_element_type=F32
                )
        grad_gain_one = grad_gain_one[:1] / wide(gain_one[...])
        for part in range(8):
            gain_rows[part : part + 1, :] = grad_gain_one[:, part * 128 : (part + 1) * 128]
        head_rows[0:1, :] = query_gain_sum[...]
        head_rows[1:2, :] = grad_key_gain

    def attention_steps():
        filled, early_line = [], []

        def send_line(part, slots):
            return [
                post.go(part, at(slots, number), partner)
                for number, partner in enumerate((ahead, behind, across))
            ]

        def arrived(place):
            if not filled:
                filled.append(place)
                fill_router()
                early_line.extend(send_line(at(small, 0), small_early))
                for copy in late:
                    copy.wait()
            yield from attention(place)

        yield from line_gather_steps(
            post, grad_all.at[tp], grad_all, clock, 11.5, 17.5, arrived
        )
        grad_raw, grad_key_gain = head_back(
            (keys_sum[0] + exchange(keys_sum[1])) * 0.125,
            raw[:, 256:],
            both_heads(key_gain[...]),
            cosine[...],
            sine[...],
        )
        low[:, 256:384] = grad_raw.astype(BF16)
        low[:, 384:] = (values_sum[0] + exchange(values_sum[1])).astype(BF16)
        weights = lax.dot_general(
            normed[...], low[...], CONTRACT_ROWS, preferred_element_type=F32
        )
        fill_small(weights, grad_key_gain)
        line = early_line + send_line(at(small, 1, 0, pl.ds(0, 2)), small_late)
        fill_dense(weights)
        now = clock.spend(8.0)
        yield from side_by_side(
            (now, dense_steps(now)),
            (now, small_steps(now, line)),
            (now, line_scatter_steps(post, make, far, near, finish, clock, 3.5, 11.5)),
        )

    def fill_dense(weights):
        weights = weights.astype(BF16)
        for part in range(32):
            dense[(*brief_number(part), slice(None), slice(0, 512))] = weights[
                part * 32 : (part + 1) * 32
            ]
        for part in range(4):
            block = output_sum[:, part * 256 : (part + 1) * 256].astype(BF16)
            for piece in range(8):
                dense[(*brief_number(part * 8 + piece), slice(None), slice(512, 768))] = block[
                    piece * 32 : (piece + 1) * 32
                ]

    def dense_steps(begin):
        yield from brief_scatter_steps(post, dense, dense_own, dense_scratch, begin)
        yield from brief_gather_steps(post, dense_own, dense_all, begin + 12.0)

    def small_steps(begin, line):
        for copy in line:
            copy.wait_recv()
        small_total[...] = jnp.zeros_like(small_total)
        for place in range(4):
            small_total[0, place] = small[0, place] + (
                small_early[0, place] + small_early[1, place] + small_early[2, place]
            )
        small_total[1, 0, :2] = small[1, 0, :2] + small_late[0] + small_late[1] + small_late[2]
        yield from brief_scatter_steps(post, small_total, small_own, small_scratch, begin)
        yield from brief_gather_steps(post, small_own, small_all, begin + 12.0)

    def make_weights(offset):
        yield 0.0
        if offset == 2:
            return weight_parts.at[wrap(tp + 2)]
        return weights.at[(1, -1, 0).index(offset)]

    def finish_weights(own, first, second):
        add_rows(weight_sum, [(own, 0), (first, 0), (second, 0)], 0, own.shape[0])

    def weight_steps():
        yield WEIGHTS_AT
        yield from line_scatter_steps(
            post, make_weights, weights_far, weights_near, finish_weights, Clock(WEIGHTS_AT), 14.0, 60.0
        )

    together(attention_steps(), resumed(out_due, out_steps), weight_steps())
    post.finish()


def closing(arguments, number):
    count = 3 * LINE_COPIES + PLANE_COPIES + 4 * BRIEF_COPIES + 6
    return pl.pallas_call(
        closing_kernel,
        out_shape=[
            jax.ShapeDtypeStruct((256, 1024), BF16),
            jax.ShapeDtypeStruct((2, 4, 4, 32, 768), BF16),
            jax.ShapeDtypeStruct((2, 4, 4, SMALL_ROWS, 128), F32),
            jax.ShapeDtypeStruct((256, 1024), F32),
            jax.ShapeDtypeStruct((3072, 128), F32),
        ],
        in_specs=[VMEM] * 6 + [ANY] * 4 + [VMEM] + [ANY] * 6 + [VMEM] * 7 + [ANY] * 2,
        out_specs=[VMEM] * 5,
        scratch_shapes=[
            pltpu.VMEM((4, 256, 1024), BF16),
            pltpu.VMEM((256, 1024), F32),
            pltpu.VMEM((1024, 512), BF16),
            pltpu.VMEM((2, 1024, 128), F32),
            pltpu.VMEM((2, 1024, 128), F32),
            pltpu.VMEM((256, 1024), F32),
            pltpu.VMEM((4, 256, 1024), BF16),
            pltpu.VMEM((256, 1024), BF16),
            pltpu.VMEM((2, 256, 1024), BF16),
            pltpu.VMEM((2, 4, 4, 32, 768), BF16),
            pltpu.VMEM((32, 768), BF16),
            pltpu.VMEM((2, 4, 4, SMALL_ROWS, 128), F32),
            pltpu.VMEM((SMALL_ROWS, 128), F32),
            pltpu.VMEM((3, 4, 4, SMALL_ROWS, 128), F32),
            pltpu.VMEM((3, 2, SMALL_ROWS, 128), F32),
            pltpu.VMEM((2, 4, 4, SMALL_ROWS, 128), F32),
            pltpu.VMEM((1, 128), F32),
            pltpu.VMEM((3, 3072, 128), BF16),
            pltpu.VMEM((3072, 128), BF16),
            pltpu.VMEM((2, 3072, 128), BF16),
            pltpu.VMEM((1024, 256), BF16),
            pltpu.VMEM((1024, 128), BF16),
            pltpu.VMEM((1024, 128), BF16),
            pltpu.VMEM((1024, 256), BF16),
            pltpu.VMEM((1024, 256), BF16),
            pltpu.VMEM((1024, 128), BF16),
            pltpu.VMEM((1024, 128), BF16),
            pltpu.VMEM((1024, 384), F32),
            pltpu.VMEM((1024, 1024), BF16),
            pltpu.VMEM((256, 1024), BF16),
            pltpu.SemaphoreType.DMA((13,)),
        ]
        + plane_scatter_scratch(256, 1024, BF16)
        + brief_scatter_scratch(32, 768, BF16)
        + brief_scatter_scratch(SMALL_ROWS, 128, F32)
        + [pltpu.SemaphoreType.DMA((count,)), pltpu.SemaphoreType.DMA((count,))],
        compiler_params=pltpu.CompilerParams(
            collective_id=number, has_side_effects=True, vmem_limit_bytes=63 << 20
        ),
        name="closing",
    )(*arguments)


def finish_kernel(
    dense_far, weights_far, residual_far, combined_far, small_far, inputs_far,
    result, grad_inputs, grad_query, grad_key, grad_value, grad_output, grad_gate, grad_up,
    grad_down, gain_one, gain_two, query_gain, key_gain, router,
    dense, weights, residual, combined, small, sems,
):
    copies = [
        pltpu.make_async_copy(src, dst, sems.at[number])
        for number, (src, dst) in enumerate(
            (
                (weights_far, weights), (dense_far, dense), (residual_far, residual),
                (combined_far, combined), (small_far, small), (inputs_far, grad_inputs),
            )
        )
    ]
    for copy in copies:
        copy.start()
    copies[0].wait()
    grad_gate[0] = weights[:1024, :]
    grad_up[0] = weights[1024:2048, :]
    grad_down[0] = weights[2048:, :].T
    copies[1].wait()
    grad_query[...] = dense[:, :256].astype(F32)
    grad_key[...] = dense[:, 256:384].astype(F32)
    grad_value[...] = dense[:, 384:512].astype(F32)
    for part in range(4):
        grad_output[:, part * 256 : (part + 1) * 256] = dense[
            part * 256 : (part + 1) * 256, 512:
        ].astype(F32)
    copies[2].wait()
    copies[3].wait()
    result[...] = (residual[...] + combined[...]).astype(BF16)
    copies[4].wait()
    for part in range(8):
        lanes = slice(part * 128, (part + 1) * 128)
        router[:16, lanes] = small[2 * part]
        router[16:, lanes] = small[2 * part + 1]
        gain_one[:, lanes] = small[16, part : part + 1, :]
        gain_two[:, lanes] = small[16, 8 + part : 9 + part, :]
    heads = small[17]
    heads = heads[:, :64] + heads[:, 64:]
    query_gain[...] = heads[0:1]
    key_gain[...] = heads[1:2]
    copies[5].wait()


def finish_all(arguments):
    return pl.pallas_call(
        finish_kernel,
        out_shape=[
            jax.ShapeDtypeStruct((256, 1024), BF16),
            jax.ShapeDtypeStruct((256, 1024), BF16),
            jax.ShapeDtypeStruct((1024, 256), F32),
            jax.ShapeDtypeStruct((1024, 128), F32),
            jax.ShapeDtypeStruct((1024, 128), F32),
            jax.ShapeDtypeStruct((256, 1024), F32),
            jax.ShapeDtypeStruct((1, 1024, 128), F32),
            jax.ShapeDtypeStruct((1, 1024, 128), F32),
            jax.ShapeDtypeStruct((1, 128, 1024), F32),
            jax.ShapeDtypeStruct((1, 1024), F32),
            jax.ShapeDtypeStruct((1, 1024), F32),
            jax.ShapeDtypeStruct((1, 64), F32),
            jax.ShapeDtypeStruct((1, 64), F32),
            jax.ShapeDtypeStruct((32, 1024), F32),
        ],
        in_specs=[ANY] * 6,
        out_specs=[VMEM] * 14,
        scratch_shapes=[
            pltpu.VMEM((1024, 768), BF16),
            pltpu.VMEM((3072, 128), F32),
            pltpu.VMEM((256, 1024), F32),
            pltpu.VMEM((256, 1024), F32),
            pltpu.VMEM((32, SMALL_ROWS, 128), F32),
            pltpu.SemaphoreType.DMA((6,)),
        ],
        compiler_params=pltpu.CompilerParams(vmem_limit_bytes=60 << 20),
        name="finish_all",
    )(*arguments)


STEPS = ((0, 1), (3, 4), (6, 7), (12, 13), (14, 15), (10, 11), (8, 9), (2, 5))
GROUP = 4


def experts_kernel(
    block, grads, gate_all, up, down,
    rows_all, out_parts, back_sum, weight_parts,
    rows_in, grads_in, both_full, down_full, both_sum, down_sum, rows_own, grads_own, gates_own,
    select, weighted, grad_rows, grad_gates, mine, other, stage, out_stage,
    b_far, b_near, a_far, a_near, line, send_sems, recv_sems, credit, load_sems, store_sems, weight_sems, own_sem,
):
    a, b, core = plane_place()
    me = lax.axis_index("ep")
    ahead_a, behind_a, ahead_b, behind_b, sibling = plane_partners()
    here = [plane_index(a + place[0], b + place[1], core) for place in ARRIVAL]
    there = [plane_index(b + place[0], a + place[1], 1 - core) for place in ARRIVAL]
    lane_row = lax.rem(me, 16)
    upper = me >= 16
    tp = lax.axis_index("tp")
    ahead, behind = line_partners()
    greet(plane_partners() + (ahead, behind))
    post = Post(send_sems, recv_sems)
    go = post.go
    events, held = plane_gather_events(post, block, rows_all)
    events[0][1]()
    own_copy = pltpu.make_async_copy(block, stage.at[0], own_sem)
    own_copy.start()
    before_me, after_me = wrap(tp - 1), wrap(tp + 1)

    def up_part(place, rows=slice(None)):
        return at(both_full, rows, pl.ds(pl.multiple_of(512 + place * 128, 128), 128))

    def down_part(place, first=0, count=128):
        return at(down_full, pl.ds(pl.multiple_of(place * 128 + first, 64), count))

    up_near = (
        post.go(up, up_part(tp), ahead), post.go(up, up_part(tp), behind)
    )
    down_near = (
        post.go(down, down_part(tp), ahead), post.go(down, down_part(tp), behind)
    )
    up_top, up_bottom = up_part(before_me, pl.ds(0, 512)), up_part(after_me, pl.ds(512, 512))
    up_far = (
        post.prepare(up_top, up_top, ahead), post.prepare(up_bottom, up_bottom, behind)
    )
    down_top, down_bottom = down_part(before_me, 0, 64), down_part(after_me, 64, 64)
    down_far = (
        post.prepare(down_top, down_top, ahead), post.prepare(down_bottom, down_bottom, behind)
    )

    def relay(near, far):
        for one, other_one in zip(near, far, strict=True):
            one.wait_recv()
            other_one.start()

    weight_loads = [
        pltpu.make_async_copy(
            gate_all.at[part], both_full.at[:, part * 128 : (part + 1) * 128], weight_sems.at[part]
        )
        for part in range(4)
    ]
    weight_loads.append(pltpu.make_async_copy(up, up_part(tp)(), weight_sems.at[4]))
    weight_loads.append(pltpu.make_async_copy(down, down_part(tp)(), weight_sems.at[5]))
    for copy in weight_loads:
        copy.start()
    both_sum[...] = jnp.zeros_like(both_sum)
    down_sum[...] = jnp.zeros_like(down_sum)

    def blocks(step):
        first, second = STEPS[step]
        return (here[first], here[second], there[first], there[second])

    loads, crossing, stores = {}, {}, {}
    for step in range(len(STEPS)):
        slot = step % 2
        loads[step], stores[step] = [], []
        crossing[step] = [
            post.prepare(at(stage, part), at(other, slot, part), sibling) for part in range(2)
        ]
        for part, index in enumerate(blocks(step)):
            loads[step] += [
                Local(
                    at(rows_all, index), at(rows_in, slot, part), at(load_sems, slot, 0, part)
                ),
                Local(at(grads, index), at(grads_in, slot, part), at(load_sems, slot, 1, part)),
            ]
            stores[step].append(
                Local(at(out_stage, part), at(out_parts, index), at(store_sems, part))
            )

    def load(step):
        for place in STEPS[step]:
            held[place].wait_recv()
        for copy in loads[step]:
            copy.start()

    def take(step):
        for part, place in enumerate(STEPS[step]):
            crossing[step][part].wait_recv()
            add_rows(
                mine.at[place], [(mine.at[place], 0), (other.at[step % 2, part], 0)], 0, rows
            )
        if step + 2 < len(STEPS):
            pl.semaphore_signal(credit, inc=1, device_id=sibling, device_id_type=MESH)

    rows = a_far.shape[0]
    top, bottom = halves(a_far)
    high = top.size
    low = rows - high
    far_b, near_b = {}, {}

    def number_of(k, j):
        return ARRIVAL.index((OFFSETS[k], OFFSETS[j]))

    def slot_of(k, j):
        return mine.at[number_of(k, j)]

    def far_step(k):
        part = number_of(k, 0)
        far_b[k] = (
            go(at(mine, part, top), at(b_far, k, top), ahead_b),
            go(at(mine, part, bottom), at(b_far, k, bottom), behind_b),
        )

    def near_step(k):
        far = b_far.at[k]
        far_b[k][0].wait_recv()
        part = slot_of(k, 1)
        add_rows(part, [(part, 0), (far, 0)], 0, high)
        first = go(at(mine, number_of(k, 1)), at(b_near, 0, k), ahead_b)
        far_b[k][1].wait_recv()
        part = slot_of(k, 2)
        add_rows(part, [(part, high), (far, high)], high, low)
        near_b[k] = (first, go(at(mine, number_of(k, 2)), at(b_near, 1, k), behind_b))

    def before(step):
        for copy in loads[step]:
            copy.wait()

    def between(step):
        if step > 0:
            for copy in crossing[step - 1]:
                copy.wait_send()
            for copy in stores[step - 1]:
                copy.wait()
        onward({0: (4,), 1: (6,), 2: (7, 8, 9), 3: (10, 11)}.get(step, ()))
        if step + 1 < len(STEPS):
            load(step + 1)
        if step > 0:
            take(step - 1)
        if step == 4:
            far_step(2)
            far_step(3)
        if step == 5:
            far_step(0)
            far_step(1)
            near_step(3)
            near_step(2)
        if step == 6:
            near_step(0)
        if step == 7:
            near_step(1)

    def onward(numbers):
        for number in numbers:
            events[number][1]()

    def early(step):
        if step == 0:
            for copy in up_far + down_far:
                copy.wait_recv()

    def after(step):
        onward({0: (5,)}.get(step, ()))
        if step >= 2:
            pl.semaphore_wait(credit, 1)
        for copy in crossing[step] + stores[step]:
            copy.start()

    def at_step(step, task):
        for number in range(len(STEPS)):

            @pl.when(step == number)
            def _(number=number):
                task(number)

    def from_table(step, table):
        value = step * 0 + table[0]
        for number in range(1, len(table)):
            value = jnp.where(step == number, table[number], value)
        return value

    own_copy.wait()
    own_copy = pltpu.make_async_copy(stage.at[0], rows_all.at[me], own_sem)
    own_copy.start()
    onward((1, 2))
    own_copy.wait()
    load(0)
    relay(up_near, up_far)
    onward((3,))
    relay(down_near, down_far)
    for copy in weight_loads:
        copy.wait()
    extra_row = lax.broadcasted_iota(jnp.int32, (EXTRA, 1024), 0) == lane_row

    def one_step(step, carry):
        slot = lax.rem(step, 2)
        at_step(step, before)
        earlier = (
            lax.broadcasted_iota(jnp.int32, (256, 256), 0)
            <= lax.broadcasted_iota(jnp.int32, (256, 256), 1)
        ).astype(BF16)
        place = lax.broadcasted_iota(jnp.int32, (SLOTS, 256), 0).astype(F32)
        for part in range(GROUP):
            extras = jnp.where(extra_row, rows_in[slot, part, 256:, :].astype(F32), 0.0)
            extras = jnp.sum(extras, axis=0, keepdims=True)
            gates = jnp.where(
                upper, extras[:, 512:768] + extras[:, 768:], extras[:, :256] + extras[:, 256:512]
            )
            named = jnp.broadcast_to(gates, (16, 256)) > 0.0
            rank = jnp.dot(named.astype(BF16), earlier, preferred_element_type=F32)[:1] - 1.0
            chosen = (place == rank) & (gates > 0.0)
            chosen_low = chosen.astype(BF16)
            at = slice(part * SLOTS, (part + 1) * SLOTS)
            select[at, :] = chosen_low
            rows_own[at, :] = jnp.dot(
                chosen_low, rows_in[slot, part, :256, :], preferred_element_type=F32
            ).astype(BF16)
            grads_own[at, :] = jnp.dot(
                chosen_low, grads_in[slot, part], preferred_element_type=F32
            ).astype(BF16)
            gates_own[at, :] = jnp.sum(jnp.where(chosen, gates, 0.0), axis=1, keepdims=True)

        at_step(step, early)
        both_pre = jnp.dot(rows_own[...], both_full[...], preferred_element_type=F32)
        gate_pre, up_pre = both_pre[:, :512], both_pre[:, 512:]
        sigmoid = 1.0 / (1.0 + jnp.exp(-gate_pre))
        silu = gate_pre * sigmoid
        act = (silu * up_pre).astype(BF16)
        out = jnp.dot(act, down_full[...], preferred_element_type=F32).astype(BF16).astype(F32)
        gate_factor = gates_own[...]
        grads_float = grads_own[...].astype(F32)
        grad_gates[...] = jnp.sum(grads_float * out, axis=1, keepdims=True)
        weighted[...] = (gate_factor * out).astype(BF16)
        grad_out = (gate_factor * grads_float).astype(BF16)
        grad_act = lax.dot_general(
            grad_out, down_full[...], CONTRACT_LAST, preferred_element_type=F32
        )
        down_sum[...] += lax.dot_general(
            grad_out, act, CONTRACT_ROWS, preferred_element_type=F32
        )
        grad_gate_pre = grad_act * up_pre * sigmoid * (1.0 + gate_pre * (1.0 - sigmoid))
        grad_up_pre = grad_act * silu
        grad_pre = jnp.concatenate(
            [grad_gate_pre.astype(BF16), grad_up_pre.astype(BF16)], axis=1
        )
        both_sum[...] += lax.dot_general(
            rows_own[...], grad_pre, CONTRACT_ROWS, preferred_element_type=F32
        )
        grad_rows[...] = lax.dot_general(
            grad_pre, both_full[...], CONTRACT_LAST, preferred_element_type=F32
        ).astype(BF16)
        at_step(step, between)
        nothing = jnp.zeros((1, 512), F32)
        slots = [from_table(step, [pair[part] for pair in STEPS]) for part in range(2)]
        for part in range(GROUP):
            at = slice(part * SLOTS, (part + 1) * SLOTS)
            chosen_low = select[at, :]
            out_stage[part] = lax.dot_general(
                chosen_low, weighted[at], CONTRACT_ROWS, preferred_element_type=F32
            ).astype(BF16)
            target = mine.at[slots[part]] if part < 2 else stage.at[part - 2]
            target[:256, :] = lax.dot_general(
                chosen_low, grad_rows[at], CONTRACT_ROWS, preferred_element_type=F32
            ).astype(BF16)
            spread = jnp.sum(chosen_low.astype(F32) * grad_gates[at], axis=0, keepdims=True)
            upper_bits = spread.astype(BF16).astype(F32)
            both = jnp.concatenate([upper_bits, spread - upper_bits], axis=1)
            line_now = jnp.concatenate(
                [jnp.where(upper, nothing, both), jnp.where(upper, both, nothing)], axis=1
            )
            target[256:, :] = jnp.where(extra_row, line_now, 0.0).astype(BF16)
        at_step(step, after)
        return carry

    lax.fori_loop(0, len(STEPS), one_step, 0)
    last = len(STEPS) - 1

    def weight_steps():
        for part in range(4):
            yield 2.5 + part
            lanes = slice(part * 128, (part + 1) * 128)
            upper_lanes = slice(512 + part * 128, 512 + (part + 1) * 128)
            line[part, :1024, :] = both_sum[:, lanes].astype(BF16)
            line[part, 1024:2048, :] = both_sum[:, upper_lanes].astype(BF16)
            line[part, 2048:, :] = down_sum[:, lanes].astype(BF16)
            Local(at(line, part), at(weight_parts, part), at(weight_sems, part)).start()
        yield 100.0
        for part in range(4):
            Local(at(line, part), at(weight_parts, part), at(weight_sems, part)).wait()

    def back_steps():
        yield 0.0
        take(last)
        far_a, near_a = [], []
        for k in range(4):
            yield (2.0, 4.0, 8.0, 12.0)[k]
            part = slot_of(k, 3)
            near_b[k][0].wait_recv()
            near_b[k][1].wait_recv()
            base = [part, b_near.at[0, k], b_near.at[1, k]]
            first_rows = [(ref, 0) for ref in base]
            last_rows = [(ref, high) for ref in base]
            if k == 0:
                add_rows(part, first_rows, 0, high)
                add_rows(part, last_rows, high, low)
                far_a = [
                    go(part.at[top], a_far.at[top], ahead_a),
                    go(part.at[bottom], a_far.at[bottom], behind_a),
                ]
            elif k == 1:
                far_a[0].wait_recv()
                add_rows(part, first_rows + [(a_far, 0)], 0, high)
                add_rows(part, last_rows, high, low)
                near_a.append(go(part, a_near.at[0], ahead_a))
            elif k == 2:
                far_a[1].wait_recv()
                add_rows(part, first_rows, 0, high)
                add_rows(part, last_rows + [(a_far, high)], high, low)
                near_a.append(go(part, a_near.at[1], behind_a))
            else:
                near_a[0].wait_recv()
                near_a[1].wait_recv()
                add_rows(
                    back_sum, first_rows + [(a_near.at[0], 0), (a_near.at[1], 0)], 0, rows
                )

    together(back_steps(), weight_steps())
    for copy in stores[last]:
        copy.wait()
    waited = [copy for step in range(last) for copy in crossing[step]]
    for copy in post.started:
        if not any(copy is other_copy for other_copy in waited):
            copy.wait_send()


def run_experts(block, grads, gate_all, up, down, number):
    rows, columns = block.shape
    sources = grads.shape[0]
    count = GROUP * SLOTS
    copies = PLANE_COPIES + 16 + 8 + 8 + 4 + 2 * LINE_COPIES
    whole = (rows, columns)
    return pl.pallas_call(
        experts_kernel,
        out_shape=[
            jax.ShapeDtypeStruct((sources,) + whole, BF16),
            jax.ShapeDtypeStruct((sources, 256, columns), BF16),
            jax.ShapeDtypeStruct(whole, F32),
            jax.ShapeDtypeStruct((4, 3072, 128), BF16),
        ],
        in_specs=[ANY] * 5,
        out_specs=[ANY, ANY, VMEM, ANY],
        scratch_shapes=[
            pltpu.VMEM((2, GROUP) + whole, BF16),
            pltpu.VMEM((2, GROUP, 256, columns), BF16),
            pltpu.VMEM((1024, 1024), BF16),
            pltpu.VMEM((512, 1024), BF16),
            pltpu.VMEM((1024, 1024), F32),
            pltpu.VMEM((1024, 512), F32),
            pltpu.VMEM((count, 1024), BF16),
            pltpu.VMEM((count, 1024), BF16),
            pltpu.VMEM((count, 1), F32),
            pltpu.VMEM((count, 256), BF16),
            pltpu.VMEM((count, 1024), BF16),
            pltpu.VMEM((count, 1024), BF16),
            pltpu.VMEM((count, 1), F32),
            pltpu.VMEM((16,) + whole, BF16),
            pltpu.VMEM((2, 2) + whole, BF16),
            pltpu.VMEM((2,) + whole, BF16),
            pltpu.VMEM((GROUP, 256, columns), BF16),
            pltpu.VMEM((4,) + whole, BF16),
            pltpu.VMEM((2, 4) + whole, BF16),
            pltpu.VMEM(whole, BF16),
            pltpu.VMEM((2,) + whole, BF16),
            pltpu.VMEM((4, 3072, 128), BF16),
            pltpu.SemaphoreType.DMA((copies,)),
            pltpu.SemaphoreType.DMA((copies,)),
            pltpu.SemaphoreType.REGULAR,
            pltpu.SemaphoreType.DMA((2, 2, GROUP)),
            pltpu.SemaphoreType.DMA((GROUP,)),
            pltpu.SemaphoreType.DMA((12,)),
            pltpu.SemaphoreType.DMA,
        ],
        compiler_params=pltpu.CompilerParams(
            collective_id=number, has_side_effects=True, vmem_limit_bytes=63 << 20
        ),
        name="run_experts",
    )(block, grads, gate_all, up, down)


def rotary_constants():
    position = np.arange(SEQ_LEN, dtype=np.float32)
    power = -(np.arange(32, dtype=np.float32) * np.float32(2.0)) / np.float32(64.0)
    frequency = np.float32(10000.0) ** power
    angles = position[:, None] * frequency[None, :]
    cosine, sine = np.cos(angles), np.sin(angles)
    return (np.tile(cosine, (1, 4)), np.concatenate([-sine, sine, -sine, sine], axis=1))


def shards(
    inputs,
    first_gain,
    query_weight,
    key_weight,
    value_weight,
    query_gain,
    key_gain,
    output_weight,
    second_gain,
    router_weight,
    gate_weight,
    up_weight,
    down_weight,
    segments,
    live_mask,
    routes,
    cotangent,
):
    gain_one, gain_two = first_gain.reshape(8, 128), second_gain.reshape(8, 128)
    query_scale, key_scale = query_gain.reshape(1, -1), key_gain.reshape(1, -1)
    cosine, sine = rotary_constants()
    seg_row, live_row = segments.reshape(1, -1), live_mask.reshape(1, -1)
    router = router_weight.T
    (
        normed, raw, query, keys, values, mixed, residual, block, gates, grad_all, gate_all,
    ) = opening(
        (
            inputs, gain_one, query_weight, key_weight, value_weight, query_scale, key_scale,
            cosine, sine, seg_row, live_row, output_weight, gain_two, router, routes.T,
            cotangent, gate_weight[0],
        ),
        1,
    )
    rows_all, out_parts, back, weight_parts = run_experts(
        block, grad_all, gate_all, up_weight[0], down_weight[0], 2
    )
    grad_inputs, dense, small, combined, weight_sums = closing(
        (
            back, residual, gates, cotangent, gain_two, router, query, keys, values, mixed,
            output_weight, query_weight, key_weight, value_weight, raw, normed.reshape(1024, 1024),
            inputs, gain_one, query_scale, key_scale, cosine, sine, seg_row,
            live_row, out_parts, weight_parts,
        ),
        4,
    )
    (
        result, grad_inputs, grad_query, grad_key, grad_value, grad_output, grad_gate, grad_up,
        grad_down, grad_gain_one, grad_gain_two, grad_query_gain, grad_key_gain, grad_router,
    ) = finish_all(
        (
            dense.reshape(1024, 768), weight_sums, residual, combined,
            small.reshape(32, SMALL_ROWS, 128), grad_inputs,
        )
    )
    return (
        result,
        grad_inputs,
        grad_gain_one.reshape(-1),
        grad_query,
        grad_key,
        grad_value,
        grad_query_gain.reshape(-1),
        grad_key_gain.reshape(-1),
        grad_output,
        grad_gain_two.reshape(-1),
        grad_router.T,
        grad_gate,
        grad_up,
        grad_down,
    )


def solution(mesh):
    return jax.shard_map(
        shards,
        mesh=mesh,
        in_specs=(
            P(("ep", "tp"), None),
            P(),
            P(None, "tp"),
            P(None, "tp"),
            P(None, "tp"),
            P(),
            P(),
            P("tp", None),
            P(),
            P(),
            P("ep", None, "tp"),
            P("ep", None, "tp"),
            P("ep", "tp", None),
            P("ep"),
            P("ep"),
            P(("ep", "tp"), None),
            P(("ep", "tp"), None),
        ),
        out_specs=(
            P(("ep", "tp"), None),
            P(("ep", "tp"), None),
            P(),
            P(None, "tp"),
            P(None, "tp"),
            P(None, "tp"),
            P(),
            P(),
            P("tp", None),
            P(),
            P(),
            P("ep", None, "tp"),
            P("ep", None, "tp"),
            P("ep", "tp", None),
        ),
        check_vma=False,
    )
```

```python
import jax
import jax.numpy as jnp
import numpy as np
from jax import lax
from jax.experimental import pallas as pl
from jax.experimental.pallas import tpu as pltpu
from jax.sharding import PartitionSpec as P

SEQ_LEN = 1024
HIGHEST_PRECISION = lax.Precision.HIGHEST
CONTRACT_ROWS = (((0,), (0,)), ((), ()))
CONTRACT_LAST = (((1,), (1,)), ((), ()))
MESH = pl.DeviceIdType.MESH
ANY = pl.BlockSpec(memory_space=pl.ANY)
VMEM = pl.BlockSpec(memory_space=pltpu.VMEM)
F32 = jnp.float32
BF16 = jnp.bfloat16
SLOTS = 96
EXTRA = 16


def wrap(value):
    return lax.rem(value + 4, 4)


def pick(core, first, second):
    return first * (1 - core) + second * core


def plane_place():
    ep = lax.axis_index("ep")
    core = lax.rem(ep, 2)
    z = lax.rem(lax.div(ep, 2), 4)
    x = lax.div(ep, 8)
    return (pick(core, x, z), pick(core, z, x), core)


def plane_index(a, b, core):
    a, b = wrap(a), wrap(b)
    return (pick(core, a, b) * 4 + pick(core, b, a)) * 2 + core


def plane_partners():
    a, b, core = plane_place()
    tp = lax.axis_index("tp")
    return (
        (plane_index(a + 1, b, core), tp),
        (plane_index(a - 1, b, core), tp),
        (plane_index(a, b + 1, core), tp),
        (plane_index(a, b - 1, core), tp),
        (plane_index(b, a, 1 - core), tp),
    )


def line_partners():
    ep, tp = lax.axis_index("ep"), lax.axis_index("tp")
    return ((ep, wrap(tp + 1)), (ep, wrap(tp - 1)))


def greet(partners):
    barrier = pltpu.get_barrier_semaphore()
    for partner in partners:
        pl.semaphore_signal(barrier, inc=1, device_id=partner, device_id_type=MESH)
    pl.semaphore_wait(barrier, len(partners))


def halves(ref):
    unit = 16 if ref.dtype == BF16 else 8
    rows = ref.shape[-2]
    top = (rows // 2 + unit - 1) // unit * unit
    return (pl.ds(0, top), pl.ds(top, rows - top))


def together(*tasks):
    waiting = [(0.0, number, task) for number, task in enumerate(tasks)]
    while waiting:
        waiting.sort(key=lambda entry: entry[:2])
        _, number, task = waiting.pop(0)
        due = next(task, None)
        if due is not None:
            waiting.append((due, number, task))


def resumed(due, task):
    yield due
    yield from task


def side_by_side(*tasks):
    waiting = [(due, number, task) for number, (due, task) in enumerate(tasks)]
    while waiting:
        waiting.sort(key=lambda entry: entry[:2])
        due, number, task = waiting.pop(0)
        yield due
        due = next(task, None)
        if due is not None:
            waiting.append((due, number, task))


class Clock:
    def __init__(self, now=0.0):
        self.now = now

    def spend(self, amount):
        self.now += amount
        return self.now

    def until(self, moment):
        self.now = max(self.now, moment)
        return self.now


def at(ref, *where):
    return lambda: ref.at[where]


def part_of(place):
    return place() if callable(place) else place


class Remote:
    def __init__(self, src, dst, send_sem, recv_sem, partner):
        self.all = (src, dst, send_sem, recv_sem, partner)

    def copy(self):
        src, dst, send_sem, recv_sem, partner = self.all
        return pltpu.make_async_remote_copy(
            src_ref=part_of(src),
            dst_ref=part_of(dst),
            send_sem=part_of(send_sem),
            recv_sem=part_of(recv_sem),
            device_id=partner,
            device_id_type=MESH,
        )

    def start(self):
        self.copy().start()

    def wait_send(self):
        self.copy().wait_send()

    def wait_recv(self):
        self.copy().wait_recv()


class Local:
    def __init__(self, src, dst, sem):
        self.all = (src, dst, sem)

    def start(self):
        pltpu.make_async_copy(*map(part_of, self.all)).start()

    def wait(self):
        pltpu.make_async_copy(*map(part_of, self.all)).wait()


class Post:
    def __init__(self, send_sems, recv_sems):
        self.send_sems, self.recv_sems, self.started = send_sems, recv_sems, []

    def go(self, src, dst, partner):
        copy = self.prepare(src, dst, partner)
        copy.start()
        return copy

    def prepare(self, src, dst, partner):
        number = len(self.started)
        copy = Remote(src, dst, at(self.send_sems, number), at(self.recv_sems, number), partner)
        self.started.append(copy)
        return copy

    def finish(self):
        for copy in self.started:
            copy.wait_send()


ARRIVAL = (
    (0, 0), (-1, 0), (1, 0), (0, -1), (0, 1), (2, 0), (-1, -1), (-1, 1),
    (1, -1), (1, 1), (2, -1), (2, 1), (0, 2), (-1, 2), (1, 2), (2, 2),
)


def plane_gather_events(post, own_ref, all_ref):
    a, b, core = plane_place()
    ahead_a, behind_a, ahead_b, behind_b, sibling = plane_partners()
    index = {place: plane_index(a + place[0], b + place[1], core) for place in ARRIVAL}
    top, bottom = halves(own_ref)

    def block(place):
        return own_ref if place == (0, 0) else at(all_ref, index[place])

    def copy(place, partner):
        return post.prepare(block(place), at(all_ref, index[place]), partner)

    def half_copy(place, half, partner):
        part = at(all_ref, index[place], half)
        return post.prepare(part, part, partner)

    a_copies = (copy((0, 0), ahead_a), copy((0, 0), behind_a))
    a_halves = (half_copy((-1, 0), top, ahead_a), half_copy((1, 0), bottom, behind_a))
    column = (0, -1, 1, 2)
    b_copies = [(copy((k, 0), ahead_b), copy((k, 0), behind_b)) for k in column]
    b_halves = [
        (half_copy((k, -1), top, ahead_b), half_copy((k, 1), bottom, behind_b)) for k in column
    ]
    crossing = [copy(place, sibling) for place in ARRIVAL]

    def start(*copies):
        for one in copies:
            one.start()

    def begin():
        start(*a_copies, *b_copies[0], crossing[0])

    def near_a(number):
        a_copies[number].wait_recv()
        start(a_halves[number], *b_copies[1 + number], crossing[1 + number])

    def far_a():
        a_halves[0].wait_recv()
        a_halves[1].wait_recv()
        start(*b_copies[3], crossing[5])

    def near_b(k):
        first = ARRIVAL.index((column[k], -1))
        for number in range(2):
            b_copies[k][number].wait_recv()
            start(b_halves[k][number], crossing[first + number])

    def far_b(k):
        b_halves[k][0].wait_recv()
        b_halves[k][1].wait_recv()
        start(crossing[12 + k])

    events = [
        (0.0, begin),
        (6.5, lambda: near_a(0)),
        (6.5, lambda: near_a(1)),
        (7.5, lambda: near_b(0)),
        (11.0, far_a),
        (15.0, lambda: near_b(1)),
        (21.0, lambda: near_b(2)),
        (24.0, lambda: far_b(0)),
        (28.0, lambda: near_b(3)),
        (32.0, lambda: far_b(1)),
        (40.0, lambda: far_b(2)),
        (44.0, lambda: far_b(3)),
    ]
    return (events, crossing)


def plane_gather_steps(post, own_ref, all_ref):
    events, crossing = plane_gather_events(post, own_ref, all_ref)
    for due, event in events:
        if due > 0.0:
            yield due
        event()
    yield 46.0
    for copy in crossing:
        copy.wait_recv()


PLANE_COPIES = 36


def add_rows(dst, sources, start, rows):
    step = 16 if rows % 16 == 0 else 8

    @pl.loop(0, rows // step)
    def _(i):
        at = pl.multiple_of(i * step, step)
        total = None
        for ref, first in sources:
            part = ref[pl.ds(first + at, step), :].astype(F32)
            total = part if total is None else total + part
        dst[pl.ds(start + at, step), :] = total.astype(dst.dtype)


def plane_scatter_steps(post, parts_ref, sum_ref, scratch, begin=0.0):
    mine, other, b_far, b_near, a_far, a_near, local_sems = scratch
    a, b, core = plane_place()
    ahead_a, behind_a, ahead_b, behind_b, sibling = plane_partners()
    rows = a_far.shape[0]
    top, bottom = halves(a_far)
    high = top.size
    low = rows - high
    offsets = (2, 1, -1, 0)
    go = post.go
    crossing = {}
    order = [(k, 0) for k in range(4)] + [(k, j) for k in range(4) for j in (1, 2)]
    order += [(k, 3) for k in range(4)]
    for k, j in order:
        there = plane_index(b + offsets[k], a + offsets[j], 1 - core)
        crossing[k, j] = go(parts_ref.at[there], other.at[k, j], sibling)
    slots = mine.shape[0]
    loads = []

    def load():
        number = len(loads)
        if number < len(order):
            k, j = order[number]
            here = plane_index(a + offsets[k], b + offsets[j], core)
            slot = number % slots
            copy = pltpu.make_async_copy(
                parts_ref.at[here], mine.at[slot], local_sems.at[slot]
            )
            copy.start()
            loads.append(copy)

    for _ in range(slots - 1):
        load()

    def ready(k, j):
        number = order.index((k, j))
        load()
        crossing[k, j].wait_recv()
        loads[number].wait()
        return (other.at[k, j], mine.at[number % slots])

    far_b, near_b = {}, {}
    for k in range(4):
        yield begin + 2.0 + 1.5 * k
        block, extra = ready(k, 0)
        add_rows(block, [(block, 0), (extra, 0)], 0, rows)
        far_b[k] = (
            go(block.at[top], b_far.at[k, top], ahead_b),
            go(block.at[bottom], b_far.at[k, bottom], behind_b),
        )
    for k in range(4):
        far = b_far.at[k]
        yield begin + 9.0 + 3.0 * k
        block, extra = ready(k, 1)
        far_b[k][0].wait_recv()
        add_rows(block, [(block, 0), (extra, 0), (far, 0)], 0, high)
        add_rows(block, [(block, high), (extra, high)], high, low)
        first = go(block, b_near.at[0, k], ahead_b)
        block, extra = ready(k, 2)
        far_b[k][1].wait_recv()
        add_rows(block, [(block, 0), (extra, 0)], 0, high)
        add_rows(block, [(block, high), (extra, high), (far, high)], high, low)
        near_b[k] = (first, go(block, b_near.at[1, k], behind_b))
    far_a, near_a = [], []
    for k in range(4):
        yield begin + (25.0, 31.0, 37.0, 45.0)[k]
        block, extra = ready(k, 3)
        near_b[k][0].wait_recv()
        near_b[k][1].wait_recv()
        base = [block, extra, b_near.at[0, k], b_near.at[1, k]]
        upper = [(ref, 0) for ref in base]
        lower = [(ref, high) for ref in base]
        if k == 0:
            add_rows(block, upper, 0, high)
            add_rows(block, lower, high, low)
            far_a = [
                go(block.at[top], a_far.at[top], ahead_a),
                go(block.at[bottom], a_far.at[bottom], behind_a),
            ]
        elif k == 1:
            far_a[0].wait_recv()
            add_rows(block, upper + [(a_far, 0)], 0, high)
            add_rows(block, lower, high, low)
            near_a.append(go(block, a_near.at[0], ahead_a))
        elif k == 2:
            far_a[1].wait_recv()
            add_rows(block, upper, 0, high)
            add_rows(block, lower + [(a_far, high)], high, low)
            near_a.append(go(block, a_near.at[1], behind_a))
        else:
            near_a[0].wait_recv()
            near_a[1].wait_recv()
            add_rows(sum_ref, upper + [(a_near.at[0], 0), (a_near.at[1], 0)], 0, rows)


def plane_scatter_scratch(rows, columns, kind):
    return [
        pltpu.VMEM((4, rows, columns), kind),
        pltpu.VMEM((4, 4, rows, columns), kind),
        pltpu.VMEM((4, rows, columns), kind),
        pltpu.VMEM((2, 4, rows, columns), kind),
        pltpu.VMEM((rows, columns), kind),
        pltpu.VMEM((2, rows, columns), kind),
        pltpu.SemaphoreType.DMA((4,)),
    ]


OFFSETS = (2, 1, -1, 0)


def ring_places(a, b, core, tp):
    along_a = [(plane_index(a + offset, b, core), tp) for offset in OFFSETS[:3]]
    along_b = [(plane_index(a, b + offset, core), tp) for offset in OFFSETS[:3]]
    return (along_a, along_b, (plane_index(b, a, 1 - core), tp))


def brief_partners():
    along_a, along_b, sibling = ring_places(*plane_place(), lax.axis_index("tp"))
    return tuple(along_a + along_b + [sibling])


BRIEF_COPIES = 1 + 3 + 3


def brief_number(number):
    return (number // 16, number // 4 % 4, number % 4)


def brief_scatter_steps(post, parts_ref, sum_ref, scratch, begin=0.0):
    other, from_b, total, from_a = scratch
    a, b, core = plane_place()
    along_a, along_b, sibling = ring_places(a, b, core, lax.axis_index("tp"))
    crossing = post.go(at(parts_ref, 1 - core), other, sibling)
    yield begin + 3.0
    crossing.wait_recv()
    for i in range(4):
        other[i] = (other[i].astype(F32) + parts_ref[core, i].astype(F32)).astype(other.dtype)
    copies = [
        post.go(at(other, slice(None), wrap(b + OFFSETS[j])), at(from_b, j), along_b[j])
        for j in range(3)
    ]
    yield begin + 8.0
    for copy in copies:
        copy.wait_recv()
    for i in range(4):
        part = other[i, b].astype(F32)
        for j in range(3):
            part = part + from_b[j, i].astype(F32)
        total[i] = part.astype(total.dtype)
    copies = [
        post.go(at(total, wrap(a + OFFSETS[j])), at(from_a, j), along_a[j]) for j in range(3)
    ]
    yield begin + 11.0
    part = total[a].astype(F32)
    for j in range(3):
        copies[j].wait_recv()
        part = part + from_a[j].astype(F32)
    sum_ref[...] = part.astype(sum_ref.dtype)


def brief_scatter_scratch(rows, columns, kind):
    return [
        pltpu.VMEM((4, 4, rows, columns), kind),
        pltpu.VMEM((3, 4, rows, columns), kind),
        pltpu.VMEM((4, rows, columns), kind),
        pltpu.VMEM((3, rows, columns), kind),
    ]


def brief_gather_steps(post, own_ref, all_ref, begin=0.0):
    a, b, core = plane_place()
    along_a, along_b, sibling = ring_places(a, b, core, lax.axis_index("tp"))
    all_ref[core, a, b] = own_ref[...]
    copies = [post.go(own_ref, at(all_ref, core, a, b), place) for place in along_a]
    yield begin + 3.0
    for copy in copies:
        copy.wait_recv()
    line = at(all_ref, core, slice(None), b)
    copies = [post.go(line, line, place) for place in along_b]
    yield begin + 8.0
    for copy in copies:
        copy.wait_recv()
    crossing = post.go(at(all_ref, core), at(all_ref, core), sibling)
    yield begin + 11.0
    crossing.wait_recv()


LINE_COPIES = 4


def line_gather_steps(post, own_ref, all_ref, clock, near_time, far_time, arrived=None):
    tp = lax.axis_index("tp")
    ahead, behind = line_partners()
    top, bottom = halves(own_ref)
    before, after, far = wrap(tp - 1), wrap(tp + 1), wrap(tp + 2)
    begin = clock.now
    first = post.go(own_ref, all_ref.at[tp], ahead)
    second = post.go(own_ref, all_ref.at[tp], behind)
    if arrived is not None:
        yield from arrived(tp)
    yield clock.until(begin + near_time)
    first.wait_recv()
    third = post.go(all_ref.at[before, top], all_ref.at[before, top], ahead)
    second.wait_recv()
    fourth = post.go(all_ref.at[after, bottom], all_ref.at[after, bottom], behind)
    if arrived is not None:
        yield from arrived(before)
        yield from arrived(after)
    yield clock.until(begin + far_time)
    third.wait_recv()
    fourth.wait_recv()
    if arrived is not None:
        yield from arrived(far)


def line_scatter_steps(post, make, far, near, finish, clock, far_time, near_time):
    ahead, behind = line_partners()
    top, bottom = halves(far)
    high = top.size
    rows = far.shape[0]
    block = yield from make(2)
    begin = clock.now
    first = post.go(block.at[top], far.at[top], ahead)
    second = post.go(block.at[bottom], far.at[bottom], behind)
    block = yield from make(1)
    yield clock.until(begin + far_time)
    first.wait_recv()
    add_rows(block, [(block, 0), (far, 0)], 0, high)
    third = post.go(block, near.at[0], ahead)
    other = yield from make(-1)
    second.wait_recv()
    add_rows(other, [(other, high), (far, high)], high, rows - high)
    fourth = post.go(other, near.at[1], behind)
    begin = clock.now
    own = yield from make(0)
    yield clock.until(begin + near_time)
    third.wait_recv()
    fourth.wait_recv()
    finish(own, near.at[0], near.at[1])


def split_float(values):
    high = values.astype(BF16)
    return (high, (values - high.astype(F32)).astype(BF16))


def split_three(values):
    high = values.astype(BF16)
    rest = values - high.astype(F32)
    middle = rest.astype(BF16)
    return (high, middle, (rest - middle.astype(F32)).astype(BF16))


def head_mean(values):
    same = (
        lax.broadcasted_iota(jnp.int32, (128, 128), 0) // 64
        == lax.broadcasted_iota(jnp.int32, (128, 128), 1) // 64
    ).astype(BF16)
    high, low = split_float(values)
    total = jnp.dot(high, same, preferred_element_type=F32)
    total = total + jnp.dot(low, same, preferred_element_type=F32)
    return total * (1.0 / 64.0)


def other_half(values):
    lane = lax.broadcasted_iota(jnp.int32, values.shape, 1)
    return jnp.where(
        lax.rem(lane, 64) < 32, pltpu.roll(values, 96, 1), pltpu.roll(values, 32, 1)
    )


def head_ready(raw, gain, cosine, sine):
    normed = raw * lax.rsqrt(head_mean(raw * raw) + 1e-06) * gain
    return normed * cosine + other_half(normed) * sine


def head_back(grad, raw, gain, cosine, sine):
    grad = grad * cosine + other_half(grad * sine)
    scale = lax.rsqrt(head_mean(raw * raw) + 1e-06)
    plain = raw * scale
    grad_gain = jnp.sum(grad * plain, axis=0, keepdims=True)
    grad = grad * gain
    return (scale * (grad - plain * head_mean(grad * plain)), grad_gain)


def wide(gain):
    gain = gain.astype(F32)
    return jnp.concatenate([gain[part : part + 1] for part in range(8)], axis=1)


def both_heads(gain):
    gain = gain.astype(F32)
    return jnp.concatenate([gain, gain], axis=1)


def row_scale(values):
    return lax.rsqrt(jnp.mean(values * values, axis=1, keepdims=True) + 1e-05)


def exchange(values):
    return jnp.concatenate([values[:, 64:], values[:, :64]], axis=1)


def head_pairs(block):
    rows = block.shape[0]
    low = lax.broadcasted_iota(jnp.int32, (rows, 128), 1) < 64
    left, right = block[:, :128], block[:, 128:]
    zero = jnp.zeros_like(left)
    straight = jnp.concatenate([jnp.where(low, left, zero), jnp.where(low, zero, right)], axis=0)
    crossed = jnp.concatenate([jnp.where(low, zero, left), jnp.where(low, right, zero)], axis=0)
    return (straight, crossed)


def heads_back(straight, crossed):
    rows = straight.shape[0] // 2
    low = lax.broadcasted_iota(jnp.int32, (rows, 128), 1) < 64
    left = jnp.where(low, straight[:rows], crossed[:rows])
    right = jnp.where(low, crossed[rows:], straight[rows:])
    return jnp.concatenate([left, right], axis=1)


def attend_block(query, keys, values, bias, clock):
    rows = query.shape[0]
    outs = []
    for pair, key_part, value_part in zip(
        head_pairs(query), (keys, exchange(keys)), (values, exchange(values)), strict=True
    ):
        halves_out = []
        for number in range(2):
            part = pair[number * rows : (number + 1) * rows]
            scores = lax.dot_general(part, key_part, CONTRACT_LAST, preferred_element_type=F32)
            weights = jnp.exp(scores * 0.125 + bias)
            total_weight = jnp.sum(weights, axis=1, keepdims=True)
            out = jnp.dot(weights.astype(BF16), value_part, preferred_element_type=F32)
            halves_out.append(out / total_weight)
            yield clock.spend(0.45)
        outs.append(jnp.concatenate(halves_out, axis=0))
    return heads_back(*outs).astype(BF16)


def document_bounds(segments, live_mask):
    one = jnp.ones_like(segments)
    zero = jnp.zeros_like(segments)

    def count(chosen):
        return jnp.sum(jnp.where(chosen, one, zero), axis=1, keepdims=True)

    return (count(segments < 1), count(segments < 2), count(live_mask == 1))


def score_bias(bounds, query, key):
    first, second, living = bounds

    def document(position):
        return (position >= first).astype(jnp.int32) + (position >= second).astype(jnp.int32)

    seen = jnp.where(key < living, 1, 0)
    same = document(query) == document(key)
    return jnp.where(same & ((seen == 1) | (query == key)), 0.0, -1e30).astype(F32)


def block_rows(block):
    return pl.ds(pl.multiple_of(block * 256, 256), 256)


def opening_kernel(
    inputs, gain_one, query_weight, key_weight, value_weight, query_gain, key_gain, cosine, sine,
    segments, live_mask, output_weight, gain_two, router, routes, cotangent,
    gate,
    normed_out, raw_out, query_out, keys_out, values_out, mixed_out,
    residual, block, gates, grad_all, gate_all,
    normed, raw, query, keys, values, mixed,
    parts, far, near, hold, send_sems, recv_sems, local_sems, out_sems,
):
    tp = lax.axis_index("tp")
    own_parts = (
        (cotangent, parts.at[0], grad_all.at[lax.axis_index("ep")]),
        (gate, hold, gate_all.at[tp]),
    )
    inward = [
        pltpu.make_async_copy(src, through, local_sems.at[number])
        for number, (src, through, _) in enumerate(own_parts)
    ]
    outward = [
        pltpu.make_async_copy(through, dst, local_sems.at[number])
        for number, (_, through, dst) in enumerate(own_parts)
    ]
    for copy in inward:
        copy.start()
    greet(plane_partners() + line_partners())
    post = Post(send_sems, recv_sems)
    clock = Clock()
    bounds = document_bounds(segments[...], live_mask[...])

    def project(place):
        rows = block_rows(place)
        part = normed[place]
        cos, sin = cosine[rows, :], sine[rows, :]
        both = jnp.dot(part, query_weight[...], preferred_element_type=F32)
        raw[rows, :256] = both
        for lanes in (slice(0, 128), slice(128, 256)):
            query[rows, lanes] = head_ready(both[:, lanes], both_heads(query_gain[...]), cos, sin).astype(BF16)
        one = jnp.dot(part, key_weight[...], preferred_element_type=F32)
        raw[rows, 256:] = one
        keys[rows, :] = head_ready(one, both_heads(key_gain[...]), cos, sin).astype(BF16)
        values[rows, :] = jnp.dot(part, value_weight[...], preferred_element_type=F32).astype(BF16)
        yield clock.spend(1.5)

    def make(offset):
        place = wrap(tp + offset)
        rows = block_rows(place)
        bias = score_bias(
            bounds,
            place * 256 + lax.broadcasted_iota(jnp.int32, (256, 1), 0),
            lax.broadcasted_iota(jnp.int32, (1, 1024), 1),
        )
        out = yield from attend_block(query[rows, :], keys[...], values[...], bias, clock)
        mixed[rows, :] = out
        part = parts.at[(2, 1, -1, 0).index(offset)]
        part[...] = jnp.dot(out, output_weight[...], preferred_element_type=F32).astype(BF16)
        yield clock.spend(0.4)
        return part

    results = [
        pltpu.make_async_copy(src, dst, out_sems.at[number])
        for number, (src, dst) in enumerate(
            (
                (normed, normed_out), (raw, raw_out), (query, query_out), (keys, keys_out),
                (values, values_out), (mixed, mixed_out),
            )
        )
    ]

    def finish(own, first, second):
        results[5].start()
        total = own[...].astype(F32) + first[...].astype(F32) + second[...].astype(F32)
        total = inputs[...].astype(F32) + total
        residual[...] = total
        normed_two = total * row_scale(total) * wide(gain_two[...])
        block[:256, :] = normed_two.astype(BF16)
        logits = jnp.zeros((32, 256), F32)
        for piece in split_three(normed_two):
            logits = logits + lax.dot_general(
                router[...], piece, CONTRACT_LAST, preferred_element_type=F32
            )
        expert = lax.broadcasted_iota(jnp.int32, (32, 256), 0)
        named = expert < 0
        for choice in range(8):
            named = named | (routes[choice : choice + 1, :] == expert)
        top_logit = jnp.max(jnp.where(named, logits, -1e30), axis=0, keepdims=True)
        raised = jnp.where(named, jnp.exp(jnp.where(named, logits - top_logit, 0.0)), 0.0)
        probs = raised / jnp.sum(raised, axis=0, keepdims=True)
        gates[...] = probs
        high, low = split_float(probs)
        block[256:, :] = jnp.concatenate([high[:16], low[:16], high[16:], low[16:]], axis=1)

    def attention_steps():
        hidden = inputs[...].astype(F32)
        normed[tp] = (hidden * row_scale(hidden) * wide(gain_one[...])).astype(BF16)
        for copy, onward in zip(inward, outward, strict=True):
            copy.wait()
            onward.start()
        clock.spend(1.0)
        yield from line_gather_steps(post, normed.at[tp], normed, clock, 11.5, 17.5, project)
        for copy in outward:
            copy.wait()
        for copy in results[:5]:
            copy.start()
        yield from line_scatter_steps(post, make, far, near, finish, clock, 5.0, 22.0)

    def weight_steps(own, everyone, begin, near_time, far_time):
        yield begin
        yield from line_gather_steps(post, own, everyone, Clock(begin), near_time, far_time)

    together(
        attention_steps(),
        plane_gather_steps(post, cotangent, grad_all),
        weight_steps(gate, gate_all, 20.5, 22.0, 32.0),
    )
    post.finish()
    for copy in results:
        copy.wait()


def opening(arguments, number):
    count = 3 * LINE_COPIES + PLANE_COPIES
    return pl.pallas_call(
        opening_kernel,
        out_shape=[
            jax.ShapeDtypeStruct((4, 256, 1024), BF16),
            jax.ShapeDtypeStruct((1024, 384), F32),
            jax.ShapeDtypeStruct((1024, 256), BF16),
            jax.ShapeDtypeStruct((1024, 128), BF16),
            jax.ShapeDtypeStruct((1024, 128), BF16),
            jax.ShapeDtypeStruct((1024, 256), BF16),
            jax.ShapeDtypeStruct((256, 1024), F32),
            jax.ShapeDtypeStruct((256 + EXTRA, 1024), BF16),
            jax.ShapeDtypeStruct((32, 256), F32),
            jax.ShapeDtypeStruct((32, 256, 1024), BF16),
            jax.ShapeDtypeStruct((4, 1024, 128), BF16),
        ],
        in_specs=[VMEM] * (len(arguments) - 2) + [ANY] * 2,
        out_specs=[ANY] * 6 + [VMEM] * 3 + [ANY] * 2,
        scratch_shapes=[
            pltpu.VMEM((4, 256, 1024), BF16),
            pltpu.VMEM((1024, 384), F32),
            pltpu.VMEM((1024, 256), BF16),
            pltpu.VMEM((1024, 128), BF16),
            pltpu.VMEM((1024, 128), BF16),
            pltpu.VMEM((1024, 256), BF16),
            pltpu.VMEM((4, 256, 1024), BF16),
            pltpu.VMEM((256, 1024), BF16),
            pltpu.VMEM((2, 256, 1024), BF16),
            pltpu.VMEM((1024, 128), BF16),
            pltpu.SemaphoreType.DMA((count,)),
            pltpu.SemaphoreType.DMA((count,)),
            pltpu.SemaphoreType.DMA((2,)),
            pltpu.SemaphoreType.DMA((6,)),
        ],
        compiler_params=pltpu.CompilerParams(
            collective_id=number, has_side_effects=True, vmem_limit_bytes=56 << 20
        ),
        name="opening",
    )(*arguments)


def attend_back_block(query, grad, keys, values, bias, keys_sum, values_sum, clock):
    query_pairs = head_pairs(query)
    grad_pairs = head_pairs(grad)
    key_parts = (keys, exchange(keys))
    value_parts = (values, exchange(values))
    outs = []
    bias = jnp.concatenate([bias, bias], axis=1)
    for side in range(2):
        part, grad_part = query_pairs[side], grad_pairs[side]
        scores = lax.dot_general(key_parts[side], part, CONTRACT_LAST, preferred_element_type=F32)
        raised = jnp.exp(scores * 0.125 + bias)
        weights = raised * (1.0 / jnp.sum(raised, axis=0, keepdims=True))
        grad_weights = lax.dot_general(
            value_parts[side], grad_part, CONTRACT_LAST, preferred_element_type=F32
        )
        inner = jnp.sum(weights * grad_weights, axis=0, keepdims=True)
        grad_scores = (weights * (grad_weights - inner)).astype(BF16)
        outs.append(
            lax.dot_general(
                grad_scores, key_parts[side], CONTRACT_ROWS, preferred_element_type=F32
            )
        )
        keys_sum[side] += jnp.dot(grad_scores, part, preferred_element_type=F32)
        values_sum[side] += jnp.dot(weights.astype(BF16), grad_part, preferred_element_type=F32)
        yield clock.spend(2.3)
    return heads_back(*outs) * 0.125


SMALL_ROWS = 16
WEIGHTS_AT = 20.0


def closing_kernel(
    back, residual, gates, cotangent, gain_two, router, query_far, keys_far, values_far, mixed_far,
    output_weight_far, query_weight_far, key_weight_far, value_weight_far, raw_far, normed_far,
    inputs_far, gain_one, query_gain, key_gain, cosine_far, sine_far, segments, live_mask,
    out_parts, weight_parts, grad_inputs, dense_all, small_all, result, weight_sum,
    grad_all, grad_residual, low, keys_sum, values_sum, output_sum, parts, far, near,
    dense, dense_own, small, small_own, small_early, small_late, small_total, query_gain_sum,
    weights, weights_far, weights_near, query, keys, values, mixed, query_weight, key_weight, value_weight, raw, normed, inputs,
    output_weight, cosine, sine, combined, late_sems, *rest,
):
    out_scratch, dense_scratch, small_scratch = rest[:7], rest[7:11], rest[11:15]
    post = Post(rest[15], rest[16])
    me = lax.axis_index("ep")
    tp = lax.axis_index("tp")
    ahead, behind = line_partners()
    across = (me, wrap(tp + 2))
    late = [
        pltpu.make_async_copy(src, dst, late_sems.at[number])
        for number, (src, dst) in enumerate(
            (
                (query_far, query), (keys_far, keys), (values_far, values), (mixed_far, mixed),
                (query_weight_far, query_weight), (key_weight_far, key_weight),
                (value_weight_far, value_weight), (raw_far, raw), (normed_far, normed),
                (inputs_far, inputs),
                (output_weight_far, output_weight),
                (cosine_far, cosine),
                (sine_far, sine),
                (weight_parts.at[wrap(tp + 1)], weights.at[0]),
                (weight_parts.at[wrap(tp - 1)], weights.at[1]),
                (weight_parts.at[tp], weights.at[2]),
            )
        )
    ]
    for copy in late:
        copy.start()
    greet(brief_partners() + (ahead, behind, across))
    clock = Clock()
    out_steps = plane_scatter_steps(post, out_parts, combined, out_scratch)
    out_due = next(out_steps)

    lines = back[256:, :]
    grad_gates = jnp.concatenate(
        [lines[:, :256] + lines[:, 256:512], lines[:, 512:768] + lines[:, 768:]], axis=0
    )
    probs = gates[...]
    grad_logits = probs * (grad_gates - jnp.sum(probs * grad_gates, axis=0, keepdims=True))
    grad_two = back[:256, :]
    logit_pieces = split_three(grad_logits)
    for piece in logit_pieces:
        grad_two = grad_two + lax.dot_general(
            piece, router[...], CONTRACT_ROWS, preferred_element_type=F32
        )
    total = residual[...]
    scale = row_scale(total)
    plain = total * scale
    grad_gain_two = jnp.sum(grad_two * plain, axis=0, keepdims=True)
    grad_two = grad_two * wide(gain_two[...])
    grad_total = cotangent[...].astype(F32) + scale * (
        grad_two - plain * jnp.mean(grad_two * plain, axis=1, keepdims=True)
    )
    grad_residual[...] = grad_total
    grad_all[tp] = grad_total.astype(BF16)
    clock.spend(4.0)

    bounds = document_bounds(segments[...], live_mask[...])
    keys_sum[...] = jnp.zeros_like(keys_sum)
    values_sum[...] = jnp.zeros_like(values_sum)
    output_sum[...] = jnp.zeros_like(output_sum)
    query_gain_sum[...] = jnp.zeros_like(query_gain_sum)

    def attention(place):
        rows = block_rows(place)
        grad = grad_all[place]
        output_sum[...] += lax.dot_general(
            mixed[rows, :], grad, CONTRACT_ROWS, preferred_element_type=F32
        )
        grad_mixed = lax.dot_general(
            grad, output_weight[...], CONTRACT_LAST, preferred_element_type=F32
        ).astype(BF16)
        bias = score_bias(
            bounds,
            place * 256 + lax.broadcasted_iota(jnp.int32, (1, 256), 1),
            lax.broadcasted_iota(jnp.int32, (1024, 1), 0),
        )
        clock.spend(0.8)
        grad_query = yield from attend_back_block(
            query[rows, :], grad_mixed, keys[...], values[...], bias, keys_sum, values_sum, clock
        )
        for lanes in (slice(0, 128), slice(128, 256)):
            grad_raw, grad_gain = head_back(
                grad_query[:, lanes],
                raw[rows, lanes],
                both_heads(query_gain[...]),
                cosine[rows, :],
                sine[rows, :],
            )
            low[rows, lanes] = grad_raw.astype(BF16)
            query_gain_sum[...] += grad_gain
        yield clock.spend(0.5)

    def make(offset):
        rows = block_rows(wrap(tp + offset))
        total = lax.dot_general(
            low[rows, :256], query_weight[...], CONTRACT_LAST, preferred_element_type=F32
        )
        total = total + lax.dot_general(
            low[rows, 256:384], key_weight[...], CONTRACT_LAST, preferred_element_type=F32
        )
        total = total + lax.dot_general(
            low[rows, 384:], value_weight[...], CONTRACT_LAST, preferred_element_type=F32
        )
        part = parts.at[(2, 1, -1, 0).index(offset)]
        part[...] = total.astype(BF16)
        yield clock.spend(0.8)
        return part

    def finish(own, first, second):
        grad_one = own[...].astype(F32) + first[...].astype(F32) + second[...].astype(F32)
        hidden = inputs[...].astype(F32)
        scale = row_scale(hidden)
        plain = hidden * scale
        grad_one = grad_one * wide(gain_one[...])
        grad_inputs[...] = (
            grad_residual[...]
            + scale * (grad_one - plain * jnp.mean(grad_one * plain, axis=1, keepdims=True))
        ).astype(BF16)

    def router_gradient():
        normed_pieces = split_three(plain * wide(gain_two[...]))
        total = jnp.zeros((32, 1024), F32)
        for first, second in ((0, 0), (0, 1), (1, 0), (1, 1), (0, 2), (2, 0)):
            total = total + jnp.dot(
                logit_pieces[first], normed_pieces[second], preferred_element_type=F32
            )
        return total

    gain_rows = small.at[brief_number(16)]
    head_rows = small.at[brief_number(17)]

    def fill_router():
        grad_router = router_gradient()
        small[...] = jnp.zeros_like(small)
        for part in range(8):
            lanes = slice(part * 128, (part + 1) * 128)
            small[brief_number(2 * part)] = grad_router[:16, lanes]
            small[brief_number(2 * part + 1)] = grad_router[16:, lanes]
            gain_rows[8 + part : 9 + part, :] = grad_gain_two[:, lanes]

    def fill_small(weights, grad_key_gain):
        grad_gain_one = jnp.zeros((8, 1024), F32)
        ones = jnp.ones((8, 128), BF16)
        parts = [query_weight[:, :128], query_weight[:, 128:], key_weight[...], value_weight[...]]
        for number, part in enumerate(parts):
            product = weights[:, number * 128 : (number + 1) * 128] * part.astype(F32)
            for piece in split_float(product):
                grad_gain_one = grad_gain_one + lax.dot_general(
                    ones, piece, CONTRACT_LAST, preferred_element_type=F32
                )
        grad_gain_one = grad_gain_one[:1] / wide(gain_one[...])
        for part in range(8):
            gain_rows[part : part + 1, :] = grad_gain_one[:, part * 128 : (part + 1) * 128]
        head_rows[0:1, :] = query_gain_sum[...]
        head_rows[1:2, :] = grad_key_gain

    def attention_steps():
        filled, early_line = [], []

        def send_line(part, slots):
            return [
                post.go(part, at(slots, number), partner)
                for number, partner in enumerate((ahead, behind, across))
            ]

        def arrived(place):
            if not filled:
                filled.append(place)
                fill_router()
                early_line.extend(send_line(at(small, 0), small_early))
                for copy in late:
                    copy.wait()
            yield from attention(place)

        yield from line_gather_steps(
            post, grad_all.at[tp], grad_all, clock, 11.5, 17.5, arrived
        )
        grad_raw, grad_key_gain = head_back(
            (keys_sum[0] + exchange(keys_sum[1])) * 0.125,
            raw[:, 256:],
            both_heads(key_gain[...]),
            cosine[...],
            sine[...],
        )
        low[:, 256:384] = grad_raw.astype(BF16)
        low[:, 384:] = (values_sum[0] + exchange(values_sum[1])).astype(BF16)
        weights = lax.dot_general(
            normed[...], low[...], CONTRACT_ROWS, preferred_element_type=F32
        )
        fill_small(weights, grad_key_gain)
        line = early_line + send_line(at(small, 1, 0, pl.ds(0, 2)), small_late)
        fill_dense(weights)
        now = clock.spend(8.0)
        yield from side_by_side(
            (now, dense_steps(now)),
            (now, small_steps(now, line)),
            (now, line_scatter_steps(post, make, far, near, finish, clock, 3.5, 11.5)),
        )

    def fill_dense(weights):
        weights = weights.astype(BF16)
        for part in range(32):
            dense[(*brief_number(part), slice(None), slice(0, 512))] = weights[
                part * 32 : (part + 1) * 32
            ]
        for part in range(4):
            block = output_sum[:, part * 256 : (part + 1) * 256].astype(BF16)
            for piece in range(8):
                dense[(*brief_number(part * 8 + piece), slice(None), slice(512, 768))] = block[
                    piece * 32 : (piece + 1) * 32
                ]

    def dense_steps(begin):
        yield from brief_scatter_steps(post, dense, dense_own, dense_scratch, begin)
        yield from brief_gather_steps(post, dense_own, dense_all, begin + 12.0)

    def small_steps(begin, line):
        for copy in line:
            copy.wait_recv()
        small_total[...] = jnp.zeros_like(small_total)
        for place in range(4):
            small_total[0, place] = small[0, place] + (
                small_early[0, place] + small_early[1, place] + small_early[2, place]
            )
        small_total[1, 0, :2] = small[1, 0, :2] + small_late[0] + small_late[1] + small_late[2]
        yield from brief_scatter_steps(post, small_total, small_own, small_scratch, begin)
        yield from brief_gather_steps(post, small_own, small_all, begin + 12.0)

    def make_weights(offset):
        yield 0.0
        if offset == 2:
            return weight_parts.at[wrap(tp + 2)]
        return weights.at[(1, -1, 0).index(offset)]

    def finish_weights(own, first, second):
        add_rows(weight_sum, [(own, 0), (first, 0), (second, 0)], 0, own.shape[0])

    def weight_steps():
        yield WEIGHTS_AT
        yield from line_scatter_steps(
            post, make_weights, weights_far, weights_near, finish_weights, Clock(WEIGHTS_AT), 14.0, 60.0
        )

    together(attention_steps(), resumed(out_due, out_steps), weight_steps())
    result[...] = (residual[...] + combined[...]).astype(BF16)
    post.finish()


def closing(arguments, number):
    count = 3 * LINE_COPIES + PLANE_COPIES + 4 * BRIEF_COPIES + 6
    return pl.pallas_call(
        closing_kernel,
        out_shape=[
            jax.ShapeDtypeStruct((256, 1024), BF16),
            jax.ShapeDtypeStruct((2, 4, 4, 32, 768), BF16),
            jax.ShapeDtypeStruct((2, 4, 4, SMALL_ROWS, 128), F32),
            jax.ShapeDtypeStruct((256, 1024), BF16),
            jax.ShapeDtypeStruct((3072, 128), F32),
        ],
        in_specs=[VMEM] * 6 + [ANY] * 11 + [VMEM] * 3 + [ANY] * 2 + [VMEM] * 2 + [ANY] * 2,
        out_specs=[VMEM] * 5,
        scratch_shapes=[
            pltpu.VMEM((4, 256, 1024), BF16),
            pltpu.VMEM((256, 1024), F32),
            pltpu.VMEM((1024, 512), BF16),
            pltpu.VMEM((2, 1024, 128), F32),
            pltpu.VMEM((2, 1024, 128), F32),
            pltpu.VMEM((256, 1024), F32),
            pltpu.VMEM((4, 256, 1024), BF16),
            pltpu.VMEM((256, 1024), BF16),
            pltpu.VMEM((2, 256, 1024), BF16),
            pltpu.VMEM((2, 4, 4, 32, 768), BF16),
            pltpu.VMEM((32, 768), BF16),
            pltpu.VMEM((2, 4, 4, SMALL_ROWS, 128), F32),
            pltpu.VMEM((SMALL_ROWS, 128), F32),
            pltpu.VMEM((3, 4, 4, SMALL_ROWS, 128), F32),
            pltpu.VMEM((3, 2, SMALL_ROWS, 128), F32),
            pltpu.VMEM((2, 4, 4, SMALL_ROWS, 128), F32),
            pltpu.VMEM((1, 128), F32),
            pltpu.VMEM((3, 3072, 128), BF16),
            pltpu.VMEM((3072, 128), BF16),
            pltpu.VMEM((2, 3072, 128), BF16),
            pltpu.VMEM((1024, 256), BF16),
            pltpu.VMEM((1024, 128), BF16),
            pltpu.VMEM((1024, 128), BF16),
            pltpu.VMEM((1024, 256), BF16),
            pltpu.VMEM((1024, 256), BF16),
            pltpu.VMEM((1024, 128), BF16),
            pltpu.VMEM((1024, 128), BF16),
            pltpu.VMEM((1024, 384), F32),
            pltpu.VMEM((1024, 1024), BF16),
            pltpu.VMEM((256, 1024), BF16),
            pltpu.VMEM((256, 1024), BF16),
            pltpu.VMEM((1024, 128), F32),
            pltpu.VMEM((1024, 128), F32),
            pltpu.VMEM((256, 1024), F32),
            pltpu.SemaphoreType.DMA((16,)),
        ]
        + plane_scatter_scratch(256, 1024, BF16)
        + brief_scatter_scratch(32, 768, BF16)
        + brief_scatter_scratch(SMALL_ROWS, 128, F32)
        + [pltpu.SemaphoreType.DMA((count,)), pltpu.SemaphoreType.DMA((count,))],
        compiler_params=pltpu.CompilerParams(
            collective_id=number, has_side_effects=True, vmem_limit_bytes=63 << 20
        ),
        name="closing",
    )(*arguments)


def finish_kernel(
    dense_far, weights_far, result_far, small_far, inputs_far,
    result, grad_inputs, grad_query, grad_key, grad_value, grad_output, grad_gate, grad_up,
    grad_down, gain_one, gain_two, query_gain, key_gain, router,
    dense, weights, small, sems,
):
    copies = [
        pltpu.make_async_copy(src, dst, sems.at[number])
        for number, (src, dst) in enumerate(
            (
                (weights_far, weights), (dense_far, dense), (small_far, small),
                (inputs_far, grad_inputs), (result_far, result),
            )
        )
    ]
    for copy in copies:
        copy.start()
    copies[0].wait()
    grad_gate[0] = weights[:1024, :]
    grad_up[0] = weights[1024:2048, :]
    grad_down[0] = weights[2048:, :].T
    copies[1].wait()
    grad_query[...] = dense[:, :256].astype(F32)
    grad_key[...] = dense[:, 256:384].astype(F32)
    grad_value[...] = dense[:, 384:512].astype(F32)
    for part in range(4):
        grad_output[:, part * 256 : (part + 1) * 256] = dense[
            part * 256 : (part + 1) * 256, 512:
        ].astype(F32)
    copies[2].wait()
    for part in range(8):
        lanes = slice(part * 128, (part + 1) * 128)
        router[:16, lanes] = small[2 * part]
        router[16:, lanes] = small[2 * part + 1]
        gain_one[:, lanes] = small[16, part : part + 1, :]
        gain_two[:, lanes] = small[16, 8 + part : 9 + part, :]
    heads = small[17]
    heads = heads[:, :64] + heads[:, 64:]
    query_gain[...] = heads[0:1]
    key_gain[...] = heads[1:2]
    copies[3].wait()
    copies[4].wait()


def finish_all(arguments):
    return pl.pallas_call(
        finish_kernel,
        out_shape=[
            jax.ShapeDtypeStruct((256, 1024), BF16),
            jax.ShapeDtypeStruct((256, 1024), BF16),
            jax.ShapeDtypeStruct((1024, 256), F32),
            jax.ShapeDtypeStruct((1024, 128), F32),
            jax.ShapeDtypeStruct((1024, 128), F32),
            jax.ShapeDtypeStruct((256, 1024), F32),
            jax.ShapeDtypeStruct((1, 1024, 128), F32),
            jax.ShapeDtypeStruct((1, 1024, 128), F32),
            jax.ShapeDtypeStruct((1, 128, 1024), F32),
            jax.ShapeDtypeStruct((1, 1024), F32),
            jax.ShapeDtypeStruct((1, 1024), F32),
            jax.ShapeDtypeStruct((1, 64), F32),
            jax.ShapeDtypeStruct((1, 64), F32),
            jax.ShapeDtypeStruct((32, 1024), F32),
        ],
        in_specs=[ANY] * 5,
        out_specs=[VMEM] * 14,
        scratch_shapes=[
            pltpu.VMEM((1024, 768), BF16),
            pltpu.VMEM((3072, 128), F32),
            pltpu.VMEM((32, SMALL_ROWS, 128), F32),
            pltpu.SemaphoreType.DMA((5,)),
        ],
        compiler_params=pltpu.CompilerParams(vmem_limit_bytes=60 << 20),
        name="finish_all",
    )(*arguments)


STEPS = ((0, 1), (3, 4), (6, 7), (12, 13), (14, 15), (10, 11), (8, 9), (2, 5))
GROUP = 4


def experts_kernel(
    block, grads, gate_all, up, down,
    rows_all, out_parts, back_sum, weight_parts,
    rows_in, grads_in, both_full, down_full, both_sum, down_sum, rows_own, grads_own, gates_own,
    select, weighted, grad_rows, grad_gates, mine, other, stage, out_stage,
    b_far, b_near, a_far, a_near, line, send_sems, recv_sems, credit, load_sems, store_sems, weight_sems, own_sem,
):
    a, b, core = plane_place()
    me = lax.axis_index("ep")
    ahead_a, behind_a, ahead_b, behind_b, sibling = plane_partners()
    here = [plane_index(a + place[0], b + place[1], core) for place in ARRIVAL]
    there = [plane_index(b + place[0], a + place[1], 1 - core) for place in ARRIVAL]
    lane_row = lax.rem(me, 16)
    upper = me >= 16
    tp = lax.axis_index("tp")
    ahead, behind = line_partners()
    greet(plane_partners() + (ahead, behind))
    post = Post(send_sems, recv_sems)
    go = post.go
    events, held = plane_gather_events(post, block, rows_all)
    events[0][1]()
    own_copy = pltpu.make_async_copy(block, stage.at[0], own_sem)
    own_copy.start()
    before_me, after_me = wrap(tp - 1), wrap(tp + 1)

    def up_part(place, rows=slice(None)):
        return at(both_full, rows, pl.ds(pl.multiple_of(512 + place * 128, 128), 128))

    def down_part(place, first=0, count=128):
        return at(down_full, pl.ds(pl.multiple_of(place * 128 + first, 64), count))

    up_near = (
        post.go(up, up_part(tp), ahead), post.go(up, up_part(tp), behind)
    )
    down_near = (
        post.go(down, down_part(tp), ahead), post.go(down, down_part(tp), behind)
    )
    up_top, up_bottom = up_part(before_me, pl.ds(0, 512)), up_part(after_me, pl.ds(512, 512))
    up_far = (
        post.prepare(up_top, up_top, ahead), post.prepare(up_bottom, up_bottom, behind)
    )
    down_top, down_bottom = down_part(before_me, 0, 64), down_part(after_me, 64, 64)
    down_far = (
        post.prepare(down_top, down_top, ahead), post.prepare(down_bottom, down_bottom, behind)
    )

    def relay(near, far):
        for one, other_one in zip(near, far, strict=True):
            one.wait_recv()
            other_one.start()

    weight_loads = [
        pltpu.make_async_copy(
            gate_all.at[part], both_full.at[:, part * 128 : (part + 1) * 128], weight_sems.at[part]
        )
        for part in range(4)
    ]
    weight_loads.append(pltpu.make_async_copy(up, up_part(tp)(), weight_sems.at[4]))
    weight_loads.append(pltpu.make_async_copy(down, down_part(tp)(), weight_sems.at[5]))
    for copy in weight_loads:
        copy.start()
    both_sum[...] = jnp.zeros_like(both_sum)
    down_sum[...] = jnp.zeros_like(down_sum)

    def blocks(step):
        first, second = STEPS[step]
        return (here[first], here[second], there[first], there[second])

    loads, crossing, stores = {}, {}, {}
    for step in range(len(STEPS)):
        slot = step % 2
        loads[step], stores[step] = [], []
        crossing[step] = [
            post.prepare(at(stage, part), at(other, slot, part), sibling) for part in range(2)
        ]
        for part, index in enumerate(blocks(step)):
            loads[step] += [
                Local(
                    at(rows_all, index), at(rows_in, slot, part), at(load_sems, slot, 0, part)
                ),
                Local(at(grads, index), at(grads_in, slot, part), at(load_sems, slot, 1, part)),
            ]
            stores[step].append(
                Local(at(out_stage, part), at(out_parts, index), at(store_sems, part))
            )

    def load(step):
        for place in STEPS[step]:
            held[place].wait_recv()
        for copy in loads[step]:
            copy.start()

    def take(step):
        for part, place in enumerate(STEPS[step]):
            crossing[step][part].wait_recv()
            add_rows(
                mine.at[place], [(mine.at[place], 0), (other.at[step % 2, part], 0)], 0, rows
            )
        if step + 2 < len(STEPS):
            pl.semaphore_signal(credit, inc=1, device_id=sibling, device_id_type=MESH)

    rows = a_far.shape[0]
    top, bottom = halves(a_far)
    high = top.size
    low = rows - high
    far_b, near_b = {}, {}

    def number_of(k, j):
        return ARRIVAL.index((OFFSETS[k], OFFSETS[j]))

    def slot_of(k, j):
        return mine.at[number_of(k, j)]

    def far_step(k):
        part = number_of(k, 0)
        far_b[k] = (
            go(at(mine, part, top), at(b_far, k, top), ahead_b),
            go(at(mine, part, bottom), at(b_far, k, bottom), behind_b),
        )

    def near_step(k):
        far = b_far.at[k]
        far_b[k][0].wait_recv()
        part = slot_of(k, 1)
        add_rows(part, [(part, 0), (far, 0)], 0, high)
        first = go(at(mine, number_of(k, 1)), at(b_near, 0, k), ahead_b)
        far_b[k][1].wait_recv()
        part = slot_of(k, 2)
        add_rows(part, [(part, high), (far, high)], high, low)
        near_b[k] = (first, go(at(mine, number_of(k, 2)), at(b_near, 1, k), behind_b))

    def before(step):
        for copy in loads[step]:
            copy.wait()

    def between(step):
        if step > 0:
            for copy in crossing[step - 1]:
                copy.wait_send()
            for copy in stores[step - 1]:
                copy.wait()
        onward({0: (4,), 1: (6,), 2: (7, 8, 9), 3: (10, 11)}.get(step, ()))
        if step + 1 < len(STEPS):
            load(step + 1)
        if step > 0:
            take(step - 1)
        if step == 4:
            far_step(2)
            far_step(3)
        if step == 5:
            far_step(0)
            far_step(1)
            near_step(3)
            near_step(2)
        if step == 6:
            near_step(0)
        if step == 7:
            near_step(1)

    def onward(numbers):
        for number in numbers:
            events[number][1]()

    def early(step):
        if step == 0:
            for copy in up_far + down_far:
                copy.wait_recv()

    def after(step):
        onward({0: (5,)}.get(step, ()))
        if step >= 2:
            pl.semaphore_wait(credit, 1)
        for copy in crossing[step] + stores[step]:
            copy.start()

    def at_step(step, task):
        for number in range(len(STEPS)):

            @pl.when(step == number)
            def _(number=number):
                task(number)

    def from_table(step, table):
        value = step * 0 + table[0]
        for number in range(1, len(table)):
            value = jnp.where(step == number, table[number], value)
        return value

    own_copy.wait()
    own_copy = pltpu.make_async_copy(stage.at[0], rows_all.at[me], own_sem)
    own_copy.start()
    onward((1, 2))
    own_copy.wait()
    load(0)
    relay(up_near, up_far)
    onward((3,))
    relay(down_near, down_far)
    for copy in weight_loads:
        copy.wait()
    extra_row = lax.broadcasted_iota(jnp.int32, (EXTRA, 1024), 0) == lane_row

    def one_step(step, carry):
        slot = lax.rem(step, 2)
        at_step(step, before)
        earlier = (
            lax.broadcasted_iota(jnp.int32, (256, 256), 0)
            <= lax.broadcasted_iota(jnp.int32, (256, 256), 1)
        ).astype(BF16)
        place = lax.broadcasted_iota(jnp.int32, (SLOTS, 256), 0).astype(F32)
        for part in range(GROUP):
            extras = jnp.where(extra_row, rows_in[slot, part, 256:, :].astype(F32), 0.0)
            extras = jnp.sum(extras, axis=0, keepdims=True)
            gates = jnp.where(
                upper, extras[:, 512:768] + extras[:, 768:], extras[:, :256] + extras[:, 256:512]
            )
            named = jnp.broadcast_to(gates, (16, 256)) > 0.0
            rank = jnp.dot(named.astype(BF16), earlier, preferred_element_type=F32)[:1] - 1.0
            chosen = (place == rank) & (gates > 0.0)
            chosen_low = chosen.astype(BF16)
            at = slice(part * SLOTS, (part + 1) * SLOTS)
            select[at, :] = chosen_low
            rows_own[at, :] = jnp.dot(
                chosen_low, rows_in[slot, part, :256, :], preferred_element_type=F32
            ).astype(BF16)
            grads_own[at, :] = jnp.dot(
                chosen_low, grads_in[slot, part], preferred_element_type=F32
            ).astype(BF16)
            gates_own[at, :] = jnp.sum(jnp.where(chosen, gates, 0.0), axis=1, keepdims=True)

        at_step(step, early)
        both_pre = jnp.dot(rows_own[...], both_full[...], preferred_element_type=F32)
        gate_pre, up_pre = both_pre[:, :512], both_pre[:, 512:]
        sigmoid = 1.0 / (1.0 + jnp.exp(-gate_pre))
        silu = gate_pre * sigmoid
        act = (silu * up_pre).astype(BF16)
        out = jnp.dot(act, down_full[...], preferred_element_type=F32).astype(BF16).astype(F32)
        gate_factor = gates_own[...]
        grads_float = grads_own[...].astype(F32)
        grad_gates[...] = jnp.sum(grads_float * out, axis=1, keepdims=True)
        weighted[...] = (gate_factor * out).astype(BF16)
        grad_out = (gate_factor * grads_float).astype(BF16)
        grad_act = lax.dot_general(
            grad_out, down_full[...], CONTRACT_LAST, preferred_element_type=F32
        )
        down_sum[...] += lax.dot_general(
            grad_out, act, CONTRACT_ROWS, preferred_element_type=F32
        )
        grad_gate_pre = grad_act * up_pre * sigmoid * (1.0 + gate_pre * (1.0 - sigmoid))
        grad_up_pre = grad_act * silu
        grad_pre = jnp.concatenate(
            [grad_gate_pre.astype(BF16), grad_up_pre.astype(BF16)], axis=1
        )
        both_sum[...] += lax.dot_general(
            rows_own[...], grad_pre, CONTRACT_ROWS, preferred_element_type=F32
        )
        grad_rows[...] = lax.dot_general(
            grad_pre, both_full[...], CONTRACT_LAST, preferred_element_type=F32
        ).astype(BF16)
        at_step(step, between)
        nothing = jnp.zeros((1, 512), F32)
        slots = [from_table(step, [pair[part] for pair in STEPS]) for part in range(2)]
        for part in range(GROUP):
            at = slice(part * SLOTS, (part + 1) * SLOTS)
            chosen_low = select[at, :]
            out_stage[part] = lax.dot_general(
                chosen_low, weighted[at], CONTRACT_ROWS, preferred_element_type=F32
            ).astype(BF16)
            target = mine.at[slots[part]] if part < 2 else stage.at[part - 2]
            target[:256, :] = lax.dot_general(
                chosen_low, grad_rows[at], CONTRACT_ROWS, preferred_element_type=F32
            ).astype(BF16)
            spread = jnp.sum(chosen_low.astype(F32) * grad_gates[at], axis=0, keepdims=True)
            upper_bits = spread.astype(BF16).astype(F32)
            both = jnp.concatenate([upper_bits, spread - upper_bits], axis=1)
            line_now = jnp.concatenate(
                [jnp.where(upper, nothing, both), jnp.where(upper, both, nothing)], axis=1
            )
            target[256:, :] = jnp.where(extra_row, line_now, 0.0).astype(BF16)
        at_step(step, after)
        return carry

    lax.fori_loop(0, len(STEPS), one_step, 0)
    last = len(STEPS) - 1

    def weight_steps():
        for part in range(4):
            yield 2.5 + part
            lanes = slice(part * 128, (part + 1) * 128)
            upper_lanes = slice(512 + part * 128, 512 + (part + 1) * 128)
            line[part, :1024, :] = both_sum[:, lanes].astype(BF16)
            line[part, 1024:2048, :] = both_sum[:, upper_lanes].astype(BF16)
            line[part, 2048:, :] = down_sum[:, lanes].astype(BF16)
            Local(at(line, part), at(weight_parts, part), at(weight_sems, part)).start()
        yield 100.0
        for part in range(4):
            Local(at(line, part), at(weight_parts, part), at(weight_sems, part)).wait()

    def back_steps():
        yield 0.0
        take(last)
        far_a, near_a = [], []
        for k in range(4):
            yield (2.0, 4.0, 8.0, 12.0)[k]
            part = slot_of(k, 3)
            near_b[k][0].wait_recv()
            near_b[k][1].wait_recv()
            base = [part, b_near.at[0, k], b_near.at[1, k]]
            first_rows = [(ref, 0) for ref in base]
            last_rows = [(ref, high) for ref in base]
            if k == 0:
                add_rows(part, first_rows, 0, high)
                add_rows(part, last_rows, high, low)
                far_a = [
                    go(part.at[top], a_far.at[top], ahead_a),
                    go(part.at[bottom], a_far.at[bottom], behind_a),
                ]
            elif k == 1:
                far_a[0].wait_recv()
                add_rows(part, first_rows + [(a_far, 0)], 0, high)
                add_rows(part, last_rows, high, low)
                near_a.append(go(part, a_near.at[0], ahead_a))
            elif k == 2:
                far_a[1].wait_recv()
                add_rows(part, first_rows, 0, high)
                add_rows(part, last_rows + [(a_far, high)], high, low)
                near_a.append(go(part, a_near.at[1], behind_a))
            else:
                near_a[0].wait_recv()
                near_a[1].wait_recv()
                add_rows(
                    back_sum, first_rows + [(a_near.at[0], 0), (a_near.at[1], 0)], 0, rows
                )

    together(back_steps(), weight_steps())
    for copy in stores[last]:
        copy.wait()
    waited = [copy for step in range(last) for copy in crossing[step]]
    for copy in post.started:
        if not any(copy is other_copy for other_copy in waited):
            copy.wait_send()


def run_experts(block, grads, gate_all, up, down, number):
    rows, columns = block.shape
    sources = grads.shape[0]
    count = GROUP * SLOTS
    copies = PLANE_COPIES + 16 + 8 + 8 + 4 + 2 * LINE_COPIES
    whole = (rows, columns)
    return pl.pallas_call(
        experts_kernel,
        out_shape=[
            jax.ShapeDtypeStruct((sources,) + whole, BF16),
            jax.ShapeDtypeStruct((sources, 256, columns), BF16),
            jax.ShapeDtypeStruct(whole, F32),
            jax.ShapeDtypeStruct((4, 3072, 128), BF16),
        ],
        in_specs=[ANY] * 5,
        out_specs=[ANY, ANY, VMEM, ANY],
        scratch_shapes=[
            pltpu.VMEM((2, GROUP) + whole, BF16),
            pltpu.VMEM((2, GROUP, 256, columns), BF16),
            pltpu.VMEM((1024, 1024), BF16),
            pltpu.VMEM((512, 1024), BF16),
            pltpu.VMEM((1024, 1024), F32),
            pltpu.VMEM((1024, 512), F32),
            pltpu.VMEM((count, 1024), BF16),
            pltpu.VMEM((count, 1024), BF16),
            pltpu.VMEM((count, 1), F32),
            pltpu.VMEM((count, 256), BF16),
            pltpu.VMEM((count, 1024), BF16),
            pltpu.VMEM((count, 1024), BF16),
            pltpu.VMEM((count, 1), F32),
            pltpu.VMEM((16,) + whole, BF16),
            pltpu.VMEM((2, 2) + whole, BF16),
            pltpu.VMEM((2,) + whole, BF16),
            pltpu.VMEM((GROUP, 256, columns), BF16),
            pltpu.VMEM((4,) + whole, BF16),
            pltpu.VMEM((2, 4) + whole, BF16),
            pltpu.VMEM(whole, BF16),
            pltpu.VMEM((2,) + whole, BF16),
            pltpu.VMEM((4, 3072, 128), BF16),
            pltpu.SemaphoreType.DMA((copies,)),
            pltpu.SemaphoreType.DMA((copies,)),
            pltpu.SemaphoreType.REGULAR,
            pltpu.SemaphoreType.DMA((2, 2, GROUP)),
            pltpu.SemaphoreType.DMA((GROUP,)),
            pltpu.SemaphoreType.DMA((12,)),
            pltpu.SemaphoreType.DMA,
        ],
        compiler_params=pltpu.CompilerParams(
            collective_id=number, has_side_effects=True, vmem_limit_bytes=63 << 20
        ),
        name="run_experts",
    )(block, grads, gate_all, up, down)


def rotary_constants():
    position = np.arange(SEQ_LEN, dtype=np.float32)
    power = -(np.arange(32, dtype=np.float32) * np.float32(2.0)) / np.float32(64.0)
    frequency = np.float32(10000.0) ** power
    angles = position[:, None] * frequency[None, :]
    cosine, sine = np.cos(angles), np.sin(angles)
    return (np.tile(cosine, (1, 4)), np.concatenate([-sine, sine, -sine, sine], axis=1))


def shards(
    inputs,
    first_gain,
    query_weight,
    key_weight,
    value_weight,
    query_gain,
    key_gain,
    output_weight,
    second_gain,
    router_weight,
    gate_weight,
    up_weight,
    down_weight,
    segments,
    live_mask,
    routes,
    cotangent,
):
    gain_one, gain_two = first_gain.reshape(8, 128), second_gain.reshape(8, 128)
    query_scale, key_scale = query_gain.reshape(1, -1), key_gain.reshape(1, -1)
    cosine, sine = rotary_constants()
    seg_row, live_row = segments.reshape(1, -1), live_mask.reshape(1, -1)
    router = router_weight.T
    (
        normed, raw, query, keys, values, mixed, residual, block, gates, grad_all, gate_all,
    ) = opening(
        (
            inputs, gain_one, query_weight, key_weight, value_weight, query_scale, key_scale,
            cosine, sine, seg_row, live_row, output_weight, gain_two, router, routes.T,
            cotangent, gate_weight[0],
        ),
        1,
    )
    rows_all, out_parts, back, weight_parts = run_experts(
        block, grad_all, gate_all, up_weight[0], down_weight[0], 2
    )
    grad_inputs, dense, small, result, weight_sums = closing(
        (
            back, residual, gates, cotangent, gain_two, router, query, keys, values, mixed,
            output_weight, query_weight, key_weight, value_weight, raw, normed.reshape(1024, 1024),
            inputs, gain_one, query_scale, key_scale, cosine, sine, seg_row,
            live_row, out_parts, weight_parts,
        ),
        4,
    )
    (
        result, grad_inputs, grad_query, grad_key, grad_value, grad_output, grad_gate, grad_up,
        grad_down, grad_gain_one, grad_gain_two, grad_query_gain, grad_key_gain, grad_router,
    ) = finish_all(
        (
            dense.reshape(1024, 768), weight_sums, result,
            small.reshape(32, SMALL_ROWS, 128), grad_inputs,
        )
    )
    return (
        result,
        grad_inputs,
        grad_gain_one.reshape(-1),
        grad_query,
        grad_key,
        grad_value,
        grad_query_gain.reshape(-1),
        grad_key_gain.reshape(-1),
        grad_output,
        grad_gain_two.reshape(-1),
        grad_router.T,
        grad_gate,
        grad_up,
        grad_down,
    )


def solution(mesh):
    return jax.shard_map(
        shards,
        mesh=mesh,
        in_specs=(
            P(("ep", "tp"), None),
            P(),
            P(None, "tp"),
            P(None, "tp"),
            P(None, "tp"),
            P(),
            P(),
            P("tp", None),
            P(),
            P(),
            P("ep", None, "tp"),
            P("ep", None, "tp"),
            P("ep", "tp", None),
            P("ep"),
            P("ep"),
            P(("ep", "tp"), None),
            P(("ep", "tp"), None),
        ),
        out_specs=(
            P(("ep", "tp"), None),
            P(("ep", "tp"), None),
            P(),
            P(None, "tp"),
            P(None, "tp"),
            P(None, "tp"),
            P(),
            P(),
            P("tp", None),
            P(),
            P(),
            P("ep", None, "tp"),
            P("ep", None, "tp"),
            P("ep", "tp", None),
        ),
        check_vma=False,
    )
```
